32 devices in a mesh: section: 4 (over y, x), dp: 8 (over z, core).
Axes of the slice: x: 2, y: 2, z: 4, core: 2. Of those that a mesh axis runs over, the one named last changes fastest.
Arguments:
- patches: bfloat16 [2, 2048, 192], P(None, 'dp'), may hold values from -6 to 6
- lead_times: float32 [2, 8], P(None, 'dp'), may hold values from 0.1 to 1
- short_lengths: int32 [8, 4], P('dp'), may hold values from 1 to 64, 224 in all within a row
- cotangent: bfloat16 [2, 2048, 1024], P(None, 'dp'), may hold values from -6 to 6
- bank: bfloat16 [4, 4096, 1024], P('section', 'dp'), may hold values from -0.25 to 0.25
- patch_w: bfloat16 [48, 4, 1024], replicated, may hold values from -3 to 3
- patch_b: bfloat16 [48, 1024], replicated, may hold values from -3 to 3
- var_emb: bfloat16 [48, 1024], replicated, may hold values from -3 to 3
- agg_query: bfloat16 [1024], replicated, may hold values from -6 to 6
- agg_bias: bfloat16 [3, 1024], replicated, may hold values from -2 to 2
- lead_embed: bfloat16 [2, 1024], replicated, may hold values from -3 to 3
- norm_gain: bfloat16 [2, 1024], replicated, may hold values from 0.5 to 1.5
- norm_bias: bfloat16 [2, 1024], replicated, may hold values from -1.5 to 1.5
- attn_bias: bfloat16 [3, 1024], replicated, may hold values from -2 to 2
- fc1_bias: bfloat16 [4096], replicated, may hold values from -2 to 2
- fc2_bias: bfloat16 [1024], replicated, may hold values from -2 to 2
Outputs:
- output: bfloat16 [2, 2048, 1024], P(None, 'dp', 'section')
- grad_patches: float32 [2, 2048, 192], P(None, 'dp', 'section')
- grad_bank: float32 [4, 4096, 1024], P('section', 'dp')
- grad_patch_w: float32 [48, 4, 1024], replicated
- grad_patch_b: float32 [48, 1024], replicated
- grad_var_emb: float32 [48, 1024], replicated
- grad_agg_query: float32 [1024], replicated
- grad_agg_bias: float32 [3, 1024], replicated
- grad_lead_embed: float32 [2, 1024], replicated
- grad_norm_gain: float32 [2, 1024], replicated
- grad_norm_bias: float32 [2, 1024], replicated
- grad_attn_bias: float32 [3, 1024], replicated
- grad_fc1_bias: float32 [4096], replicated
- grad_fc2_bias: float32 [1024], replicated
The draws below stay inside these ranges and needn't reach their ends.
Inputs may be any that keep to these rules, and one draw needn't show every extreme that they name: `short_lengths`: the 4 lengths of one index of dp sum to 224; the largest is 64 in every row.
All inputs are finite; a program needn't handle non-finite values.
Results may differ from the reference program's by a relative error of at most 0.03.
Values may be sent and summed in bfloat16 or wider, within the bound.
A program may use at most 448 MiB of HBM per device.

```python
import math
from functools import partial
import jax
import jax.numpy as jnp
import numpy as np
from jax import lax

D = 1024
HEADS = 16
HEAD = 64
FF = 4096
VARS = 48
PIX = 4
TOK_MB = 256
SLOTS = 4
MICRO = 2
TOKENS_MB = 2048
N_SECTION = 4
N_DP = 8


def steps_of(own_key, dims, split, low, largest):
    gain = 1.0
    for axis_at, parts in split:
        draws = jax.random.uniform(jax.random.fold_in(jax.random.fold_in(own_key, 6), axis_at), (parts,), jnp.float32, low / len(split), largest / len(split))
        gain = gain * jnp.repeat(jnp.exp(draws), dims[axis_at] // parts).reshape((-1,) + (1,) * (len(dims) - 1 - axis_at))
    return gain


def split_up(number_of, total, most, skew):
    portions = [(1 << 20) // math.isqrt(standing ** skew) + 1 for standing in range(2, number_of + 1)]
    spare, holding = total - most - (number_of - 1), [1] * (number_of - 1)
    while spare > 0:
        candidates = [i for i in range(number_of - 1) if holding[i] < most]
        mass, remaining = sum([portions[i] for i in candidates]), spare
        for i in candidates:
            addition = min(most - holding[i], max(1, remaining * portions[i] // mass), spare)
            holding[i] = holding[i] + addition
            spare = spare - addition
    return np.array([most] + holding)


def ragged_sizes(own_key, number_of, total, most, skew):
    if number_of == 2:
        one = jax.random.randint(own_key, (), max(1, total - most), min(most, total - 1) + 1)
        return jnp.stack([one, total - one])
    tallies = jnp.asarray(split_up(number_of, total, most, skew), jnp.int32)
    twos = (number_of - 1) // 2
    giver, taker = tallies[1:1 + 2 * twos:2], tallies[2:2 + 2 * twos:2]
    room = jnp.minimum(giver - 1, most - taker)
    moved = jax.random.randint(jax.random.fold_in(own_key, 1), (twos,), 0, 1 << 20) % (room + 1)
    tallies = tallies.at[1:1 + 2 * twos:2].set(giver - moved).at[2:2 + 2 * twos:2].set(taker + moved)
    return tallies[jax.random.permutation(jax.random.fold_in(own_key, 2), number_of)]


def normal_values(own_key, shape, scale, most, pieces=(), kind=jnp.bfloat16):
    level = steps_of(own_key, shape, pieces, -0.22, 0.18) if pieces else 1.0
    values = jax.random.normal(own_key, shape, jnp.float32) * scale * level
    return jnp.minimum(jnp.maximum(values, -most), most).astype(kind)


def setup_inputs(seed: int = 0) -> dict:
    arg_keys = jax.random.split(jax.random.key(seed), 17)
    return {
        "patches": normal_values(arg_keys[0], (MICRO, TOKENS_MB, VARS * PIX), 1.0, 6.0, ((1, 8),)),
        "lead_times": jnp.clip(0.1 + 0.9 * jax.random.uniform(arg_keys[1], (MICRO, N_DP), jnp.float32) ** steps_of(arg_keys[1], (MICRO, N_DP), ((1, 8),), -0.2, 0.2), 0.1, 1.0),
        "short_lengths": jax.vmap(lambda own: ragged_sizes(own, SLOTS, TOK_MB * 7 // 8, TOK_MB // 4, 1))(jax.random.split(arg_keys[2], N_DP)).reshape((N_DP, SLOTS)).astype(jnp.int32),
        "cotangent": normal_values(arg_keys[3], (MICRO, TOKENS_MB, D), 1.0, 6.0, ((1, 8),)),
        "bank": normal_values(arg_keys[4], (N_SECTION, 4 * D, D), (D // 2) ** -0.5, 0.25, ((0, 4), (1, 8))),
        "patch_w": normal_values(arg_keys[5], (VARS, PIX, D), PIX ** -0.5, 3.0),
        "patch_b": normal_values(arg_keys[6], (VARS, D), 0.5, 3.0),
        "var_emb": normal_values(arg_keys[7], (VARS, D), 0.5, 3.0),
        "agg_query": normal_values(arg_keys[8], (D,), 1.0, 6.0),
        "agg_bias": normal_values(arg_keys[9], (3, D), 0.3, 2.0),
        "lead_embed": normal_values(arg_keys[10], (2, D), 0.5, 3.0),
        "norm_gain": jnp.clip(1.0 + 0.1 * jax.random.normal(arg_keys[11], (2, D), jnp.float32), 0.5, 1.5).astype(jnp.bfloat16),
        "norm_bias": normal_values(arg_keys[12], (2, D), 0.2, 1.5),
        "attn_bias": normal_values(arg_keys[13], (3, D), 0.3, 2.0),
        "fc1_bias": normal_values(arg_keys[14], (FF,), 0.3, 2.0),
        "fc2_bias": normal_values(arg_keys[15], (D,), 0.3, 2.0),
    }


@jax.custom_vjp
def low(v):
    return lax.optimization_barrier(v.astype(jnp.bfloat16)).astype(jnp.float32)

@jax.custom_vjp
def low_back(v):
    return v

def low_keep(v):
    return (low(v), None)

def low_pass(kept, grad):
    return (grad,)

def back_keep(v):
    return (v, None)

def back_low(kept, grad):
    return (low(grad),)
low.defvjp(low_keep, low_pass)
low_back.defvjp(back_keep, back_low)
highest = lax.Precision.HIGHEST

def matmul(factor_left, factor_right):
    return jnp.dot(factor_left, factor_right, precision=highest)

def norm_layer(stream, gain_row, shift_row):
    centre = stream - lax.optimization_barrier(jnp.mean(stream, axis=-1, keepdims=True))
    spread = lax.optimization_barrier(jnp.mean(centre * centre, axis=-1, keepdims=True))
    return centre * lax.rsqrt(spread + 1e-05) * gain_row + shift_row

def position_table(places):
    half_width = D // 2
    frequency = jnp.exp(-math.log(10000.0) * 2.0 * jnp.arange(half_width, dtype=jnp.float32) / D)
    angles = places.astype(jnp.float32)[:, None] * frequency[None, :]
    return jnp.concatenate([jnp.sin(angles), jnp.cos(angles)], axis=1)

def layout(lengths_row, row_count):
    segment_ends = jnp.cumsum(lengths_row).astype(jnp.int32)
    starts = (segment_ends - lengths_row).astype(jnp.int32)
    places = jnp.arange(row_count, dtype=jnp.int32)
    segment = lax.optimization_barrier(jnp.sum((places[:, None] >= segment_ends[None, :]).astype(jnp.int32), axis=1))
    member = segment[:, None] == jnp.arange(lengths_row.shape[0], dtype=jnp.int32)[None, :]
    offset = lax.optimization_barrier(jnp.sum(jnp.where(member, starts[None, :], 0), axis=1)).astype(jnp.int32)
    offset = jnp.where(segment == lengths_row.shape[0], segment_ends[-1], offset)
    return (segment, places - offset)

def blocks_of(section_bank):
    return tuple((section_bank[number * D:(number + 1) * D] for number in range(4)))

def gelu_exact(values_in):
    return jax.nn.gelu(values_in, approximate=False)

def aggregate(pixel_rows, places, lead_time, weights, patch_w, patch_b, var_emb, agg_query, agg_bias, lead_embed):
    row_count = pixel_rows.shape[0]
    query_row = low(low_back(matmul(agg_query[None, :], weights[0])[0] + agg_bias[0]))
    key_query = jnp.einsum('dhe,he->dh', weights[1].reshape(D, HEADS, HEAD), query_row.reshape(HEADS, HEAD), precision=highest)
    key_query = low(low_back(key_query))
    constant = low(patch_b + var_emb)
    filters = jnp.einsum('vpd,dh->vph', patch_w, key_query, precision=highest)
    offsets = matmul(constant, key_query)
    pixels = pixel_rows.reshape(row_count, VARS, PIX)
    scores = (jnp.einsum('tvp,vph->tvh', pixels, filters, precision=highest) + offsets[None]) / math.sqrt(HEAD)
    attend_low = low(jax.nn.softmax(scores, axis=1))
    weighted = low(attend_low[:, :, :, None] * pixels[:, :, None, :])
    weighted = jnp.transpose(weighted, (0, 2, 1, 3)).reshape(row_count * HEADS, VARS * PIX)
    mixing = jnp.transpose(attend_low, (0, 2, 1)).reshape(row_count * HEADS, VARS)
    pooled = matmul(weighted, patch_w.reshape(VARS * PIX, D)) + matmul(mixing, constant)
    pooled = low(low_back(pooled)).reshape(row_count, HEADS, D)
    heads_out = jnp.einsum('thd,dhe->the', pooled, weights[2].reshape(D, HEADS, HEAD), precision=highest).reshape(row_count, D)
    heads_out = low(low_back(heads_out + agg_bias[1]))
    merged = matmul(heads_out, weights[3]) + agg_bias[2]
    stream = merged + position_table(places) + lead_time * lead_embed[0] + lead_embed[1]
    return low(low_back(stream))

def attend_block(stream, segment, weights, gain_row, shift_row, attn_bias):
    row_count = stream.shape[0]
    normed = low(norm_layer(stream, gain_row, shift_row))
    queries = low(low_back(matmul(normed, weights[0]) + attn_bias[0])).reshape(row_count, HEADS, HEAD)
    key_rows = low(low_back(matmul(normed, weights[1]))).reshape(row_count, HEADS, HEAD)
    values = low(low_back(matmul(normed, weights[2]) + attn_bias[1])).reshape(row_count, HEADS, HEAD)
    scores = low_back(jnp.einsum('qhe,khe->hqk', queries, key_rows, precision=highest) / math.sqrt(HEAD))
    allowed = (segment[:, None] == segment[None, :])[None]
    probabilities = low(jax.nn.softmax(jnp.where(allowed, scores, -1e+30), axis=-1))
    mixed_heads = jnp.einsum('hqk,khe->qhe', probabilities, values, precision=highest).reshape(row_count, D)
    mixed_heads = low(low_back(mixed_heads))
    return low(low_back(stream + matmul(mixed_heads, weights[3]) + attn_bias[2]))

def feed_first(stream, weights, gain_row, shift_row, bias_in):
    normed = low(norm_layer(stream, gain_row, shift_row))
    w_in = jnp.concatenate([weights[0], weights[1]], axis=1)
    w_back = jnp.concatenate([weights[2], weights[3]], axis=0)
    inner_rows = low_back(matmul(normed, w_in) + bias_in)
    active = low(gelu_exact(inner_rows))
    carry_rows = low(stream + matmul(active, w_back))
    return (normed, carry_rows)

def feed_second(normed, carry_rows, weights, bias_in, bias_out):
    normed_use = low_back(normed)
    w_in = jnp.concatenate([weights[0], weights[1]], axis=1)
    w_back = jnp.concatenate([weights[2], weights[3]], axis=0)
    inner_rows = low_back(matmul(normed_use, w_in) + bias_in)
    active = low(gelu_exact(inner_rows))
    return carry_rows + matmul(active, w_back) + bias_out

def row_forward(params, pixel_rows, places, segment, lead_time):
    bank_all, patch_w, patch_b, var_emb, agg_query, agg_bias, lead_embed, norm_gain, norm_bias, attn_bias, fc1_bias, fc2_bias = params
    stream = aggregate(pixel_rows, places, lead_time, blocks_of(bank_all[0]), patch_w, patch_b, var_emb, agg_query, agg_bias, lead_embed)
    stream = attend_block(stream, segment, blocks_of(bank_all[1]), norm_gain[0], norm_bias[0], attn_bias)
    normed, carry_rows = feed_first(stream, blocks_of(bank_all[2]), norm_gain[1], norm_bias[1], fc1_bias[:FF // 2])
    return feed_second(normed, carry_rows, blocks_of(bank_all[3]), fc1_bias[FF // 2:], fc2_bias)

def reference(patches, lead_times, short_lengths, cotangent, bank, patch_w, patch_b, var_emb, agg_query, agg_bias, lead_embed, norm_gain, norm_bias, attn_bias, fc1_bias, fc2_bias):
    row_total = MICRO * N_DP
    short_segment, short_places = jax.vmap(partial(layout, row_count=TOK_MB))(short_lengths)
    long_segment = jnp.zeros((N_DP, TOK_MB), jnp.int32)
    long_places = jnp.broadcast_to(jnp.arange(TOK_MB, dtype=jnp.int32)[None, :], (N_DP, TOK_MB))
    segments = jnp.concatenate([short_segment, long_segment], axis=0)
    places_all = jnp.concatenate([short_places, long_places], axis=0)
    valid_rows = jnp.concatenate([short_segment < SLOTS, jnp.ones((N_DP, TOK_MB), bool)], axis=0)
    pixels = patches.astype(jnp.float32).reshape(row_total, TOK_MB, VARS * PIX)
    leads = lead_times.astype(jnp.float32).reshape(row_total)
    cot_rows = cotangent.reshape(row_total, TOK_MB, D)
    grad_out = jnp.where(valid_rows[:, :, None], cot_rows, jnp.zeros_like(cot_rows)).astype(jnp.float32)
    params = tuple((array_item.astype(jnp.float32) for array_item in (bank, patch_w, patch_b, var_emb, agg_query, agg_bias, lead_embed, norm_gain, norm_bias, attn_bias, fc1_bias, fc2_bias)))

    def whole_layer(params_in, pixels_in):

        def run_row(row_items):
            return row_forward(params_in, *row_items)
        return lax.map(jax.checkpoint(run_row), (pixels_in, places_all, segments, leads))
    outputs, pullback = jax.vjp(whole_layer, params, pixels)
    grad_params, grad_pixels = pullback(grad_out)
    output = outputs.reshape(MICRO, N_DP * TOK_MB, D).astype(jnp.bfloat16)
    grad_patches = grad_pixels.reshape(MICRO, N_DP * TOK_MB, VARS * PIX)
    return (output, grad_patches) + tuple(grad_params)
```

```python
import functools
import math

import jax
import jax.numpy as jnp
from jax import lax
from jax.experimental import pallas as pl
from jax.experimental.pallas import tpu as pltpu
from jax.sharding import PartitionSpec as P

D = 1024
HEADS = 16
HEAD = 64
FF = 4096
VARS = 48
PIX = 4
F32 = jnp.float32
BF = jnp.bfloat16
MESH = pl.DeviceIdType.MESH
ROWS = 512
GROUP = 256
OWN = 128


def mm(a, b):
    return jnp.dot(a, b, preferred_element_type=F32)


def mm_nt(a, b):
    return lax.dot_general(a, b, (((1,), (1,)), ((), ())), preferred_element_type=F32)


def mm_tn(a, b):
    return lax.dot_general(a, b, (((0,), (0,)), ((), ())), preferred_element_type=F32)


def loop(count, body):
    def step(i, carry):
        body(i)
        return carry

    lax.fori_loop(0, count, step, 0)


def at(start, size, unit):
    return pl.ds(pl.multiple_of(start, unit), size)


def iota(shape, axis):
    return lax.broadcasted_iota(jnp.int32, shape, axis)


def normed_rows(x, gain, shift):
    centre = x - jnp.mean(x, axis=1, keepdims=True)
    rs = lax.rsqrt(jnp.mean(centre * centre, axis=1, keepdims=True) + 1e-5)
    return centre * rs * gain + shift


def norm_back(x, g, gain):
    centre = x - jnp.mean(x, axis=1, keepdims=True)
    rs = lax.rsqrt(jnp.mean(centre * centre, axis=1, keepdims=True) + 1e-5)
    xhat = centre * rs
    q = g * gain
    gx = rs * (q - jnp.mean(q, axis=1, keepdims=True) - xhat * jnp.mean(q * xhat, axis=1, keepdims=True))
    return gx, jnp.sum(g * xhat, axis=0, keepdims=True), jnp.sum(g, axis=0, keepdims=True)


def column_sum(x):
    return jnp.sum(x, axis=0, keepdims=True)


class Place:
    def __init__(self):
        self.s = lax.axis_index("section")
        j = lax.axis_index("dp")
        self.z = lax.div(j, 2)
        self.c = lax.rem(j, 2)
        self.outer = (self.z == 0) | (self.z == 3)
        self.far = jnp.where(self.outer, self.z ^ 2, self.z ^ 3)

    def dev(self, s, z, c):
        return (s, z * 2 + c)


def remote(src, dst, ss, rs, dev):
    return pltpu.make_async_remote_copy(
        src_ref=src, dst_ref=dst, send_sem=ss, recv_sem=rs, device_id=dev, device_id_type=MESH
    )


def arrived(dst, sem):
    pltpu.make_async_copy(dst, dst, sem).wait()


def sent(src, sem):
    pltpu.make_async_copy(src, src, sem).wait()


def barrier(devs):
    sem = pltpu.get_barrier_semaphore()
    for dev in devs:
        pl.semaphore_signal(sem, 1, device_id=dev, device_id_type=MESH)
    pl.semaphore_wait(sem, len(devs))


SCRATCH = dict(
    msgs=((4, 512, 256), BF),
    W=((4, 4, 2, 512, 256), BF),
    WF=((3, 4, 2, 512, 256), BF),
    qbuf=((2, 8, 1024), F32),
    qb=((16, 1024), BF),
    kq=((2, 16, 512), BF),
    mT=((1024, 256), BF),
    patT=((192, 512), BF),
    fill=((1536, 192), BF),
    fo=((16, 256), F32),
    foc=((256, 128), F32),
    att=((768, 512), F32),
    op=((256, 512), BF),
    hT=((1024, 512), BF),
    hrow=((512, 1024), BF),
    acc=((512, 1024), F32),
    st0=((512, 1024), BF),
    nrm=((512, 1024), BF),
    nrm2=((512, 1024), BF),
    tr=((1024, 512), BF),
    q=((512, 256), BF),
    k=((512, 256), BF),
    v=((512, 256), BF),
    attp=((8, 256, 256), F32),
    mix=((512, 1024), BF),
    st1=((512, 1024), BF),
    act=((4, 512, 256), BF),
    gp=((4, 512, 256), F32),
    gin=((4, 512, 256), BF),
    rsS=((512, 1024), BF),
    rsR=((4, 128, 1024), BF),
    gs1=((512, 1024), BF),
    gm=((512, 256), BF),
    gq=((3, 512, 256), BF),
    gs0=((512, 1024), BF),
    ga=((512, 1024), BF),
    CR=((4, 4, 512, 256), BF),
    RC=((2, 4, 512, 256), BF),
    RA=((4, 512, 256), BF),
    RB=((4, 512, 256), BF),
    FR=((4, 512, 256), BF),
    outR=((4, 512, 256), BF),
    gh=((512, 256), BF),
    ghT=((256, 512), BF),
    gpT=((192, 512), F32),
    G=((256, 256), F32),
    pixS=((4, 48, 512), BF),
    pixR=((4, 48, 512), BF),
)

SEMS = dict(
    rW=(4, 4, 2),
    rF=(3, 4, 2),
    sMsg=(4,),
    sOwn=(4, 3),
    sFwd=(4, 4, 2),
    sFx=(3, 3),
    sFc=(3, 4),
    rQ=(2,),
    sQ=(2,),
    rK=(2,),
    sK=(7,),
    sMix=(3,),
    rMix=(4,),
    sOut=(4,),
    rOut=(4,),
    sR=(2, 4),
    rR=(2, 4),
    sG=(2, 4),
    rG=(2, 4),
    sC=(4, 4),
    rC=(4, 4),
    sZ=(4, 4),
    rRC=(2, 4),
    rRA=(4,),
    rRB=(4,),
    sFin=(4,),
    rFin=(4,),
    sP=(4,),
    rP=(4,),
)
NAMES = list(SCRATCH) + list(SEMS)


class Refs:
    pass


def block_kernel(
    pat, lead, lens, cot, bank, table, vec, out, gpix, gbank, gtab, small, gfo, kq_out, q_out, *scratch
):
    R = Refs()
    for name, ref in zip(NAMES, scratch):
        setattr(R, name, ref)
    here = Place()
    s, z, c = here.s, here.z, here.c
    dev = here.dev
    outer = here.outer
    inner = jnp.logical_not(outer)
    sib = dev(s, z, 1 - c)
    is_row = (s >= 2) & (z >= 2)
    peers = [s ^ 1, s ^ 2, s ^ 3]

    barrier(
        [dev(p, z, c) for p in peers]
        + [dev(p, z, 1 - c) for p in peers]
        + [sib]
        + [dev(s, z ^ i, c) for i in (1, 2, 3)]
    )

    first_owner = (s == 0) & (z == 0)
    key_owner = (s == 0) & (z == 1)

    @pl.when(first_owner)
    def _():
        part = vec[17:18, at(c * 512, 512, 512)].astype(BF)
        part = jnp.broadcast_to(part, (16, 512))
        R.qbuf[0] = mm(part, bank[...])[0:8]
        remote(R.qbuf.at[0], R.qbuf.at[1], R.sQ.at[0], R.rQ.at[0], sib).start()

    used = jnp.logical_not((s == 0) & (z < 2))

    @pl.when(used & jnp.logical_not(is_row))
    def _():
        for p in range(4):
            R.msgs[p] = bank[:, p * 256 : (p + 1) * 256]

    @pl.when(used & is_row)
    def _():
        for m in range(4):
            q, h = m // 2, m % 2
            for n in range(2):
                lo = (2 * h + n) * 256
                R.msgs[m, n * 256 : (n + 1) * 256, :] = bank[q * 256 : (q + 1) * 256, lo : lo + 256]

    for m in range(4):
        tp = jnp.where(is_row, 2 * c + m // 2, m)
        tc = jnp.where(is_row, m % 2, c)
        own = (tp == s) & (tc == c)

        @pl.when(used & own)
        def _():
            pltpu.make_async_copy(R.msgs.at[m], R.W.at[z, s, c], R.rW.at[z, s, c]).start()

        @pl.when(used & jnp.logical_not(own))
        def _():
            remote(R.msgs.at[m], R.W.at[z, s, tc], R.sMsg.at[m], R.rW.at[z, s, tc], dev(tp, z, tc)).start()

    @pl.when(first_owner)
    def _():
        arrived(R.qbuf.at[1], R.rQ.at[0])
        total = R.qbuf[0] + R.qbuf[1] + vec[0:1, :]
        total = total.astype(BF)
        R.qb[...] = jnp.concatenate([total, total], axis=0)
        remote(R.qb, R.qb, R.sQ.at[1], R.rQ.at[1], dev(0, 1, c)).start()

    def has(zz, b):
        return zz >= 2 if b == 0 else zz >= 0

    def full_of(zz, b):
        if b == 0:
            return zz >= 2, jnp.maximum(zz - 2, 0)
        if b == 1:
            return zz == 3, 2
        return None, None

    def spread(zz, b, k):
        block = R.W.at[zz, b, c]
        whole, f = full_of(zz, b)

        def to_sibling():
            remote(block, block, R.sFwd.at[zz, b, 0], R.rW.at[zz, b, c], sib).start()

        def to_layer():
            pltpu.make_async_copy(block, R.WF.at[f, s, c], R.rF.at[f, s, c]).start()
            for i, p in enumerate(peers):
                remote(block, R.WF.at[f, s, c], R.sFx.at[f, i], R.rF.at[f, s, c], dev(p, z, c)).start()

        if whole is None:
            to_sibling()
        else:
            if b == 1:
                pl.when(jnp.logical_not(whole))(to_sibling)
            pl.when(whole)(to_layer)

    def own_bundle(b):
        @pl.when(has(z, b))
        def _():
            block = R.W.at[z, b, c]
            arrived(block, R.rW.at[z, b, c])
            remote(block, block, R.sOwn.at[b, 0], R.rW.at[z, b, c], dev(s, z ^ 1, c)).start()
            remote(block, block, R.sOwn.at[b, 1], R.rW.at[z, b, c], dev(s, here.far, c)).start()
            spread(z, b, 0)

    def foreign(b, k):
        zz = z ^ k

        @pl.when(has(zz, b))
        def _():
            block = R.W.at[zz, b, c]
            arrived(block, R.rW.at[zz, b, c])
            if k > 1:

                @pl.when(inner)
                def _():
                    remote(block, block, R.sFwd.at[zz, b, 1], R.rW.at[zz, b, c], dev(s, z ^ 1, c)).start()

            spread(zz, b, k)

    own_bundle(0)
    own_bundle(1)

    lens_f = lens[...].astype(F32)
    tcol = iota((GROUP, 1), 0).astype(F32)
    trow = iota((1, GROUP), 1).astype(F32)
    lane4 = iota((1, 4), 1)
    start_col = jnp.zeros((GROUP, 1), F32)
    seg_col = jnp.zeros((GROUP, 1), F32)
    seg_row = jnp.zeros((1, GROUP), F32)
    for i in range(4):
        end = jnp.sum(jnp.where(lane4 <= i, lens_f, 0.0), axis=1, keepdims=True)
        past = tcol >= end
        seg_col = seg_col + jnp.where(past, 1.0, 0.0)
        seg_row = seg_row + jnp.where(trow >= end, 1.0, 0.0)
        start_col = jnp.maximum(start_col, jnp.where(past, end, 0.0))
    place_short = tcol - start_col
    valid = seg_col < 3.5
    lead_short = lead[0:1, 0:1]
    lead_long = lead[1:2, 0:1]

    freq = jnp.exp(-math.log(10000.0) * 2.0 * iota((1, 512), 1).astype(F32) / D)
    for g in range(2):
        place = place_short if g == 0 else tcol
        lead_g = lead_short if g == 0 else lead_long
        base = lead_g * vec[3:4, :] + vec[4:5, :] + vec[2:3, :]
        angle = place * freq
        R.acc[g * GROUP : (g + 1) * GROUP, 0:512] = jnp.sin(angle) + base[:, 0:512]
        R.acc[g * GROUP : (g + 1) * GROUP, 512:1024] = jnp.cos(angle) + base[:, 512:1024]
    R.gs1[0:GROUP, :] = jnp.where(valid, cot[0:GROUP, :].astype(F32), 0.0).astype(BF)
    R.gs1[GROUP:ROWS, :] = cot[GROUP:ROWS, :]

    own_bundle(2)
    own_bundle(3)

    @pl.when(key_owner)
    def _():
        arrived(R.qb, R.rQ.at[1])
        head_of = iota((16, 1024), 1) // HEAD
        masked = jnp.where(head_of == iota((16, 1024), 0), R.qb[...].astype(F32), 0.0).astype(BF)
        R.kq[c] = mm_nt(masked, bank[...]).astype(BF)
        for i in range(3):
            remote(R.kq.at[c], R.kq.at[c], R.sK.at[i], R.rK.at[c], dev(s, z ^ (i + 1), c)).start()

    @pl.when((s == 0) & (z != 1))
    def _():
        arrived(R.kq.at[c], R.rK.at[c])

    @pl.when(s == 0)
    def _():
        for i, p in enumerate(peers):
            remote(R.kq.at[c], R.kq.at[c], R.sK.at[3 + i], R.rK.at[c], dev(p, z, c)).start()

    @pl.when(s != 0)
    def _():
        arrived(R.kq.at[c], R.rK.at[c])

    remote(R.kq.at[c], R.kq.at[c], R.sK.at[6], R.rK.at[c], sib).start()

    for b in (0, 1):
        for k in (1, 2, 3):
            foreign(b, k)

    arrived(R.kq.at[1 - c], R.rK.at[1 - c])
    kq_full = jnp.concatenate([R.kq[0], R.kq[1]], axis=1)
    kq_out[...] = kq_full

    @pl.when(key_owner)
    def _():
        q_out[...] = R.qb[...]

    @pl.when(jnp.logical_not(key_owner))
    def _():
        q_out[...] = jnp.zeros((16, 1024), BF)

    R.fo[...] = mm_nt(kq_full, table[...])
    eye = iota((128, 16), 0) == iota((128, 16), 1)
    fo16 = R.fo[...]
    fo_wide = jnp.concatenate([fo16, jnp.zeros((112, 256), F32)], axis=0)
    R.foc[...] = fo_wide.T
    perm = jnp.where(
        (iota((192, 192), 0) // 48 == iota((192, 192), 1) % 4) & (iota((192, 192), 0) % 48 == iota((192, 192), 1) // 4),
        1.0,
        0.0,
    ).astype(BF)
    R.patT[...] = mm_nt(perm, pat[...]).astype(BF)

    def fill_head(h):
        row = R.fo[pl.ds(h, 1), 0:192]
        r = iota((48, 192), 0)
        col = iota((48, 192), 1)
        value = jnp.where(col % 48 == r, row, 0.0)
        high = value.astype(BF)
        R.fill[at(h * 48, 48, 16), :] = high
        R.fill[at(768 + h * 48, 48, 16), :] = (value - high.astype(F32)).astype(BF)

    loop(HEADS, fill_head)

    def score_part(i):
        lo = i * 256
        R.att[at(lo, 256, 256), :] = mm(R.fill[at(lo, 256, 256), :], R.patT[...]) + mm(
            R.fill[at(768 + lo, 256, 256), :], R.patT[...]
        )

    loop(3, score_part)

    def pass_on(f):
        for p in [s] + peers:
            block = R.WF.at[f, p, c]
            arrived(block, R.rF.at[f, p, c])
            remote(block, block, R.sFc.at[f, p], R.rF.at[f, p, c], sib).start()

    def wait_whole(f):
        for p in range(4):
            arrived(R.WF.at[f, p, 1 - c], R.rF.at[f, p, 1 - c])

    pass_on(0)
    wait_whole(0)

    for i in range(4):
        R.tr[i * 256 : (i + 1) * 256, 0:256] = table[:, i * 256 : (i + 1) * 256].T
    bias_lane = iota((1, 256), 1) == 240

    def table_part(p):
        rows = at(p * 256, 256, 256)
        value = mm_tn(R.WF[0, p, 0], R.tr[0:512, 0:256]) + mm_tn(R.WF[0, p, 1], R.tr[512:1024, 0:256])
        bias = jnp.broadcast_to(vec[1:2, rows], (8, 256)).T[:, 0:1]
        R.mT[rows, :] = jnp.where(bias_lane, bias, value).astype(BF)

    loop(4, table_part)
    pass_on(1)

    R.op[240:256, :] = jnp.where(iota((16, 512), 0) == 0, 1.0, 0.0).astype(BF)
    r48 = iota((48, 256), 0)
    c48 = iota((48, 256), 1)

    def weights_of(h, low):
        lowf = low.astype(F32)
        for p in range(4):
            R.op[p * 48 : (p + 1) * 48, :] = (lowf * R.patT[p * 48 : (p + 1) * 48, :].astype(F32)).astype(BF)
        R.op[192:240, :] = low

    def embed_head(h):
        offset = jnp.sum(jnp.where(c48 == r48 + 192, R.fo[pl.ds(h, 1), :], 0.0), axis=1, keepdims=True)
        rows = at(h * 48, 48, 16)
        scores = (R.att[rows, :] + offset) * (1.0 / math.sqrt(HEAD))
        peak = jnp.max(scores, axis=0, keepdims=True)
        e = jnp.exp(scores - peak)
        prob = e / jnp.sum(e, axis=0, keepdims=True)
        R.att[rows, :] = prob
        weights_of(h, prob.astype(BF))
        hrows = at(h * 64, 64, 64)
        R.hT[hrows, :] = mm(R.mT[hrows, :], R.op[...]).astype(BF)

    loop(HEADS, embed_head)

    def turn_tile(i):
        rows = at(i * 256, 256, 256)
        R.hrow[:, rows] = R.hT[rows, :].T

    loop(4, turn_tile)

    wait_whole(1)

    def stream0_part(i):
        g = lax.div(i, 4)
        n = lax.rem(i, 4)
        rows = at(g * 256, 256, 256)
        cols = at(n * 256, 256, 256)
        value = mm(R.hrow[rows, 0:512], R.WF[1, n, 0]) + mm(R.hrow[rows, 512:1024], R.WF[1, n, 1])
        R.st0[rows, cols] = (value + R.acc[rows, cols]).astype(BF)

    loop(8, stream0_part)

    def norm_into(src, dst, which):
        def part(i):
            rows = at(i * 64, 64, 64)
            dst[rows, :] = normed_rows(
                src[rows, :].astype(F32), vec[5 + which : 6 + which, :], vec[7 + which : 8 + which, :]
            ).astype(BF)

        loop(8, part)

    norm_into(R.st0, R.nrm, 0)

    own_cols = at(s * 256, 256, 256)
    for zz in range(3):
        arrived(R.W.at[zz, 1, 1 - c], R.rW.at[zz, 1, 1 - c])

    def project(zz, dst, bias):
        weight = R.W[zz, 1].reshape(1024, 256)
        for g in range(2):
            rows = slice(g * 256, (g + 1) * 256)
            value = mm(R.nrm[rows, :], weight)
            if bias is not None:
                value = value + vec[bias : bias + 1, own_cols]
            dst[rows, :] = value.astype(BF)

    project(0, R.q, 9)
    project(1, R.k, None)
    project(2, R.v, 10)

    pass_on(2)
    for k in (1, 2, 3):
        foreign(2, k)

    lane_head = iota((1, 256), 1) // HEAD

    def only(hh, x):
        return jnp.where(lane_head == hh, x.astype(F32), 0.0).astype(BF)

    allowed = seg_col == seg_row

    def attend(g):
        rows = slice(g * 256, (g + 1) * 256)
        total = jnp.zeros((256, 256), F32)
        for hh in range(4):
            scores = mm_nt(R.q[rows, :], only(hh, R.k[rows, :])) * (1.0 / math.sqrt(HEAD))
            if g == 0:
                scores = jnp.where(allowed, scores, -1e30)
            e = jnp.exp(scores - jnp.max(scores, axis=1, keepdims=True))
            prob = e / jnp.sum(e, axis=1, keepdims=True)
            R.attp[g * 4 + hh] = prob
            total = total + mm(prob.astype(BF), only(hh, R.v[rows, :]))
        R.mix[rows, own_cols] = total.astype(BF)

    attend(0)
    attend(1)
    mine = R.mix.at[:, own_cols]
    for i, p in enumerate(peers):
        remote(mine, mine, R.sMix.at[i], R.rMix.at[s], dev(p, z, c)).start()
    for k in (1, 2, 3):
        foreign(3, k)
    wait_whole(2)
    for p in peers:
        theirs = R.mix.at[:, at(p * 256, 256, 256)]
        arrived(theirs, R.rMix.at[p])

    def stream1_part(i):
        g = lax.div(i, 4)
        n = lax.rem(i, 4)
        rows = at(g * 256, 256, 256)
        cols = at(n * 256, 256, 256)
        value = mm(R.mix[rows, 0:512], R.WF[2, n, 0]) + mm(R.mix[rows, 512:1024], R.WF[2, n, 1])
        value = value + vec[11:12, cols] + R.st0[rows, cols].astype(F32)
        R.st1[rows, cols] = value.astype(BF)

    loop(8, stream1_part)
    norm_into(R.st1, R.nrm2, 1)

    gout = R.gs1

    def wait_half(zz, b):
        arrived(R.W.at[zz, b, 1 - c], R.rW.at[zz, b, 1 - c])

    for zz in (0, 1):
        for b in (2, 3):
            wait_half(zz, b)

    def feed_in(i):
        b = lax.div(i, 2)
        g = lax.rem(i, 2)
        rows = at(g * 256, 256, 256)
        bias = vec[pl.ds(12 + b, 1), own_cols]
        weight = R.W[lax.rem(b, 2), 2 + lax.div(b, 2)].reshape(1024, 256)
        x = mm(R.nrm2[rows, :], weight) + bias
        half_cdf = 0.5 + 0.5 * lax.erf(x * math.sqrt(0.5))
        R.act[b, rows, :] = (x * half_cdf).astype(BF)
        R.gp[b, rows, :] = half_cdf + x * (jnp.exp(-0.5 * x * x) * (1.0 / math.sqrt(2.0 * math.pi)))

    loop(8, feed_in)
    for zz in (2, 3):
        for b in (2, 3):
            wait_half(zz, b)

    def feed_back(i):
        b = lax.div(i, 2)
        g = lax.rem(i, 2)
        rows = at(g * 256, 256, 256)
        block = R.W.at[2 + lax.rem(b, 2), 2 + lax.div(b, 2)]
        total = jnp.zeros((256, 256), F32)
        for n in range(4):
            tile = block[n // 2, (n % 2) * 256 : (n % 2 + 1) * 256, :]
            total = total + mm_nt(gout[rows, n * 256 : (n + 1) * 256], tile)
        gin = (total * R.gp[b, rows, :]).astype(BF)
        R.gin[b, rows, :] = gin

    loop(8, feed_back)

    def reduce_rows(phase, make):
        for i, p in enumerate(peers):
            make(p)
            block = R.rsS.at[at(p * OWN, OWN, OWN), :]
            remote(block, R.rsR.at[s], R.sR.at[phase, i], R.rR.at[phase, s], dev(p, z, c)).start()
        make(s)

    own_rows = at(s * OWN, OWN, OWN)

    def reduced(phase):
        total = R.rsS[own_rows, :].astype(F32)
        for p in peers:
            arrived(R.rsR.at[p], R.rR.at[phase, p])
            total = total + R.rsR[p].astype(F32)
        return total

    def gather_rows(phase, ref):
        block = ref.at[own_rows, :]
        for i, p in enumerate(peers):
            remote(block, block, R.sG.at[phase, i], R.rG.at[phase, s], dev(p, z, c)).start()

    def gathered(phase, ref):
        for p in peers:
            arrived(ref.at[at(p * OWN, OWN, OWN), :], R.rG.at[phase, p])

    def feed_norm(p):
        rows = at(p * OWN, OWN, OWN)
        total = jnp.zeros((OWN, 1024), F32)
        for b in range(4):
            total = total + mm_nt(R.gin[b, rows, :], R.W[b % 2, 2 + b // 2].reshape(1024, 256))
        R.rsS[rows, :] = total.astype(BF)

    reduce_rows(0, feed_norm)

    def out_part(i):
        g = lax.div(i, 4)
        n = lax.rem(i, 4)
        rows = at(g * 256, 256, 256)
        total = jnp.zeros((256, 256), F32)
        for b in range(4):
            tile = R.W[2 + b % 2, 2 + b // 2, lax.div(n, 2), at(lax.rem(n, 2) * 256, 256, 256), :]
            total = total + mm(R.act[b, rows, :], tile)
        R.hrow[rows, at(n * 256, 256, 256)] = total.astype(BF)

    loop(8, out_part)
    for i, p in enumerate(peers):
        block = R.hrow.at[:, at(p * 256, 256, 256)]
        remote(block, R.outR.at[s], R.sOut.at[i], R.rOut.at[s], dev(p, z, c)).start()

    def drain(b):
        @pl.when(has(z, b))
        def _():
            block = R.W.at[z, b, c]
            sent(block, R.sOwn.at[b, 0])
            sent(block, R.sOwn.at[b, 1])

        for k in range(4):
            zz = z ^ k
            block = R.W.at[zz, b, c]
            if k > 1:

                @pl.when(inner & has(zz, b))
                def _():
                    sent(block, R.sFwd.at[zz, b, 1])

            whole, f = full_of(zz, b)

            def side():
                sent(block, R.sFwd.at[zz, b, 0])

            def layer():
                for i in range(3):
                    sent(block, R.sFx.at[f, i])

            if whole is None:
                side()
            else:
                if b == 1:
                    pl.when(jnp.logical_not(whole))(side)
                pl.when(whole)(layer)

    drain(2)
    drain(3)

    def transposed(src):
        def part(i):
            a = lax.div(i, 2)
            b = lax.rem(i, 2)
            R.tr[at(a * 256, 256, 256), at(b * 256, 256, 256)] = src[
                at(b * 256, 256, 256), at(a * 256, 256, 256)
            ].T

        loop(8, part)

    def exchange(zz, b):
        block = R.W.at[zz, b, 1 - c]
        remote(block, R.CR.at[zz, b], R.sC.at[zz, b], R.rC.at[zz, b], sib).start()

    def column_gradient(zz, b, left, right):
        for h in range(2):
            R.W[zz, b, h] = mm(left[h * 512 : (h + 1) * 512, :], right).astype(BF)
        exchange(zz, b)

    transposed(R.nrm2)

    def first_gradient(b):
        column_gradient(lax.rem(b, 2), 2 + lax.div(b, 2), R.tr, R.gin[b])

    loop(4, first_gradient)

    def second_gradient(b):
        zz = 2 + lax.rem(b, 2)
        bb = 2 + lax.div(b, 2)
        for n in range(4):
            tile = mm_tn(R.act[b], gout[:, n * 256 : (n + 1) * 256])
            R.W[zz, bb, n // 2, (n % 2) * 256 : (n % 2 + 1) * 256, :] = tile.astype(BF)
        exchange(zz, bb)

    loop(4, second_gradient)

    small[...] = jnp.zeros((16, 1024), F32)
    for b in range(4):
        small[10 + b : 11 + b, own_cols] = column_sum(R.gin[b].astype(F32))
    small[14:15, :] = column_sum(gout[own_rows, :].astype(F32))

    g2 = reduced(0)
    gx, gw, gb = norm_back(R.st1[own_rows, :].astype(F32), g2, vec[6:7, :])
    small[4:5, :] = gw
    small[6:7, :] = gb
    gs1_own = (gout[own_rows, :].astype(F32) + gx).astype(BF)
    small[9:10, :] = column_sum(gs1_own.astype(F32))
    R.ga[own_rows, :] = gs1_own
    gather_rows(0, R.ga)

    def summed(zz, b):
        arrived(R.CR.at[zz, b], R.rC.at[zz, b])
        sent(R.CR.at[zz, b], R.sC.at[zz, b])
        R.W[zz, b, c] = (R.W[zz, b, c].astype(F32) + R.CR[zz, b].astype(F32)).astype(BF)

    def first_sends(b):
        for k in (0, 1, 2, 3):
            zz = z ^ k

            @pl.when(has(zz, b))
            def _():
                summed(zz, b)
                block = R.W.at[zz, b, c]
                if k == 1:
                    remote(block, R.RA.at[b], R.sZ.at[zz, b], R.rRA.at[b], dev(s, z ^ 1, c)).start()
                if k > 1:

                    @pl.when(outer)
                    def _():
                        remote(
                            block, R.RC.at[3 - k, b], R.sZ.at[zz, b], R.rRC.at[3 - k, b], dev(s, z ^ 1, c)
                        ).start()

    def second_sends(b):
        for k in (2, 3):
            zz = z ^ k

            @pl.when(inner & has(zz, b))
            def _():
                block = R.W.at[zz, b, c]
                arrived(R.RC.at[k - 2, b], R.rRC.at[k - 2, b])
                R.W[zz, b, c] = (R.W[zz, b, c].astype(F32) + R.RC[k - 2, b].astype(F32)).astype(BF)
                remote(block, R.RB.at[b], R.sZ.at[zz, b], R.rRB.at[b], dev(s, zz, c)).start()

    row_b = [jnp.logical_and(z >= 2, b >= 2) for b in range(4)]

    def last_sends(b):
        @pl.when(has(z, b))
        def _():
            arrived(R.RA.at[b], R.rRA.at[b])
            arrived(R.RB.at[b], R.rRB.at[b])
            R.W[z, b, c] = (R.W[z, b, c].astype(F32) + R.RA[b].astype(F32) + R.RB[b].astype(F32)).astype(BF)
            row = row_b[b]
            tc = jnp.where(row, lax.div(s, 2), c)
            m = jnp.where(row, lax.rem(s, 2) * 2 + c, s)
            own = (s == b) & (tc == c)
            block = R.W.at[z, b, c]

            @pl.when(own)
            def _():
                pltpu.make_async_copy(block, R.FR.at[m], R.rFin.at[m]).start()

            @pl.when(jnp.logical_not(own))
            def _():
                remote(block, R.FR.at[m], R.sFin.at[b], R.rFin.at[m], dev(b, z, tc)).start()

    first_sends(2)
    first_sends(3)

    total = R.hrow[:, own_cols].astype(F32) + R.st1[:, own_cols].astype(F32) + vec[16:17, own_cols]
    for p in peers:
        arrived(R.outR.at[p], R.rOut.at[p])
        total = total + R.outR[p].astype(F32)
    out[...] = total.astype(BF)

    gathered(0, R.ga)
    gs1 = R.ga

    def grad_mixed(g):
        rows = at(g * 256, 256, 256)
        total = jnp.zeros((256, 256), F32)
        for n in range(4):
            half = lax.div(s, 2)
            tile = R.WF[2, n, half, at(lax.rem(s, 2) * 256, 256, 256), :]
            total = total + mm_nt(gs1[rows, n * 256 : (n + 1) * 256], tile)
        R.gm[rows, :] = total.astype(BF)

    loop(2, grad_mixed)

    def attend_back(g):
        rows = at(g * 256, 256, 256)
        qg, kg, vg, gmg = R.q[rows, :], R.k[rows, :], R.v[rows, :], R.gm[rows, :]
        zero = jnp.zeros((256, 256), F32)
        tq, tk, tv = zero, zero, zero
        for hh in range(4):
            prob = R.attp[g * 4 + hh]
            gmh = only(hh, gmg)
            dprob = mm_nt(gmh, vg)
            tv = tv + mm_tn(prob.astype(BF), gmh)
            ds = (prob * (dprob - jnp.sum(prob * dprob, axis=1, keepdims=True))).astype(BF)
            tq = tq + mm(ds, only(hh, kg))
            tk = tk + mm_tn(ds, only(hh, qg))
        scale = 1.0 / math.sqrt(HEAD)
        R.gq[0, rows, :] = (tq * scale).astype(BF)
        R.gq[1, rows, :] = (tk * scale).astype(BF)
        R.gq[2, rows, :] = tv.astype(BF)

    loop(2, attend_back)

    for i, p in enumerate(peers):
        block = R.rsS.at[at(p * OWN, OWN, OWN), :]
        sent(block, R.sR.at[0, i])

    def attend_norm(p):
        rows = at(p * OWN, OWN, OWN)
        total = jnp.zeros((OWN, 1024), F32)
        for i in range(3):
            total = total + mm_nt(R.gq[i, rows, :], R.W[i, 1].reshape(1024, 256))
        R.rsS[rows, :] = total.astype(BF)

    reduce_rows(1, attend_norm)

    second_sends(2)
    second_sends(3)

    transposed(R.nrm)
    drain(1)
    drain(0)

    def attend_gradient(i):
        column_gradient(i, 1, R.tr, R.gq[i])

    loop(3, attend_gradient)
    transposed(R.mix)
    column_gradient(3, 1, R.tr, gs1[:, own_cols])
    small[7:8, own_cols] = column_sum(R.gq[0].astype(F32))
    small[8:9, own_cols] = column_sum(R.gq[2].astype(F32))

    g1 = reduced(1)
    gx, gw, gb = norm_back(R.st0[own_rows, :].astype(F32), g1, vec[5:6, :])
    small[3:4, :] = gw
    small[5:6, :] = gb
    gs0_own = (R.ga[own_rows, :].astype(F32) + gx).astype(BF)
    gs0_sum = column_sum(gs0_own.astype(F32))
    small[1:2, :] = gs0_sum
    small[2:3, :] = jnp.where(s < 2, lead_short, lead_long) * gs0_sum
    R.gs0[own_rows, :] = gs0_own
    gather_rows(1, R.gs0)
    first_sends(1)
    gathered(1, R.gs0)

    gs0 = R.gs0
    half_s = lax.div(s, 2)
    row_s = at(lax.rem(s, 2) * 256, 256, 256)
    total = jnp.zeros((256, 512), F32)
    for n in range(4):
        total = total + mm_nt(R.WF[1, n, half_s, row_s, :], gs0[:, n * 256 : (n + 1) * 256])
    R.ghT[...] = total.astype(BF)
    R.gh[...] = R.ghT[...].T
    small[0:1, own_cols] = column_sum(R.gh[...].astype(F32))
    column_gradient(3, 0, R.hT, gs0[:, own_cols])

    R.gpT[...] = jnp.zeros((192, 512), F32)
    R.G[...] = jnp.zeros((256, 256), F32)
    gfo[...] = jnp.zeros((256, 128), F32)
    lane128 = iota((1, 128), 1)

    def embed_back(hh):
        h = 4 * s + hh
        prob = R.att[at(h * 48, 48, 16), :]
        low = prob.astype(BF)
        lowf = low.astype(F32)
        weights_of(h, low)
        gop = mm_tn(R.mT[at(h * 64, 64, 64), :], R.ghT[at(hh * 64, 64, 64), :])
        keep = (iota((1, 256), 1) // HEAD) == hh
        R.G[...] += jnp.where(keep, mm(R.op[...], R.gh[...]), 0.0)
        gatt = gop[192:240, :]
        for p in range(4):
            gatt = gatt + gop[p * 48 : (p + 1) * 48, :] * R.patT[p * 48 : (p + 1) * 48, :].astype(F32)
        gsc = prob * (gatt - jnp.sum(prob * gatt, axis=0, keepdims=True)) * (1.0 / math.sqrt(HEAD))
        pick = jnp.where(lane128 == h, 1.0, 0.0)
        for p in range(4):
            rows = slice(p * 48, (p + 1) * 48)
            fcol = jnp.sum(R.foc[rows, :] * pick, axis=1, keepdims=True)
            R.gpT[rows, :] += gop[rows, :] * lowf + gsc * fcol
            gcol = jnp.sum(R.patT[rows, :].astype(F32) * gsc, axis=1, keepdims=True)
            gfo[rows, :] += gcol * pick
        gfo[192:240, :] += jnp.sum(gsc, axis=1, keepdims=True) * pick

    loop(4, embed_back)

    gpt = R.gpT[...].astype(BF)
    for p in range(4):
        r = iota((48, 192), 0) + p * 48
        col = iota((48, 192), 1)
        select = jnp.where(col == (r % 4) * 48 + r // 4, 1.0, 0.0).astype(BF)
        R.pixS[p] = mm(select, gpt).astype(BF)
    for i, p in enumerate(peers):
        remote(R.pixS.at[p], R.pixR.at[s], R.sP.at[i], R.rP.at[s], dev(p, z, c)).start()

    G = R.G[...].astype(BF)
    for h in range(2):
        R.W[2, 0, h] = mm_tn(table[:, h * 512 : (h + 1) * 512], G).astype(BF)
    exchange(2, 0)
    gf = gfo[...]
    gf_high = gf.astype(BF)
    gf_low = (gf - gf_high.astype(F32)).astype(BF)
    kq_wide = jnp.concatenate([kq_full, jnp.zeros((112, 1024), BF)], axis=0)
    weight = R.WF[0, s].reshape(1024, 256)
    gtab[...] = mm_nt(G, weight) + mm(gf_high, kq_wide) + mm(gf_low, kq_wide)

    second_sends(1)
    first_sends(0)
    last_sends(2)
    last_sends(3)
    last_sends(1)
    second_sends(0)

    total = R.pixS[s].astype(F32)
    for p in peers:
        arrived(R.pixR.at[p], R.rP.at[p])
        total = total + R.pixR[p].astype(F32)
    gpix[...] = total.T

    last_sends(0)

    @pl.when(used)
    def _():
        for m in range(4):
            arrived(R.FR.at[m], R.rFin.at[m])

    @pl.when(used & jnp.logical_not(is_row))
    def _():
        for m in range(4):
            gbank[:, m * 256 : (m + 1) * 256] = R.FR[m].astype(F32)

    @pl.when(used & is_row)
    def _():
        for m in range(4):
            q, h = m // 2, m % 2
            for n in range(2):
                lo = (2 * h + n) * 256
                gbank[q * 256 : (q + 1) * 256, lo : lo + 256] = R.FR[m, n * 256 : (n + 1) * 256, :].astype(F32)

    @pl.when(jnp.logical_not(used))
    def _():
        gbank[...] = jnp.zeros((512, 1024), F32)

    for m in range(4):
        tp = jnp.where(is_row, 2 * c + m // 2, m)
        tc = jnp.where(is_row, m % 2, c)
        own = (tp == s) & (tc == c)

        @pl.when(used & jnp.logical_not(own))
        def _():
            sent(R.msgs.at[m], R.sMsg.at[m])

    @pl.when(first_owner)
    def _():
        sent(R.qbuf.at[0], R.sQ.at[0])
        sent(R.qb, R.sQ.at[1])

    @pl.when(key_owner)
    def _():
        for i in range(3):
            sent(R.kq.at[c], R.sK.at[i])

    @pl.when(s == 0)
    def _():
        for i in range(3):
            sent(R.kq.at[c], R.sK.at[3 + i])

    sent(R.kq.at[c], R.sK.at[6])
    for f in range(3):
        for p in range(4):
            sent(R.WF.at[f, p, c], R.sFc.at[f, p])
    for i, p in enumerate(peers):
        sent(mine, R.sMix.at[i])
        sent(R.outR.at[p], R.sOut.at[i])
        sent(R.rsR.at[p], R.sR.at[1, i])
        sent(R.rsR.at[p], R.sG.at[0, i])
        sent(R.rsR.at[p], R.sG.at[1, i])
        sent(R.pixS.at[p], R.sP.at[i])
    for b in range(4):
        for k in (1, 2, 3):
            zz = z ^ k

            @pl.when(has(zz, b))
            def _():
                sent(R.W.at[zz, b, c], R.sZ.at[zz, b])

        tc = jnp.where(row_b[b], lax.div(s, 2), c)
        own = (s == b) & (tc == c)

        @pl.when(has(z, b) & jnp.logical_not(own))
        def _():
            sent(R.W.at[z, b, c], R.sFin.at[b])


def block_call(*args):
    shape = jax.ShapeDtypeStruct
    vmem = pl.BlockSpec(memory_space=pltpu.VMEM)
    outs = [
        shape((512, 256), BF),
        shape((512, 48), F32),
        shape((512, 1024), F32),
        shape((256, 1024), F32),
        shape((16, 1024), F32),
        shape((256, 128), F32),
        shape((16, 1024), BF),
        shape((16, 1024), BF),
    ]
    return pl.pallas_call(
        block_kernel,
        out_shape=outs,
        in_specs=[vmem] * len(args),
        out_specs=[vmem] * len(outs),
        scratch_shapes=[pltpu.VMEM(*v) for v in SCRATCH.values()]
        + [pltpu.SemaphoreType.DMA(v) for v in SEMS.values()],
        compiler_params=pltpu.CompilerParams(
            collective_id=1, has_side_effects=True, vmem_limit_bytes=63 * 2**20
        ),
    )(*args)


FINAL_SCRATCH = dict(
    all_=((384, 1024), BF),
    fin=((384, 1024), BF),
    fromc=((192, 1024), BF),
    fromp=((4, 48, 1024), BF),
    part=((4, 48, 1024), BF),
    gq=((16, 1024), BF),
    qx=((2, 8, 1024), F32),
    ga=((2, 8, 512), F32),
)
FINAL_SEMS = dict(
    sA=(1,), rA=(1,), sB=(4,), rB=(4,), sD=(4,), rD=(4,), sE=(4,), rE=(4,), sH=(1,), rH=(1,),
    sQ=(1,), rQ=(1,), sN=(6,), rN=(1,), sL=(7,), rL=(2,),
)
FINAL_NAMES = list(FINAL_SCRATCH) + list(FINAL_SEMS)


def final_kernel(gtab, small, gfo, kq, q, bank, table, vec, tab_out, small_out, rows_out, bank_out, *scratch):
    R = Refs()
    for name, ref in zip(FINAL_NAMES, scratch):
        setattr(R, name, ref)
    here = Place()
    s, z, c = here.s, here.z, here.c
    dev = here.dev
    sib = dev(s, z, 1 - c)
    peers = [s ^ 1, s ^ 2, s ^ 3]
    layers = [z ^ 1, z ^ 2, z ^ 3]
    barrier([dev(p, z, c) for p in peers] + [sib] + [dev(s, i, c) for i in layers])

    R.all_[0:256, :] = gtab[...].astype(BF)
    R.all_[256:272, :] = small[...].astype(BF)
    for i in range(8):
        R.all_[272:304, i * 128 : (i + 1) * 128] = gfo[i * 32 : (i + 1) * 32, :].astype(BF)
    R.all_[304:384, :] = jnp.zeros((80, 1024), BF)

    half = at(c * 192, 192, 64)
    other = R.all_.at[at((1 - c) * 192, 192, 64), :]
    remote(other, R.fromc, R.sA.at[0], R.rA.at[0], sib).start()
    arrived(R.fromc, R.rA.at[0])
    R.all_[half, :] = (R.all_[half, :].astype(F32) + R.fromc[...].astype(F32)).astype(BF)

    def piece(p):
        return at(c * 192 + p * 48, 48, 16)

    for i, p in enumerate(peers):
        remote(R.all_.at[piece(p), :], R.fromp.at[s], R.sB.at[i], R.rB.at[s], dev(p, z, c)).start()
    total = R.all_[piece(s), :].astype(F32)
    for p in peers:
        arrived(R.fromp.at[p], R.rB.at[p])
        total = total + R.fromp[p].astype(F32)
    R.part[z] = total.astype(BF)
    for i, zz in enumerate(layers):
        remote(R.part.at[z], R.part.at[z], R.sD.at[i], R.rD.at[z], dev(s, zz, c)).start()
    for zz in layers:
        arrived(R.part.at[zz], R.rD.at[zz])
    total = R.part[0].astype(F32)
    for zz in range(1, 4):
        total = total + R.part[zz].astype(F32)
    for i in range(3):
        sent(R.part.at[0], R.sB.at[i])
    R.fin[piece(s), :] = total.astype(BF)
    mine = R.fin.at[piece(s), :]
    for i, p in enumerate(peers):
        remote(mine, mine, R.sE.at[i], R.rE.at[s], dev(p, z, c)).start()
    for p in peers:
        arrived(R.fin.at[piece(p), :], R.rE.at[p])
    sent(R.fromc, R.sA.at[0])
    whole = R.fin.at[half, :]
    remote(whole, whole, R.sH.at[0], R.rH.at[0], sib).start()
    arrived(R.fin.at[at((1 - c) * 192, 192, 64), :], R.rH.at[0])

    tab_out[...] = R.fin[0:256, :].astype(F32)
    small_out[...] = R.fin[256:272, :].astype(F32)
    gf = jnp.concatenate([R.fin[272:304, i * 128 : (i + 1) * 128] for i in range(8)], axis=0)
    gkq = mm_tn(gf, table[...])[0:16].astype(BF)

    key_owner = (s == 0) & (z == 1)
    first_owner = (s == 0) & (z == 0)

    @pl.when(jnp.logical_not(key_owner | first_owner))
    def _():
        bank_out[...] = jnp.zeros((512, 1024), F32)

    @pl.when(key_owner)
    def _():
        head_of = iota((16, 1024), 1) // HEAD
        diag = head_of == iota((16, 1024), 0)
        masked = jnp.where(diag, q[...].astype(F32), 0.0).astype(BF)
        own = jnp.where(c == 0, gkq[:, 0:512].astype(F32), gkq[:, 512:1024].astype(F32)).astype(BF)
        row = column_sum(jnp.where(diag, mm(own, bank[...]), 0.0))
        R.qx[0] = jnp.broadcast_to(row, (8, 1024))
        remote(R.qx.at[0], R.qx.at[1], R.sQ.at[0], R.rQ.at[0], sib).start()
        bank_out[...] = mm_tn(own, masked)
        arrived(R.qx.at[1], R.rQ.at[0])
        row = (R.qx[0] + R.qx[1]).astype(BF)
        R.gq[...] = jnp.concatenate([row, row], axis=0)
        for i, zz in enumerate(layers):
            remote(R.gq, R.gq, R.sN.at[i], R.rN.at[0], dev(s, zz, c)).start()
        sent(R.qx.at[0], R.sQ.at[0])

    @pl.when((s == 0) & (z != 1))
    def _():
        arrived(R.gq, R.rN.at[0])

    @pl.when(s == 0)
    def _():
        for i, p in enumerate(peers):
            remote(R.gq, R.gq, R.sN.at[3 + i], R.rN.at[0], dev(p, z, c)).start()

    @pl.when(first_owner)
    def _():
        R.ga[c] = mm_nt(R.gq[...], bank[...])[0:8]
        for i, zz in enumerate(layers):
            remote(R.ga.at[c], R.ga.at[c], R.sL.at[i], R.rL.at[c], dev(s, zz, c)).start()
        aq = jnp.where(c == 0, vec[17:18, 0:512], vec[17:18, 512:1024])
        aq = jnp.where(iota((16, 512), 0) == 0, aq, 0.0).astype(BF)
        bank_out[...] = mm_tn(aq, R.gq[...])

    @pl.when((s == 0) & (z != 0))
    def _():
        arrived(R.ga.at[c], R.rL.at[c])

    @pl.when(s == 0)
    def _():
        for i, p in enumerate(peers):
            remote(R.ga.at[c], R.ga.at[c], R.sL.at[3 + i], R.rL.at[c], dev(p, z, c)).start()

    @pl.when(s != 0)
    def _():
        arrived(R.gq, R.rN.at[0])
        arrived(R.ga.at[c], R.rL.at[c])

    remote(R.ga.at[c], R.ga.at[c], R.sL.at[6], R.rL.at[c], sib).start()
    arrived(R.ga.at[1 - c], R.rL.at[1 - c])
    rows_out[0:8, :] = R.gq[0:8, :].astype(F32)
    rows_out[8:16, 0:512] = R.ga[0]
    rows_out[8:16, 512:1024] = R.ga[1]

    for i in range(3):
        sent(R.part.at[0], R.sD.at[i])
        sent(R.part.at[0], R.sE.at[i])
    sent(R.fromc, R.sH.at[0])

    @pl.when(key_owner)
    def _():
        for i in range(3):
            sent(R.gq, R.sN.at[i])

    @pl.when(first_owner)
    def _():
        for i in range(3):
            sent(R.ga.at[c], R.sL.at[i])

    @pl.when(s == 0)
    def _():
        for i in range(3):
            sent(R.gq, R.sN.at[3 + i])
            sent(R.ga.at[c], R.sL.at[3 + i])

    sent(R.ga.at[c], R.sL.at[6])


def final_call(*args):
    shape = jax.ShapeDtypeStruct
    vmem = pl.BlockSpec(memory_space=pltpu.VMEM)
    outs = [
        shape((256, 1024), F32),
        shape((16, 1024), F32),
        shape((16, 1024), F32),
        shape((512, 1024), F32),
    ]
    return pl.pallas_call(
        final_kernel,
        out_shape=outs,
        in_specs=[vmem] * len(args),
        out_specs=[vmem] * len(outs),
        scratch_shapes=[pltpu.VMEM(*v) for v in FINAL_SCRATCH.values()]
        + [pltpu.SemaphoreType.DMA(v) for v in FINAL_SEMS.values()],
        compiler_params=pltpu.CompilerParams(
            collective_id=2, has_side_effects=True, vmem_limit_bytes=40 * 2**20
        ),
    )(*args)


def on_device_fast(
    patches,
    lead_times,
    short_lengths,
    cotangent,
    bank,
    patch_w,
    patch_b,
    var_emb,
    agg_query,
    agg_bias,
    lead_embed,
    norm_gain,
    norm_bias,
    attn_bias,
    fc1_bias,
    fc2_bias,
):
    constant = (patch_b.astype(F32) + var_emb.astype(F32)).astype(BF)
    table = jnp.concatenate(
        [jnp.transpose(patch_w, (1, 0, 2)).reshape(VARS * PIX, D), constant, jnp.zeros((16, D), BF)], axis=0
    )
    vec = jnp.concatenate(
        [
            agg_bias,
            lead_embed,
            norm_gain,
            norm_bias,
            attn_bias,
            fc1_bias.reshape(4, D),
            fc2_bias[None],
            agg_query[None],
            jnp.zeros((6, D), BF),
        ],
        axis=0,
    ).astype(F32)
    own_bank = bank[0]
    out, gpix, gbank, gtab, small, gfo, kq, q = block_call(
        patches.reshape(ROWS, VARS * PIX),
        lead_times,
        short_lengths,
        cotangent.reshape(ROWS, D),
        own_bank,
        table,
        vec,
    )
    tab, sums, rows, bank_rows = final_call(gtab, small, gfo, kq, q, own_bank, table, vec)
    vector_owner = (lax.axis_index("section") == 0) & (lax.axis_index("dp") < 4)
    grad_bank = jnp.where(vector_owner, bank_rows, gbank)[None]
    grad_patch_w = jnp.transpose(tab[: VARS * PIX].reshape(PIX, VARS, D), (1, 0, 2))
    grad_constant = tab[VARS * PIX : VARS * PIX + VARS]
    return (
        out.reshape(2, GROUP, 256),
        gpix.reshape(2, GROUP, 48),
        grad_bank,
        grad_patch_w,
        grad_constant,
        grad_constant,
        rows[8],
        jnp.stack([rows[0], sums[0], sums[1]]),
        jnp.stack([sums[2], sums[1]]),
        sums[3:5],
        sums[5:7],
        sums[7:10],
        sums[10:14].reshape(FF),
        sums[14],
    )


def specs():
    ins = (
        (P(None, "dp", None), P(None, "dp"), P("dp", None), P(None, "dp", None), P("section", "dp", None))
        + (P(),) * 11
    )
    outs = (P(None, "dp", "section"), P(None, "dp", "section"), P("section", "dp", None)) + (P(),) * 11
    return ins, outs


wide_type = jnp.float32
narrow_type = jnp.bfloat16
highest = lax.Precision.HIGHEST


def shortened(array):

    def short(part):
        return part.astype(jnp.bfloat16) if part.dtype == jnp.float32 else part

    return jax.tree.map(short, array)


def from_behind(array, axis, by):
    length = lax.axis_size(axis)
    pairs = [(i, i + by) for i in range(length) if 0 <= i + by < length]
    return lax.ppermute(array, axis, pairs)


def product(factor_left, factor_right):
    return jnp.dot(factor_left, factor_right, preferred_element_type=wide_type)


def product_left(factor_left, factor_right):
    return lax.dot_general(
        factor_left, factor_right, (((0,), (0,)), ((), ())), preferred_element_type=wide_type
    )


def product_right(factor_left, factor_right):
    return lax.dot_general(
        factor_left, factor_right, (((1,), (1,)), ((), ())), preferred_element_type=wide_type
    )


def norm_layer(stream, gain_row, shift_row):
    centre = stream - jnp.mean(stream, axis=-1, keepdims=True)
    spread = jnp.mean(centre * centre, axis=-1, keepdims=True)
    return centre * lax.rsqrt(spread + 1e-05) * gain_row + shift_row


def gelu_exact(values_in):
    return jax.nn.gelu(values_in, approximate=False)


def position_table(places):
    half_width = D // 2
    frequency = jnp.exp(-math.log(10000.0) * 2.0 * jnp.arange(half_width, dtype=wide_type) / D)
    angles = places.astype(wide_type)[:, None] * frequency[None, :]
    return jnp.concatenate([jnp.sin(angles), jnp.cos(angles)], axis=1)


def layout(lengths_row, row_count):
    segment_ends = jnp.cumsum(lengths_row)
    starts = segment_ends - lengths_row
    places = jnp.arange(row_count, dtype=jnp.int32)
    segment = jnp.sum((places[:, None] >= segment_ends[None, :]).astype(jnp.int32), axis=1)
    member = segment[:, None] == jnp.arange(lengths_row.shape[0], dtype=jnp.int32)[None, :]
    offset = jnp.sum(jnp.where(member, starts[None, :], 0), axis=1)
    offset = jnp.where(segment == lengths_row.shape[0], segment_ends[-1], offset)
    return (segment, places - offset)


def embed_setup(weights, params):
    patch_w, patch_b, var_emb, agg_query, agg_bias = params[:5]
    query_row = product(agg_query[None, :], weights[0])[0] + agg_bias[0].astype(wide_type)
    query_low = query_row.astype(narrow_type)
    key_query = jnp.einsum(
        "dhe,he->dh",
        weights[1].reshape(D, HEADS, HEAD),
        query_low.reshape(HEADS, HEAD),
        preferred_element_type=wide_type,
    )
    key_low = key_query.astype(narrow_type)
    constant = (patch_b.astype(wide_type) + var_emb.astype(wide_type)).astype(narrow_type)
    filters = jnp.einsum("vpd,dh->vph", patch_w, key_low, preferred_element_type=wide_type)
    offsets = product(constant, key_low)
    embed_table = jnp.concatenate([patch_w.reshape(VARS * PIX, D), constant], axis=0)
    return (query_low, key_low, constant, filters, offsets, embed_table)


def embed_rows(pixel_rows, places, lead_time, setup, weights, params):
    query_low, key_low, constant, filters, offsets, embed_table = setup
    agg_bias, lead_embed = (params[4], params[5])
    row_count = pixel_rows.shape[0]
    pixels = pixel_rows.reshape(row_count, VARS, PIX).astype(wide_type)
    scores = (
        jnp.einsum("tvp,vph->tvh", pixels, filters, precision=highest) + offsets[None]
    ) / math.sqrt(HEAD)
    attend = jax.nn.softmax(scores, axis=1)
    attend_low = attend.astype(narrow_type)
    weighted = (attend_low.astype(wide_type)[:, :, :, None] * pixels[:, :, None, :]).astype(
        narrow_type
    )
    operand = jnp.concatenate(
        [
            jnp.transpose(weighted, (0, 2, 1, 3)).reshape(row_count * HEADS, VARS * PIX),
            jnp.transpose(attend_low, (0, 2, 1)).reshape(row_count * HEADS, VARS),
        ],
        axis=1,
    )
    pooled = product(operand, embed_table).astype(narrow_type).reshape(row_count, HEADS, D)
    heads_out = jnp.einsum(
        "thd,dhe->the", pooled, weights[2].reshape(D, HEADS, HEAD), preferred_element_type=wide_type
    ).reshape(row_count, D)
    heads_low = (heads_out + agg_bias[1].astype(wide_type)).astype(narrow_type)
    merged = product(heads_low, weights[3]) + agg_bias[2].astype(wide_type)
    stream = (
        merged
        + position_table(places)
        + lead_time * lead_embed[0].astype(wide_type)
        + lead_embed[1].astype(wide_type)
    )
    return (stream.astype(narrow_type), (pixels, attend, attend_low, operand, pooled, heads_low))


def embed_back(grad_rows, lead_time, setup, saved_state, weights):
    query_low, key_low, constant, filters, offsets, embed_table = setup
    pixels, attend, attend_low, operand, pooled, heads_low = saved_state
    row_count = grad_rows.shape[0]
    grad_wide = grad_rows.astype(wide_type)
    grad_w_out = product_left(heads_low, grad_rows)
    grad_bias_out = jnp.sum(grad_wide, axis=0)
    grad_heads = product_right(grad_rows, weights[3]).astype(narrow_type)
    grad_bias_value = jnp.sum(grad_heads.astype(wide_type), axis=0)
    grad_heads_split = grad_heads.reshape(row_count, HEADS, HEAD)
    grad_w_value = jnp.einsum(
        "thd,the->dhe", pooled, grad_heads_split, preferred_element_type=wide_type
    ).reshape(D, D)
    grad_pooled = jnp.einsum(
        "the,dhe->thd",
        grad_heads_split,
        weights[2].reshape(D, HEADS, HEAD),
        preferred_element_type=wide_type,
    )
    grad_pooled = grad_pooled.astype(narrow_type).reshape(row_count * HEADS, D)
    grad_operand = product_right(grad_pooled, embed_table)
    grad_table = product_left(operand, grad_pooled)
    grad_weighted = grad_operand[:, : VARS * PIX].reshape(row_count, HEADS, VARS, PIX)
    grad_mixing = jnp.transpose(
        grad_operand[:, VARS * PIX :].reshape(row_count, HEADS, VARS), (0, 2, 1)
    )
    grad_attend = (
        jnp.einsum("thvp,tvp->tvh", grad_weighted, pixels, precision=highest) + grad_mixing
    )
    grad_scores = (
        attend
        * (grad_attend - jnp.sum(attend * grad_attend, axis=1, keepdims=True))
        / math.sqrt(HEAD)
    )
    grad_pixels = jnp.einsum(
        "thvp,tvh->tvp", grad_weighted, attend_low.astype(wide_type), precision=highest
    )
    grad_pixels = grad_pixels + jnp.einsum("tvh,vph->tvp", grad_scores, filters, precision=highest)
    grad_filters = jnp.einsum("tvp,tvh->vph", pixels, grad_scores, precision=highest)
    grad_offsets = jnp.sum(grad_scores, axis=0)
    grad_lead = jnp.stack([lead_time * grad_bias_out, grad_bias_out])
    sums = (
        grad_w_out,
        grad_bias_out,
        grad_bias_value,
        grad_w_value,
        grad_table,
        grad_filters,
        grad_offsets,
        grad_lead,
    )
    return (grad_pixels.reshape(row_count, VARS * PIX), sums)


def embed_finish(totals, setup, weights, params):
    (
        grad_w_out,
        grad_bias_out,
        grad_bias_value,
        grad_w_value,
        grad_table,
        grad_filters,
        grad_offsets,
        grad_lead,
    ) = totals
    query_low, key_low, constant, filters, offsets, embed_table = setup
    patch_w, agg_query = (params[0], params[3])
    key_wide = key_low.astype(wide_type)
    grad_patch_w = grad_table[: VARS * PIX].reshape(VARS, PIX, D) + jnp.einsum(
        "vph,dh->vpd", grad_filters, key_wide, precision=highest
    )
    grad_constant = grad_table[VARS * PIX :] + jnp.dot(grad_offsets, key_wide.T, precision=highest)
    grad_key = jnp.einsum("vpd,vph->dh", patch_w.astype(wide_type), grad_filters, precision=highest)
    grad_key = grad_key + jnp.dot(constant.astype(wide_type).T, grad_offsets, precision=highest)
    grad_key_low = grad_key.astype(narrow_type)
    query_heads = query_low.reshape(HEADS, HEAD).astype(wide_type)
    grad_w_key = (grad_key_low.astype(wide_type)[:, :, None] * query_heads[None, :, :]).reshape(
        D, D
    )
    grad_query = jnp.einsum(
        "dhe,dh->he",
        weights[1].reshape(D, HEADS, HEAD),
        grad_key_low,
        preferred_element_type=wide_type,
    )
    grad_query = grad_query.reshape(D).astype(narrow_type)
    grad_query_wide = grad_query.astype(wide_type)
    grad_w_query = agg_query.astype(wide_type)[:, None] * grad_query_wide[None, :]
    grad_agg_query = product(weights[0], grad_query[:, None])[:, 0]
    grad_bank = jnp.concatenate([grad_w_query, grad_w_key, grad_w_value, grad_w_out], axis=0)
    smalls = (
        grad_patch_w,
        grad_constant,
        grad_constant,
        grad_agg_query,
        jnp.stack([grad_query_wide, grad_bias_value, grad_bias_out]),
        grad_lead,
        jnp.zeros((2, D), wide_type),
        jnp.zeros((2, D), wide_type),
        jnp.zeros((3, D), wide_type),
        jnp.zeros((FF,), wide_type),
        jnp.zeros((D,), wide_type),
    )
    return (grad_bank, smalls)


def attention_scores(block_query, block_segment, key_heads, segment):
    raw_scores = jnp.einsum(
        "qhe,khe->hqk", block_query, key_heads, preferred_element_type=wide_type
    ) / math.sqrt(HEAD)
    allowed = (block_segment[:, None] == segment[None, :])[None]
    return jnp.where(allowed, raw_scores, -1e30)


def attention_forward(queries, key_rows, values, segment):
    row_count = queries.shape[0]
    block_rows = min(512, row_count)
    block_total = row_count // block_rows
    key_heads = key_rows.reshape(row_count, HEADS, HEAD)
    value_heads = values.reshape(row_count, HEADS, HEAD)

    def one_block(block_items):
        block_query, block_segment = block_items
        scores = attention_scores(block_query, block_segment, key_heads, segment)
        row_peak = jnp.max(scores, axis=-1, keepdims=True)
        exp_scores = jnp.exp(scores - row_peak)
        exp_total = jnp.sum(exp_scores, axis=-1, keepdims=True)
        probabilities = (exp_scores / exp_total).astype(narrow_type)
        mixed_heads = jnp.einsum(
            "hqk,khe->qhe", probabilities, value_heads, preferred_element_type=wide_type
        )
        return (mixed_heads.astype(narrow_type), (row_peak + jnp.log(exp_total))[:, :, 0])

    mixed_heads, log_totals = lax.map(
        one_block,
        (
            queries.reshape(block_total, block_rows, HEADS, HEAD),
            segment.reshape(block_total, block_rows),
        ),
    )
    return (mixed_heads.reshape(row_count, D), log_totals)


def attention_backward(queries, key_rows, values, segment, log_totals, grad_mixed):
    row_count = queries.shape[0]
    block_rows = min(512, row_count)
    block_total = row_count // block_rows
    key_heads = key_rows.reshape(row_count, HEADS, HEAD)
    value_heads = values.reshape(row_count, HEADS, HEAD)

    def one_block(carry_sums, block_items):
        grad_key_sum, grad_value_sum = carry_sums
        block_query, block_segment, block_log, block_grad = block_items
        scores = attention_scores(block_query, block_segment, key_heads, segment)
        probabilities = jnp.exp(scores - block_log[:, :, None])
        probs_low = probabilities.astype(narrow_type)
        grad_value_sum = grad_value_sum + jnp.einsum(
            "hqk,qhe->khe", probs_low, block_grad, preferred_element_type=wide_type
        )
        grad_probs = jnp.einsum(
            "qhe,khe->hqk", block_grad, value_heads, preferred_element_type=wide_type
        )
        grad_scores = probabilities * (
            grad_probs - jnp.sum(probabilities * grad_probs, axis=-1, keepdims=True)
        )
        grad_low = grad_scores.astype(narrow_type)
        grad_query = jnp.einsum(
            "hqk,khe->qhe", grad_low, key_heads, preferred_element_type=wide_type
        ) / math.sqrt(HEAD)
        grad_key_sum = grad_key_sum + jnp.einsum(
            "hqk,qhe->khe", grad_low, block_query, preferred_element_type=wide_type
        ) / math.sqrt(HEAD)
        return ((grad_key_sum, grad_value_sum), grad_query)

    zero_heads = jnp.zeros((row_count, HEADS, HEAD), wide_type)
    block_items = (
        queries.reshape(block_total, block_rows, HEADS, HEAD),
        segment.reshape(block_total, block_rows),
        log_totals,
        grad_mixed.reshape(block_total, block_rows, HEADS, HEAD),
    )
    (grad_key_sum, grad_value_sum), grad_queries = lax.scan(
        one_block, (zero_heads, zero_heads), block_items
    )
    return (
        grad_queries.reshape(row_count, D),
        grad_key_sum.reshape(row_count, D),
        grad_value_sum.reshape(row_count, D),
    )


def project_heads(normed_low, weights, attn_bias):
    queries = (product(normed_low, weights[0]) + attn_bias[0].astype(wide_type)).astype(narrow_type)
    key_rows = product(normed_low, weights[1]).astype(narrow_type)
    values = (product(normed_low, weights[2]) + attn_bias[1].astype(wide_type)).astype(narrow_type)
    return (queries, key_rows, values)


def feed_half(normed_low, weights, bias_in):
    inner_first = product(normed_low, weights[0]) + bias_in[:D].astype(wide_type)
    inner_second = product(normed_low, weights[1]) + bias_in[D:].astype(wide_type)
    active_first = gelu_exact(inner_first).astype(narrow_type)
    active_second = gelu_exact(inner_second).astype(narrow_type)
    partial_sum = product(active_first, weights[2]) + product(active_second, weights[3])
    return ((inner_first, inner_second), (active_first, active_second), partial_sum)


def feed_half_back(normed_low, weights, inners, actives, grad_rows):
    grad_inners = []
    for number in range(2):
        grad_active = product_right(grad_rows, weights[2 + number])
        value_out, gelu_pull = jax.vjp(gelu_exact, inners[number])
        grad_inners.append(gelu_pull(grad_active)[0].astype(narrow_type))
    grad_normed = product_right(grad_inners[0], weights[0]) + product_right(
        grad_inners[1], weights[1]
    )
    grad_bank = jnp.concatenate(
        [
            product_left(normed_low, grad_inners[0]),
            product_left(normed_low, grad_inners[1]),
            product_left(actives[0], grad_rows),
            product_left(actives[1], grad_rows),
        ],
        axis=0,
    )
    grad_bias_in = jnp.concatenate(
        [
            jnp.sum(grad_inners[0].astype(wide_type), axis=0),
            jnp.sum(grad_inners[1].astype(wide_type), axis=0),
        ]
    )
    return (grad_normed, grad_bank, grad_bias_in)


def on_device(
    patches,
    lead_times,
    short_lengths,
    cotangent,
    bank,
    patch_w,
    patch_b,
    var_emb,
    agg_query,
    agg_bias,
    lead_embed,
    norm_gain,
    norm_bias,
    attn_bias,
    fc1_bias,
    fc2_bias,
):
    params = (
        patch_w,
        patch_b,
        var_emb,
        agg_query,
        agg_bias,
        lead_embed,
        norm_gain,
        norm_bias,
        attn_bias,
        fc1_bias,
        fc2_bias,
    )
    micro_total = patches.shape[0]
    row_count = patches.shape[1]
    section_total = lax.axis_size("section")
    section_index = lax.axis_index("section")
    gathered = lax.all_gather(bank, "dp", axis=1, tiled=True)[0]
    weights = tuple((gathered[number * D : (number + 1) * D] for number in range(4)))
    short_segment, short_places = layout(short_lengths[0], row_count)
    segments = jnp.stack([short_segment, jnp.zeros((row_count,), jnp.int32)])
    places_all = jnp.stack([short_places, jnp.arange(row_count, dtype=jnp.int32)])
    valid_rows = jnp.stack([short_segment < short_lengths.shape[1], jnp.ones((row_count,), bool)])
    grad_out_all = jnp.where(valid_rows[:, :, None], cotangent, jnp.zeros_like(cotangent))
    block_rows = min(512, row_count)
    block_total = row_count // block_rows
    zeros_stream = jnp.zeros((row_count, D), narrow_type)
    zeros_final = jnp.zeros((row_count, D), wide_type)
    zeros_pixels = jnp.zeros((row_count, VARS * PIX), wide_type)
    stash_zero = (
        zeros_stream,
        zeros_stream,
        zeros_stream,
        zeros_stream,
        jnp.zeros((block_total, HEADS, block_rows), wide_type),
    )
    small_zero = tuple((jnp.zeros(array_item.shape, wide_type) for array_item in params))

    def forward_embed(operands):
        first_in, second_in, pixel_rows, places, lead_time, segment = operands
        setup = embed_setup(weights, params)

        def one_block(block_items):
            return embed_rows(block_items[0], block_items[1], lead_time, setup, weights, params)[0]

        streams = lax.map(
            one_block,
            (
                pixel_rows.reshape(block_total, block_rows, VARS * PIX),
                places.reshape(block_total, block_rows),
            ),
        )
        return (streams.reshape(row_count, D), zeros_stream, zeros_final, stash_zero)

    def forward_attend(operands):
        first_in, second_in, pixel_rows, places, lead_time, segment = operands
        stream = first_in.astype(wide_type)
        normed_low = norm_layer(
            stream, norm_gain[0].astype(wide_type), norm_bias[0].astype(wide_type)
        ).astype(narrow_type)
        queries, key_rows, values = project_heads(normed_low, weights, attn_bias)
        mixed_heads, log_totals = attention_forward(queries, key_rows, values, segment)
        new_stream = stream + product(mixed_heads, weights[3]) + attn_bias[2].astype(wide_type)
        return (new_stream.astype(narrow_type), zeros_stream, zeros_final, stash_zero)

    def forward_first(operands):
        first_in, second_in, pixel_rows, places, lead_time, segment = operands
        stream = first_in.astype(wide_type)
        normed_low = norm_layer(
            stream, norm_gain[1].astype(wide_type), norm_bias[1].astype(wide_type)
        ).astype(narrow_type)
        inners, actives, partial_sum = feed_half(normed_low, weights, fc1_bias[: 2 * D])
        return (normed_low, (stream + partial_sum).astype(narrow_type), zeros_final, stash_zero)

    def forward_second(operands):
        first_in, second_in, pixel_rows, places, lead_time, segment = operands
        inners, actives, partial_sum = feed_half(first_in, weights, fc1_bias[2 * D :])
        final_rows = second_in.astype(wide_type) + partial_sum + fc2_bias.astype(wide_type)
        return (zeros_stream, zeros_stream, final_rows, stash_zero)

    def forward_none(operands):
        return (zeros_stream, zeros_stream, zeros_final, stash_zero)

    def backward_embed(operands):
        (
            first_kept,
            second_kept,
            grad_in,
            pixel_rows,
            places,
            lead_time,
            segment,
            grad_rows,
            stash_items,
        ) = operands
        setup = embed_setup(weights, params)

        def one_block(totals, block_items):
            block_pixels, block_places, block_grad = block_items
            block_stream, saved_state = embed_rows(
                block_pixels, block_places, lead_time, setup, weights, params
            )
            block_dx, sums = embed_back(block_grad, lead_time, setup, saved_state, weights)
            return (
                tuple((total_item + sum_item for total_item, sum_item in zip(totals, sums))),
                block_dx,
            )

        zero_totals = (
            jnp.zeros((D, D), wide_type),
            jnp.zeros((D,), wide_type),
            jnp.zeros((D,), wide_type),
            jnp.zeros((D, D), wide_type),
            jnp.zeros((VARS * PIX + VARS, D), wide_type),
            jnp.zeros((VARS, PIX, HEADS), wide_type),
            jnp.zeros((VARS, HEADS), wide_type),
            jnp.zeros((2, D), wide_type),
        )
        block_items = (
            pixel_rows.reshape(block_total, block_rows, VARS * PIX),
            places.reshape(block_total, block_rows),
            grad_in.reshape(block_total, block_rows, D),
        )
        totals, grad_pixels = lax.scan(one_block, zero_totals, block_items)
        grad_bank, smalls = embed_finish(totals, setup, weights, params)
        return (zeros_stream, grad_bank, smalls, grad_pixels.reshape(row_count, VARS * PIX))

    def backward_attend(operands):
        (
            first_kept,
            second_kept,
            grad_in,
            pixel_rows,
            places,
            lead_time,
            segment,
            grad_rows,
            stash_items,
        ) = operands
        stream = first_kept.astype(wide_type)
        normed, norm_pull = jax.vjp(
            norm_layer, stream, norm_gain[0].astype(wide_type), norm_bias[0].astype(wide_type)
        )
        normed_low = normed.astype(narrow_type)
        queries, key_rows, values = project_heads(normed_low, weights, attn_bias)
        mixed_heads, log_totals = attention_forward(queries, key_rows, values, segment)
        grad_in_wide = grad_in.astype(wide_type)
        grad_w_out = product_left(mixed_heads, grad_in)
        grad_mixed = product_right(grad_in, weights[3]).astype(narrow_type)
        grad_queries, grad_keys, grad_values = attention_backward(
            queries, key_rows, values, segment, log_totals, grad_mixed
        )
        grad_queries = grad_queries.astype(narrow_type)
        grad_keys = grad_keys.astype(narrow_type)
        grad_values = grad_values.astype(narrow_type)
        grad_normed = (
            product_right(grad_queries, weights[0])
            + product_right(grad_keys, weights[1])
            + product_right(grad_values, weights[2])
        )
        grad_stream, grad_gain, grad_shift = norm_pull(grad_normed)
        grad_send = (grad_in_wide + grad_stream).astype(narrow_type)
        grad_bank = jnp.concatenate(
            [
                product_left(normed_low, grad_queries),
                product_left(normed_low, grad_keys),
                product_left(normed_low, grad_values),
                grad_w_out,
            ],
            axis=0,
        )
        bias_rows = jnp.stack(
            [
                jnp.sum(grad_queries.astype(wide_type), axis=0),
                jnp.sum(grad_values.astype(wide_type), axis=0),
                jnp.sum(grad_in_wide, axis=0),
            ]
        )
        smalls = (
            small_zero[:6]
            + (
                jnp.zeros((2, D), wide_type).at[0].set(grad_gain),
                jnp.zeros((2, D), wide_type).at[0].set(grad_shift),
                bias_rows,
            )
            + small_zero[9:]
        )
        return (grad_send, grad_bank, smalls, zeros_pixels)

    def backward_first(operands):
        (
            first_kept,
            second_kept,
            grad_in,
            pixel_rows,
            places,
            lead_time,
            segment,
            grad_rows,
            stash_items,
        ) = operands
        stream = first_kept.astype(wide_type)
        normed, norm_pull = jax.vjp(
            norm_layer, stream, norm_gain[1].astype(wide_type), norm_bias[1].astype(wide_type)
        )
        normed_low = normed.astype(narrow_type)
        inners, actives, partial_sum = feed_half(normed_low, weights, fc1_bias[: 2 * D])
        grad_normed, grad_bank, grad_bias_in = feed_half_back(
            normed_low, weights, inners, actives, grad_rows
        )
        grad_stream, grad_gain, grad_shift = norm_pull(grad_normed + grad_in.astype(wide_type))
        grad_send = (grad_rows.astype(wide_type) + grad_stream).astype(narrow_type)
        smalls = small_zero[:6] + (
            jnp.zeros((2, D), wide_type).at[1].set(grad_gain),
            jnp.zeros((2, D), wide_type).at[1].set(grad_shift),
            small_zero[8],
            jnp.zeros((FF,), wide_type).at[: 2 * D].set(grad_bias_in),
            small_zero[10],
        )
        return (grad_send, grad_bank, smalls, zeros_pixels)

    def backward_second(operands):
        (
            first_kept,
            second_kept,
            grad_in,
            pixel_rows,
            places,
            lead_time,
            segment,
            grad_rows,
            stash_items,
        ) = operands
        inners, actives, partial_sum = feed_half(first_kept, weights, fc1_bias[2 * D :])
        grad_normed, grad_bank, grad_bias_in = feed_half_back(
            first_kept, weights, inners, actives, grad_rows
        )
        smalls = small_zero[:9] + (
            jnp.zeros((FF,), wide_type).at[2 * D :].set(grad_bias_in),
            jnp.sum(grad_rows.astype(wide_type), axis=0),
        )
        return (grad_normed.astype(narrow_type), grad_bank, smalls, zeros_pixels)

    def backward_none(operands):
        return (zeros_stream, jnp.zeros((4 * D, D), wide_type), small_zero, zeros_pixels)

    forward_list = [forward_embed, forward_attend, forward_first, forward_second, forward_none]
    backward_list = [
        backward_embed,
        backward_attend,
        backward_first,
        backward_second,
        backward_none,
    ]
    tick_total = micro_total + section_total - 1
    first_message, second_message = (zeros_stream, zeros_stream)
    kept_first = jnp.zeros((micro_total, row_count, D), narrow_type)
    kept_second = jnp.zeros((micro_total, row_count, D), narrow_type)
    stash_all = tuple(
        (
            jnp.zeros((micro_total,) + array_item.shape, array_item.dtype)
            for array_item in stash_zero
        )
    )
    final_all = jnp.zeros((micro_total, row_count, D), wide_type)
    for tick_number in range(tick_total):
        micro_index = tick_number - section_index
        running = jnp.logical_and(micro_index >= 0, micro_index < micro_total)
        slot_index = jnp.clip(micro_index, 0, micro_total - 1)
        kept_first = kept_first.at[slot_index].set(
            jnp.where(running, first_message, kept_first[slot_index])
        )
        kept_second = kept_second.at[slot_index].set(
            jnp.where(running, second_message, kept_second[slot_index])
        )
        branch = jnp.where(running, section_index, section_total)
        operands = (
            first_message,
            second_message,
            patches[slot_index],
            places_all[slot_index],
            lead_times[slot_index, 0],
            segments[slot_index],
        )
        first_out, second_out, final_rows, stash_items = lax.switch(branch, forward_list, operands)
        final_all = final_all.at[slot_index].add(final_rows)
        stash_all = tuple(
            (
                buffer.at[slot_index].set(jnp.where(running, array_item, buffer[slot_index]))
                for buffer, array_item in zip(stash_all, stash_items)
            )
        )
        if tick_number < tick_total - 1:
            first_message, second_message = (
                from_behind(shortened(first_out), "section", 1).astype(first_out.dtype),
                from_behind(shortened(second_out), "section", 1).astype(second_out.dtype),
            )
    grad_message = zeros_stream
    bank_total = jnp.zeros((4 * D, D), wide_type)
    small_total = small_zero
    pixel_total = jnp.zeros((micro_total, row_count, VARS * PIX), wide_type)
    for tick_number in range(tick_total):
        micro_index = tick_number - (section_total - 1 - section_index)
        running = jnp.logical_and(micro_index >= 0, micro_index < micro_total)
        slot_index = jnp.clip(micro_index, 0, micro_total - 1)
        branch = jnp.where(running, section_index, section_total)
        operands = (
            kept_first[slot_index],
            kept_second[slot_index],
            grad_message,
            patches[slot_index],
            places_all[slot_index],
            lead_times[slot_index, 0],
            segments[slot_index],
            grad_out_all[slot_index],
            tuple((buffer[slot_index] for buffer in stash_all)),
        )
        grad_send, grad_bank, smalls, grad_pixels = lax.switch(branch, backward_list, operands)
        bank_total = bank_total + grad_bank
        small_total = tuple(
            (total_item + sum_item for total_item, sum_item in zip(small_total, smalls))
        )
        pixel_total = pixel_total.at[slot_index].add(grad_pixels)
        if tick_number < tick_total - 1:
            grad_message = jax.tree.map(
                lambda part, own: part.astype(own.dtype),
                from_behind(shortened(grad_send), "section", -1),
                grad_send,
            )
    bank_share = lax.psum_scatter(
        bank_total.astype(jnp.bfloat16), "dp", scatter_dimension=0, tiled=True
    ).astype(jnp.float32)[None]
    small_sums = lax.psum(small_total, ("section", "dp"))
    output_share, pixel_share = (
        lax.psum_scatter(
            final_all.astype(jnp.bfloat16), "section", scatter_dimension=2, tiled=True
        ).astype(jnp.float32),
        lax.psum_scatter(
            pixel_total.astype(jnp.bfloat16), "section", scatter_dimension=2, tiled=True
        ).astype(jnp.float32),
    )
    output_low = output_share.astype(narrow_type)
    return (output_low, pixel_share, bank_share) + tuple(small_sums)


def solution(mesh):
    ins, outs = specs()
    small_slice = mesh.shape["section"] == 4 and mesh.shape["dp"] == 8
    body = on_device_fast if small_slice else on_device
    return jax.shard_map(body, mesh=mesh, in_specs=ins, out_specs=outs, check_vma=False)
```

```python
import functools
import math

import jax
import jax.numpy as jnp
from jax import lax
from jax.experimental import pallas as pl
from jax.experimental.pallas import tpu as pltpu
from jax.sharding import PartitionSpec as P

D = 1024
HEADS = 16
HEAD = 64
FF = 4096
VARS = 48
PIX = 4
F32 = jnp.float32
BF = jnp.bfloat16
MESH = pl.DeviceIdType.MESH
ROWS = 512
GROUP = 256
OWN = 128


def mm(a, b):
    return jnp.dot(a, b, preferred_element_type=F32)


def mm_nt(a, b):
    return lax.dot_general(a, b, (((1,), (1,)), ((), ())), preferred_element_type=F32)


def mm_tn(a, b):
    return lax.dot_general(a, b, (((0,), (0,)), ((), ())), preferred_element_type=F32)


def loop(count, body):
    def step(i, carry):
        body(i)
        return carry

    lax.fori_loop(0, count, step, 0)


def at(start, size, unit):
    return pl.ds(pl.multiple_of(start, unit), size)


def iota(shape, axis):
    return lax.broadcasted_iota(jnp.int32, shape, axis)


def normed_rows(x, gain, shift):
    centre = x - jnp.mean(x, axis=1, keepdims=True)
    rs = lax.rsqrt(jnp.mean(centre * centre, axis=1, keepdims=True) + 1e-5)
    return centre * rs * gain + shift


def norm_back(x, g, gain):
    centre = x - jnp.mean(x, axis=1, keepdims=True)
    rs = lax.rsqrt(jnp.mean(centre * centre, axis=1, keepdims=True) + 1e-5)
    xhat = centre * rs
    q = g * gain
    gx = rs * (q - jnp.mean(q, axis=1, keepdims=True) - xhat * jnp.mean(q * xhat, axis=1, keepdims=True))
    return gx, jnp.sum(g * xhat, axis=0, keepdims=True), jnp.sum(g, axis=0, keepdims=True)


def column_sum(x):
    return jnp.sum(x, axis=0, keepdims=True)


class Place:
    def __init__(self):
        self.s = lax.axis_index("section")
        j = lax.axis_index("dp")
        self.z = lax.div(j, 2)
        self.c = lax.rem(j, 2)
        self.outer = (self.z == 0) | (self.z == 3)
        self.far = jnp.where(self.outer, self.z ^ 2, self.z ^ 3)

    def dev(self, s, z, c):
        return (s, z * 2 + c)


def remote(src, dst, ss, rs, dev):
    return pltpu.make_async_remote_copy(
        src_ref=src, dst_ref=dst, send_sem=ss, recv_sem=rs, device_id=dev, device_id_type=MESH
    )


def arrived(dst, sem):
    pltpu.make_async_copy(dst, dst, sem).wait()


def sent(src, sem):
    pltpu.make_async_copy(src, src, sem).wait()


def barrier(devs):
    sem = pltpu.get_barrier_semaphore()
    for dev in devs:
        pl.semaphore_signal(sem, 1, device_id=dev, device_id_type=MESH)
    pl.semaphore_wait(sem, len(devs))


SCRATCH = dict(
    vec=((24, 1024), F32),
    table=((256, 1024), BF),
    tabT=((1024, 256), BF),
    msgs=((4, 512, 256), BF),
    W=((4, 4, 2, 512, 256), BF),
    WF=((3, 4, 2, 512, 256), BF),
    qbuf=((2, 8, 1024), F32),
    qb=((16, 1024), BF),
    kq=((2, 16, 512), BF),
    mT=((1024, 256), BF),
    mS=((512, 256), BF),
    patT=((192, 512), BF),
    fill=((1536, 192), BF),
    fo=((16, 256), F32),
    att=((768, 512), F32),
    op=((256, 512), BF),
    op1=((256, 128), BF),
    hT=((1024, 512), BF),
    hrow=((512, 1024), BF),
    acc=((512, 1024), F32),
    st0=((512, 1024), BF),
    nrm=((512, 1024), BF),
    nrm2=((512, 1024), BF),
    tr=((1024, 512), BF),
    q=((512, 256), BF),
    k=((512, 256), BF),
    v=((512, 256), BF),
    attp=((8, 256, 256), F32),
    mix=((512, 1024), BF),
    st1=((512, 1024), BF),
    act=((4, 512, 256), BF),
    gact=((4, 512, 256), F32),
    gin=((4, 512, 256), BF),
    gout=((512, 1024), BF),
    rsS=((512, 1024), BF),
    rsR=((4, 128, 1024), BF),
    gs=((2, 128, 1024), BF),
    gmS=((4, 128, 256), BF),
    gm=((512, 256), BF),
    ga=((512, 256), BF),
    gb=((512, 256), BF),
    gq=((3, 512, 256), BF),
    CR=((13, 512, 256), BF),
    RC=((2, 4, 512, 256), BF),
    RA=((4, 512, 256), BF),
    RB=((4, 512, 256), BF),
    FR=((4, 512, 256), BF),
    outR=((4, 512, 256), BF),
    gh=((128, 1024), BF),
    ghT=((1024, 128), BF),
    gpT=((192, 128), F32),
    gsc=((768, 128), F32),
    small=((16, 1024), F32),
    pixS=((4, 48, 128), BF),
    pixR=((4, 48, 128), BF),
    gall=((256, 1024), BF),
    fin=((256, 1024), BF),
    fromc=((128, 1024), BF),
    fromp=((4, 32, 1024), BF),
    fromz=((4, 32, 1024), BF),
    fc=((2, 16, 256), F32),
    fp=((4, 16, 256), F32),
    fz=((4, 16, 256), F32),
    gqv=((16, 1024), BF),
    qx=((2, 8, 1024), F32),
    gaq=((2, 8, 512), F32),
)

SEMS = dict(
    rW=(4, 4, 2),
    rF=(3, 4, 2),
    sMsg=(4,),
    sOwn=(4, 2),
    sFwd=(4, 4, 2),
    sFx=(3, 3),
    sFc=(3, 4),
    rQ=(2,),
    sQ=(2,),
    rK=(2,),
    sK=(16,),
    rMx=(1,),
    sMx=(1,),
    rM=(4, 2),
    sMa=(4,),
    sMz=(3,),
    sMp=(3,),
    sMc=(4,),
    sMix=(3,),
    rMix=(4,),
    sOut=(4,),
    rOut=(4,),
    sR=(2, 4),
    rR=(2, 4),
    sG=(3, 4),
    rG=(3, 4),
    sC=(4, 4),
    rC=(4, 4),
    sZ=(4, 4),
    rRC=(2, 4),
    rRA=(4,),
    rRB=(4,),
    sFin=(4,),
    rFin=(4,),
    sP=(4,),
    rP=(4,),
    sAll=(14,),
    rAll=(14,),
    sFo=(8,),
    rFo=(12,),
    sGq=(18,),
    rGq=(2,),
    sGa=(16,),
    rGa=(2,),
)
NAMES = list(SCRATCH) + list(SEMS)


class Refs:
    pass


def block_kernel(
    pat,
    lead,
    lens,
    cot,
    bank,
    patch,
    patch_b,
    var_emb,
    agg_query,
    agg_bias,
    lead_embed,
    norm_gain,
    norm_bias,
    attn_bias,
    fc1,
    fc2,
    out,
    gpix,
    gbank,
    gtab,
    sums,
    rows_out,
    *scratch,
):
    R = Refs()
    for name, ref in zip(NAMES, scratch):
        setattr(R, name, ref)
    here = Place()
    s, z, c = here.s, here.z, here.c
    dev = here.dev
    outer = here.outer
    inner = jnp.logical_not(outer)
    sib = dev(s, z, 1 - c)
    is_row = (s >= 2) & (z >= 2)
    peers = [s ^ 1, s ^ 2, s ^ 3]
    layers = [z ^ 1, z ^ 2, z ^ 3]
    others = [(s ^ i, z ^ k) for k in range(4) for i in range(4) if (i, k) != (0, 0)]
    vec, table = R.vec, R.table
    when = pl.when
    no = jnp.logical_not

    barrier([dev(p, k, c) for p, k in others] + [dev(p, z, 1 - c) for p in peers] + [sib])

    first_owner = (s == 0) & (z == 0)
    key_owner = (s == 0) & (z == 1)
    value_owner = (s == 0) & (z == 2)

    late = value_owner
    used = no((s == 0) & (z < 3))

    @when(no(is_row) & (used | late))
    def _():
        for p in range(4):
            R.msgs[p] = bank[:, p * 256 : (p + 1) * 256]

    @when(is_row)
    def _():
        for m in range(4):
            q, h = m // 2, m % 2
            for n in range(2):
                lo = (2 * h + n) * 256
                R.msgs[m, n * 256 : (n + 1) * 256, :] = bank[q * 256 : (q + 1) * 256, lo : lo + 256]

    def message(m):
        tp = jnp.where(is_row, 2 * c + m // 2, m)
        tc = jnp.where(is_row, m % 2, c)
        return tp, tc, (tp == s) & (tc == c)

    def scatter(cond):
        for m in range(4):
            tp, tc, own = message(m)

            @when(cond & own)
            def _():
                pltpu.make_async_copy(R.msgs.at[m], R.W.at[z, s, c], R.rW.at[z, s, c]).start()

            @when(cond & no(own))
            def _():
                remote(R.msgs.at[m], R.W.at[z, s, tc], R.sMsg.at[m], R.rW.at[z, s, tc], dev(tp, z, tc)).start()

    scatter(used)

    vec[0:3, :] = agg_bias[...].astype(F32)
    vec[3:5, :] = lead_embed[...].astype(F32)
    vec[5:7, :] = norm_gain[...].astype(F32)
    vec[7:9, :] = norm_bias[...].astype(F32)
    vec[9:12, :] = attn_bias[...].astype(F32)
    vec[12:16, :] = fc1[...].astype(F32)
    vec[16:17, :] = fc2[...].astype(F32)
    vec[17:18, :] = agg_query[...].astype(F32)

    @when(first_owner)
    def _():
        part = jnp.broadcast_to(vec[17:18, at(c * 512, 512, 512)].astype(BF), (16, 512))
        R.qbuf[0] = mm(part, bank[...])[0:8]
        remote(R.qbuf.at[0], R.qbuf.at[1], R.sQ.at[0], R.rQ.at[0], sib).start()

    perm = jnp.where(
        (iota((192, 192), 0) // 48 == iota((192, 192), 1) % 4) & (iota((192, 192), 0) % 48 == iota((192, 192), 1) // 4),
        1.0,
        0.0,
    ).astype(BF)
    for i in range(4):
        cols = slice(i * 256, (i + 1) * 256)
        table[0:192, cols] = mm(perm, patch[:, cols]).astype(BF)
    table[192:240, :] = (patch_b[...].astype(F32) + var_emb[...].astype(F32)).astype(BF)
    table[240:256, :] = jnp.zeros((16, 1024), BF)

    other_rows = at((1 - c) * 512, 512, 512)
    half_rows = at(c * 512, 512, 512)

    @when(value_owner)
    def _():
        for i in range(4):
            R.tabT[i * 256 : (i + 1) * 256, :] = table[:, i * 256 : (i + 1) * 256].T
        for h in range(2):
            R.gact[h] = mm_tn(bank[:, h * 512 : (h + 1) * 512], R.tabT[half_rows, :])
        remote(R.gact.at[1 - c], R.gact.at[2], R.sMx.at[0], R.rMx.at[0], sib).start()

    @when(first_owner)
    def _():
        arrived(R.qbuf.at[1], R.rQ.at[0])
        total = R.qbuf[0] + R.qbuf[1] + vec[0:1, :]
        total = total.astype(BF)
        R.qb[...] = jnp.concatenate([total, total], axis=0)
        remote(R.qb, R.qb, R.sQ.at[1], R.rQ.at[1], dev(0, 1, c)).start()

    def piece_of(p, h):
        return R.mT.at[at(p * 256 + h * 128, 128, 128), :]

    def my_piece(m):
        return R.mS.at[(m // 2) * 256 + (m % 2) * 128 : (m // 2) * 256 + (m % 2) * 128 + 128, :]

    @when(value_owner)
    def _():
        arrived(R.gact.at[2], R.rMx.at[0])
        sent(R.gact.at[2], R.sMx.at[0])
        bias = jnp.broadcast_to(vec[1:2, half_rows], (8, 512)).T[:, 0:1]
        total = R.gact[c] + R.gact[2]
        R.mS[...] = jnp.where(iota((1, 256), 1) == 240, bias, total).astype(BF)
        for m in range(4):
            q, h = m // 2, m % 2
            tp = 2 * c + q
            own = (tp == s) & (c == h)

            @when(own)
            def _():
                pltpu.make_async_copy(my_piece(m), piece_of(tp, h), R.rM.at[tp, h]).start()

            @when(no(own))
            def _():
                remote(my_piece(m), piece_of(tp, h), R.sMa.at[m], R.rM.at[tp, h], dev(tp, z, h)).start()

    @when(key_owner)
    def _():
        arrived(R.qb, R.rQ.at[1])
        masked = jnp.where(iota((16, 1024), 1) // HEAD == iota((16, 1024), 0), R.qb[...].astype(F32), 0.0).astype(BF)
        R.kq[c] = mm_nt(masked, bank[...]).astype(BF)
        for i, (p, k) in enumerate(others):
            remote(R.kq.at[c], R.kq.at[c], R.sK.at[i], R.rK.at[c], dev(p, k, c)).start()

    def at_least(zz, b):
        return zz == 3 if b == 0 else zz >= 0

    def full_of(zz, b):
        if b == 0:
            return True, zz - 2
        if b == 1:
            return zz == 3, 2
        return None, None

    def spread(zz, b):
        block = R.W.at[zz, b, c]
        whole, f = full_of(zz, b)

        def to_sibling():
            remote(block, block, R.sFwd.at[zz, b, 0], R.rW.at[zz, b, c], sib).start()

        def to_layer():
            pltpu.make_async_copy(block, R.WF.at[f, s, c], R.rF.at[f, s, c]).start()
            for i, p in enumerate(peers):
                remote(block, R.WF.at[f, s, c], R.sFx.at[f, i], R.rF.at[f, s, c], dev(p, z, c)).start()

        if whole is None:
            to_sibling()
        elif whole is True:
            to_layer()
        else:
            when(no(whole))(to_sibling)
            when(whole)(to_layer)

    def near(cond, b):
        block = R.W.at[z, b, c]

        @when(cond)
        def _():
            remote(block, block, R.sOwn.at[b, 0], R.rW.at[z, b, c], dev(s, z ^ 1, c)).start()

    def step(cond, b, side=True, hold=False):
        block = R.W.at[z, b, c]

        @when(cond)
        def _():
            arrived(block, R.rW.at[z, b, c])

        @when(cond & outer)
        def _():
            remote(block, block, R.sOwn.at[b, 1], R.rW.at[z, b, c], dev(s, z ^ 2, c)).start()
            remote(block, block, R.sOwn.at[b, 0], R.rW.at[z, b, c], dev(s, z ^ 1, c)).start()

        if not hold:
            near(cond & inner, b)

        @when(cond & inner)
        def _():
            remote(block, block, R.sOwn.at[b, 1], R.rW.at[z, b, c], dev(s, z ^ 3, c)).start()

        if side:

            @when(cond)
            def _():
                spread(z, b)

    def foreign(zz, b, cond=True):
        block = R.W.at[zz, b, c]

        @when(cond & (z != zz))
        def _():
            arrived(block, R.rW.at[zz, b, c])

        @when(cond & (z != zz) & inner & (z ^ 1 != zz))
        def _():
            remote(block, block, R.sFwd.at[zz, b, 1], R.rW.at[zz, b, c], dev(s, z ^ 1, c)).start()

        @when(cond & (z != zz))
        def _():
            spread(zz, b)

    always = z >= 0
    top = z == 3
    @when(z == 2)
    def _():
        arrived(piece_of(s, c), R.rM.at[s, c])
        for i, zz in enumerate(layers):
            remote(piece_of(s, c), piece_of(s, c), R.sMz.at[i], R.rM.at[s, c], dev(s, zz, c)).start()
        for i, p in enumerate(peers):
            remote(piece_of(s, c), piece_of(s, c), R.sMp.at[i], R.rM.at[s, c], dev(p, z, c)).start()

    step(top & (s == 0), 0, False)
    step(no(top) & (s == 1), 1)
    for b in (2, 3):
        step(s == b, b)

    tcol = iota((GROUP, 1), 0).astype(F32)
    trow = iota((1, GROUP), 1).astype(F32)
    start_col = jnp.zeros((GROUP, 1), F32)
    seg_col = jnp.zeros((GROUP, 1), F32)
    seg_row = jnp.zeros((1, GROUP), F32)
    end = jnp.float32(0.0)
    for i in range(4):
        end = end + lens[0, i].astype(F32)
        past = tcol >= end
        seg_col = seg_col + jnp.where(past, 1.0, 0.0)
        seg_row = seg_row + jnp.where(trow >= end, 1.0, 0.0)
        start_col = jnp.maximum(start_col, jnp.where(past, end, 0.0))
    place_short = tcol - start_col
    valid = seg_col < 3.5
    lead_short = lead[0, 0]
    lead_long = lead[1, 0]
    freq = jnp.exp(-math.log(10000.0) * 2.0 * iota((1, 512), 1).astype(F32) / D)

    def positions(g):
        place = place_short if g == 0 else tcol
        lead_g = lead_short if g == 0 else lead_long
        base = lead_g * vec[3:4, :] + vec[4:5, :] + vec[2:3, :]
        angle = place * freq
        R.acc[g * GROUP : (g + 1) * GROUP, 0:512] = jnp.sin(angle) + base[:, 0:512]
        R.acc[g * GROUP : (g + 1) * GROUP, 512:1024] = jnp.cos(angle) + base[:, 512:1024]

    positions(0)
    step(top & (s != 0), 0, False)
    step(no(top) & (s != 1), 1)
    step(top, 1, False)

    positions(1)

    gout = R.gout
    gout[0:GROUP, :] = jnp.where(valid, cot[0:GROUP, :].astype(F32), 0.0).astype(BF)
    gout[GROUP:ROWS, :] = cot[GROUP:ROWS, :]

    @when(no(key_owner))
    def _():
        arrived(R.kq.at[c], R.rK.at[c])

    remote(R.kq.at[c], R.kq.at[c], R.sK.at[15], R.rK.at[c], sib).start()
    R.patT[...] = mm_nt(perm, pat[...]).astype(BF)

    @when(z != 2)
    def _():
        arrived(piece_of(s, c), R.rM.at[s, c])
        for i, p in enumerate(peers):
            remote(piece_of(s, c), piece_of(s, c), R.sMp.at[i], R.rM.at[s, c], dev(p, z, c)).start()

    @when(top)
    def _():
        spread(3, 0)

    for b in (2, 3):
        step(s != b, b, hold=True)
    scatter(late)

    arrived(R.kq.at[1 - c], R.rK.at[1 - c])
    kq_full = jnp.concatenate([R.kq[0], R.kq[1]], axis=1)
    R.fo[...] = mm_nt(kq_full, table[...])

    def fill_head(h):
        row = R.fo[pl.ds(h, 1), 0:192]
        value = jnp.where(iota((48, 192), 1) % 48 == iota((48, 192), 0), row, 0.0)
        high = value.astype(BF)
        R.fill[at(h * 48, 48, 16), :] = high
        R.fill[at(768 + h * 48, 48, 16), :] = (value - high.astype(F32)).astype(BF)

    loop(HEADS, fill_head)

    def score_part(i):
        lo = i * 256
        R.att[at(lo, 256, 256), :] = mm(R.fill[at(lo, 256, 256), :], R.patT[...]) + mm(
            R.fill[at(768 + lo, 256, 256), :], R.patT[...]
        )

    loop(3, score_part)

    foreign(3, 0)

    for i, p in enumerate([s] + peers):
        if i > 0:
            arrived(piece_of(p, c), R.rM.at[p, c])
        remote(piece_of(p, c), piece_of(p, c), R.sMc.at[p], R.rM.at[p, c], sib).start()

    for p in range(4):
        arrived(piece_of(p, 1 - c), R.rM.at[p, 1 - c])

    for zz in range(3):
        foreign(zz, 1, inner)
    for b in (2, 3):
        near(inner & (s != b), b)
    R.op[240:256, :] = jnp.where(iota((16, 512), 0) == 0, 1.0, 0.0).astype(BF)
    r48 = iota((48, 256), 0)
    c48 = iota((48, 256), 1)

    def weights_of(op, low, cols):
        lowf = low.astype(F32)
        for p in range(4):
            op[p * 48 : (p + 1) * 48, :] = (lowf * R.patT[p * 48 : (p + 1) * 48, cols].astype(F32)).astype(BF)
        op[192:240, :] = low

    def embed_head(h):
        offset = jnp.sum(jnp.where(c48 == r48 + 192, R.fo[pl.ds(h, 1), :], 0.0), axis=1, keepdims=True)
        rows = at(h * 48, 48, 16)
        scores = (R.att[rows, :] + offset) * (1.0 / math.sqrt(HEAD))
        peak = jnp.max(scores, axis=0, keepdims=True)
        e = jnp.exp(scores - peak)
        prob = e / jnp.sum(e, axis=0, keepdims=True)
        R.att[rows, :] = prob
        weights_of(R.op, prob.astype(BF), slice(None))
        hrows = at(h * 64, 64, 64)
        R.hT[hrows, :] = mm(R.mT[hrows, :], R.op[...]).astype(BF)

    loop(HEADS, embed_head)

    def pass_on(f):
        for p in [s] + peers:
            block = R.WF.at[f, p, c]
            arrived(block, R.rF.at[f, p, c])
            remote(block, block, R.sFc.at[f, p], R.rF.at[f, p, c], sib).start()

    def wait_whole(f):
        for p in range(4):
            arrived(R.WF.at[f, p, 1 - c], R.rF.at[f, p, 1 - c])

    pass_on(1)

    def turn_tile(i):
        rows = at(i * 256, 256, 256)
        R.hrow[:, rows] = R.hT[rows, :].T

    loop(4, turn_tile)
    for zz in range(3):
        foreign(zz, 1, outer)
    foreign(3, 1, inner)

    @when(top)
    def _():
        spread(3, 1)

    foreign(z ^ 3, 2, inner)
    wait_whole(1)

    def stream0_part(i):
        g = lax.div(i, 4)
        n = lax.rem(i, 4)
        rows = at(g * 256, 256, 256)
        cols = at(n * 256, 256, 256)
        value = mm(R.hrow[rows, 0:512], R.WF[1, n, 0]) + mm(R.hrow[rows, 512:1024], R.WF[1, n, 1])
        R.st0[rows, cols] = (value + R.acc[rows, cols]).astype(BF)

    loop(8, stream0_part)

    def norm_into(src, dst, which):
        def part(i):
            rows = at(i * 64, 64, 64)
            dst[rows, :] = normed_rows(
                src[rows, :].astype(F32), vec[5 + which : 6 + which, :], vec[7 + which : 8 + which, :]
            ).astype(BF)

        loop(8, part)

    norm_into(R.st0, R.nrm, 0)
    foreign(z ^ 3, 3, inner)

    foreign(3, 1, outer)

    own_cols = at(s * 256, 256, 256)
    own_rows = at(s * OWN, OWN, OWN)

    def wait_half(zz, b):
        arrived(R.W.at[zz, b, 1 - c], R.rW.at[zz, b, 1 - c])

    def project(zz, dst, bias):
        wait_half(zz, 1)
        weight = R.W[zz, 1].reshape(1024, 256)
        for g in range(2):
            rows = slice(g * 256, (g + 1) * 256)
            value = mm(R.nrm[rows, :], weight)
            if bias is not None:
                value = value + vec[bias : bias + 1, own_cols]
            dst[rows, :] = value.astype(BF)

    project(0, R.q, 9)
    project(1, R.k, None)
    project(2, R.v, 10)

    lane_head = iota((1, 256), 1) // HEAD

    def only(hh, x):
        return jnp.where(lane_head == hh, x.astype(F32), 0.0).astype(BF)

    allowed = seg_col == seg_row

    def attend(g):
        rows = slice(g * 256, (g + 1) * 256)
        total = jnp.zeros((256, 256), F32)
        for hh in range(4):
            scores = mm_nt(R.q[rows, :], only(hh, R.k[rows, :])) * (1.0 / math.sqrt(HEAD))
            if g == 0:
                scores = jnp.where(allowed, scores, -1e30)
            e = jnp.exp(scores - jnp.max(scores, axis=1, keepdims=True))
            prob = e / jnp.sum(e, axis=1, keepdims=True)
            R.attp[g * 4 + hh] = prob
            total = total + mm(prob.astype(BF), only(hh, R.v[rows, :]))
        R.mix[rows, own_cols] = total.astype(BF)

    attend(0)
    attend(1)
    mine = R.mix.at[:, own_cols]
    for i, p in enumerate(peers):
        remote(mine, mine, R.sMix.at[i], R.rMix.at[s], dev(p, z, c)).start()

    step(z == 2, 0)
    for b in (2, 3):
        foreign(z ^ 2, b, inner)
    pass_on(2)
    for b in (2, 3):
        for k in (1, 2, 3):
            foreign(z ^ k, b, outer if k > 1 else True)

    def feed_out_grad(b):
        def part(g):
            rows = at(g * 256, 256, 256)
            block = R.W.at[2 + b % 2, 2 + b // 2]
            total = jnp.zeros((256, 256), F32)
            for n in range(4):
                tile = block[n // 2, (n % 2) * 256 : (n % 2 + 1) * 256, :]
                total = total + mm_nt(gout[rows, n * 256 : (n + 1) * 256], tile)
            R.gact[b, rows, :] = total

        loop(2, part)

    wait_half(2, 2)
    feed_out_grad(0)
    wait_half(3, 2)
    feed_out_grad(1)
    wait_whole(2)
    for p in peers:
        arrived(R.mix.at[:, at(p * 256, 256, 256)], R.rMix.at[p])
    foreign(2, 0)

    def stream1_part(i):
        g = lax.div(i, 4)
        n = lax.rem(i, 4)
        rows = at(g * 256, 256, 256)
        cols = at(n * 256, 256, 256)
        value = mm(R.mix[rows, 0:512], R.WF[2, n, 0]) + mm(R.mix[rows, 512:1024], R.WF[2, n, 1])
        value = value + vec[11:12, cols] + R.st0[rows, cols].astype(F32)
        R.st1[rows, cols] = value.astype(BF)

    loop(8, stream1_part)
    norm_into(R.st1, R.nrm2, 1)
    wait_half(2, 3)
    feed_out_grad(2)
    wait_half(3, 3)
    feed_out_grad(3)
    for b in (2, 3):
        for zz in (0, 1):
            wait_half(zz, b)

    def feed_in(i):
        b = lax.div(i, 2)
        g = lax.rem(i, 2)
        rows = at(g * 256, 256, 256)
        bias = vec[pl.ds(12 + b, 1), own_cols]
        weight = R.W[lax.rem(b, 2), 2 + lax.div(b, 2)].reshape(1024, 256)
        x = mm(R.nrm2[rows, :], weight) + bias
        half_cdf = 0.5 + 0.5 * lax.erf(x * math.sqrt(0.5))
        R.act[b, rows, :] = (x * half_cdf).astype(BF)
        slope = half_cdf + x * (jnp.exp(-0.5 * x * x) * (1.0 / math.sqrt(2.0 * math.pi)))
        R.gin[b, rows, :] = (R.gact[b, rows, :] * slope).astype(BF)

    loop(8, feed_in)

    def reduce_rows(phase, make):
        for i, p in enumerate(peers):
            make(p)
            block = R.rsS.at[at(p * OWN, OWN, OWN), :]
            remote(block, R.rsR.at[s], R.sR.at[phase, i], R.rR.at[phase, s], dev(p, z, c)).start()
        make(s)

    def reduced(phase):
        total = R.rsS[own_rows, :].astype(F32)
        for p in peers:
            arrived(R.rsR.at[p], R.rR.at[phase, p])
            total = total + R.rsR[p].astype(F32)
        return total

    def feed_norm(p):
        rows = at(p * OWN, OWN, OWN)
        total = jnp.zeros((OWN, 1024), F32)
        for b in range(4):
            total = total + mm_nt(R.gin[b, rows, :], R.W[b % 2, 2 + b // 2].reshape(1024, 256))
        R.rsS[rows, :] = total.astype(BF)

    reduce_rows(0, feed_norm)

    def drain_own(cond, b):
        @when(cond)
        def _():
            for i in range(2):
                sent(R.msgs.at[0], R.sOwn.at[b, i])

    def drain_spread(zz, b):
        whole, f = full_of(zz, b)

        def side():
            sent(R.msgs.at[0], R.sFwd.at[zz, b, 0])

        def layer():
            for i in range(3):
                sent(R.msgs.at[0], R.sFx.at[f, i])

        if whole is None or zz < 3:
            (layer if whole is True else side)()
        else:
            layer()

        @when((z != zz) & inner & (z ^ 1 != zz))
        def _():
            sent(R.msgs.at[0], R.sFwd.at[zz, b, 1])

    for b in (2, 3):
        drain_own(always, b)
        for zz in range(4):
            drain_spread(zz, b)

    def transposed(src):
        def part(i):
            a = lax.div(i, 2)
            b = lax.rem(i, 2)
            R.tr[at(a * 256, 256, 256), at(b * 256, 256, 256)] = src[
                at(b * 256, 256, 256), at(a * 256, 256, 256)
            ].T

        loop(8, part)

    def slot(zz, b):
        return 12 if isinstance(b, int) and b == 0 else (b - 1) * 4 + zz

    def exchange(zz, b):
        block = R.W.at[zz, b, 1 - c]
        remote(block, R.CR.at[slot(zz, b)], R.sC.at[zz, b], R.rC.at[zz, b], sib).start()

    def column_gradient(zz, b, left, right):
        for h in range(2):
            R.W[zz, b, h] = mm(left[h * 512 : (h + 1) * 512, :], right).astype(BF)
        exchange(zz, b)

    transposed(R.nrm2)

    def first_gradient(b):
        column_gradient(lax.rem(b, 2), 2 + lax.div(b, 2), R.tr, R.gin[b])

    loop(4, first_gradient)

    def out_part(i):
        g = lax.div(i, 4)
        n = lax.rem(i, 4)
        rows = at(g * 256, 256, 256)
        total = jnp.zeros((256, 256), F32)
        for b in range(4):
            tile = R.W[2 + b % 2, 2 + b // 2, lax.div(n, 2), at(lax.rem(n, 2) * 256, 256, 256), :]
            total = total + mm(R.act[b, rows, :], tile)
        R.hrow[rows, at(n * 256, 256, 256)] = total.astype(BF)

    loop(8, out_part)

    def second_gradient(b):
        zz = 2 + lax.rem(b, 2)
        bb = 2 + lax.div(b, 2)
        for n in range(4):
            tile = mm_tn(R.act[b], gout[:, n * 256 : (n + 1) * 256])
            R.W[zz, bb, n // 2, (n % 2) * 256 : (n % 2 + 1) * 256, :] = tile.astype(BF)
        exchange(zz, bb)

    loop(4, second_gradient)

    def summed(zz, b):
        arrived(R.CR.at[slot(zz, b)], R.rC.at[zz, b])
        sent(R.CR.at[slot(zz, b)], R.sC.at[zz, b])
        R.W[zz, b, c] = (R.W[zz, b, c].astype(F32) + R.CR[slot(zz, b)].astype(F32)).astype(BF)

    def first_send(k, b, cond=True):
        zz = z ^ k
        block = R.W.at[zz, b, c]

        @when(cond)
        def _():
            summed(zz, b)
            if k == 1:
                remote(block, R.RA.at[b], R.sZ.at[zz, b], R.rRA.at[b], dev(s, z ^ 1, c)).start()

        if k > 1:

            @when(cond & outer)
            def _():
                remote(block, R.RC.at[3 - k, b], R.sZ.at[zz, b], R.rRC.at[3 - k, b], dev(s, z ^ 1, c)).start()

    def second_send(zz, b):
        block = R.W.at[zz, b, c]

        @when(inner & (z != zz) & (z ^ 1 != zz))
        def _():
            k = (z ^ zz) - 2
            arrived(R.RC.at[k, b], R.rRC.at[k, b])
            R.W[zz, b, c] = (R.W[zz, b, c].astype(F32) + R.RC[k, b].astype(F32)).astype(BF)
            remote(block, R.RB.at[b], R.sZ.at[zz, b], R.rRB.at[b], dev(s, zz, c)).start()

    def owner_of(b):
        row = (z >= 2) if b >= 2 else (z < 0)
        tc = jnp.where(row, lax.div(s, 2), c)
        m = jnp.where(row, lax.rem(s, 2) * 2 + c, s)
        return tc, m, (s == b) & (tc == c)

    def last_send(cond, b):
        tc, m, own = owner_of(b)
        block = R.W.at[z, b, c]

        @when(cond)
        def _():
            arrived(R.RA.at[b], R.rRA.at[b])
            arrived(R.RB.at[b], R.rRB.at[b])
            R.W[z, b, c] = (R.W[z, b, c].astype(F32) + R.RA[b].astype(F32) + R.RB[b].astype(F32)).astype(BF)

        @when(cond & own)
        def _():
            pltpu.make_async_copy(block, R.FR.at[m], R.rFin.at[m]).start()

        @when(cond & no(own))
        def _():
            remote(block, R.FR.at[m], R.sFin.at[b], R.rFin.at[m], dev(b, z, tc)).start()

    for k in (2, 3, 1, 0):
        for b in (2, 3):
            first_send(k, b)

    R.small[...] = jnp.zeros((16, 1024), F32)
    for b in range(4):
        R.small[10 + b : 11 + b, own_cols] = column_sum(R.gin[b].astype(F32))
    R.small[14:15, :] = column_sum(gout[own_rows, :].astype(F32))

    g2 = reduced(0)
    gx, gw, gb = norm_back(R.st1[own_rows, :].astype(F32), g2, vec[6:7, :])
    R.small[4:5, :] = gw
    R.small[6:7, :] = gb
    gs1_own = (gout[own_rows, :].astype(F32) + gx).astype(BF)
    R.small[9:10, :] = column_sum(gs1_own.astype(F32))
    R.gs[0] = gs1_own

    def mixed_grad(p):
        total = jnp.zeros((OWN, 256), F32)
        for n in range(4):
            tile = R.WF[2, n, lax.div(p, 2), at(lax.rem(p, 2) * 256, 256, 256), :]
            total = total + mm_nt(R.gs[0, :, n * 256 : (n + 1) * 256], tile)
        return total.astype(BF)

    def swap(phase, src_of, dst):
        for i, p in enumerate(peers):
            remote(src_of(p), dst.at[own_rows, :], R.sG.at[phase, i], R.rG.at[phase, s], dev(p, z, c)).start()

    def swapped(phase, dst):
        for p in peers:
            arrived(dst.at[at(p * OWN, OWN, OWN), :], R.rG.at[phase, p])

    for i, p in enumerate(peers):
        R.gmS[i] = mixed_grad(p)
        remote(R.gmS.at[i], R.gm.at[own_rows, :], R.sG.at[0, i], R.rG.at[0, s], dev(p, z, c)).start()
    R.gm[own_rows, :] = mixed_grad(s)
    swap(1, lambda p: R.gs.at[0, :, at(p * 256, 256, 256)], R.ga)
    R.ga[own_rows, :] = R.gs[0, :, own_cols]

    def send_out(i):
        p = peers[i]
        block = R.hrow.at[:, at(p * 256, 256, 256)]
        remote(block, R.outR.at[s], R.sOut.at[i], R.rOut.at[s], dev(p, z, c)).start()

    send_out(0)
    send_out(1)
    pass_on(0)

    swapped(0, R.gm)

    def attend_back(g):
        rows = at(g * 256, 256, 256)
        qg, kg, vg, gmg = R.q[rows, :], R.k[rows, :], R.v[rows, :], R.gm[rows, :]
        zero = jnp.zeros((256, 256), F32)
        tq, tk, tv = zero, zero, zero
        for hh in range(4):
            prob = R.attp[g * 4 + hh]
            gmh = only(hh, gmg)
            dprob = mm_nt(gmh, vg)
            tv = tv + mm_tn(prob.astype(BF), gmh)
            ds = (prob * (dprob - jnp.sum(prob * dprob, axis=1, keepdims=True))).astype(BF)
            tq = tq + mm(ds, only(hh, kg))
            tk = tk + mm_tn(ds, only(hh, qg))
        scale = 1.0 / math.sqrt(HEAD)
        R.gq[0, rows, :] = (tq * scale).astype(BF)
        R.gq[1, rows, :] = (tk * scale).astype(BF)
        R.gq[2, rows, :] = tv.astype(BF)

    loop(2, attend_back)

    for i in range(3):
        sent(R.rsR.at[0], R.sR.at[0, i])

    def attend_norm(p):
        rows = at(p * OWN, OWN, OWN)
        total = jnp.zeros((OWN, 1024), F32)
        for i in range(3):
            total = total + mm_nt(R.gq[i, rows, :], R.W[i, 1].reshape(1024, 256))
        R.rsS[rows, :] = total.astype(BF)

    reduce_rows(1, attend_norm)

    transposed(R.nrm)
    drain_own(always, 1)
    drain_own(top, 0)
    for zz in range(4):
        drain_spread(zz, 1)
    drain_spread(3, 0)

    def attend_gradient(i):
        column_gradient(i, 1, R.tr, R.gq[i])

    loop(3, attend_gradient)
    transposed(R.mix)
    swapped(1, R.ga)
    column_gradient(3, 1, R.tr, R.ga[...])
    R.small[7:8, own_cols] = column_sum(R.gq[0].astype(F32))
    R.small[8:9, own_cols] = column_sum(R.gq[2].astype(F32))
    for k in (2, 3, 1, 0):
        first_send(k, 1)

    g1 = reduced(1)
    gx, gw, gb = norm_back(R.st0[own_rows, :].astype(F32), g1, vec[5:6, :])
    R.small[3:4, :] = gw
    R.small[5:6, :] = gb
    gs0_own = (R.gs[0].astype(F32) + gx).astype(BF)
    gs0_sum = column_sum(gs0_own.astype(F32))
    R.small[1:2, :] = gs0_sum
    R.small[2:3, :] = jnp.where(s < 2, lead_short, lead_long) * gs0_sum
    R.gs[1] = gs0_own
    swap(2, lambda p: R.gs.at[1, :, at(p * 256, 256, 256)], R.gb)
    R.gb[own_rows, :] = R.gs[1, :, own_cols]
    def heads_grad(i):
        rows = at(lax.rem(i, 2) * 256, 256, 256)
        total = jnp.zeros((256, OWN), F32)
        for n in range(4):
            total = total + mm_nt(R.WF[1, n, lax.div(i, 2), rows, :], R.gs[1, :, n * 256 : (n + 1) * 256])
        block = at(i * 256, 256, 256)
        R.ghT[block, :] = total.astype(BF)
        R.gh[:, block] = total.astype(BF).T

    loop(4, heads_grad)
    R.G = R.acc.at[0:256, :]
    R.gpT[...] = jnp.zeros((192, OWN), F32)
    R.G[...] = jnp.zeros((256, 1024), F32)
    R.op1[240:256, :] = jnp.where(iota((16, OWN), 0) == 0, 1.0, 0.0).astype(BF)

    def embed_back(h):
        rows = at(h * 48, 48, 16)
        prob = R.att[rows, own_rows]
        low = prob.astype(BF)
        lowf = low.astype(F32)
        weights_of(R.op1, low, own_rows)
        hrows = at(h * 64, 64, 64)
        gop = mm_tn(R.mT[hrows, :], R.ghT[hrows, :])
        cols = at(lax.div(h, 4) * 256, 256, 256)
        keep = lane_head == lax.rem(h, 4)
        R.G[:, cols] += jnp.where(keep, mm(R.op1[...], R.gh[:, cols]), 0.0)
        gatt = gop[192:240, :]
        for p in range(4):
            gatt = gatt + gop[p * 48 : (p + 1) * 48, :] * R.patT[p * 48 : (p + 1) * 48, own_rows].astype(F32)
        R.gsc[rows, :] = prob * (gatt - jnp.sum(prob * gatt, axis=0, keepdims=True)) * (1.0 / math.sqrt(HEAD))
        for p in range(4):
            prow = slice(p * 48, (p + 1) * 48)
            R.gpT[prow, :] += gop[prow, :] * lowf

    loop(HEADS, embed_back)

    gsc = R.gsc[...]
    gsc_high = gsc.astype(BF)
    gsc_low = (gsc - gsc_high.astype(F32)).astype(BF)
    fold = jnp.where(iota((16, 768), 0) == iota((16, 768), 1) // 48, 1.0, 0.0).astype(BF)

    def folded(x, right):
        x_high = x.astype(BF)
        x_low = (x - x_high.astype(F32)).astype(BF)
        return mm(fold, x_high) + mm(fold, x_low)

    ones = jnp.ones((192, OWN), BF)
    pat_own = R.patT[:, own_rows]
    same = iota((768, 192), 0) % 48 == iota((768, 192), 1) % 48
    cross = mm_nt(gsc_high, pat_own) + mm_nt(gsc_low, pat_own)
    plain = mm_nt(gsc_high, ones) + mm_nt(gsc_low, ones)
    R.fc[0, :, 0:192] = folded(jnp.where(same, cross, 0.0), None)
    R.fc[0, :, 192:256] = folded(jnp.where(same, plain, 0.0), None)[:, 0:64] * jnp.where(
        iota((1, 64), 1) < 48, 1.0, 0.0
    )
    remote(R.fc.at[0], R.fc.at[1], R.sFo.at[0], R.rFo.at[0], sib).start()

    R.G[240:256, :] += R.small[...]
    R.gall[...] = R.G[...].astype(BF)
    half = at(c * 128, 128, 128)
    other = at((1 - c) * 128, 128, 128)
    remote(R.gall.at[other, :], R.fromc, R.sAll.at[0], R.rAll.at[0], sib).start()

    gpt = (R.gpT[...] + mm_tn(R.fill[0:768, :], gsc_high)).astype(BF)
    for p in range(4):
        r = iota((48, 192), 0) + p * 48
        select = jnp.where(iota((48, 192), 1) == (r % 4) * 48 + r // 4, 1.0, 0.0).astype(BF)
        R.pixS[p] = mm(select, gpt).astype(BF)
    for i, p in enumerate(peers):
        remote(R.pixS.at[p], R.pixR.at[s], R.sP.at[i], R.rP.at[s], dev(p, z, c)).start()

    for b in (2, 3):
        for zz in range(4):
            second_send(zz, b)
    arrived(R.fc.at[1], R.rFo.at[0])
    R.fp[s] = R.fc[0] + R.fc[1]
    for i, p in enumerate(peers):
        remote(R.fp.at[s], R.fp.at[s], R.sFo.at[1 + i], R.rFo.at[1 + s], dev(p, z, c)).start()

    arrived(R.fromc, R.rAll.at[0])
    R.gall[half, :] = (R.gall[half, :].astype(F32) + R.fromc[...].astype(F32)).astype(BF)

    def part_of(p):
        return at(c * 128 + p * 32, 32, 32)

    for i, p in enumerate(peers):
        remote(R.gall.at[part_of(p), :], R.fromp.at[s], R.sAll.at[1 + i], R.rAll.at[1 + s], dev(p, z, c)).start()

    swapped(2, R.gb)
    column_gradient(3, 0, R.hT, R.gb[...])

    for p in peers:
        arrived(R.fp.at[p], R.rFo.at[1 + p])
    R.fz[z] = R.fp[0] + R.fp[1] + R.fp[2] + R.fp[3]
    for i, zz in enumerate(layers):
        remote(R.fz.at[z], R.fz.at[z], R.sFo.at[4 + i], R.rFo.at[5 + z], dev(s, zz, c)).start()

    total = R.gall[part_of(s), :].astype(F32)
    for p in peers:
        arrived(R.fromp.at[p], R.rAll.at[1 + p])
        total = total + R.fromp[p].astype(F32)
    R.fromz[z] = total.astype(BF)
    for i, zz in enumerate(layers):
        remote(R.fromz.at[z], R.fromz.at[z], R.sAll.at[4 + i], R.rAll.at[5 + z], dev(s, zz, c)).start()

    for zz in range(4):
        second_send(zz, 1)
    for k in (2, 3, 1, 0):
        first_send(k, 0, z ^ k == 3)
    send_out(2)

    for zz in layers:
        arrived(R.fz.at[zz], R.rFo.at[5 + zz])
    fo_grad = (R.fz[0] + R.fz[1]) + (R.fz[2] + R.fz[3])
    fo_high = fo_grad.astype(BF)
    fo_low = (fo_grad - fo_high.astype(F32)).astype(BF)
    gkq = (mm(fo_high, table[...]) + mm(fo_low, table[...])).astype(BF)

    @when(key_owner)
    def _():
        diag = iota((16, 1024), 1) // HEAD == iota((16, 1024), 0)
        own = jnp.where(c == 0, gkq[:, 0:512].astype(F32), gkq[:, 512:1024].astype(F32)).astype(BF)
        row = column_sum(jnp.where(diag, mm(own, bank[...]), 0.0))
        R.qx[0] = jnp.broadcast_to(row, (8, 1024))
        remote(R.qx.at[0], R.qx.at[1], R.sGq.at[15], R.rGq.at[0], sib).start()
        masked = jnp.where(diag, R.qb[...].astype(F32), 0.0).astype(BF)
        gbank[...] = mm_tn(own, masked).astype(BF)
        arrived(R.qx.at[1], R.rGq.at[0])
        row = (R.qx[0] + R.qx[1]).astype(BF)
        R.gqv[...] = jnp.concatenate([row, row], axis=0)
        for i, (p, k) in enumerate(others):
            remote(R.gqv, R.gqv, R.sGq.at[i], R.rGq.at[1], dev(p, k, c)).start()

    for zz in layers:
        arrived(R.fromz.at[zz], R.rAll.at[5 + zz])
    total = R.fromz[0].astype(F32)
    for zz in range(1, 4):
        total = total + R.fromz[zz].astype(F32)
    R.fin[part_of(s), :] = total.astype(BF)
    for i, p in enumerate(peers):
        block = R.fin.at[part_of(s), :]
        remote(block, block, R.sAll.at[7 + i], R.rAll.at[9 + s], dev(p, z, c)).start()

    @when(first_owner)
    def _():
        arrived(R.gqv, R.rGq.at[1])
        R.gaq[c] = mm_nt(R.gqv[...], bank[...])[0:8]
        for i, (p, k) in enumerate(others):
            remote(R.gaq.at[c], R.gaq.at[c], R.sGa.at[i], R.rGa.at[c], dev(p, k, c)).start()
        aq = jnp.where(c == 0, vec[17:18, 0:512], vec[17:18, 512:1024])
        aq = jnp.where(iota((16, 512), 0) == 0, aq, 0.0).astype(BF)
        gbank[...] = mm_tn(aq, R.gqv[...]).astype(BF)

    last_send(always, 2)
    last_send(always, 3)

    for p in peers:
        arrived(R.fin.at[part_of(p), :], R.rAll.at[9 + p])
    remote(R.fin.at[half, :], R.fin.at[half, :], R.sAll.at[10], R.rAll.at[13], sib).start()

    second_send(3, 0)
    last_send(always, 1)

    total = R.hrow[:, own_cols].astype(F32) + R.st1[:, own_cols].astype(F32) + vec[16:17, own_cols]
    for p in peers:
        arrived(R.outR.at[p], R.rOut.at[p])
        total = total + R.outR[p].astype(F32)
    out[...] = total.astype(BF)

    for i, p in enumerate(peers):
        arrived(R.pixR.at[p], R.rP.at[p])
    R.pixR[s] = R.pixS[s]
    for p in range(4):
        gpix[p * OWN : (p + 1) * OWN, :] = R.pixR[p].astype(F32).T

    wait_whole(0)
    arrived(R.fin.at[other, :], R.rAll.at[13])
    sums[...] = R.fin[240:256, :].astype(F32)
    kq_wide = jnp.concatenate([kq_full, jnp.zeros((112, 1024), BF)], axis=0)
    wide = jnp.zeros((112, 256), BF)
    gfh = jnp.concatenate([fo_high, wide], axis=0)
    gfl = jnp.concatenate([fo_low, wide], axis=0)

    def table_grad(h):
        value = jnp.zeros((256, 512), F32)
        for p in range(4):
            value = value + mm_nt(R.fin[:, p * 256 : (p + 1) * 256], R.WF[0, p, h])
        return value

    for h in range(2):
        cols = slice(h * 512, (h + 1) * 512)
        gtab[:, cols] = (table_grad(h) + mm_tn(gfh, kq_wide[:, cols]) + mm_tn(gfl, kq_wide[:, cols])).astype(BF)

    @when(value_owner)
    def _():
        gbank[...] = mm_tn(table[:, half_rows], R.fin[...]).astype(BF)

    last_send(top, 0)

    @when(no(first_owner))
    def _():
        arrived(R.gaq.at[c], R.rGa.at[c])

    @when(no(key_owner | first_owner))
    def _():
        arrived(R.gqv, R.rGq.at[1])

    remote(R.gaq.at[c], R.gaq.at[c], R.sGa.at[15], R.rGa.at[c], sib).start()
    arrived(R.gaq.at[1 - c], R.rGa.at[1 - c])
    rows_out[0:8, :] = R.gqv[0:8, :].astype(F32)
    rows_out[8:16, 0:512] = R.gaq[0]
    rows_out[8:16, 512:1024] = R.gaq[1]

    @when(used)
    def _():
        for m in range(4):
            arrived(R.FR.at[m], R.rFin.at[m])

    @when(used & no(is_row))
    def _():
        for m in range(4):
            gbank[:, m * 256 : (m + 1) * 256] = R.FR[m]

    @when(is_row)
    def _():
        for m in range(4):
            q, h = m // 2, m % 2
            for n in range(2):
                lo = (2 * h + n) * 256
                gbank[q * 256 : (q + 1) * 256, lo : lo + 256] = R.FR[m, n * 256 : (n + 1) * 256, :]

    for m in range(4):
        tp, tc, own = message(m)

        @when((used | late) & no(own))
        def _():
            sent(R.msgs.at[m], R.sMsg.at[m])

        @when(value_owner & no((2 * c + m // 2 == s) & (c == m % 2)))
        def _():
            sent(my_piece(m), R.sMa.at[m])

    @when(first_owner)
    def _():
        sent(R.qbuf.at[0], R.sQ.at[0])
        sent(R.qb, R.sQ.at[1])
        for i in range(15):
            sent(R.gaq.at[c], R.sGa.at[i])

    @when(key_owner)
    def _():
        sent(R.qx.at[0], R.sGq.at[15])
        for i in range(15):
            sent(R.kq.at[c], R.sK.at[i])
            sent(R.gqv, R.sGq.at[i])

    @when(z == 2)
    def _():
        for i in range(3):
            sent(R.mS.at[0:128, :], R.sMz.at[i])

    drain_own(z == 2, 0)
    drain_spread(2, 0)
    sent(R.kq.at[c], R.sK.at[15])
    sent(R.gaq.at[c], R.sGa.at[15])
    for f in range(3):
        for p in range(4):
            sent(R.msgs.at[0], R.sFc.at[f, p])
    for p in range(4):
        sent(R.mS.at[0:128, :], R.sMc.at[p])
    sent(R.fc.at[0], R.sFo.at[0])
    sent(R.fromc, R.sAll.at[0])
    sent(R.fromc, R.sAll.at[10])
    for i in range(3):
        sent(R.mS.at[0:128, :], R.sMp.at[i])
        sent(mine, R.sMix.at[i])
        sent(R.msgs.at[0], R.sOut.at[i])
        sent(R.rsR.at[0], R.sR.at[1, i])
        for phase in range(3):
            sent(R.gmS.at[0], R.sG.at[phase, i])
        sent(R.pixS.at[0], R.sP.at[i])
        sent(R.fp.at[0], R.sFo.at[1 + i])
        sent(R.fp.at[0], R.sFo.at[4 + i])
        for phase in range(3):
            sent(R.fromp.at[0], R.sAll.at[1 + 3 * phase + i])
    for b in range(4):
        for zz in range(4):

            @when(at_least(jnp.int32(zz), b) & (z != zz) & (always if b > 0 or zz == 3 else z < 0))
            def _():
                sent(R.msgs.at[0], R.sZ.at[zz, b])

        tc, m, own = owner_of(b)

        @when((top if b == 0 else always) & no(own))
        def _():
            sent(R.msgs.at[0], R.sFin.at[b])


VMEM = pl.BlockSpec(memory_space=pltpu.VMEM)
SMEM = pl.BlockSpec(memory_space=pltpu.SMEM)
ARG_SHAPES = (
    [((512, 192), BF), ((2, 1), F32), ((1, 4), jnp.int32), ((512, 1024), BF), ((512, 1024), BF), ((192, 1024), BF)]
    + [((48, 1024), BF)] * 2
    + [((n, 1024), BF) for n in (1, 3, 2, 2, 2, 3, 4, 1)]
)


def block_call(*args):
    shape = jax.ShapeDtypeStruct
    outs = [
        shape((512, 256), BF),
        shape((512, 48), F32),
        shape((512, 1024), BF),
        shape((256, 1024), BF),
        shape((16, 1024), F32),
        shape((16, 1024), F32),
    ]
    return pl.pallas_call(
        block_kernel,
        out_shape=outs,
        in_specs=[VMEM, SMEM, SMEM] + [VMEM] * (len(args) - 3),
        out_specs=[VMEM] * len(outs),
        scratch_shapes=[pltpu.VMEM(*v) for v in SCRATCH.values()]
        + [pltpu.SemaphoreType.DMA(v) for v in SEMS.values()],
        compiler_params=pltpu.CompilerParams(
            collective_id=1, has_side_effects=True, vmem_limit_bytes=63 * 2**20
        ),
    )(*args)


def finish_kernel(
    out,
    gpix,
    gbank,
    gtab,
    sums,
    rows,
    o_out,
    o_pix,
    o_bank,
    o_patch,
    o_patch_b,
    o_var,
    o_query,
    o_agg,
    o_lead,
    o_gain,
    o_bias,
    o_attn,
    o_fc1,
    o_fc2,
):
    o_out[...] = out[...]
    o_pix[...] = gpix[...]
    o_bank[...] = gbank[...].astype(F32)
    for p in range(PIX):
        o_patch[:, p, :] = gtab[p * VARS : (p + 1) * VARS, :].astype(F32)
    o_patch_b[...] = gtab[192:240, :].astype(F32)
    o_var[...] = gtab[192:240, :].astype(F32)
    o_query[...] = rows[8:9, :]
    o_agg[0:1, :] = rows[0:1, :]
    o_agg[1:3, :] = sums[0:2, :]
    o_lead[0:1, :] = sums[2:3, :]
    o_lead[1:2, :] = sums[1:2, :]
    o_gain[...] = sums[3:5, :]
    o_bias[...] = sums[5:7, :]
    o_attn[...] = sums[7:10, :]
    o_fc1[...] = sums[10:14, :]
    o_fc2[...] = sums[14:15, :]


def finish_call(*args):
    shape = jax.ShapeDtypeStruct
    outs = [shape((512, 256), BF), shape((512, 48), F32), shape((512, 1024), F32), shape((48, 4, 1024), F32)]
    outs += [shape((48, 1024), F32)] * 2 + [shape((n, 1024), F32) for n in (1, 3, 2, 2, 2, 3, 4, 1)]
    return pl.pallas_call(
        finish_kernel,
        out_shape=outs,
        in_specs=[VMEM] * len(args),
        out_specs=[VMEM] * len(outs),
        compiler_params=pltpu.CompilerParams(vmem_limit_bytes=40 * 2**20),
    )(*args)


def on_device_fast(
    patches,
    lead_times,
    short_lengths,
    cotangent,
    bank,
    patch_w,
    patch_b,
    var_emb,
    agg_query,
    agg_bias,
    lead_embed,
    norm_gain,
    norm_bias,
    attn_bias,
    fc1_bias,
    fc2_bias,
):
    parts = block_call(
        patches.reshape(ROWS, VARS * PIX),
        lead_times,
        short_lengths,
        cotangent.reshape(ROWS, D),
        bank[0],
        patch_w.reshape(VARS * PIX, D),
        patch_b,
        var_emb,
        agg_query[None],
        agg_bias,
        lead_embed,
        norm_gain,
        norm_bias,
        attn_bias,
        fc1_bias.reshape(4, D),
        fc2_bias[None],
    )
    o = finish_call(*parts)
    return (
        (o[0].reshape(2, GROUP, 256), o[1].reshape(2, GROUP, 48), o[2][None])
        + tuple(o[3:6])
        + (o[6][0],)
        + tuple(o[7:12])
        + (o[12].reshape(FF), o[13][0])
    )


def specs():
    ins = (
        (P(None, "dp", None), P(None, "dp"), P("dp", None), P(None, "dp", None), P("section", "dp", None))
        + (P(),) * 11
    )
    outs = (P(None, "dp", "section"), P(None, "dp", "section"), P("section", "dp", None)) + (P(),) * 11
    return ins, outs


wide_type = jnp.float32
narrow_type = jnp.bfloat16
highest = lax.Precision.HIGHEST


def shortened(array):

    def short(part):
        return part.astype(jnp.bfloat16) if part.dtype == jnp.float32 else part

    return jax.tree.map(short, array)


def from_behind(array, axis, by):
    length = lax.axis_size(axis)
    pairs = [(i, i + by) for i in range(length) if 0 <= i + by < length]
    return lax.ppermute(array, axis, pairs)


def product(factor_left, factor_right):
    return jnp.dot(factor_left, factor_right, preferred_element_type=wide_type)


def product_left(factor_left, factor_right):
    return lax.dot_general(
        factor_left, factor_right, (((0,), (0,)), ((), ())), preferred_element_type=wide_type
    )


def product_right(factor_left, factor_right):
    return lax.dot_general(
        factor_left, factor_right, (((1,), (1,)), ((), ())), preferred_element_type=wide_type
    )


def norm_layer(stream, gain_row, shift_row):
    centre = stream - jnp.mean(stream, axis=-1, keepdims=True)
    spread = jnp.mean(centre * centre, axis=-1, keepdims=True)
    return centre * lax.rsqrt(spread + 1e-05) * gain_row + shift_row


def gelu_exact(values_in):
    return jax.nn.gelu(values_in, approximate=False)


def position_table(places):
    half_width = D // 2
    frequency = jnp.exp(-math.log(10000.0) * 2.0 * jnp.arange(half_width, dtype=wide_type) / D)
    angles = places.astype(wide_type)[:, None] * frequency[None, :]
    return jnp.concatenate([jnp.sin(angles), jnp.cos(angles)], axis=1)


def layout(lengths_row, row_count):
    segment_ends = jnp.cumsum(lengths_row)
    starts = segment_ends - lengths_row
    places = jnp.arange(row_count, dtype=jnp.int32)
    segment = jnp.sum((places[:, None] >= segment_ends[None, :]).astype(jnp.int32), axis=1)
    member = segment[:, None] == jnp.arange(lengths_row.shape[0], dtype=jnp.int32)[None, :]
    offset = jnp.sum(jnp.where(member, starts[None, :], 0), axis=1)
    offset = jnp.where(segment == lengths_row.shape[0], segment_ends[-1], offset)
    return (segment, places - offset)


def embed_setup(weights, params):
    patch_w, patch_b, var_emb, agg_query, agg_bias = params[:5]
    query_row = product(agg_query[None, :], weights[0])[0] + agg_bias[0].astype(wide_type)
    query_low = query_row.astype(narrow_type)
    key_query = jnp.einsum(
        "dhe,he->dh",
        weights[1].reshape(D, HEADS, HEAD),
        query_low.reshape(HEADS, HEAD),
        preferred_element_type=wide_type,
    )
    key_low = key_query.astype(narrow_type)
    constant = (patch_b.astype(wide_type) + var_emb.astype(wide_type)).astype(narrow_type)
    filters = jnp.einsum("vpd,dh->vph", patch_w, key_low, preferred_element_type=wide_type)
    offsets = product(constant, key_low)
    embed_table = jnp.concatenate([patch_w.reshape(VARS * PIX, D), constant], axis=0)
    return (query_low, key_low, constant, filters, offsets, embed_table)


def embed_rows(pixel_rows, places, lead_time, setup, weights, params):
    query_low, key_low, constant, filters, offsets, embed_table = setup
    agg_bias, lead_embed = (params[4], params[5])
    row_count = pixel_rows.shape[0]
    pixels = pixel_rows.reshape(row_count, VARS, PIX).astype(wide_type)
    scores = (
        jnp.einsum("tvp,vph->tvh", pixels, filters, precision=highest) + offsets[None]
    ) / math.sqrt(HEAD)
    attend = jax.nn.softmax(scores, axis=1)
    attend_low = attend.astype(narrow_type)
    weighted = (attend_low.astype(wide_type)[:, :, :, None] * pixels[:, :, None, :]).astype(
        narrow_type
    )
    operand = jnp.concatenate(
        [
            jnp.transpose(weighted, (0, 2, 1, 3)).reshape(row_count * HEADS, VARS * PIX),
            jnp.transpose(attend_low, (0, 2, 1)).reshape(row_count * HEADS, VARS),
        ],
        axis=1,
    )
    pooled = product(operand, embed_table).astype(narrow_type).reshape(row_count, HEADS, D)
    heads_out = jnp.einsum(
        "thd,dhe->the", pooled, weights[2].reshape(D, HEADS, HEAD), preferred_element_type=wide_type
    ).reshape(row_count, D)
    heads_low = (heads_out + agg_bias[1].astype(wide_type)).astype(narrow_type)
    merged = product(heads_low, weights[3]) + agg_bias[2].astype(wide_type)
    stream = (
        merged
        + position_table(places)
        + lead_time * lead_embed[0].astype(wide_type)
        + lead_embed[1].astype(wide_type)
    )
    return (stream.astype(narrow_type), (pixels, attend, attend_low, operand, pooled, heads_low))


def embed_back(grad_rows, lead_time, setup, saved_state, weights):
    query_low, key_low, constant, filters, offsets, embed_table = setup
    pixels, attend, attend_low, operand, pooled, heads_low = saved_state
    row_count = grad_rows.shape[0]
    grad_wide = grad_rows.astype(wide_type)
    grad_w_out = product_left(heads_low, grad_rows)
    grad_bias_out = jnp.sum(grad_wide, axis=0)
    grad_heads = product_right(grad_rows, weights[3]).astype(narrow_type)
    grad_bias_value = jnp.sum(grad_heads.astype(wide_type), axis=0)
    grad_heads_split = grad_heads.reshape(row_count, HEADS, HEAD)
    grad_w_value = jnp.einsum(
        "thd,the->dhe", pooled, grad_heads_split, preferred_element_type=wide_type
    ).reshape(D, D)
    grad_pooled = jnp.einsum(
        "the,dhe->thd",
        grad_heads_split,
        weights[2].reshape(D, HEADS, HEAD),
        preferred_element_type=wide_type,
    )
    grad_pooled = grad_pooled.astype(narrow_type).reshape(row_count * HEADS, D)
    grad_operand = product_right(grad_pooled, embed_table)
    grad_table = product_left(operand, grad_pooled)
    grad_weighted = grad_operand[:, : VARS * PIX].reshape(row_count, HEADS, VARS, PIX)
    grad_mixing = jnp.transpose(
        grad_operand[:, VARS * PIX :].reshape(row_count, HEADS, VARS), (0, 2, 1)
    )
    grad_attend = (
        jnp.einsum("thvp,tvp->tvh", grad_weighted, pixels, precision=highest) + grad_mixing
    )
    grad_scores = (
        attend
        * (grad_attend - jnp.sum(attend * grad_attend, axis=1, keepdims=True))
        / math.sqrt(HEAD)
    )
    grad_pixels = jnp.einsum(
        "thvp,tvh->tvp", grad_weighted, attend_low.astype(wide_type), precision=highest
    )
    grad_pixels = grad_pixels + jnp.einsum("tvh,vph->tvp", grad_scores, filters, precision=highest)
    grad_filters = jnp.einsum("tvp,tvh->vph", pixels, grad_scores, precision=highest)
    grad_offsets = jnp.sum(grad_scores, axis=0)
    grad_lead = jnp.stack([lead_time * grad_bias_out, grad_bias_out])
    sums = (
        grad_w_out,
        grad_bias_out,
        grad_bias_value,
        grad_w_value,
        grad_table,
        grad_filters,
        grad_offsets,
        grad_lead,
    )
    return (grad_pixels.reshape(row_count, VARS * PIX), sums)


def embed_finish(totals, setup, weights, params):
    (
        grad_w_out,
        grad_bias_out,
        grad_bias_value,
        grad_w_value,
        grad_table,
        grad_filters,
        grad_offsets,
        grad_lead,
    ) = totals
    query_low, key_low, constant, filters, offsets, embed_table = setup
    patch_w, agg_query = (params[0], params[3])
    key_wide = key_low.astype(wide_type)
    grad_patch_w = grad_table[: VARS * PIX].reshape(VARS, PIX, D) + jnp.einsum(
        "vph,dh->vpd", grad_filters, key_wide, precision=highest
    )
    grad_constant = grad_table[VARS * PIX :] + jnp.dot(grad_offsets, key_wide.T, precision=highest)
    grad_key = jnp.einsum("vpd,vph->dh", patch_w.astype(wide_type), grad_filters, precision=highest)
    grad_key = grad_key + jnp.dot(constant.astype(wide_type).T, grad_offsets, precision=highest)
    grad_key_low = grad_key.astype(narrow_type)
    query_heads = query_low.reshape(HEADS, HEAD).astype(wide_type)
    grad_w_key = (grad_key_low.astype(wide_type)[:, :, None] * query_heads[None, :, :]).reshape(
        D, D
    )
    grad_query = jnp.einsum(
        "dhe,dh->he",
        weights[1].reshape(D, HEADS, HEAD),
        grad_key_low,
        preferred_element_type=wide_type,
    )
    grad_query = grad_query.reshape(D).astype(narrow_type)
    grad_query_wide = grad_query.astype(wide_type)
    grad_w_query = agg_query.astype(wide_type)[:, None] * grad_query_wide[None, :]
    grad_agg_query = product(weights[0], grad_query[:, None])[:, 0]
    grad_bank = jnp.concatenate([grad_w_query, grad_w_key, grad_w_value, grad_w_out], axis=0)
    smalls = (
        grad_patch_w,
        grad_constant,
        grad_constant,
        grad_agg_query,
        jnp.stack([grad_query_wide, grad_bias_value, grad_bias_out]),
        grad_lead,
        jnp.zeros((2, D), wide_type),
        jnp.zeros((2, D), wide_type),
        jnp.zeros((3, D), wide_type),
        jnp.zeros((FF,), wide_type),
        jnp.zeros((D,), wide_type),
    )
    return (grad_bank, smalls)


def attention_scores(block_query, block_segment, key_heads, segment):
    raw_scores = jnp.einsum(
        "qhe,khe->hqk", block_query, key_heads, preferred_element_type=wide_type
    ) / math.sqrt(HEAD)
    allowed = (block_segment[:, None] == segment[None, :])[None]
    return jnp.where(allowed, raw_scores, -1e30)


def attention_forward(queries, key_rows, values, segment):
    row_count = queries.shape[0]
    block_rows = min(512, row_count)
    block_total = row_count // block_rows
    key_heads = key_rows.reshape(row_count, HEADS, HEAD)
    value_heads = values.reshape(row_count, HEADS, HEAD)

    def one_block(block_items):
        block_query, block_segment = block_items
        scores = attention_scores(block_query, block_segment, key_heads, segment)
        row_peak = jnp.max(scores, axis=-1, keepdims=True)
        exp_scores = jnp.exp(scores - row_peak)
        exp_total = jnp.sum(exp_scores, axis=-1, keepdims=True)
        probabilities = (exp_scores / exp_total).astype(narrow_type)
        mixed_heads = jnp.einsum(
            "hqk,khe->qhe", probabilities, value_heads, preferred_element_type=wide_type
        )
        return (mixed_heads.astype(narrow_type), (row_peak + jnp.log(exp_total))[:, :, 0])

    mixed_heads, log_totals = lax.map(
        one_block,
        (
            queries.reshape(block_total, block_rows, HEADS, HEAD),
            segment.reshape(block_total, block_rows),
        ),
    )
    return (mixed_heads.reshape(row_count, D), log_totals)


def attention_backward(queries, key_rows, values, segment, log_totals, grad_mixed):
    row_count = queries.shape[0]
    block_rows = min(512, row_count)
    block_total = row_count // block_rows
    key_heads = key_rows.reshape(row_count, HEADS, HEAD)
    value_heads = values.reshape(row_count, HEADS, HEAD)

    def one_block(carry_sums, block_items):
        grad_key_sum, grad_value_sum = carry_sums
        block_query, block_segment, block_log, block_grad = block_items
        scores = attention_scores(block_query, block_segment, key_heads, segment)
        probabilities = jnp.exp(scores - block_log[:, :, None])
        probs_low = probabilities.astype(narrow_type)
        grad_value_sum = grad_value_sum + jnp.einsum(
            "hqk,qhe->khe", probs_low, block_grad, preferred_element_type=wide_type
        )
        grad_probs = jnp.einsum(
            "qhe,khe->hqk", block_grad, value_heads, preferred_element_type=wide_type
        )
        grad_scores = probabilities * (
            grad_probs - jnp.sum(probabilities * grad_probs, axis=-1, keepdims=True)
        )
        grad_low = grad_scores.astype(narrow_type)
        grad_query = jnp.einsum(
            "hqk,khe->qhe", grad_low, key_heads, preferred_element_type=wide_type
        ) / math.sqrt(HEAD)
        grad_key_sum = grad_key_sum + jnp.einsum(
            "hqk,qhe->khe", grad_low, block_query, preferred_element_type=wide_type
        ) / math.sqrt(HEAD)
        return ((grad_key_sum, grad_value_sum), grad_query)

    zero_heads = jnp.zeros((row_count, HEADS, HEAD), wide_type)
    block_items = (
        queries.reshape(block_total, block_rows, HEADS, HEAD),
        segment.reshape(block_total, block_rows),
        log_totals,
        grad_mixed.reshape(block_total, block_rows, HEADS, HEAD),
    )
    (grad_key_sum, grad_value_sum), grad_queries = lax.scan(
        one_block, (zero_heads, zero_heads), block_items
    )
    return (
        grad_queries.reshape(row_count, D),
        grad_key_sum.reshape(row_count, D),
        grad_value_sum.reshape(row_count, D),
    )


def project_heads(normed_low, weights, attn_bias):
    queries = (product(normed_low, weights[0]) + attn_bias[0].astype(wide_type)).astype(narrow_type)
    key_rows = product(normed_low, weights[1]).astype(narrow_type)
    values = (product(normed_low, weights[2]) + attn_bias[1].astype(wide_type)).astype(narrow_type)
    return (queries, key_rows, values)


def feed_half(normed_low, weights, bias_in):
    inner_first = product(normed_low, weights[0]) + bias_in[:D].astype(wide_type)
    inner_second = product(normed_low, weights[1]) + bias_in[D:].astype(wide_type)
    active_first = gelu_exact(inner_first).astype(narrow_type)
    active_second = gelu_exact(inner_second).astype(narrow_type)
    partial_sum = product(active_first, weights[2]) + product(active_second, weights[3])
    return ((inner_first, inner_second), (active_first, active_second), partial_sum)


def feed_half_back(normed_low, weights, inners, actives, grad_rows):
    grad_inners = []
    for number in range(2):
        grad_active = product_right(grad_rows, weights[2 + number])
        value_out, gelu_pull = jax.vjp(gelu_exact, inners[number])
        grad_inners.append(gelu_pull(grad_active)[0].astype(narrow_type))
    grad_normed = product_right(grad_inners[0], weights[0]) + product_right(
        grad_inners[1], weights[1]
    )
    grad_bank = jnp.concatenate(
        [
            product_left(normed_low, grad_inners[0]),
            product_left(normed_low, grad_inners[1]),
            product_left(actives[0], grad_rows),
            product_left(actives[1], grad_rows),
        ],
        axis=0,
    )
    grad_bias_in = jnp.concatenate(
        [
            jnp.sum(grad_inners[0].astype(wide_type), axis=0),
            jnp.sum(grad_inners[1].astype(wide_type), axis=0),
        ]
    )
    return (grad_normed, grad_bank, grad_bias_in)


def on_device(
    patches,
    lead_times,
    short_lengths,
    cotangent,
    bank,
    patch_w,
    patch_b,
    var_emb,
    agg_query,
    agg_bias,
    lead_embed,
    norm_gain,
    norm_bias,
    attn_bias,
    fc1_bias,
    fc2_bias,
):
    params = (
        patch_w,
        patch_b,
        var_emb,
        agg_query,
        agg_bias,
        lead_embed,
        norm_gain,
        norm_bias,
        attn_bias,
        fc1_bias,
        fc2_bias,
    )
    micro_total = patches.shape[0]
    row_count = patches.shape[1]
    section_total = lax.axis_size("section")
    section_index = lax.axis_index("section")
    gathered = lax.all_gather(bank, "dp", axis=1, tiled=True)[0]
    weights = tuple((gathered[number * D : (number + 1) * D] for number in range(4)))
    short_segment, short_places = layout(short_lengths[0], row_count)
    segments = jnp.stack([short_segment, jnp.zeros((row_count,), jnp.int32)])
    places_all = jnp.stack([short_places, jnp.arange(row_count, dtype=jnp.int32)])
    valid_rows = jnp.stack([short_segment < short_lengths.shape[1], jnp.ones((row_count,), bool)])
    grad_out_all = jnp.where(valid_rows[:, :, None], cotangent, jnp.zeros_like(cotangent))
    block_rows = min(512, row_count)
    block_total = row_count // block_rows
    zeros_stream = jnp.zeros((row_count, D), narrow_type)
    zeros_final = jnp.zeros((row_count, D), wide_type)
    zeros_pixels = jnp.zeros((row_count, VARS * PIX), wide_type)
    stash_zero = (
        zeros_stream,
        zeros_stream,
        zeros_stream,
        zeros_stream,
        jnp.zeros((block_total, HEADS, block_rows), wide_type),
    )
    small_zero = tuple((jnp.zeros(array_item.shape, wide_type) for array_item in params))

    def forward_embed(operands):
        first_in, second_in, pixel_rows, places, lead_time, segment = operands
        setup = embed_setup(weights, params)

        def one_block(block_items):
            return embed_rows(block_items[0], block_items[1], lead_time, setup, weights, params)[0]

        streams = lax.map(
            one_block,
            (
                pixel_rows.reshape(block_total, block_rows, VARS * PIX),
                places.reshape(block_total, block_rows),
            ),
        )
        return (streams.reshape(row_count, D), zeros_stream, zeros_final, stash_zero)

    def forward_attend(operands):
        first_in, second_in, pixel_rows, places, lead_time, segment = operands
        stream = first_in.astype(wide_type)
        normed_low = norm_layer(
            stream, norm_gain[0].astype(wide_type), norm_bias[0].astype(wide_type)
        ).astype(narrow_type)
        queries, key_rows, values = project_heads(normed_low, weights, attn_bias)
        mixed_heads, log_totals = attention_forward(queries, key_rows, values, segment)
        new_stream = stream + product(mixed_heads, weights[3]) + attn_bias[2].astype(wide_type)
        return (new_stream.astype(narrow_type), zeros_stream, zeros_final, stash_zero)

    def forward_first(operands):
        first_in, second_in, pixel_rows, places, lead_time, segment = operands
        stream = first_in.astype(wide_type)
        normed_low = norm_layer(
            stream, norm_gain[1].astype(wide_type), norm_bias[1].astype(wide_type)
        ).astype(narrow_type)
        inners, actives, partial_sum = feed_half(normed_low, weights, fc1_bias[: 2 * D])
        return (normed_low, (stream + partial_sum).astype(narrow_type), zeros_final, stash_zero)

    def forward_second(operands):
        first_in, second_in, pixel_rows, places, lead_time, segment = operands
        inners, actives, partial_sum = feed_half(first_in, weights, fc1_bias[2 * D :])
        final_rows = second_in.astype(wide_type) + partial_sum + fc2_bias.astype(wide_type)
        return (zeros_stream, zeros_stream, final_rows, stash_zero)

    def forward_none(operands):
        return (zeros_stream, zeros_stream, zeros_final, stash_zero)

    def backward_embed(operands):
        (
            first_kept,
            second_kept,
            grad_in,
            pixel_rows,
            places,
            lead_time,
            segment,
            grad_rows,
            stash_items,
        ) = operands
        setup = embed_setup(weights, params)

        def one_block(totals, block_items):
            block_pixels, block_places, block_grad = block_items
            block_stream, saved_state = embed_rows(
                block_pixels, block_places, lead_time, setup, weights, params
            )
            block_dx, sums = embed_back(block_grad, lead_time, setup, saved_state, weights)
            return (
                tuple((total_item + sum_item for total_item, sum_item in zip(totals, sums))),
                block_dx,
            )

        zero_totals = (
            jnp.zeros((D, D), wide_type),
            jnp.zeros((D,), wide_type),
            jnp.zeros((D,), wide_type),
            jnp.zeros((D, D), wide_type),
            jnp.zeros((VARS * PIX + VARS, D), wide_type),
            jnp.zeros((VARS, PIX, HEADS), wide_type),
            jnp.zeros((VARS, HEADS), wide_type),
            jnp.zeros((2, D), wide_type),
        )
        block_items = (
            pixel_rows.reshape(block_total, block_rows, VARS * PIX),
            places.reshape(block_total, block_rows),
            grad_in.reshape(block_total, block_rows, D),
        )
        totals, grad_pixels = lax.scan(one_block, zero_totals, block_items)
        grad_bank, smalls = embed_finish(totals, setup, weights, params)
        return (zeros_stream, grad_bank, smalls, grad_pixels.reshape(row_count, VARS * PIX))

    def backward_attend(operands):
        (
            first_kept,
            second_kept,
            grad_in,
            pixel_rows,
            places,
            lead_time,
            segment,
            grad_rows,
            stash_items,
        ) = operands
        stream = first_kept.astype(wide_type)
        normed, norm_pull = jax.vjp(
            norm_layer, stream, norm_gain[0].astype(wide_type), norm_bias[0].astype(wide_type)
        )
        normed_low = normed.astype(narrow_type)
        queries, key_rows, values = project_heads(normed_low, weights, attn_bias)
        mixed_heads, log_totals = attention_forward(queries, key_rows, values, segment)
        grad_in_wide = grad_in.astype(wide_type)
        grad_w_out = product_left(mixed_heads, grad_in)
        grad_mixed = product_right(grad_in, weights[3]).astype(narrow_type)
        grad_queries, grad_keys, grad_values = attention_backward(
            queries, key_rows, values, segment, log_totals, grad_mixed
        )
        grad_queries = grad_queries.astype(narrow_type)
        grad_keys = grad_keys.astype(narrow_type)
        grad_values = grad_values.astype(narrow_type)
        grad_normed = (
            product_right(grad_queries, weights[0])
            + product_right(grad_keys, weights[1])
            + product_right(grad_values, weights[2])
        )
        grad_stream, grad_gain, grad_shift = norm_pull(grad_normed)
        grad_send = (grad_in_wide + grad_stream).astype(narrow_type)
        grad_bank = jnp.concatenate(
            [
                product_left(normed_low, grad_queries),
                product_left(normed_low, grad_keys),
                product_left(normed_low, grad_values),
                grad_w_out,
            ],
            axis=0,
        )
        bias_rows = jnp.stack(
            [
                jnp.sum(grad_queries.astype(wide_type), axis=0),
                jnp.sum(grad_values.astype(wide_type), axis=0),
                jnp.sum(grad_in_wide, axis=0),
            ]
        )
        smalls = (
            small_zero[:6]
            + (
                jnp.zeros((2, D), wide_type).at[0].set(grad_gain),
                jnp.zeros((2, D), wide_type).at[0].set(grad_shift),
                bias_rows,
            )
            + small_zero[9:]
        )
        return (grad_send, grad_bank, smalls, zeros_pixels)

    def backward_first(operands):
        (
            first_kept,
            second_kept,
            grad_in,
            pixel_rows,
            places,
            lead_time,
            segment,
            grad_rows,
            stash_items,
        ) = operands
        stream = first_kept.astype(wide_type)
        normed, norm_pull = jax.vjp(
            norm_layer, stream, norm_gain[1].astype(wide_type), norm_bias[1].astype(wide_type)
        )
        normed_low = normed.astype(narrow_type)
        inners, actives, partial_sum = feed_half(normed_low, weights, fc1_bias[: 2 * D])
        grad_normed, grad_bank, grad_bias_in = feed_half_back(
            normed_low, weights, inners, actives, grad_rows
        )
        grad_stream, grad_gain, grad_shift = norm_pull(grad_normed + grad_in.astype(wide_type))
        grad_send = (grad_rows.astype(wide_type) + grad_stream).astype(narrow_type)
        smalls = small_zero[:6] + (
            jnp.zeros((2, D), wide_type).at[1].set(grad_gain),
            jnp.zeros((2, D), wide_type).at[1].set(grad_shift),
            small_zero[8],
            jnp.zeros((FF,), wide_type).at[: 2 * D].set(grad_bias_in),
            small_zero[10],
        )
        return (grad_send, grad_bank, smalls, zeros_pixels)

    def backward_second(operands):
        (
            first_kept,
            second_kept,
            grad_in,
            pixel_rows,
            places,
            lead_time,
            segment,
            grad_rows,
            stash_items,
        ) = operands
        inners, actives, partial_sum = feed_half(first_kept, weights, fc1_bias[2 * D :])
        grad_normed, grad_bank, grad_bias_in = feed_half_back(
            first_kept, weights, inners, actives, grad_rows
        )
        smalls = small_zero[:9] + (
            jnp.zeros((FF,), wide_type).at[2 * D :].set(grad_bias_in),
            jnp.sum(grad_rows.astype(wide_type), axis=0),
        )
        return (grad_normed.astype(narrow_type), grad_bank, smalls, zeros_pixels)

    def backward_none(operands):
        return (zeros_stream, jnp.zeros((4 * D, D), wide_type), small_zero, zeros_pixels)

    forward_list = [forward_embed, forward_attend, forward_first, forward_second, forward_none]
    backward_list = [
        backward_embed,
        backward_attend,
        backward_first,
        backward_second,
        backward_none,
    ]
    tick_total = micro_total + section_total - 1
    first_message, second_message = (zeros_stream, zeros_stream)
    kept_first = jnp.zeros((micro_total, row_count, D), narrow_type)
    kept_second = jnp.zeros((micro_total, row_count, D), narrow_type)
    stash_all = tuple(
        (
            jnp.zeros((micro_total,) + array_item.shape, array_item.dtype)
            for array_item in stash_zero
        )
    )
    final_all = jnp.zeros((micro_total, row_count, D), wide_type)
    for tick_number in range(tick_total):
        micro_index = tick_number - section_index
        running = jnp.logical_and(micro_index >= 0, micro_index < micro_total)
        slot_index = jnp.clip(micro_index, 0, micro_total - 1)
        kept_first = kept_first.at[slot_index].set(
            jnp.where(running, first_message, kept_first[slot_index])
        )
        kept_second = kept_second.at[slot_index].set(
            jnp.where(running, second_message, kept_second[slot_index])
        )
        branch = jnp.where(running, section_index, section_total)
        operands = (
            first_message,
            second_message,
            patches[slot_index],
            places_all[slot_index],
            lead_times[slot_index, 0],
            segments[slot_index],
        )
        first_out, second_out, final_rows, stash_items = lax.switch(branch, forward_list, operands)
        final_all = final_all.at[slot_index].add(final_rows)
        stash_all = tuple(
            (
                buffer.at[slot_index].set(jnp.where(running, array_item, buffer[slot_index]))
                for buffer, array_item in zip(stash_all, stash_items)
            )
        )
        if tick_number < tick_total - 1:
            first_message, second_message = (
                from_behind(shortened(first_out), "section", 1).astype(first_out.dtype),
                from_behind(shortened(second_out), "section", 1).astype(second_out.dtype),
            )
    grad_message = zeros_stream
    bank_total = jnp.zeros((4 * D, D), wide_type)
    small_total = small_zero
    pixel_total = jnp.zeros((micro_total, row_count, VARS * PIX), wide_type)
    for tick_number in range(tick_total):
        micro_index = tick_number - (section_total - 1 - section_index)
        running = jnp.logical_and(micro_index >= 0, micro_index < micro_total)
        slot_index = jnp.clip(micro_index, 0, micro_total - 1)
        branch = jnp.where(running, section_index, section_total)
        operands = (
            kept_first[slot_index],
            kept_second[slot_index],
            grad_message,
            patches[slot_index],
            places_all[slot_index],
            lead_times[slot_index, 0],
            segments[slot_index],
            grad_out_all[slot_index],
            tuple((buffer[slot_index] for buffer in stash_all)),
        )
        grad_send, grad_bank, smalls, grad_pixels = lax.switch(branch, backward_list, operands)
        bank_total = bank_total + grad_bank
        small_total = tuple(
            (total_item + sum_item for total_item, sum_item in zip(small_total, smalls))
        )
        pixel_total = pixel_total.at[slot_index].add(grad_pixels)
        if tick_number < tick_total - 1:
            grad_message = jax.tree.map(
                lambda part, own: part.astype(own.dtype),
                from_behind(shortened(grad_send), "section", -1),
                grad_send,
            )
    bank_share = lax.psum_scatter(
        bank_total.astype(jnp.bfloat16), "dp", scatter_dimension=0, tiled=True
    ).astype(jnp.float32)[None]
    small_sums = lax.psum(small_total, ("section", "dp"))
    output_share, pixel_share = (
        lax.psum_scatter(
            final_all.astype(jnp.bfloat16), "section", scatter_dimension=2, tiled=True
        ).astype(jnp.float32),
        lax.psum_scatter(
            pixel_total.astype(jnp.bfloat16), "section", scatter_dimension=2, tiled=True
        ).astype(jnp.float32),
    )
    output_low = output_share.astype(narrow_type)
    return (output_low, pixel_share, bank_share) + tuple(small_sums)


def solution(mesh):
    ins, outs = specs()
    small_slice = mesh.shape["section"] == 4 and mesh.shape["dp"] == 8
    body = on_device_fast if small_slice else on_device
    return jax.shard_map(body, mesh=mesh, in_specs=ins, out_specs=outs, check_vma=False)
```

```python
import functools
import math

import jax
import jax.numpy as jnp
from jax import lax
from jax.experimental import pallas as pl
from jax.experimental.pallas import tpu as pltpu
from jax.sharding import PartitionSpec as P

D = 1024
HEADS = 16
HEAD = 64
FF = 4096
VARS = 48
PIX = 4
F32 = jnp.float32
BF = jnp.bfloat16
MESH = pl.DeviceIdType.MESH
ROWS = 512
GROUP = 256
OWN = 128


def mm(a, b):
    return jnp.dot(a, b, preferred_element_type=F32)


def mm_nt(a, b):
    return lax.dot_general(a, b, (((1,), (1,)), ((), ())), preferred_element_type=F32)


def mm_tn(a, b):
    return lax.dot_general(a, b, (((0,), (0,)), ((), ())), preferred_element_type=F32)


def loop(count, body):
    def step(i, carry):
        body(i)
        return carry

    lax.fori_loop(0, count, step, 0)


def at(start, size, unit):
    return pl.ds(pl.multiple_of(start, unit), size)


def iota(shape, axis):
    return lax.broadcasted_iota(jnp.int32, shape, axis)


def normed_rows(x, gain, shift):
    centre = x - jnp.mean(x, axis=1, keepdims=True)
    rs = lax.rsqrt(jnp.mean(centre * centre, axis=1, keepdims=True) + 1e-5)
    return centre * rs * gain + shift


def norm_back(x, g, gain):
    centre = x - jnp.mean(x, axis=1, keepdims=True)
    rs = lax.rsqrt(jnp.mean(centre * centre, axis=1, keepdims=True) + 1e-5)
    xhat = centre * rs
    q = g * gain
    gx = rs * (q - jnp.mean(q, axis=1, keepdims=True) - xhat * jnp.mean(q * xhat, axis=1, keepdims=True))
    return gx, jnp.sum(g * xhat, axis=0, keepdims=True), jnp.sum(g, axis=0, keepdims=True)


def column_sum(x):
    return jnp.sum(x, axis=0, keepdims=True)


class Place:
    def __init__(self):
        self.s = lax.axis_index("section")
        j = lax.axis_index("dp")
        self.z = lax.div(j, 2)
        self.c = lax.rem(j, 2)
        self.outer = (self.z == 0) | (self.z == 3)
        self.far = jnp.where(self.outer, self.z ^ 2, self.z ^ 3)

    def dev(self, s, z, c):
        return (s, z * 2 + c)


def remote(src, dst, ss, rs, dev):
    return pltpu.make_async_remote_copy(
        src_ref=src, dst_ref=dst, send_sem=ss, recv_sem=rs, device_id=dev, device_id_type=MESH
    )


def arrived(dst, sem):
    pltpu.make_async_copy(dst, dst, sem).wait()


def sent(src, sem):
    pltpu.make_async_copy(src, src, sem).wait()


def barrier(devs):
    sem = pltpu.get_barrier_semaphore()
    for dev in devs:
        pl.semaphore_signal(sem, 1, device_id=dev, device_id_type=MESH)
    pl.semaphore_wait(sem, len(devs))


SCRATCH = dict(
    vec=((24, 1024), F32),
    table=((256, 1024), BF),
    tabT=((1024, 256), BF),
    msgs=((4, 512, 256), BF),
    W=((4, 4, 2, 512, 256), BF),
    WF=((3, 4, 2, 512, 256), BF),
    qbuf=((2, 8, 1024), F32),
    qb=((16, 1024), BF),
    kq=((2, 16, 512), BF),
    mT=((1024, 256), BF),
    mS=((512, 256), BF),
    patT=((192, 512), BF),
    fill=((1536, 192), BF),
    fo=((16, 256), F32),
    att=((768, 512), F32),
    op=((256, 512), BF),
    op1=((4, 256, 128), BF),
    hT=((1024, 512), BF),
    hrow=((512, 1024), BF),
    acc=((512, 1024), F32),
    st0=((512, 1024), BF),
    nrm=((512, 1024), BF),
    nrm2=((512, 1024), BF),
    tr=((1024, 512), BF),
    q=((512, 256), BF),
    k=((512, 256), BF),
    v=((512, 256), BF),
    attp=((8, 256, 256), F32),
    mix=((512, 1024), BF),
    st1=((512, 1024), BF),
    act=((4, 512, 256), BF),
    gact=((4, 512, 256), F32),
    gin=((4, 512, 256), BF),
    gout=((512, 1024), BF),
    rsS=((512, 1024), BF),
    rsR=((4, 128, 1024), BF),
    gs=((2, 128, 1024), BF),
    gmS=((4, 128, 256), BF),
    gm=((512, 256), BF),
    ga=((512, 256), BF),
    gb=((512, 256), BF),
    gq=((3, 512, 256), BF),
    CR=((13, 512, 256), BF),
    RC=((2, 4, 512, 256), BF),
    RA=((4, 512, 256), BF),
    RB=((4, 512, 256), BF),
    FR=((4, 512, 256), BF),
    outR=((4, 512, 256), BF),
    gh=((128, 1024), BF),
    ghT=((1024, 128), BF),
    gpT=((192, 128), F32),
    gsc=((768, 128), F32),
    small=((16, 1024), F32),
    pixS=((4, 48, 128), BF),
    pixR=((4, 48, 128), BF),
    gall=((256, 1024), BF),
    fin=((256, 1024), BF),
    fromc=((128, 1024), BF),
    fromp=((4, 32, 1024), BF),
    fromz=((4, 32, 1024), BF),
    fc=((2, 16, 256), F32),
    fp=((4, 16, 256), F32),
    fz=((4, 16, 256), F32),
    gqv=((16, 1024), BF),
    qx=((2, 8, 1024), F32),
    gaq=((2, 8, 512), F32),
)

SEMS = dict(
    rW=(4, 4, 2),
    rF=(3, 4, 2),
    sMsg=(4,),
    sOwn=(4, 2),
    sFwd=(4, 4, 2),
    sFx=(3, 3),
    sFc=(3, 4),
    rQ=(2,),
    sQ=(2,),
    rK=(2,),
    sK=(16,),
    rMx=(1,),
    sMx=(1,),
    rM=(4, 2),
    sMa=(4,),
    sMz=(3,),
    sMp=(3,),
    sMc=(4,),
    sMix=(3,),
    rMix=(4,),
    sOut=(4,),
    rOut=(4,),
    sR=(2, 4),
    rR=(2, 4),
    sG=(3, 4),
    rG=(3, 4),
    sC=(4, 4),
    rC=(4, 4),
    sZ=(4, 4),
    rRC=(2, 4),
    rRA=(4,),
    rRB=(4,),
    sFin=(4,),
    rFin=(4,),
    sP=(4,),
    rP=(4,),
    sAll=(14,),
    rAll=(14,),
    sFo=(8,),
    rFo=(12,),
    sGq=(18,),
    rGq=(2,),
    sGa=(16,),
    rGa=(2,),
)
NAMES = list(SCRATCH) + list(SEMS)


class Refs:
    pass


def block_kernel(
    pat,
    lead,
    lens,
    cot,
    bank,
    patch,
    patch_b,
    var_emb,
    agg_query,
    agg_bias,
    lead_embed,
    norm_gain,
    norm_bias,
    attn_bias,
    fc1,
    fc2,
    out,
    gpix,
    gbank,
    gtab,
    sums,
    rows_out,
    *scratch,
):
    R = Refs()
    for name, ref in zip(NAMES, scratch):
        setattr(R, name, ref)
    here = Place()
    s, z, c = here.s, here.z, here.c
    dev = here.dev
    outer = here.outer
    inner = jnp.logical_not(outer)
    sib = dev(s, z, 1 - c)
    is_row = (s >= 2) & (z >= 2)
    peers = [s ^ 1, s ^ 2, s ^ 3]
    layers = [z ^ 1, z ^ 2, z ^ 3]
    others = [(s ^ i, z ^ k) for k in range(4) for i in range(4) if (i, k) != (0, 0)]
    vec, table = R.vec, R.table
    when = pl.when
    no = jnp.logical_not

    barrier([dev(p, k, c) for p, k in others] + [dev(p, z, 1 - c) for p in peers] + [sib])

    first_owner = (s == 0) & (z == 0)
    key_owner = (s == 0) & (z == 1)
    value_owner = (s == 0) & (z == 2)

    late = value_owner
    used = no((s == 0) & (z < 3))

    @when(no(is_row) & (used | late))
    def _():
        for p in range(4):
            R.msgs[p] = bank[:, p * 256 : (p + 1) * 256]

    @when(is_row)
    def _():
        for m in range(4):
            q, h = m // 2, m % 2
            for n in range(2):
                lo = (2 * h + n) * 256
                R.msgs[m, n * 256 : (n + 1) * 256, :] = bank[q * 256 : (q + 1) * 256, lo : lo + 256]

    def message(m):
        tp = jnp.where(is_row, 2 * c + m // 2, m)
        tc = jnp.where(is_row, m % 2, c)
        return tp, tc, (tp == s) & (tc == c)

    def scatter(cond):
        for m in range(4):
            tp, tc, own = message(m)

            @when(cond & own)
            def _():
                pltpu.make_async_copy(R.msgs.at[m], R.W.at[z, s, c], R.rW.at[z, s, c]).start()

            @when(cond & no(own))
            def _():
                remote(R.msgs.at[m], R.W.at[z, s, tc], R.sMsg.at[m], R.rW.at[z, s, tc], dev(tp, z, tc)).start()

    scatter(used)

    vec[0:3, :] = agg_bias[...].astype(F32)
    vec[3:5, :] = lead_embed[...].astype(F32)
    vec[5:7, :] = norm_gain[...].astype(F32)
    vec[7:9, :] = norm_bias[...].astype(F32)
    vec[9:12, :] = attn_bias[...].astype(F32)
    for i in range(4):
        vec[12 + i : 13 + i, :] = fc1[i * 1024 : (i + 1) * 1024][None].astype(F32)
    vec[16:17, :] = fc2[...][None].astype(F32)
    vec[17:18, :] = agg_query[...][None].astype(F32)

    @when(first_owner)
    def _():
        part = jnp.broadcast_to(vec[17:18, at(c * 512, 512, 512)].astype(BF), (16, 512))
        R.qbuf[0] = mm(part, bank[...])[0:8]
        remote(R.qbuf.at[0], R.qbuf.at[1], R.sQ.at[0], R.rQ.at[0], sib).start()

    perm = jnp.where(
        (iota((192, 192), 0) // 48 == iota((192, 192), 1) % 4) & (iota((192, 192), 0) % 48 == iota((192, 192), 1) // 4),
        1.0,
        0.0,
    ).astype(BF)
    for p in range(PIX):
        table[p * 48 : (p + 1) * 48, :] = patch[:, p, :]
    table[192:240, :] = (patch_b[...].astype(F32) + var_emb[...].astype(F32)).astype(BF)
    table[240:256, :] = jnp.zeros((16, 1024), BF)

    other_rows = at((1 - c) * 512, 512, 512)
    half_rows = at(c * 512, 512, 512)

    @when(value_owner)
    def _():
        for i in range(4):
            R.tabT[i * 256 : (i + 1) * 256, :] = table[:, i * 256 : (i + 1) * 256].T
        for h in range(2):
            R.gact[h] = mm_tn(bank[:, h * 512 : (h + 1) * 512], R.tabT[half_rows, :])
        remote(R.gact.at[1 - c], R.gact.at[2], R.sMx.at[0], R.rMx.at[0], sib).start()

    @when(first_owner)
    def _():
        arrived(R.qbuf.at[1], R.rQ.at[0])
        total = R.qbuf[0] + R.qbuf[1] + vec[0:1, :]
        total = total.astype(BF)
        R.qb[...] = jnp.concatenate([total, total], axis=0)
        remote(R.qb, R.qb, R.sQ.at[1], R.rQ.at[1], dev(0, 1, c)).start()

    def piece_of(p, h):
        return R.mT.at[at(p * 256 + h * 128, 128, 128), :]

    def my_piece(m):
        return R.mS.at[(m // 2) * 256 + (m % 2) * 128 : (m // 2) * 256 + (m % 2) * 128 + 128, :]

    @when(value_owner)
    def _():
        arrived(R.gact.at[2], R.rMx.at[0])
        sent(R.gact.at[2], R.sMx.at[0])
        bias = jnp.broadcast_to(vec[1:2, half_rows], (8, 512)).T[:, 0:1]
        total = R.gact[c] + R.gact[2]
        R.mS[...] = jnp.where(iota((1, 256), 1) == 240, bias, total).astype(BF)
        for m in range(4):
            q, h = m // 2, m % 2
            tp = 2 * c + q
            own = (tp == s) & (c == h)

            @when(own)
            def _():
                pltpu.make_async_copy(my_piece(m), piece_of(tp, h), R.rM.at[tp, h]).start()

            @when(no(own))
            def _():
                remote(my_piece(m), piece_of(tp, h), R.sMa.at[m], R.rM.at[tp, h], dev(tp, z, h)).start()

    @when(key_owner)
    def _():
        arrived(R.qb, R.rQ.at[1])
        masked = jnp.where(iota((16, 1024), 1) // HEAD == iota((16, 1024), 0), R.qb[...].astype(F32), 0.0).astype(BF)
        R.kq[c] = mm_nt(masked, bank[...]).astype(BF)
        for i, (p, k) in enumerate(others):
            remote(R.kq.at[c], R.kq.at[c], R.sK.at[i], R.rK.at[c], dev(p, k, c)).start()

    def at_least(zz, b):
        return zz == 3 if b == 0 else zz >= 0

    def full_of(zz, b):
        if b == 0:
            return True, zz - 2
        if b == 1:
            return zz == 3, 2
        return None, None

    def spread(zz, b):
        block = R.W.at[zz, b, c]
        whole, f = full_of(zz, b)

        def to_sibling():
            remote(block, block, R.sFwd.at[zz, b, 0], R.rW.at[zz, b, c], sib).start()

        def to_layer():
            pltpu.make_async_copy(block, R.WF.at[f, s, c], R.rF.at[f, s, c]).start()
            for i, p in enumerate(peers):
                remote(block, R.WF.at[f, s, c], R.sFx.at[f, i], R.rF.at[f, s, c], dev(p, z, c)).start()

        if whole is None:
            to_sibling()
        elif whole is True:
            to_layer()
        else:
            when(no(whole))(to_sibling)
            when(whole)(to_layer)

    def along(cond, b, way):
        block = R.W.at[z, b, c]
        zz = z ^ 1 if way == 0 else here.far

        @when(cond)
        def _():
            remote(block, block, R.sOwn.at[b, way], R.rW.at[z, b, c], dev(s, zz, c)).start()

    def ready(cond, b):
        @when(cond)
        def _():
            arrived(R.W.at[z, b, c], R.rW.at[z, b, c])

    def aside(cond, b):
        @when(cond)
        def _():
            spread(z, b)

    def step(cond, b, side=True):
        ready(cond, b)
        along(cond, b, 1)
        along(cond, b, 0)
        if side:
            aside(cond, b)

    def foreign(zz, b, cond=True):
        block = R.W.at[zz, b, c]

        @when(cond & (z != zz))
        def _():
            arrived(block, R.rW.at[zz, b, c])

        @when(cond & (z != zz) & inner & (z ^ 1 != zz))
        def _():
            remote(block, block, R.sFwd.at[zz, b, 1], R.rW.at[zz, b, c], dev(s, z ^ 1, c)).start()

        @when(cond & (z != zz))
        def _():
            spread(zz, b)

    always = z >= 0
    top = z == 3
    @when(z == 2)
    def _():
        arrived(piece_of(s, c), R.rM.at[s, c])
        for i, zz in enumerate(layers):
            remote(piece_of(s, c), piece_of(s, c), R.sMz.at[i], R.rM.at[s, c], dev(s, zz, c)).start()
        for i, p in enumerate(peers):
            remote(piece_of(s, c), piece_of(s, c), R.sMp.at[i], R.rM.at[s, c], dev(p, z, c)).start()

    step(top & (s == 0), 0, False)
    step(no(top) & (s == 1), 1)
    first_feed = z != 2
    for b in (2, 3):
        mine_first = (s == b) & first_feed
        ready(mine_first, b)
        along(mine_first, b, 1)
        along(mine_first & inner, b, 0)
        aside(mine_first, b)

    tcol = iota((GROUP, 1), 0).astype(F32)
    trow = iota((1, GROUP), 1).astype(F32)
    start_col = jnp.zeros((GROUP, 1), F32)
    seg_col = jnp.zeros((GROUP, 1), F32)
    seg_row = jnp.zeros((1, GROUP), F32)
    end = jnp.float32(0.0)
    for i in range(4):
        end = end + lens[0, i].astype(F32)
        past = tcol >= end
        seg_col = seg_col + jnp.where(past, 1.0, 0.0)
        seg_row = seg_row + jnp.where(trow >= end, 1.0, 0.0)
        start_col = jnp.maximum(start_col, jnp.where(past, end, 0.0))
    place_short = tcol - start_col
    valid = seg_col < 3.5
    lead_short = lead[0, 0]
    lead_long = lead[0, 1]
    freq = jnp.exp(-math.log(10000.0) * 2.0 * iota((1, 512), 1).astype(F32) / D)

    def positions(g):
        place = place_short if g == 0 else tcol
        lead_g = lead_short if g == 0 else lead_long
        base = lead_g * vec[3:4, :] + vec[4:5, :] + vec[2:3, :]
        angle = place * freq
        R.acc[g * GROUP : (g + 1) * GROUP, 0:512] = jnp.sin(angle) + base[:, 0:512]
        R.acc[g * GROUP : (g + 1) * GROUP, 512:1024] = jnp.cos(angle) + base[:, 512:1024]

    positions(0)
    step(top & (s != 0), 0, False)
    step(no(top) & (s != 1), 1)
    step(top, 1, False)

    positions(1)

    gout = R.gout
    gout[0:GROUP, :] = jnp.where(valid, cot[0:GROUP, :].astype(F32), 0.0).astype(BF)
    gout[GROUP:ROWS, :] = cot[GROUP:ROWS, :]

    @when(no(key_owner))
    def _():
        arrived(R.kq.at[c], R.rK.at[c])

    remote(R.kq.at[c], R.kq.at[c], R.sK.at[15], R.rK.at[c], sib).start()
    for g in range(2):
        R.patT[:, g * 256 : (g + 1) * 256] = mm(perm, pat[g]).astype(BF)

    @when(z != 2)
    def _():
        arrived(piece_of(s, c), R.rM.at[s, c])
        for i, p in enumerate(peers):
            remote(piece_of(s, c), piece_of(s, c), R.sMp.at[i], R.rM.at[s, c], dev(p, z, c)).start()

    @when(top)
    def _():
        spread(3, 0)

    for b in (2, 3):
        mine_first = (s == b) & first_feed
        ready(no(mine_first), b)
        along(no(mine_first), b, 1)
        aside(no(mine_first), b)
    along(outer, 2, 0)
    along(outer, 3, 0)
    along(inner & no((s == 2) & first_feed), 2, 0)
    scatter(late)

    arrived(R.kq.at[1 - c], R.rK.at[1 - c])
    kq_full = jnp.concatenate([R.kq[0], R.kq[1]], axis=1)
    R.fo[...] = mm_nt(kq_full, table[...])

    def fill_head(h):
        row = R.fo[pl.ds(h, 1), 0:192]
        value = jnp.where(iota((48, 192), 1) % 48 == iota((48, 192), 0), row, 0.0)
        high = value.astype(BF)
        R.fill[at(h * 48, 48, 16), :] = high
        R.fill[at(768 + h * 48, 48, 16), :] = (value - high.astype(F32)).astype(BF)

    loop(HEADS, fill_head)

    def score_part(i):
        lo = i * 256
        R.att[at(lo, 256, 256), :] = mm(R.fill[at(lo, 256, 256), :], R.patT[...]) + mm(
            R.fill[at(768 + lo, 256, 256), :], R.patT[...]
        )

    loop(3, score_part)

    foreign(3, 0)

    for i, p in enumerate([s] + peers):
        if i > 0:
            arrived(piece_of(p, c), R.rM.at[p, c])
        remote(piece_of(p, c), piece_of(p, c), R.sMc.at[p], R.rM.at[p, c], sib).start()

    for p in range(4):
        arrived(piece_of(p, 1 - c), R.rM.at[p, 1 - c])

    for zz in range(3):
        foreign(zz, 1, inner)
    R.op[240:256, :] = jnp.where(iota((16, 512), 0) == 0, 1.0, 0.0).astype(BF)
    r48 = iota((48, 256), 0)
    c48 = iota((48, 256), 1)

    def weights_of(op, low, cols):
        lowf = low.astype(F32)
        for p in range(4):
            op[p * 48 : (p + 1) * 48, :] = (lowf * R.patT[p * 48 : (p + 1) * 48, cols].astype(F32)).astype(BF)
        op[192:240, :] = low

    def embed_head(h):
        offset = jnp.sum(jnp.where(c48 == r48 + 192, R.fo[pl.ds(h, 1), :], 0.0), axis=1, keepdims=True)
        rows = at(h * 48, 48, 16)
        scores = (R.att[rows, :] + offset) * (1.0 / math.sqrt(HEAD))
        peak = jnp.max(scores, axis=0, keepdims=True)
        e = jnp.exp(scores - peak)
        prob = e / jnp.sum(e, axis=0, keepdims=True)
        R.att[rows, :] = prob
        weights_of(R.op, prob.astype(BF), slice(None))
        hrows = at(h * 64, 64, 64)
        R.hT[hrows, :] = mm(R.mT[hrows, :], R.op[...]).astype(BF)

    loop(HEADS, embed_head)

    def pass_on(f):
        for p in [s] + peers:
            block = R.WF.at[f, p, c]
            arrived(block, R.rF.at[f, p, c])
            remote(block, block, R.sFc.at[f, p], R.rF.at[f, p, c], sib).start()

    def wait_whole(f):
        for p in range(4):
            arrived(R.WF.at[f, p, 1 - c], R.rF.at[f, p, 1 - c])

    pass_on(1)

    def turn_tile(i):
        rows = at(i * 256, 256, 256)
        R.hrow[:, rows] = R.hT[rows, :].T

    loop(4, turn_tile)
    for zz in range(3):
        foreign(zz, 1, outer)
    foreign(3, 1, inner)

    @when(top)
    def _():
        spread(3, 1)

    foreign(z ^ 3, 2, inner)
    along(inner & no((s == 3) & first_feed), 3, 0)
    foreign(3, 1, outer)
    wait_whole(1)

    def stream0_part(n):
        cols = at(n * 256, 256, 256)
        R.st0[:, cols] = (mm(R.hrow[...], R.WF[1, n].reshape(1024, 256)) + R.acc[:, cols]).astype(BF)

    loop(4, stream0_part)

    def norm_into(src, dst, which):
        def part(i):
            rows = at(i * 64, 64, 64)
            dst[rows, :] = normed_rows(
                src[rows, :].astype(F32), vec[5 + which : 6 + which, :], vec[7 + which : 8 + which, :]
            ).astype(BF)

        loop(8, part)

    norm_into(R.st0, R.nrm, 0)
    foreign(z ^ 3, 3, inner)


    own_cols = at(s * 256, 256, 256)
    own_rows = at(s * OWN, OWN, OWN)

    def wait_half(zz, b):
        arrived(R.W.at[zz, b, 1 - c], R.rW.at[zz, b, 1 - c])

    def project(zz, dst, bias):
        wait_half(zz, 1)
        weight = R.W[zz, 1].reshape(1024, 256)
        for g in range(2):
            rows = slice(g * 256, (g + 1) * 256)
            value = mm(R.nrm[rows, :], weight)
            if bias is not None:
                value = value + vec[bias : bias + 1, own_cols]
            dst[rows, :] = value.astype(BF)

    project(0, R.q, 9)
    project(1, R.k, None)
    project(2, R.v, 10)

    lane_head = iota((1, 256), 1) // HEAD

    def only(hh, x):
        return jnp.where(lane_head == hh, x.astype(F32), 0.0).astype(BF)

    allowed = seg_col == seg_row

    def attend(g):
        rows = slice(g * 256, (g + 1) * 256)
        total = jnp.zeros((256, 256), F32)
        for hh in range(4):
            scores = mm_nt(R.q[rows, :], only(hh, R.k[rows, :])) * (1.0 / math.sqrt(HEAD))
            if g == 0:
                scores = jnp.where(allowed, scores, -1e30)
            e = jnp.exp(scores - jnp.max(scores, axis=1, keepdims=True))
            prob = e / jnp.sum(e, axis=1, keepdims=True)
            R.attp[g * 4 + hh] = prob
            total = total + mm(prob.astype(BF), only(hh, R.v[rows, :]))
        R.mix[rows, own_cols] = total.astype(BF)

    attend(0)
    attend(1)
    mine = R.mix.at[:, own_cols]
    for i, p in enumerate(peers):
        remote(mine, mine, R.sMix.at[i], R.rMix.at[s], dev(p, z, c)).start()

    step(z == 2, 0)
    for b in (2, 3):
        foreign(z ^ 2, b, inner)
        foreign(z ^ 1, b)
    pass_on(2)
    wait_whole(2)
    for p in peers:
        arrived(R.mix.at[:, at(p * 256, 256, 256)], R.rMix.at[p])
    def stream1_part(n):
        cols = at(n * 256, 256, 256)
        value = mm(R.mix[...], R.WF[2, n].reshape(1024, 256)) + vec[11:12, cols]
        R.st1[:, cols] = (value + R.st0[:, cols].astype(F32)).astype(BF)

    loop(4, stream1_part)
    norm_into(R.st1, R.nrm2, 1)
    early = jnp.where(z < 2, 0, 1)

    def feed(par):
        def part(i):
            bb = lax.div(i, 2)
            b = par + 2 * bb
            rows = at(lax.rem(i, 2) * 256, 256, 256)
            block = R.W.at[2 + par, 2 + bb]
            grad = jnp.zeros((256, 256), F32)
            for n in range(4):
                tile = block[n // 2, (n % 2) * 256 : (n % 2 + 1) * 256, :]
                grad = grad + mm_nt(gout[rows, n * 256 : (n + 1) * 256], tile)
            bias = vec[pl.ds(12 + b, 1), own_cols]
            x = mm(R.nrm2[rows, :], R.W[par, 2 + bb].reshape(1024, 256)) + bias
            half_cdf = 0.5 + 0.5 * lax.erf(x * math.sqrt(0.5))
            R.act[b, rows, :] = (x * half_cdf).astype(BF)
            slope = half_cdf + x * (jnp.exp(-0.5 * x * x) * (1.0 / math.sqrt(2.0 * math.pi)))
            R.gin[b, rows, :] = (grad * slope).astype(BF)

        loop(4, part)

    def feed_norm(par, rows):
        total = mm_nt(R.gin[par, rows, :], R.W[par, 2].reshape(1024, 256))
        return total + mm_nt(R.gin[par + 2, rows, :], R.W[par, 3].reshape(1024, 256))

    def feed_out(par, n, rows):
        total = jnp.zeros((256, 256), F32)
        for bb in range(2):
            tile = R.W[2 + par, 2 + bb, lax.div(n, 2), at(lax.rem(n, 2) * 256, 256, 256), :]
            total = total + mm(R.act[par + 2 * bb, rows, :], tile)
        return total

    def tiles(body):
        loop(8, lambda i: body(lax.rem(i, 4), at(lax.div(i, 4) * 256, 256, 256)))

    def drain_feed(zz):
        for b in (2, 3):
            sent(R.msgs.at[0], R.sFwd.at[zz, b, 0])

            @when((z != zz) & inner & (z ^ 1 != zz))
            def _():
                sent(R.msgs.at[0], R.sFwd.at[zz, b, 1])

            @when(z == zz)
            def _():
                for i in range(2):
                    sent(R.msgs.at[0], R.sOwn.at[b, i])

    def transposed(src):
        def part(i):
            a = lax.div(i, 2)
            b = lax.rem(i, 2)
            R.tr[at(a * 256, 256, 256), at(b * 256, 256, 256)] = src[
                at(b * 256, 256, 256), at(a * 256, 256, 256)
            ].T

        loop(8, part)

    def slot(zz, b):
        return 12 if isinstance(b, int) and b == 0 else (b - 1) * 4 + zz

    def exchange(zz, b):
        block = R.W.at[zz, b, 1 - c]
        remote(block, R.CR.at[slot(zz, b)], R.sC.at[zz, b], R.rC.at[zz, b], sib).start()

    def column_gradient(zz, b, left, right):
        for h in range(2):
            R.W[zz, b, h] = mm(left[h * 512 : (h + 1) * 512, :], right).astype(BF)
        exchange(zz, b)

    def feed_gradients(par):
        drain_feed(par)
        drain_feed(2 + par)

        def part(bb):
            b = par + 2 * bb
            for n in range(4):
                tile = mm_tn(R.act[b], gout[:, n * 256 : (n + 1) * 256])
                R.W[2 + par, 2 + bb, n // 2, (n % 2) * 256 : (n % 2 + 1) * 256, :] = tile.astype(BF)
            exchange(2 + par, 2 + bb)
            column_gradient(par, 2 + bb, R.tr, R.gin[b])

        loop(2, part)

    def summed(zz, b):
        arrived(R.CR.at[slot(zz, b)], R.rC.at[zz, b])
        sent(R.CR.at[slot(zz, b)], R.sC.at[zz, b])
        R.W[zz, b, c] = (R.W[zz, b, c].astype(F32) + R.CR[slot(zz, b)].astype(F32)).astype(BF)

    def first_send(k, b, cond=True):
        zz = z ^ k
        block = R.W.at[zz, b, c]

        @when(cond)
        def _():
            summed(zz, b)
            if k == 1:
                remote(block, R.RA.at[b], R.sZ.at[zz, b], R.rRA.at[b], dev(s, z ^ 1, c)).start()

        if k > 1:

            @when(cond & outer)
            def _():
                remote(block, R.RC.at[3 - k, b], R.sZ.at[zz, b], R.rRC.at[3 - k, b], dev(s, z ^ 1, c)).start()

    def gradient_sends(cond, ks):
        for k in ks:
            for b in (2, 3):
                first_send(k, b, cond)

    def wait_feed(par):
        for b in (2, 3):
            wait_half(par, b)
            wait_half(2 + par, b)

    for b in (2, 3):
        foreign(z ^ 2, b, outer)
    wait_feed(early)
    feed(early)

    def norm_start(g):
        rows = at(g * 256, 256, 256)
        R.acc[rows, :] = feed_norm(early, rows)

    def out_start(n, rows):
        R.gact[n, rows, :] = feed_out(early, n, rows)

    loop(2, norm_start)
    tiles(out_start)
    transposed(R.nrm2)
    feed_gradients(early)
    for b in (2, 3):
        foreign(z ^ 3, b, outer)
    later = 1 - early
    gradient_sends(outer, (2, 0))
    foreign(2, 0)
    wait_feed(later)
    feed(later)

    def reduce_rows(phase, make):
        for i, p in enumerate(peers):
            make(p)
            block = R.rsS.at[at(p * OWN, OWN, OWN), :]
            remote(block, R.rsR.at[s], R.sR.at[phase, i], R.rR.at[phase, s], dev(p, z, c)).start()
        make(s)

    def reduced(phase):
        total = R.rsS[own_rows, :].astype(F32)
        for p in peers:
            arrived(R.rsR.at[p], R.rR.at[phase, p])
            total = total + R.rsR[p].astype(F32)
        return total

    def norm_end(p):
        rows = at(p * OWN, OWN, OWN)
        R.rsS[rows, :] = (R.acc[rows, :] + feed_norm(later, rows)).astype(BF)

    def out_end(n, rows):
        R.hrow[rows, at(n * 256, 256, 256)] = (R.gact[n, rows, :] + feed_out(later, n, rows)).astype(BF)

    reduce_rows(0, norm_end)

    def drain_own(cond, b):
        @when(cond)
        def _():
            for i in range(2):
                sent(R.msgs.at[0], R.sOwn.at[b, i])

    def drain_spread(zz, b):
        whole, f = full_of(zz, b)

        def side():
            sent(R.msgs.at[0], R.sFwd.at[zz, b, 0])

        def layer():
            for i in range(3):
                sent(R.msgs.at[0], R.sFx.at[f, i])

        if whole is None or zz < 3:
            (layer if whole is True else side)()
        else:
            layer()

        @when((z != zz) & inner & (z ^ 1 != zz))
        def _():
            sent(R.msgs.at[0], R.sFwd.at[zz, b, 1])

    def second_send(k, b, cond=True):
        zz = z ^ k
        block = R.W.at[zz, b, c]

        @when(inner & cond)
        def _():
            arrived(R.RC.at[k - 2, b], R.rRC.at[k - 2, b])
            R.W[zz, b, c] = (R.W[zz, b, c].astype(F32) + R.RC[k - 2, b].astype(F32)).astype(BF)
            remote(block, R.RB.at[b], R.sZ.at[zz, b], R.rRB.at[b], dev(s, zz, c)).start()

    def owner_of(b):
        row = (z >= 2) if b >= 2 else (z < 0)
        tc = jnp.where(row, lax.div(s, 2), c)
        m = jnp.where(row, lax.rem(s, 2) * 2 + c, s)
        return tc, m, (s == b) & (tc == c)

    def last_send(cond, b):
        tc, m, own = owner_of(b)
        block = R.W.at[z, b, c]

        @when(cond)
        def _():
            arrived(R.RA.at[b], R.rRA.at[b])
            arrived(R.RB.at[b], R.rRB.at[b])
            R.W[z, b, c] = (R.W[z, b, c].astype(F32) + R.RA[b].astype(F32) + R.RB[b].astype(F32)).astype(BF)

        @when(cond & own)
        def _():
            pltpu.make_async_copy(block, R.FR.at[m], R.rFin.at[m]).start()

        @when(cond & no(own))
        def _():
            remote(block, R.FR.at[m], R.sFin.at[b], R.rFin.at[m], dev(b, z, tc)).start()

    gradient_sends(inner, (1, 3))
    tiles(out_end)
    feed_gradients(later)

    R.small[...] = jnp.zeros((16, 1024), F32)
    for b in range(4):
        R.small[10 + b : 11 + b, own_cols] = column_sum(R.gin[b].astype(F32))
    R.small[14:15, :] = column_sum(gout[own_rows, :].astype(F32))

    gradient_sends(outer, (3, 1))
    gradient_sends(inner, (2, 0))

    g2 = reduced(0)
    gx, gw, gb = norm_back(R.st1[own_rows, :].astype(F32), g2, vec[6:7, :])
    R.small[4:5, :] = gw
    R.small[6:7, :] = gb
    gs1_own = (gout[own_rows, :].astype(F32) + gx).astype(BF)
    R.small[9:10, :] = column_sum(gs1_own.astype(F32))
    R.gs[0] = gs1_own

    def mixed_grad(p):
        total = jnp.zeros((OWN, 256), F32)
        for n in range(4):
            tile = R.WF[2, n, lax.div(p, 2), at(lax.rem(p, 2) * 256, 256, 256), :]
            total = total + mm_nt(R.gs[0, :, n * 256 : (n + 1) * 256], tile)
        return total.astype(BF)

    def swap(phase, src_of, dst):
        for i, p in enumerate(peers):
            remote(src_of(p), dst.at[own_rows, :], R.sG.at[phase, i], R.rG.at[phase, s], dev(p, z, c)).start()

    def swapped(phase, dst):
        for p in peers:
            arrived(dst.at[at(p * OWN, OWN, OWN), :], R.rG.at[phase, p])

    for i, p in enumerate(peers):
        R.gmS[i] = mixed_grad(p)
        remote(R.gmS.at[i], R.gm.at[own_rows, :], R.sG.at[0, i], R.rG.at[0, s], dev(p, z, c)).start()
    R.gm[own_rows, :] = mixed_grad(s)
    swap(1, lambda p: R.gs.at[0, :, at(p * 256, 256, 256)], R.ga)
    R.ga[own_rows, :] = R.gs[0, :, own_cols]

    def send_out(i):
        p = peers[i]
        block = R.hrow.at[:, at(p * 256, 256, 256)]
        remote(block, R.outR.at[s], R.sOut.at[i], R.rOut.at[s], dev(p, z, c)).start()

    send_out(0)
    send_out(1)
    pass_on(0)

    swapped(0, R.gm)

    def attend_back(g):
        rows = at(g * 256, 256, 256)
        qg, kg, vg, gmg = R.q[rows, :], R.k[rows, :], R.v[rows, :], R.gm[rows, :]
        zero = jnp.zeros((256, 256), F32)
        tq, tk, tv = zero, zero, zero
        for hh in range(4):
            prob = R.attp[g * 4 + hh]
            gmh = only(hh, gmg)
            dprob = mm_nt(gmh, vg)
            tv = tv + mm_tn(prob.astype(BF), gmh)
            ds = (prob * (dprob - jnp.sum(prob * dprob, axis=1, keepdims=True))).astype(BF)
            tq = tq + mm(ds, only(hh, kg))
            tk = tk + mm_tn(ds, only(hh, qg))
        scale = 1.0 / math.sqrt(HEAD)
        R.gq[0, rows, :] = (tq * scale).astype(BF)
        R.gq[1, rows, :] = (tk * scale).astype(BF)
        R.gq[2, rows, :] = tv.astype(BF)

    loop(2, attend_back)

    for i in range(3):
        sent(R.rsR.at[0], R.sR.at[0, i])

    def attend_norm(p):
        rows = at(p * OWN, OWN, OWN)
        total = jnp.zeros((OWN, 1024), F32)
        for i in range(3):
            total = total + mm_nt(R.gq[i, rows, :], R.W[i, 1].reshape(1024, 256))
        R.rsS[rows, :] = total.astype(BF)

    reduce_rows(1, attend_norm)

    transposed(R.nrm)
    drain_own(always, 1)
    drain_own(top, 0)
    for zz in range(4):
        drain_spread(zz, 1)
    drain_spread(3, 0)

    def attend_gradient(i):
        column_gradient(i, 1, R.tr, R.gq[i])

    loop(3, attend_gradient)
    transposed(R.mix)
    swapped(1, R.ga)
    column_gradient(3, 1, R.tr, R.ga[...])
    R.small[7:8, own_cols] = column_sum(R.gq[0].astype(F32))
    R.small[8:9, own_cols] = column_sum(R.gq[2].astype(F32))
    for k in (2, 3, 1, 0):
        first_send(k, 1)

    for b in (2, 3):
        second_send(3, b)
    g1 = reduced(1)
    gx, gw, gb = norm_back(R.st0[own_rows, :].astype(F32), g1, vec[5:6, :])
    R.small[3:4, :] = gw
    R.small[5:6, :] = gb
    gs0_own = (R.gs[0].astype(F32) + gx).astype(BF)
    gs0_sum = column_sum(gs0_own.astype(F32))
    R.small[1:2, :] = gs0_sum
    R.small[2:3, :] = jnp.where(s < 2, lead_short, lead_long) * gs0_sum
    R.gs[1] = gs0_own
    swap(2, lambda p: R.gs.at[1, :, at(p * 256, 256, 256)], R.gb)
    R.gb[own_rows, :] = R.gs[1, :, own_cols]
    def heads_grad(i):
        rows = at(lax.rem(i, 2) * 256, 256, 256)
        total = jnp.zeros((256, OWN), F32)
        for n in range(4):
            total = total + mm_nt(R.WF[1, n, lax.div(i, 2), rows, :], R.gs[1, :, n * 256 : (n + 1) * 256])
        block = at(i * 256, 256, 256)
        R.ghT[block, :] = total.astype(BF)
        R.gh[:, block] = total.astype(BF).T

    loop(4, heads_grad)
    R.G = R.acc.at[0:256, :]
    R.gpT[...] = jnp.zeros((192, OWN), F32)
    R.G[...] = jnp.zeros((256, 1024), F32)
    for hh in range(4):
        R.op1[hh, 240:256, :] = jnp.where(iota((16, OWN), 0) == 0, 1.0, 0.0).astype(BF)

    def embed_back(h, op1):
        rows = at(h * 48, 48, 16)
        prob = R.att[rows, own_rows]
        low = prob.astype(BF)
        lowf = low.astype(F32)
        weights_of(op1, low, own_rows)
        hrows = at(h * 64, 64, 64)
        gop = mm_tn(R.mT[hrows, :], R.ghT[hrows, :])
        cols = at(lax.div(h, 4) * 256, 256, 256)
        keep = lane_head == lax.rem(h, 4)
        R.G[:, cols] += jnp.where(keep, mm(op1[...], R.gh[:, cols]), 0.0)
        gatt = gop[192:240, :]
        for p in range(4):
            gatt = gatt + gop[p * 48 : (p + 1) * 48, :] * R.patT[p * 48 : (p + 1) * 48, own_rows].astype(F32)
        R.gsc[rows, :] = prob * (gatt - jnp.sum(prob * gatt, axis=0, keepdims=True)) * (1.0 / math.sqrt(HEAD))
        for p in range(4):
            prow = slice(p * 48, (p + 1) * 48)
            R.gpT[prow, :] += gop[prow, :] * lowf

    def embed_back_four(i):
        for hh in range(4):
            embed_back(4 * i + hh, R.op1.at[hh])

    loop(4, embed_back_four)

    gsc = R.gsc[...]
    gsc_high = gsc.astype(BF)
    gsc_low = (gsc - gsc_high.astype(F32)).astype(BF)
    fold = jnp.where(iota((16, 768), 0) == iota((16, 768), 1) // 48, 1.0, 0.0).astype(BF)

    def folded(x, right):
        x_high = x.astype(BF)
        x_low = (x - x_high.astype(F32)).astype(BF)
        return mm(fold, x_high) + mm(fold, x_low)

    ones = jnp.ones((192, OWN), BF)
    pat_own = R.patT[:, own_rows]
    same = iota((768, 192), 0) % 48 == iota((768, 192), 1) % 48
    cross = mm_nt(gsc_high, pat_own) + mm_nt(gsc_low, pat_own)
    plain = mm_nt(gsc_high, ones) + mm_nt(gsc_low, ones)
    R.fc[0, :, 0:192] = folded(jnp.where(same, cross, 0.0), None)
    R.fc[0, :, 192:256] = folded(jnp.where(same, plain, 0.0), None)[:, 0:64] * jnp.where(
        iota((1, 64), 1) < 48, 1.0, 0.0
    )
    remote(R.fc.at[0], R.fc.at[1], R.sFo.at[0], R.rFo.at[0], sib).start()

    R.G[240:256, :] += R.small[...]
    R.gall[...] = R.G[...].astype(BF)
    half = at(c * 128, 128, 128)
    other = at((1 - c) * 128, 128, 128)
    remote(R.gall.at[other, :], R.fromc, R.sAll.at[0], R.rAll.at[0], sib).start()

    gpt = (R.gpT[...] + mm_tn(R.fill[0:768, :], gsc_high)).astype(BF)
    for p in range(4):
        r = iota((48, 192), 0) + p * 48
        select = jnp.where(iota((48, 192), 1) == (r % 4) * 48 + r // 4, 1.0, 0.0).astype(BF)
        R.pixS[p] = mm(select, gpt).astype(BF)
    for i, p in enumerate(peers):
        remote(R.pixS.at[p], R.pixR.at[s], R.sP.at[i], R.rP.at[s], dev(p, z, c)).start()

    for b in (2, 3):
        second_send(2, b)
    arrived(R.fc.at[1], R.rFo.at[0])
    R.fp[s] = R.fc[0] + R.fc[1]
    for i, p in enumerate(peers):
        remote(R.fp.at[s], R.fp.at[s], R.sFo.at[1 + i], R.rFo.at[1 + s], dev(p, z, c)).start()

    arrived(R.fromc, R.rAll.at[0])
    R.gall[half, :] = (R.gall[half, :].astype(F32) + R.fromc[...].astype(F32)).astype(BF)

    def part_of(p):
        return at(c * 128 + p * 32, 32, 32)

    for i, p in enumerate(peers):
        remote(R.gall.at[part_of(p), :], R.fromp.at[s], R.sAll.at[1 + i], R.rAll.at[1 + s], dev(p, z, c)).start()

    swapped(2, R.gb)
    column_gradient(3, 0, R.hT, R.gb[...])

    for p in peers:
        arrived(R.fp.at[p], R.rFo.at[1 + p])
    R.fz[z] = R.fp[0] + R.fp[1] + R.fp[2] + R.fp[3]
    for i, zz in enumerate(layers):
        remote(R.fz.at[z], R.fz.at[z], R.sFo.at[4 + i], R.rFo.at[5 + z], dev(s, zz, c)).start()

    total = R.gall[part_of(s), :].astype(F32)
    for p in peers:
        arrived(R.fromp.at[p], R.rAll.at[1 + p])
        total = total + R.fromp[p].astype(F32)
    R.fromz[z] = total.astype(BF)
    for i, zz in enumerate(layers):
        remote(R.fromz.at[z], R.fromz.at[z], R.sAll.at[4 + i], R.rAll.at[5 + z], dev(s, zz, c)).start()

    for k in (2, 3, 1, 0):
        first_send(k, 0, z ^ k == 3)
    for k in (2, 3):
        second_send(k, 1)

    for zz in layers:
        arrived(R.fz.at[zz], R.rFo.at[5 + zz])
    fo_grad = (R.fz[0] + R.fz[1]) + (R.fz[2] + R.fz[3])
    fo_high = fo_grad.astype(BF)
    fo_low = (fo_grad - fo_high.astype(F32)).astype(BF)
    gkq = (mm(fo_high, table[...]) + mm(fo_low, table[...])).astype(BF)

    @when(key_owner)
    def _():
        diag = iota((16, 1024), 1) // HEAD == iota((16, 1024), 0)
        own = jnp.where(c == 0, gkq[:, 0:512].astype(F32), gkq[:, 512:1024].astype(F32)).astype(BF)
        row = column_sum(jnp.where(diag, mm(own, bank[...]), 0.0))
        R.qx[0] = jnp.broadcast_to(row, (8, 1024))
        remote(R.qx.at[0], R.qx.at[1], R.sGq.at[15], R.rGq.at[0], sib).start()
        masked = jnp.where(diag, R.qb[...].astype(F32), 0.0).astype(BF)
        gbank[...] = mm_tn(own, masked).astype(BF)
        arrived(R.qx.at[1], R.rGq.at[0])
        row = (R.qx[0] + R.qx[1]).astype(BF)
        R.gqv[...] = jnp.concatenate([row, row], axis=0)
        for i, (p, k) in enumerate(others):
            remote(R.gqv, R.gqv, R.sGq.at[i], R.rGq.at[1], dev(p, k, c)).start()

    for zz in layers:
        arrived(R.fromz.at[zz], R.rAll.at[5 + zz])
    total = R.fromz[0].astype(F32)
    for zz in range(1, 4):
        total = total + R.fromz[zz].astype(F32)
    R.fin[part_of(s), :] = total.astype(BF)
    for i, p in enumerate(peers):
        block = R.fin.at[part_of(s), :]
        remote(block, block, R.sAll.at[7 + i], R.rAll.at[9 + s], dev(p, z, c)).start()

    @when(first_owner)
    def _():
        arrived(R.gqv, R.rGq.at[1])
        R.gaq[c] = mm_nt(R.gqv[...], bank[...])[0:8]
        for i, (p, k) in enumerate(others):
            remote(R.gaq.at[c], R.gaq.at[c], R.sGa.at[i], R.rGa.at[c], dev(p, k, c)).start()
        aq = jnp.where(c == 0, vec[17:18, 0:512], vec[17:18, 512:1024])
        aq = jnp.where(iota((16, 512), 0) == 0, aq, 0.0).astype(BF)
        gbank[...] = mm_tn(aq, R.gqv[...]).astype(BF)

    send_out(2)
    last_send(always, 2)
    last_send(always, 3)

    for p in peers:
        arrived(R.fin.at[part_of(p), :], R.rAll.at[9 + p])
    remote(R.fin.at[half, :], R.fin.at[half, :], R.sAll.at[10], R.rAll.at[13], sib).start()

    for k in (2, 3):
        second_send(k, 0, z ^ k == 3)
    last_send(always, 1)

    wait_whole(0)
    arrived(R.fin.at[other, :], R.rAll.at[13])
    sums[...] = R.fin[240:256, :].astype(F32)
    kq_wide = jnp.concatenate([kq_full, jnp.zeros((112, 1024), BF)], axis=0)
    wide = jnp.zeros((112, 256), BF)
    gfh = jnp.concatenate([fo_high, wide], axis=0)
    gfl = jnp.concatenate([fo_low, wide], axis=0)

    def table_grad(h):
        value = jnp.zeros((256, 512), F32)
        for p in range(4):
            value = value + mm_nt(R.fin[:, p * 256 : (p + 1) * 256], R.WF[0, p, h])
        return value

    for h in range(2):
        cols = slice(h * 512, (h + 1) * 512)
        gtab[:, cols] = (table_grad(h) + mm_tn(gfh, kq_wide[:, cols]) + mm_tn(gfl, kq_wide[:, cols])).astype(BF)

    @when(value_owner)
    def _():
        gbank[...] = mm_tn(table[:, half_rows], R.fin[...]).astype(BF)

    last_send(top, 0)

    @when(no(first_owner))
    def _():
        arrived(R.gaq.at[c], R.rGa.at[c])

    @when(no(key_owner | first_owner))
    def _():
        arrived(R.gqv, R.rGq.at[1])

    remote(R.gaq.at[c], R.gaq.at[c], R.sGa.at[15], R.rGa.at[c], sib).start()
    arrived(R.gaq.at[1 - c], R.rGa.at[1 - c])
    rows_out[0:8, :] = R.gqv[0:8, :].astype(F32)
    rows_out[8:16, 0:512] = R.gaq[0]
    rows_out[8:16, 512:1024] = R.gaq[1]

    total = R.hrow[:, own_cols].astype(F32) + R.st1[:, own_cols].astype(F32) + vec[16:17, own_cols]
    for p in peers:
        arrived(R.outR.at[p], R.rOut.at[p])
        total = total + R.outR[p].astype(F32)
    out[...] = total.astype(BF)

    for i, p in enumerate(peers):
        arrived(R.pixR.at[p], R.rP.at[p])
    R.pixR[s] = R.pixS[s]
    for p in range(4):
        gpix[p // 2, :, (p % 2) * OWN : (p % 2 + 1) * OWN] = R.pixR[p].astype(F32)

    @when(used)
    def _():
        for m in range(4):
            arrived(R.FR.at[m], R.rFin.at[m])

    @when(used & no(is_row))
    def _():
        for m in range(4):
            gbank[:, m * 256 : (m + 1) * 256] = R.FR[m]

    @when(is_row)
    def _():
        for m in range(4):
            q, h = m // 2, m % 2
            for n in range(2):
                lo = (2 * h + n) * 256
                gbank[q * 256 : (q + 1) * 256, lo : lo + 256] = R.FR[m, n * 256 : (n + 1) * 256, :]

    for m in range(4):
        tp, tc, own = message(m)

        @when((used | late) & no(own))
        def _():
            sent(R.msgs.at[m], R.sMsg.at[m])

        @when(value_owner & no((2 * c + m // 2 == s) & (c == m % 2)))
        def _():
            sent(my_piece(m), R.sMa.at[m])

    @when(first_owner)
    def _():
        sent(R.qbuf.at[0], R.sQ.at[0])
        sent(R.qb, R.sQ.at[1])
        for i in range(15):
            sent(R.gaq.at[c], R.sGa.at[i])

    @when(key_owner)
    def _():
        sent(R.qx.at[0], R.sGq.at[15])
        for i in range(15):
            sent(R.kq.at[c], R.sK.at[i])
            sent(R.gqv, R.sGq.at[i])

    @when(z == 2)
    def _():
        for i in range(3):
            sent(R.mS.at[0:128, :], R.sMz.at[i])

    drain_own(z == 2, 0)
    drain_spread(2, 0)
    sent(R.kq.at[c], R.sK.at[15])
    sent(R.gaq.at[c], R.sGa.at[15])
    for f in range(3):
        for p in range(4):
            sent(R.msgs.at[0], R.sFc.at[f, p])
    for p in range(4):
        sent(R.mS.at[0:128, :], R.sMc.at[p])
    sent(R.fc.at[0], R.sFo.at[0])
    sent(R.fromc, R.sAll.at[0])
    sent(R.fromc, R.sAll.at[10])
    for i in range(3):
        sent(R.mS.at[0:128, :], R.sMp.at[i])
        sent(mine, R.sMix.at[i])
        sent(R.msgs.at[0], R.sOut.at[i])
        sent(R.rsR.at[0], R.sR.at[1, i])
        for phase in range(3):
            sent(R.gmS.at[0], R.sG.at[phase, i])
        sent(R.pixS.at[0], R.sP.at[i])
        sent(R.fp.at[0], R.sFo.at[1 + i])
        sent(R.fp.at[0], R.sFo.at[4 + i])
        for phase in range(3):
            sent(R.fromp.at[0], R.sAll.at[1 + 3 * phase + i])
    for b in range(4):
        for zz in range(4):

            @when(at_least(jnp.int32(zz), b) & (z != zz) & (always if b > 0 or zz == 3 else z < 0))
            def _():
                sent(R.msgs.at[0], R.sZ.at[zz, b])

        tc, m, own = owner_of(b)

        @when((top if b == 0 else always) & no(own))
        def _():
            sent(R.msgs.at[0], R.sFin.at[b])


VMEM = pl.BlockSpec(memory_space=pltpu.VMEM)
SMEM = pl.BlockSpec(memory_space=pltpu.SMEM)
ARG_SHAPES = (
    [((2, 192, 256), BF), ((1, 2), F32), ((1, 4), jnp.int32), ((512, 1024), BF), ((512, 1024), BF), ((48, 4, 1024), BF)]
    + [((48, 1024), BF)] * 2
    + [((1024,), BF)]
    + [((n, 1024), BF) for n in (3, 2, 2, 2, 3)]
    + [((4096,), BF), ((1024,), BF)]
)


def block_call(*args):
    shape = jax.ShapeDtypeStruct
    outs = [
        shape((512, 256), BF),
        shape((2, 48, 256), F32),
        shape((512, 1024), BF),
        shape((256, 1024), BF),
        shape((16, 1024), F32),
        shape((16, 1024), F32),
    ]
    return pl.pallas_call(
        block_kernel,
        out_shape=outs,
        in_specs=[VMEM, SMEM, SMEM] + [VMEM] * (len(args) - 3),
        out_specs=[VMEM] * len(outs),
        scratch_shapes=[pltpu.VMEM(*v) for v in SCRATCH.values()]
        + [pltpu.SemaphoreType.DMA(v) for v in SEMS.values()],
        compiler_params=pltpu.CompilerParams(
            collective_id=1, has_side_effects=True, vmem_limit_bytes=63 * 2**20
        ),
    )(*args)


def finish_kernel(*refs):
    sources, rest = refs[:6], refs[6:]
    outs, scratch = rest[:14], rest[14:]
    out, gpix, gbank, gtab, sums, rows = scratch[:6]
    sems = scratch[6]
    copies = [pltpu.make_async_copy(a, b, sems.at[i]) for i, (a, b) in enumerate(zip(sources, scratch[:6]))]
    for copy in copies:
        copy.start()
    for copy in copies:
        copy.wait()
    o_out, o_pix, o_bank, o_patch, o_patch_b, o_var, o_query, o_agg, o_lead, o_gain, o_bias, o_attn, o_fc1, o_fc2 = outs
    o_out[...] = out[...]
    o_pix[...] = gpix[...]
    o_bank[...] = gbank[...].astype(F32)
    for p in range(PIX):
        o_patch[:, p, :] = gtab[p * VARS : (p + 1) * VARS, :].astype(F32)
    o_patch_b[...] = gtab[192:240, :].astype(F32)
    o_var[...] = gtab[192:240, :].astype(F32)
    o_query[...] = rows[8, :]
    o_agg[0:1, :] = rows[0:1, :]
    o_agg[1:3, :] = sums[0:2, :]
    o_lead[0:1, :] = sums[2:3, :]
    o_lead[1:2, :] = sums[1:2, :]
    o_gain[...] = sums[3:5, :]
    o_bias[...] = sums[5:7, :]
    o_attn[...] = sums[7:10, :]
    for i in range(4):
        o_fc1[i * 1024 : (i + 1) * 1024] = sums[10 + i, :]
    o_fc2[...] = sums[14, :]


def finish_call(*args):
    shape = jax.ShapeDtypeStruct
    outs = [shape((512, 256), BF), shape((2, 48, 256), F32), shape((512, 1024), F32), shape((48, 4, 1024), F32)]
    outs += [shape((48, 1024), F32)] * 2 + [shape((1024,), F32)]
    outs += [shape((n, 1024), F32) for n in (3, 2, 2, 2, 3)] + [shape((FF,), F32), shape((1024,), F32)]
    return pl.pallas_call(
        finish_kernel,
        out_shape=outs,
        in_specs=[pl.BlockSpec(memory_space=pl.ANY)] * len(args),
        out_specs=[VMEM] * len(outs),
        scratch_shapes=[pltpu.VMEM(a.shape, a.dtype) for a in args] + [pltpu.SemaphoreType.DMA((len(args),))],
        compiler_params=pltpu.CompilerParams(vmem_limit_bytes=63 * 2**20),
    )(*args)


def on_device_fast(
    patches,
    lead_times,
    short_lengths,
    cotangent,
    bank,
    patch_w,
    patch_b,
    var_emb,
    agg_query,
    agg_bias,
    lead_embed,
    norm_gain,
    norm_bias,
    attn_bias,
    fc1_bias,
    fc2_bias,
):
    parts = block_call(
        jnp.transpose(patches, (0, 2, 1)),
        lead_times.T,
        short_lengths,
        cotangent.reshape(ROWS, D),
        bank[0],
        patch_w,
        patch_b,
        var_emb,
        agg_query,
        agg_bias,
        lead_embed,
        norm_gain,
        norm_bias,
        attn_bias,
        fc1_bias,
        fc2_bias,
    )
    o = finish_call(*parts)
    return (
        (o[0].reshape(2, GROUP, 256), jnp.transpose(o[1], (0, 2, 1)), o[2][None])
        + tuple(o[3:])
    )


def specs():
    ins = (
        (P(None, "dp", None), P(None, "dp"), P("dp", None), P(None, "dp", None), P("section", "dp", None))
        + (P(),) * 11
    )
    outs = (P(None, "dp", "section"), P(None, "dp", "section"), P("section", "dp", None)) + (P(),) * 11
    return ins, outs


wide_type = jnp.float32
narrow_type = jnp.bfloat16
highest = lax.Precision.HIGHEST


def shortened(array):

    def short(part):
        return part.astype(jnp.bfloat16) if part.dtype == jnp.float32 else part

    return jax.tree.map(short, array)


def from_behind(array, axis, by):
    length = lax.axis_size(axis)
    pairs = [(i, i + by) for i in range(length) if 0 <= i + by < length]
    return lax.ppermute(array, axis, pairs)


def product(factor_left, factor_right):
    return jnp.dot(factor_left, factor_right, preferred_element_type=wide_type)


def product_left(factor_left, factor_right):
    return lax.dot_general(
        factor_left, factor_right, (((0,), (0,)), ((), ())), preferred_element_type=wide_type
    )


def product_right(factor_left, factor_right):
    return lax.dot_general(
        factor_left, factor_right, (((1,), (1,)), ((), ())), preferred_element_type=wide_type
    )


def norm_layer(stream, gain_row, shift_row):
    centre = stream - jnp.mean(stream, axis=-1, keepdims=True)
    spread = jnp.mean(centre * centre, axis=-1, keepdims=True)
    return centre * lax.rsqrt(spread + 1e-05) * gain_row + shift_row


def gelu_exact(values_in):
    return jax.nn.gelu(values_in, approximate=False)


def position_table(places):
    half_width = D // 2
    frequency = jnp.exp(-math.log(10000.0) * 2.0 * jnp.arange(half_width, dtype=wide_type) / D)
    angles = places.astype(wide_type)[:, None] * frequency[None, :]
    return jnp.concatenate([jnp.sin(angles), jnp.cos(angles)], axis=1)


def layout(lengths_row, row_count):
    segment_ends = jnp.cumsum(lengths_row)
    starts = segment_ends - lengths_row
    places = jnp.arange(row_count, dtype=jnp.int32)
    segment = jnp.sum((places[:, None] >= segment_ends[None, :]).astype(jnp.int32), axis=1)
    member = segment[:, None] == jnp.arange(lengths_row.shape[0], dtype=jnp.int32)[None, :]
    offset = jnp.sum(jnp.where(member, starts[None, :], 0), axis=1)
    offset = jnp.where(segment == lengths_row.shape[0], segment_ends[-1], offset)
    return (segment, places - offset)


def embed_setup(weights, params):
    patch_w, patch_b, var_emb, agg_query, agg_bias = params[:5]
    query_row = product(agg_query[None, :], weights[0])[0] + agg_bias[0].astype(wide_type)
    query_low = query_row.astype(narrow_type)
    key_query = jnp.einsum(
        "dhe,he->dh",
        weights[1].reshape(D, HEADS, HEAD),
        query_low.reshape(HEADS, HEAD),
        preferred_element_type=wide_type,
    )
    key_low = key_query.astype(narrow_type)
    constant = (patch_b.astype(wide_type) + var_emb.astype(wide_type)).astype(narrow_type)
    filters = jnp.einsum("vpd,dh->vph", patch_w, key_low, preferred_element_type=wide_type)
    offsets = product(constant, key_low)
    embed_table = jnp.concatenate([patch_w.reshape(VARS * PIX, D), constant], axis=0)
    return (query_low, key_low, constant, filters, offsets, embed_table)


def embed_rows(pixel_rows, places, lead_time, setup, weights, params):
    query_low, key_low, constant, filters, offsets, embed_table = setup
    agg_bias, lead_embed = (params[4], params[5])
    row_count = pixel_rows.shape[0]
    pixels = pixel_rows.reshape(row_count, VARS, PIX).astype(wide_type)
    scores = (
        jnp.einsum("tvp,vph->tvh", pixels, filters, precision=highest) + offsets[None]
    ) / math.sqrt(HEAD)
    attend = jax.nn.softmax(scores, axis=1)
    attend_low = attend.astype(narrow_type)
    weighted = (attend_low.astype(wide_type)[:, :, :, None] * pixels[:, :, None, :]).astype(
        narrow_type
    )
    operand = jnp.concatenate(
        [
            jnp.transpose(weighted, (0, 2, 1, 3)).reshape(row_count * HEADS, VARS * PIX),
            jnp.transpose(attend_low, (0, 2, 1)).reshape(row_count * HEADS, VARS),
        ],
        axis=1,
    )
    pooled = product(operand, embed_table).astype(narrow_type).reshape(row_count, HEADS, D)
    heads_out = jnp.einsum(
        "thd,dhe->the", pooled, weights[2].reshape(D, HEADS, HEAD), preferred_element_type=wide_type
    ).reshape(row_count, D)
    heads_low = (heads_out + agg_bias[1].astype(wide_type)).astype(narrow_type)
    merged = product(heads_low, weights[3]) + agg_bias[2].astype(wide_type)
    stream = (
        merged
        + position_table(places)
        + lead_time * lead_embed[0].astype(wide_type)
        + lead_embed[1].astype(wide_type)
    )
    return (stream.astype(narrow_type), (pixels, attend, attend_low, operand, pooled, heads_low))


def embed_back(grad_rows, lead_time, setup, saved_state, weights):
    query_low, key_low, constant, filters, offsets, embed_table = setup
    pixels, attend, attend_low, operand, pooled, heads_low = saved_state
    row_count = grad_rows.shape[0]
    grad_wide = grad_rows.astype(wide_type)
    grad_w_out = product_left(heads_low, grad_rows)
    grad_bias_out = jnp.sum(grad_wide, axis=0)
    grad_heads = product_right(grad_rows, weights[3]).astype(narrow_type)
    grad_bias_value = jnp.sum(grad_heads.astype(wide_type), axis=0)
    grad_heads_split = grad_heads.reshape(row_count, HEADS, HEAD)
    grad_w_value = jnp.einsum(
        "thd,the->dhe", pooled, grad_heads_split, preferred_element_type=wide_type
    ).reshape(D, D)
    grad_pooled = jnp.einsum(
        "the,dhe->thd",
        grad_heads_split,
        weights[2].reshape(D, HEADS, HEAD),
        preferred_element_type=wide_type,
    )
    grad_pooled = grad_pooled.astype(narrow_type).reshape(row_count * HEADS, D)
    grad_operand = product_right(grad_pooled, embed_table)
    grad_table = product_left(operand, grad_pooled)
    grad_weighted = grad_operand[:, : VARS * PIX].reshape(row_count, HEADS, VARS, PIX)
    grad_mixing = jnp.transpose(
        grad_operand[:, VARS * PIX :].reshape(row_count, HEADS, VARS), (0, 2, 1)
    )
    grad_attend = (
        jnp.einsum("thvp,tvp->tvh", grad_weighted, pixels, precision=highest) + grad_mixing
    )
    grad_scores = (
        attend
        * (grad_attend - jnp.sum(attend * grad_attend, axis=1, keepdims=True))
        / math.sqrt(HEAD)
    )
    grad_pixels = jnp.einsum(
        "thvp,tvh->tvp", grad_weighted, attend_low.astype(wide_type), precision=highest
    )
    grad_pixels = grad_pixels + jnp.einsum("tvh,vph->tvp", grad_scores, filters, precision=highest)
    grad_filters = jnp.einsum("tvp,tvh->vph", pixels, grad_scores, precision=highest)
    grad_offsets = jnp.sum(grad_scores, axis=0)
    grad_lead = jnp.stack([lead_time * grad_bias_out, grad_bias_out])
    sums = (
        grad_w_out,
        grad_bias_out,
        grad_bias_value,
        grad_w_value,
        grad_table,
        grad_filters,
        grad_offsets,
        grad_lead,
    )
    return (grad_pixels.reshape(row_count, VARS * PIX), sums)


def embed_finish(totals, setup, weights, params):
    (
        grad_w_out,
        grad_bias_out,
        grad_bias_value,
        grad_w_value,
        grad_table,
        grad_filters,
        grad_offsets,
        grad_lead,
    ) = totals
    query_low, key_low, constant, filters, offsets, embed_table = setup
    patch_w, agg_query = (params[0], params[3])
    key_wide = key_low.astype(wide_type)
    grad_patch_w = grad_table[: VARS * PIX].reshape(VARS, PIX, D) + jnp.einsum(
        "vph,dh->vpd", grad_filters, key_wide, precision=highest
    )
    grad_constant = grad_table[VARS * PIX :] + jnp.dot(grad_offsets, key_wide.T, precision=highest)
    grad_key = jnp.einsum("vpd,vph->dh", patch_w.astype(wide_type), grad_filters, precision=highest)
    grad_key = grad_key + jnp.dot(constant.astype(wide_type).T, grad_offsets, precision=highest)
    grad_key_low = grad_key.astype(narrow_type)
    query_heads = query_low.reshape(HEADS, HEAD).astype(wide_type)
    grad_w_key = (grad_key_low.astype(wide_type)[:, :, None] * query_heads[None, :, :]).reshape(
        D, D
    )
    grad_query = jnp.einsum(
        "dhe,dh->he",
        weights[1].reshape(D, HEADS, HEAD),
        grad_key_low,
        preferred_element_type=wide_type,
    )
    grad_query = grad_query.reshape(D).astype(narrow_type)
    grad_query_wide = grad_query.astype(wide_type)
    grad_w_query = agg_query.astype(wide_type)[:, None] * grad_query_wide[None, :]
    grad_agg_query = product(weights[0], grad_query[:, None])[:, 0]
    grad_bank = jnp.concatenate([grad_w_query, grad_w_key, grad_w_value, grad_w_out], axis=0)
    smalls = (
        grad_patch_w,
        grad_constant,
        grad_constant,
        grad_agg_query,
        jnp.stack([grad_query_wide, grad_bias_value, grad_bias_out]),
        grad_lead,
        jnp.zeros((2, D), wide_type),
        jnp.zeros((2, D), wide_type),
        jnp.zeros((3, D), wide_type),
        jnp.zeros((FF,), wide_type),
        jnp.zeros((D,), wide_type),
    )
    return (grad_bank, smalls)


def attention_scores(block_query, block_segment, key_heads, segment):
    raw_scores = jnp.einsum(
        "qhe,khe->hqk", block_query, key_heads, preferred_element_type=wide_type
    ) / math.sqrt(HEAD)
    allowed = (block_segment[:, None] == segment[None, :])[None]
    return jnp.where(allowed, raw_scores, -1e30)


def attention_forward(queries, key_rows, values, segment):
    row_count = queries.shape[0]
    block_rows = min(512, row_count)
    block_total = row_count // block_rows
    key_heads = key_rows.reshape(row_count, HEADS, HEAD)
    value_heads = values.reshape(row_count, HEADS, HEAD)

    def one_block(block_items):
        block_query, block_segment = block_items
        scores = attention_scores(block_query, block_segment, key_heads, segment)
        row_peak = jnp.max(scores, axis=-1, keepdims=True)
        exp_scores = jnp.exp(scores - row_peak)
        exp_total = jnp.sum(exp_scores, axis=-1, keepdims=True)
        probabilities = (exp_scores / exp_total).astype(narrow_type)
        mixed_heads = jnp.einsum(
            "hqk,khe->qhe", probabilities, value_heads, preferred_element_type=wide_type
        )
        return (mixed_heads.astype(narrow_type), (row_peak + jnp.log(exp_total))[:, :, 0])

    mixed_heads, log_totals = lax.map(
        one_block,
        (
            queries.reshape(block_total, block_rows, HEADS, HEAD),
            segment.reshape(block_total, block_rows),
        ),
    )
    return (mixed_heads.reshape(row_count, D), log_totals)


def attention_backward(queries, key_rows, values, segment, log_totals, grad_mixed):
    row_count = queries.shape[0]
    block_rows = min(512, row_count)
    block_total = row_count // block_rows
    key_heads = key_rows.reshape(row_count, HEADS, HEAD)
    value_heads = values.reshape(row_count, HEADS, HEAD)

    def one_block(carry_sums, block_items):
        grad_key_sum, grad_value_sum = carry_sums
        block_query, block_segment, block_log, block_grad = block_items
        scores = attention_scores(block_query, block_segment, key_heads, segment)
        probabilities = jnp.exp(scores - block_log[:, :, None])
        probs_low = probabilities.astype(narrow_type)
        grad_value_sum = grad_value_sum + jnp.einsum(
            "hqk,qhe->khe", probs_low, block_grad, preferred_element_type=wide_type
        )
        grad_probs = jnp.einsum(
            "qhe,khe->hqk", block_grad, value_heads, preferred_element_type=wide_type
        )
        grad_scores = probabilities * (
            grad_probs - jnp.sum(probabilities * grad_probs, axis=-1, keepdims=True)
        )
        grad_low = grad_scores.astype(narrow_type)
        grad_query = jnp.einsum(
            "hqk,khe->qhe", grad_low, key_heads, preferred_element_type=wide_type
        ) / math.sqrt(HEAD)
        grad_key_sum = grad_key_sum + jnp.einsum(
            "hqk,qhe->khe", grad_low, block_query, preferred_element_type=wide_type
        ) / math.sqrt(HEAD)
        return ((grad_key_sum, grad_value_sum), grad_query)

    zero_heads = jnp.zeros((row_count, HEADS, HEAD), wide_type)
    block_items = (
        queries.reshape(block_total, block_rows, HEADS, HEAD),
        segment.reshape(block_total, block_rows),
        log_totals,
        grad_mixed.reshape(block_total, block_rows, HEADS, HEAD),
    )
    (grad_key_sum, grad_value_sum), grad_queries = lax.scan(
        one_block, (zero_heads, zero_heads), block_items
    )
    return (
        grad_queries.reshape(row_count, D),
        grad_key_sum.reshape(row_count, D),
        grad_value_sum.reshape(row_count, D),
    )


def project_heads(normed_low, weights, attn_bias):
    queries = (product(normed_low, weights[0]) + attn_bias[0].astype(wide_type)).astype(narrow_type)
    key_rows = product(normed_low, weights[1]).astype(narrow_type)
    values = (product(normed_low, weights[2]) + attn_bias[1].astype(wide_type)).astype(narrow_type)
    return (queries, key_rows, values)


def feed_half(normed_low, weights, bias_in):
    inner_first = product(normed_low, weights[0]) + bias_in[:D].astype(wide_type)
    inner_second = product(normed_low, weights[1]) + bias_in[D:].astype(wide_type)
    active_first = gelu_exact(inner_first).astype(narrow_type)
    active_second = gelu_exact(inner_second).astype(narrow_type)
    partial_sum = product(active_first, weights[2]) + product(active_second, weights[3])
    return ((inner_first, inner_second), (active_first, active_second), partial_sum)


def feed_half_back(normed_low, weights, inners, actives, grad_rows):
    grad_inners = []
    for number in range(2):
        grad_active = product_right(grad_rows, weights[2 + number])
        value_out, gelu_pull = jax.vjp(gelu_exact, inners[number])
        grad_inners.append(gelu_pull(grad_active)[0].astype(narrow_type))
    grad_normed = product_right(grad_inners[0], weights[0]) + product_right(
        grad_inners[1], weights[1]
    )
    grad_bank = jnp.concatenate(
        [
            product_left(normed_low, grad_inners[0]),
            product_left(normed_low, grad_inners[1]),
            product_left(actives[0], grad_rows),
            product_left(actives[1], grad_rows),
        ],
        axis=0,
    )
    grad_bias_in = jnp.concatenate(
        [
            jnp.sum(grad_inners[0].astype(wide_type), axis=0),
            jnp.sum(grad_inners[1].astype(wide_type), axis=0),
        ]
    )
    return (grad_normed, grad_bank, grad_bias_in)


def on_device(
    patches,
    lead_times,
    short_lengths,
    cotangent,
    bank,
    patch_w,
    patch_b,
    var_emb,
    agg_query,
    agg_bias,
    lead_embed,
    norm_gain,
    norm_bias,
    attn_bias,
    fc1_bias,
    fc2_bias,
):
    params = (
        patch_w,
        patch_b,
        var_emb,
        agg_query,
        agg_bias,
        lead_embed,
        norm_gain,
        norm_bias,
        attn_bias,
        fc1_bias,
        fc2_bias,
    )
    micro_total = patches.shape[0]
    row_count = patches.shape[1]
    section_total = lax.axis_size("section")
    section_index = lax.axis_index("section")
    gathered = lax.all_gather(bank, "dp", axis=1, tiled=True)[0]
    weights = tuple((gathered[number * D : (number + 1) * D] for number in range(4)))
    short_segment, short_places = layout(short_lengths[0], row_count)
    segments = jnp.stack([short_segment, jnp.zeros((row_count,), jnp.int32)])
    places_all = jnp.stack([short_places, jnp.arange(row_count, dtype=jnp.int32)])
    valid_rows = jnp.stack([short_segment < short_lengths.shape[1], jnp.ones((row_count,), bool)])
    grad_out_all = jnp.where(valid_rows[:, :, None], cotangent, jnp.zeros_like(cotangent))
    block_rows = min(512, row_count)
    block_total = row_count // block_rows
    zeros_stream = jnp.zeros((row_count, D), narrow_type)
    zeros_final = jnp.zeros((row_count, D), wide_type)
    zeros_pixels = jnp.zeros((row_count, VARS * PIX), wide_type)
    stash_zero = (
        zeros_stream,
        zeros_stream,
        zeros_stream,
        zeros_stream,
        jnp.zeros((block_total, HEADS, block_rows), wide_type),
    )
    small_zero = tuple((jnp.zeros(array_item.shape, wide_type) for array_item in params))

    def forward_embed(operands):
        first_in, second_in, pixel_rows, places, lead_time, segment = operands
        setup = embed_setup(weights, params)

        def one_block(block_items):
            return embed_rows(block_items[0], block_items[1], lead_time, setup, weights, params)[0]

        streams = lax.map(
            one_block,
            (
                pixel_rows.reshape(block_total, block_rows, VARS * PIX),
                places.reshape(block_total, block_rows),
            ),
        )
        return (streams.reshape(row_count, D), zeros_stream, zeros_final, stash_zero)

    def forward_attend(operands):
        first_in, second_in, pixel_rows, places, lead_time, segment = operands
        stream = first_in.astype(wide_type)
        normed_low = norm_layer(
            stream, norm_gain[0].astype(wide_type), norm_bias[0].astype(wide_type)
        ).astype(narrow_type)
        queries, key_rows, values = project_heads(normed_low, weights, attn_bias)
        mixed_heads, log_totals = attention_forward(queries, key_rows, values, segment)
        new_stream = stream + product(mixed_heads, weights[3]) + attn_bias[2].astype(wide_type)
        return (new_stream.astype(narrow_type), zeros_stream, zeros_final, stash_zero)

    def forward_first(operands):
        first_in, second_in, pixel_rows, places, lead_time, segment = operands
        stream = first_in.astype(wide_type)
        normed_low = norm_layer(
            stream, norm_gain[1].astype(wide_type), norm_bias[1].astype(wide_type)
        ).astype(narrow_type)
        inners, actives, partial_sum = feed_half(normed_low, weights, fc1_bias[: 2 * D])
        return (normed_low, (stream + partial_sum).astype(narrow_type), zeros_final, stash_zero)

    def forward_second(operands):
        first_in, second_in, pixel_rows, places, lead_time, segment = operands
        inners, actives, partial_sum = feed_half(first_in, weights, fc1_bias[2 * D :])
        final_rows = second_in.astype(wide_type) + partial_sum + fc2_bias.astype(wide_type)
        return (zeros_stream, zeros_stream, final_rows, stash_zero)

    def forward_none(operands):
        return (zeros_stream, zeros_stream, zeros_final, stash_zero)

    def backward_embed(operands):
        (
            first_kept,
            second_kept,
            grad_in,
            pixel_rows,
            places,
            lead_time,
            segment,
            grad_rows,
            stash_items,
        ) = operands
        setup = embed_setup(weights, params)

        def one_block(totals, block_items):
            block_pixels, block_places, block_grad = block_items
            block_stream, saved_state = embed_rows(
                block_pixels, block_places, lead_time, setup, weights, params
            )
            block_dx, sums = embed_back(block_grad, lead_time, setup, saved_state, weights)
            return (
                tuple((total_item + sum_item for total_item, sum_item in zip(totals, sums))),
                block_dx,
            )

        zero_totals = (
            jnp.zeros((D, D), wide_type),
            jnp.zeros((D,), wide_type),
            jnp.zeros((D,), wide_type),
            jnp.zeros((D, D), wide_type),
            jnp.zeros((VARS * PIX + VARS, D), wide_type),
            jnp.zeros((VARS, PIX, HEADS), wide_type),
            jnp.zeros((VARS, HEADS), wide_type),
            jnp.zeros((2, D), wide_type),
        )
        block_items = (
            pixel_rows.reshape(block_total, block_rows, VARS * PIX),
            places.reshape(block_total, block_rows),
            grad_in.reshape(block_total, block_rows, D),
        )
        totals, grad_pixels = lax.scan(one_block, zero_totals, block_items)
        grad_bank, smalls = embed_finish(totals, setup, weights, params)
        return (zeros_stream, grad_bank, smalls, grad_pixels.reshape(row_count, VARS * PIX))

    def backward_attend(operands):
        (
            first_kept,
            second_kept,
            grad_in,
            pixel_rows,
            places,
            lead_time,
            segment,
            grad_rows,
            stash_items,
        ) = operands
        stream = first_kept.astype(wide_type)
        normed, norm_pull = jax.vjp(
            norm_layer, stream, norm_gain[0].astype(wide_type), norm_bias[0].astype(wide_type)
        )
        normed_low = normed.astype(narrow_type)
        queries, key_rows, values = project_heads(normed_low, weights, attn_bias)
        mixed_heads, log_totals = attention_forward(queries, key_rows, values, segment)
        grad_in_wide = grad_in.astype(wide_type)
        grad_w_out = product_left(mixed_heads, grad_in)
        grad_mixed = product_right(grad_in, weights[3]).astype(narrow_type)
        grad_queries, grad_keys, grad_values = attention_backward(
            queries, key_rows, values, segment, log_totals, grad_mixed
        )
        grad_queries = grad_queries.astype(narrow_type)
        grad_keys = grad_keys.astype(narrow_type)
        grad_values = grad_values.astype(narrow_type)
        grad_normed = (
            product_right(grad_queries, weights[0])
            + product_right(grad_keys, weights[1])
            + product_right(grad_values, weights[2])
        )
        grad_stream, grad_gain, grad_shift = norm_pull(grad_normed)
        grad_send = (grad_in_wide + grad_stream).astype(narrow_type)
        grad_bank = jnp.concatenate(
            [
                product_left(normed_low, grad_queries),
                product_left(normed_low, grad_keys),
                product_left(normed_low, grad_values),
                grad_w_out,
            ],
            axis=0,
        )
        bias_rows = jnp.stack(
            [
                jnp.sum(grad_queries.astype(wide_type), axis=0),
                jnp.sum(grad_values.astype(wide_type), axis=0),
                jnp.sum(grad_in_wide, axis=0),
            ]
        )
        smalls = (
            small_zero[:6]
            + (
                jnp.zeros((2, D), wide_type).at[0].set(grad_gain),
                jnp.zeros((2, D), wide_type).at[0].set(grad_shift),
                bias_rows,
            )
            + small_zero[9:]
        )
        return (grad_send, grad_bank, smalls, zeros_pixels)

    def backward_first(operands):
        (
            first_kept,
            second_kept,
            grad_in,
            pixel_rows,
            places,
            lead_time,
            segment,
            grad_rows,
            stash_items,
        ) = operands
        stream = first_kept.astype(wide_type)
        normed, norm_pull = jax.vjp(
            norm_layer, stream, norm_gain[1].astype(wide_type), norm_bias[1].astype(wide_type)
        )
        normed_low = normed.astype(narrow_type)
        inners, actives, partial_sum = feed_half(normed_low, weights, fc1_bias[: 2 * D])
        grad_normed, grad_bank, grad_bias_in = feed_half_back(
            normed_low, weights, inners, actives, grad_rows
        )
        grad_stream, grad_gain, grad_shift = norm_pull(grad_normed + grad_in.astype(wide_type))
        grad_send = (grad_rows.astype(wide_type) + grad_stream).astype(narrow_type)
        smalls = small_zero[:6] + (
            jnp.zeros((2, D), wide_type).at[1].set(grad_gain),
            jnp.zeros((2, D), wide_type).at[1].set(grad_shift),
            small_zero[8],
            jnp.zeros((FF,), wide_type).at[: 2 * D].set(grad_bias_in),
            small_zero[10],
        )
        return (grad_send, grad_bank, smalls, zeros_pixels)

    def backward_second(operands):
        (
            first_kept,
            second_kept,
            grad_in,
            pixel_rows,
            places,
            lead_time,
            segment,
            grad_rows,
            stash_items,
        ) = operands
        inners, actives, partial_sum = feed_half(first_kept, weights, fc1_bias[2 * D :])
        grad_normed, grad_bank, grad_bias_in = feed_half_back(
            first_kept, weights, inners, actives, grad_rows
        )
        smalls = small_zero[:9] + (
            jnp.zeros((FF,), wide_type).at[2 * D :].set(grad_bias_in),
            jnp.sum(grad_rows.astype(wide_type), axis=0),
        )
        return (grad_normed.astype(narrow_type), grad_bank, smalls, zeros_pixels)

    def backward_none(operands):
        return (zeros_stream, jnp.zeros((4 * D, D), wide_type), small_zero, zeros_pixels)

    forward_list = [forward_embed, forward_attend, forward_first, forward_second, forward_none]
    backward_list = [
        backward_embed,
        backward_attend,
        backward_first,
        backward_second,
        backward_none,
    ]
    tick_total = micro_total + section_total - 1
    first_message, second_message = (zeros_stream, zeros_stream)
    kept_first = jnp.zeros((micro_total, row_count, D), narrow_type)
    kept_second = jnp.zeros((micro_total, row_count, D), narrow_type)
    stash_all = tuple(
        (
            jnp.zeros((micro_total,) + array_item.shape, array_item.dtype)
            for array_item in stash_zero
        )
    )
    final_all = jnp.zeros((micro_total, row_count, D), wide_type)
    for tick_number in range(tick_total):
        micro_index = tick_number - section_index
        running = jnp.logical_and(micro_index >= 0, micro_index < micro_total)
        slot_index = jnp.clip(micro_index, 0, micro_total - 1)
        kept_first = kept_first.at[slot_index].set(
            jnp.where(running, first_message, kept_first[slot_index])
        )
        kept_second = kept_second.at[slot_index].set(
            jnp.where(running, second_message, kept_second[slot_index])
        )
        branch = jnp.where(running, section_index, section_total)
        operands = (
            first_message,
            second_message,
            patches[slot_index],
            places_all[slot_index],
            lead_times[slot_index, 0],
            segments[slot_index],
        )
        first_out, second_out, final_rows, stash_items = lax.switch(branch, forward_list, operands)
        final_all = final_all.at[slot_index].add(final_rows)
        stash_all = tuple(
            (
                buffer.at[slot_index].set(jnp.where(running, array_item, buffer[slot_index]))
                for buffer, array_item in zip(stash_all, stash_items)
            )
        )
        if tick_number < tick_total - 1:
            first_message, second_message = (
                from_behind(shortened(first_out), "section", 1).astype(first_out.dtype),
                from_behind(shortened(second_out), "section", 1).astype(second_out.dtype),
            )
    grad_message = zeros_stream
    bank_total = jnp.zeros((4 * D, D), wide_type)
    small_total = small_zero
    pixel_total = jnp.zeros((micro_total, row_count, VARS * PIX), wide_type)
    for tick_number in range(tick_total):
        micro_index = tick_number - (section_total - 1 - section_index)
        running = jnp.logical_and(micro_index >= 0, micro_index < micro_total)
        slot_index = jnp.clip(micro_index, 0, micro_total - 1)
        branch = jnp.where(running, section_index, section_total)
        operands = (
            kept_first[slot_index],
            kept_second[slot_index],
            grad_message,
            patches[slot_index],
            places_all[slot_index],
            lead_times[slot_index, 0],
            segments[slot_index],
            grad_out_all[slot_index],
            tuple((buffer[slot_index] for buffer in stash_all)),
        )
        grad_send, grad_bank, smalls, grad_pixels = lax.switch(branch, backward_list, operands)
        bank_total = bank_total + grad_bank
        small_total = tuple(
            (total_item + sum_item for total_item, sum_item in zip(small_total, smalls))
        )
        pixel_total = pixel_total.at[slot_index].add(grad_pixels)
        if tick_number < tick_total - 1:
            grad_message = jax.tree.map(
                lambda part, own: part.astype(own.dtype),
                from_behind(shortened(grad_send), "section", -1),
                grad_send,
            )
    bank_share = lax.psum_scatter(
        bank_total.astype(jnp.bfloat16), "dp", scatter_dimension=0, tiled=True
    ).astype(jnp.float32)[None]
    small_sums = lax.psum(small_total, ("section", "dp"))
    output_share, pixel_share = (
        lax.psum_scatter(
            final_all.astype(jnp.bfloat16), "section", scatter_dimension=2, tiled=True
        ).astype(jnp.float32),
        lax.psum_scatter(
            pixel_total.astype(jnp.bfloat16), "section", scatter_dimension=2, tiled=True
        ).astype(jnp.float32),
    )
    output_low = output_share.astype(narrow_type)
    return (output_low, pixel_share, bank_share) + tuple(small_sums)


def solution(mesh):
    ins, outs = specs()
    small_slice = mesh.shape["section"] == 4 and mesh.shape["dp"] == 8
    body = on_device_fast if small_slice else on_device
    return jax.shard_map(body, mesh=mesh, in_specs=ins, out_specs=outs, check_vma=False)
```

```python
import functools
import math

import jax
import jax.numpy as jnp
from jax import lax
from jax.experimental import pallas as pl
from jax.experimental.pallas import tpu as pltpu
from jax.sharding import PartitionSpec as P

D = 1024
HEADS = 16
HEAD = 64
FF = 4096
VARS = 48
PIX = 4
F32 = jnp.float32
BF = jnp.bfloat16
MESH = pl.DeviceIdType.MESH
ROWS = 512
GROUP = 256
OWN = 128


def mm(a, b):
    return jnp.dot(a, b, preferred_element_type=F32)


def mm_nt(a, b):
    return lax.dot_general(a, b, (((1,), (1,)), ((), ())), preferred_element_type=F32)


def mm_tn(a, b):
    return lax.dot_general(a, b, (((0,), (0,)), ((), ())), preferred_element_type=F32)


def loop(count, body):
    def step(i, carry):
        body(i)
        return carry

    lax.fori_loop(0, count, step, 0)


def at(start, size, unit):
    return pl.ds(pl.multiple_of(start, unit), size)


def iota(shape, axis):
    return lax.broadcasted_iota(jnp.int32, shape, axis)


def normed_rows(x, gain, shift):
    centre = x - jnp.mean(x, axis=1, keepdims=True)
    rs = lax.rsqrt(jnp.mean(centre * centre, axis=1, keepdims=True) + 1e-5)
    return centre * rs * gain + shift


def norm_back(x, g, gain):
    centre = x - jnp.mean(x, axis=1, keepdims=True)
    rs = lax.rsqrt(jnp.mean(centre * centre, axis=1, keepdims=True) + 1e-5)
    xhat = centre * rs
    q = g * gain
    gx = rs * (q - jnp.mean(q, axis=1, keepdims=True) - xhat * jnp.mean(q * xhat, axis=1, keepdims=True))
    return gx, jnp.sum(g * xhat, axis=0, keepdims=True), jnp.sum(g, axis=0, keepdims=True)


def column_sum(x):
    return jnp.sum(x, axis=0, keepdims=True)


class Place:
    def __init__(self):
        self.s = lax.axis_index("section")
        j = lax.axis_index("dp")
        self.z = lax.div(j, 2)
        self.c = lax.rem(j, 2)
        self.outer = (self.z == 0) | (self.z == 3)
        self.far = jnp.where(self.outer, self.z ^ 2, self.z ^ 3)

    def dev(self, s, z, c):
        return (s, z * 2 + c)


def remote(src, dst, ss, rs, dev):
    return pltpu.make_async_remote_copy(
        src_ref=src, dst_ref=dst, send_sem=ss, recv_sem=rs, device_id=dev, device_id_type=MESH
    )


def arrived(dst, sem):
    pltpu.make_async_copy(dst, dst, sem).wait()


def sent(src, sem):
    pltpu.make_async_copy(src, src, sem).wait()


def barrier(devs):
    sem = pltpu.get_barrier_semaphore()
    for dev in devs:
        pl.semaphore_signal(sem, 1, device_id=dev, device_id_type=MESH)
    pl.semaphore_wait(sem, len(devs))


SCRATCH = dict(
    vec=((24, 1024), F32),
    table=((256, 1024), BF),
    tabT=((1024, 256), BF),
    msgs=((4, 512, 256), BF),
    W=((4, 4, 2, 512, 256), BF),
    WF=((2, 4, 2, 512, 256), BF),
    kqF=((16, 1024), BF),
    gt=((4, 256, 256), BF),
    qbuf=((2, 8, 1024), F32),
    qb=((16, 1024), BF),
    kq=((2, 16, 512), BF),
    mT=((1024, 256), BF),
    mS=((512, 256), BF),
    patT=((192, 512), BF),
    fill=((1536, 192), BF),
    fo=((16, 256), F32),
    att=((768, 512), F32),
    op=((256, 512), BF),
    op1=((4, 256, 128), BF),
    hT=((1024, 512), BF),
    hrow=((512, 1024), BF),
    acc=((512, 1024), F32),
    st0=((512, 1024), BF),
    nrm=((512, 1024), BF),
    nrm2=((512, 1024), BF),
    tr=((1024, 512), BF),
    q=((512, 256), BF),
    k=((512, 256), BF),
    v=((512, 256), BF),
    attp=((8, 256, 256), F32),
    mix=((512, 1024), BF),
    st1=((512, 1024), BF),
    act=((4, 512, 256), BF),
    gact=((4, 512, 256), F32),
    gin=((4, 512, 256), BF),
    gout=((512, 1024), BF),
    rsS=((512, 1024), BF),
    rsR=((4, 128, 1024), BF),
    gs=((2, 128, 1024), BF),
    gmS=((4, 128, 256), BF),
    gm=((512, 256), BF),
    ga=((512, 256), BF),
    gb=((512, 256), BF),
    gq=((3, 512, 256), BF),
    CR=((13, 512, 256), BF),
    RC=((2, 4, 512, 256), BF),
    RA=((4, 512, 256), BF),
    RB=((4, 512, 256), BF),
    FR=((4, 512, 256), BF),
    outR=((4, 512, 256), BF),
    gh=((128, 1024), BF),
    ghT=((1024, 128), BF),
    gpT=((192, 128), F32),
    gsc=((768, 128), F32),
    small=((16, 1024), F32),
    pixS=((4, 48, 128), BF),
    pixR=((4, 48, 128), BF),
    gall=((256, 1024), BF),
    fin=((256, 1024), BF),
    fromc=((128, 1024), BF),
    fromp=((4, 32, 1024), BF),
    fromz=((4, 32, 1024), BF),
    fc=((2, 16, 256), F32),
    fp=((4, 16, 256), F32),
    fz=((4, 16, 256), F32),
    gqv=((16, 1024), BF),
    qx=((2, 8, 1024), F32),
    gaq=((2, 8, 512), F32),
)

SEMS = dict(
    sIn=(14,),
    sRes=(6,),
    rW=(4, 4, 2),
    rF=(2, 4, 2),
    sMsg=(4,),
    sOwn=(4, 2),
    sFwd=(4, 4, 2),
    sFx=(2, 3),
    sFc=(2, 4),
    sGt=(3,),
    rGt=(4,),
    rQ=(2,),
    sQ=(2,),
    rK=(2,),
    sK=(16,),
    rMx=(1,),
    sMx=(1,),
    rM=(4, 2),
    sMa=(4,),
    sMz=(3,),
    sMp=(3,),
    sMc=(4,),
    sMix=(2, 3),
    rMix=(2, 4),
    sOut=(4,),
    rOut=(4,),
    sR=(2, 4),
    rR=(2, 4),
    sG=(3, 4),
    rG=(3, 4),
    sC=(4, 4),
    rC=(4, 4),
    sZ=(4, 4),
    rRC=(2, 4),
    rRA=(4,),
    rRB=(4,),
    sFin=(4,),
    rFin=(4,),
    sP=(4,),
    rP=(4,),
    sAll=(14,),
    rAll=(14,),
    sFo=(8,),
    rFo=(12,),
    sGq=(18,),
    rGq=(2,),
    sGa=(16,),
    rGa=(2,),
)
NAMES = list(SCRATCH) + list(SEMS)


class Refs:
    pass


def block_kernel(*refs):
    sources, lead, lens = refs[0:14], refs[14], refs[15]
    targets, rest = refs[16:22], refs[22:]
    held, results, scratch = rest[0:14], rest[14:20], rest[20:]
    pat, cot, bank, patch, patch_b, var_emb, agg_query, agg_bias, lead_embed = held[0:9]
    norm_gain, norm_bias, attn_bias, fc1, fc2 = held[9:14]
    out, gpix, gbank, gtab, sums, rows_out = results
    R = Refs()
    for name, ref in zip(NAMES, scratch):
        setattr(R, name, ref)
    loads = [pltpu.make_async_copy(a, b, R.sIn.at[i]) for i, (a, b) in enumerate(zip(sources, held))]
    for i in (2, *range(3, 14), 0, 1):
        loads[i].start()
    here = Place()
    s, z, c = here.s, here.z, here.c
    dev = here.dev
    outer = here.outer
    inner = jnp.logical_not(outer)
    sib = dev(s, z, 1 - c)
    is_row = (z >= 2) & ((s >= 2) | ((s == 0) & (z == 2)))
    peers = [s ^ 1, s ^ 2, s ^ 3]
    layers = [z ^ 1, z ^ 2, z ^ 3]
    others = [(s ^ i, z ^ k) for k in range(4) for i in range(4) if (i, k) != (0, 0)]
    vec, table = R.vec, R.table
    when = pl.when
    no = jnp.logical_not

    barrier([dev(p, k, c) for p, k in others] + [dev(p, z, 1 - c) for p in peers] + [sib])

    loads[2].wait()
    first_owner = (s == 0) & (z == 0)
    key_owner = (s == 0) & (z == 1)
    value_owner = (s == 0) & (z == 2)

    late = value_owner
    used = no((s == 0) & (z < 3))

    @when(no(is_row) & used)
    def _():
        for p in range(4):
            R.msgs[p] = bank[:, p * 256 : (p + 1) * 256]

    @when(is_row)
    def _():
        for m in range(4):
            q, h = m // 2, m % 2
            for n in range(2):
                lo = (2 * h + n) * 256
                R.msgs[m, n * 256 : (n + 1) * 256, :] = bank[q * 256 : (q + 1) * 256, lo : lo + 256]

    def message(m):
        tp = jnp.where(is_row, 2 * c + m // 2, m)
        tc = jnp.where(is_row, m % 2, c)
        return tp, tc, (tp == s) & (tc == c)

    def scatter(cond):
        for m in range(4):
            tp, tc, own = message(m)

            @when(cond & own)
            def _():
                pltpu.make_async_copy(R.msgs.at[m], R.W.at[z, s, c], R.rW.at[z, s, c]).start()

            @when(cond & no(own))
            def _():
                remote(R.msgs.at[m], R.W.at[z, s, tc], R.sMsg.at[m], R.rW.at[z, s, tc], dev(tp, z, tc)).start()

    scatter(used)

    for i in range(3, 14):
        loads[i].wait()
    vec[0:3, :] = agg_bias[...].astype(F32)
    vec[3:5, :] = lead_embed[...].astype(F32)
    vec[5:7, :] = norm_gain[...].astype(F32)
    vec[7:9, :] = norm_bias[...].astype(F32)
    vec[9:12, :] = attn_bias[...].astype(F32)
    for i in range(4):
        vec[12 + i : 13 + i, :] = fc1[i * 1024 : (i + 1) * 1024][None].astype(F32)
    vec[16:17, :] = fc2[...][None].astype(F32)
    vec[17:18, :] = agg_query[...][None].astype(F32)

    @when(first_owner)
    def _():
        part = jnp.broadcast_to(vec[17:18, at(c * 512, 512, 512)].astype(BF), (16, 512))
        R.qbuf[0] = mm(part, bank[...])[0:8]
        remote(R.qbuf.at[0], R.qbuf.at[1], R.sQ.at[0], R.rQ.at[0], sib).start()

    perm = jnp.where(
        (iota((192, 192), 0) // 48 == iota((192, 192), 1) % 4) & (iota((192, 192), 0) % 48 == iota((192, 192), 1) // 4),
        1.0,
        0.0,
    ).astype(BF)
    for p in range(PIX):
        table[p * 48 : (p + 1) * 48, :] = patch[:, p, :]
    table[192:240, :] = (patch_b[...].astype(F32) + var_emb[...].astype(F32)).astype(BF)
    table[240:256, :] = jnp.zeros((16, 1024), BF)

    other_rows = at((1 - c) * 512, 512, 512)
    half_rows = at(c * 512, 512, 512)

    @when(value_owner)
    def _():
        for i in range(4):
            R.tabT[i * 256 : (i + 1) * 256, :] = table[:, i * 256 : (i + 1) * 256].T
        for h in range(2):
            R.gact[h] = mm_tn(bank[:, h * 512 : (h + 1) * 512], R.tabT[half_rows, :])
        remote(R.gact.at[1 - c], R.gact.at[2], R.sMx.at[0], R.rMx.at[0], sib).start()

    @when(first_owner)
    def _():
        arrived(R.qbuf.at[1], R.rQ.at[0])
        total = R.qbuf[0] + R.qbuf[1] + vec[0:1, :]
        total = total.astype(BF)
        R.qb[...] = jnp.concatenate([total, total], axis=0)
        remote(R.qb, R.qb, R.sQ.at[1], R.rQ.at[1], dev(0, 1, c)).start()

    def piece_of(p, h):
        return R.mT.at[at(p * 256 + h * 128, 128, 128), :]

    def my_piece(m):
        return R.mS.at[(m // 2) * 256 + (m % 2) * 128 : (m // 2) * 256 + (m % 2) * 128 + 128, :]

    @when(value_owner)
    def _():
        arrived(R.gact.at[2], R.rMx.at[0])
        sent(R.gact.at[2], R.sMx.at[0])
        bias = jnp.broadcast_to(vec[1:2, half_rows], (8, 512)).T[:, 0:1]
        total = R.gact[c] + R.gact[2]
        R.mS[...] = jnp.where(iota((1, 256), 1) == 240, bias, total).astype(BF)
        for m in range(4):
            q, h = m // 2, m % 2
            tp = 2 * c + q
            own = (tp == s) & (c == h)

            @when(own)
            def _():
                pltpu.make_async_copy(my_piece(m), piece_of(tp, h), R.rM.at[tp, h]).start()

            @when(no(own))
            def _():
                remote(my_piece(m), piece_of(tp, h), R.sMa.at[m], R.rM.at[tp, h], dev(tp, z, h)).start()

    @when(key_owner)
    def _():
        arrived(R.qb, R.rQ.at[1])
        masked = jnp.where(iota((16, 1024), 1) // HEAD == iota((16, 1024), 0), R.qb[...].astype(F32), 0.0).astype(BF)
        R.kq[c] = mm_nt(masked, bank[...]).astype(BF)
        for i, (p, k) in enumerate(others):
            remote(R.kq.at[c], R.kq.at[c], R.sK.at[i], R.rK.at[c], dev(p, k, c)).start()

    def at_least(zz, b):
        return zz == 3 if b == 0 else zz >= 0

    def full_of(zz, b):
        if b == 0:
            return zz == 3, 0
        if b == 1:
            return zz == 3, 1
        return None, None

    def spread(zz, b):
        block = R.W.at[zz, b, c]
        whole, f = full_of(zz, b)

        def to_sibling():
            remote(block, block, R.sFwd.at[zz, b, 0], R.rW.at[zz, b, c], sib).start()

        def to_layer():
            pltpu.make_async_copy(block, R.WF.at[f, s, c], R.rF.at[f, s, c]).start()
            for i, p in enumerate(peers):
                remote(block, R.WF.at[f, s, c], R.sFx.at[f, i], R.rF.at[f, s, c], dev(p, z, c)).start()

        if whole is None:
            to_sibling()
        elif isinstance(whole, bool):
            (to_layer if whole else to_sibling)()
        else:
            when(no(whole))(to_sibling)
            when(whole)(to_layer)

    def along(cond, b, way):
        block = R.W.at[z, b, c]
        zz = z ^ 1 if way == 0 else here.far

        @when(cond)
        def _():
            remote(block, block, R.sOwn.at[b, way], R.rW.at[z, b, c], dev(s, zz, c)).start()

    def ready(cond, b):
        @when(cond)
        def _():
            arrived(R.W.at[z, b, c], R.rW.at[z, b, c])

    def aside(cond, b):
        @when(cond)
        def _():
            spread(z, b)

    def step(cond, b, side=True):
        ready(cond, b)
        along(cond, b, 1)
        along(cond, b, 0)
        if side:
            aside(cond, b)

    def foreign(zz, b, cond=True):
        block = R.W.at[zz, b, c]

        @when(cond & (z != zz))
        def _():
            arrived(block, R.rW.at[zz, b, c])

        @when(cond & (z != zz) & inner & (z ^ 1 != zz))
        def _():
            remote(block, block, R.sFwd.at[zz, b, 1], R.rW.at[zz, b, c], dev(s, z ^ 1, c)).start()

        @when(cond & (z != zz))
        def _():
            spread(zz, b)

    always = z >= 0
    top = z == 3
    @when(z == 2)
    def _():
        arrived(piece_of(s, c), R.rM.at[s, c])
        for i, zz in enumerate(layers):
            remote(piece_of(s, c), piece_of(s, c), R.sMz.at[i], R.rM.at[s, c], dev(s, zz, c)).start()
        for i, p in enumerate(peers):
            remote(piece_of(s, c), piece_of(s, c), R.sMp.at[i], R.rM.at[s, c], dev(p, z, c)).start()

    step(top & (s == 0), 0, False)
    step(no(top) & (s == 1), 1)
    first_feed = z != 2
    for b in (2, 3):
        mine_first = (s == b) & first_feed
        ready(mine_first, b)
        along(mine_first, b, 1)
        along(mine_first & inner, b, 0)
        aside(mine_first, b)

    tcol = iota((GROUP, 1), 0).astype(F32)
    trow = iota((1, GROUP), 1).astype(F32)
    start_col = jnp.zeros((GROUP, 1), F32)
    seg_col = jnp.zeros((GROUP, 1), F32)
    seg_row = jnp.zeros((1, GROUP), F32)
    end = jnp.float32(0.0)
    for i in range(4):
        end = end + lens[0, i].astype(F32)
        past = tcol >= end
        seg_col = seg_col + jnp.where(past, 1.0, 0.0)
        seg_row = seg_row + jnp.where(trow >= end, 1.0, 0.0)
        start_col = jnp.maximum(start_col, jnp.where(past, end, 0.0))
    place_short = tcol - start_col
    valid = seg_col < 3.5
    lead_short = lead[0, 0]
    lead_long = lead[0, 1]
    freq = jnp.exp(-math.log(10000.0) * 2.0 * iota((1, 512), 1).astype(F32) / D)

    def positions(g):
        place = place_short if g == 0 else tcol
        lead_g = lead_short if g == 0 else lead_long
        base = lead_g * vec[3:4, :] + vec[4:5, :] + vec[2:3, :]
        angle = place * freq
        R.acc[g * GROUP : (g + 1) * GROUP, 0:512] = jnp.sin(angle) + base[:, 0:512]
        R.acc[g * GROUP : (g + 1) * GROUP, 512:1024] = jnp.cos(angle) + base[:, 512:1024]

    positions(0)
    step(top & (s != 0), 0, False)
    step(no(top) & (s != 1), 1)
    step(top, 1, False)

    positions(1)

    gout = R.gout
    loads[1].wait()
    gout[0:GROUP, :] = jnp.where(valid, cot[0:GROUP, :].astype(F32), 0.0).astype(BF)
    gout[GROUP:ROWS, :] = cot[GROUP:ROWS, :]

    @when(no(key_owner))
    def _():
        arrived(R.kq.at[c], R.rK.at[c])

    remote(R.kq.at[c], R.kq.at[c], R.sK.at[15], R.rK.at[c], sib).start()
    loads[0].wait()
    for g in range(2):
        R.patT[:, g * 256 : (g + 1) * 256] = mm(perm, pat[g]).astype(BF)

    @when(z != 2)
    def _():
        arrived(piece_of(s, c), R.rM.at[s, c])
        for i, p in enumerate(peers):
            remote(piece_of(s, c), piece_of(s, c), R.sMp.at[i], R.rM.at[s, c], dev(p, z, c)).start()

    @when(top)
    def _():
        spread(3, 0)

    for b in (2, 3):
        mine_first = (s == b) & first_feed
        ready(no(mine_first), b)
        along(no(mine_first), b, 1)
        aside(no(mine_first), b)
    along(outer, 2, 0)
    along(outer, 3, 0)
    along(inner & no((s == 2) & first_feed), 2, 0)
    scatter(late)

    arrived(R.kq.at[1 - c], R.rK.at[1 - c])
    R.kqF[:, 0:512] = R.kq[0]
    R.kqF[:, 512:1024] = R.kq[1]
    kq_full = R.kqF[...]
    R.fo[...] = mm_nt(kq_full, table[...])

    def fill_head(h):
        row = R.fo[pl.ds(h, 1), 0:192]
        value = jnp.where(iota((48, 192), 1) % 48 == iota((48, 192), 0), row, 0.0)
        high = value.astype(BF)
        R.fill[at(h * 48, 48, 16), :] = high
        R.fill[at(768 + h * 48, 48, 16), :] = (value - high.astype(F32)).astype(BF)

    loop(HEADS, fill_head)

    def score_part(i):
        lo = i * 256
        R.att[at(lo, 256, 256), :] = mm(R.fill[at(lo, 256, 256), :], R.patT[...]) + mm(
            R.fill[at(768 + lo, 256, 256), :], R.patT[...]
        )

    loop(3, score_part)

    foreign(3, 0)

    for i, p in enumerate([s] + peers):
        if i > 0:
            arrived(piece_of(p, c), R.rM.at[p, c])
        remote(piece_of(p, c), piece_of(p, c), R.sMc.at[p], R.rM.at[p, c], sib).start()

    for p in range(4):
        arrived(piece_of(p, 1 - c), R.rM.at[p, 1 - c])

    for zz in range(3):
        foreign(zz, 1, inner)
    R.op[240:256, :] = jnp.where(iota((16, 512), 0) == 0, 1.0, 0.0).astype(BF)
    r48 = iota((48, 256), 0)
    c48 = iota((48, 256), 1)

    def weights_of(op, low, cols):
        lowf = low.astype(F32)
        for p in range(4):
            op[p * 48 : (p + 1) * 48, :] = (lowf * R.patT[p * 48 : (p + 1) * 48, cols].astype(F32)).astype(BF)
        op[192:240, :] = low

    def embed_head(h):
        offset = jnp.sum(jnp.where(c48 == r48 + 192, R.fo[pl.ds(h, 1), :], 0.0), axis=1, keepdims=True)
        rows = at(h * 48, 48, 16)
        scores = (R.att[rows, :] + offset) * (1.0 / math.sqrt(HEAD))
        peak = jnp.max(scores, axis=0, keepdims=True)
        e = jnp.exp(scores - peak)
        prob = e / jnp.sum(e, axis=0, keepdims=True)
        R.att[rows, :] = prob
        weights_of(R.op, prob.astype(BF), slice(None))
        hrows = at(h * 64, 64, 64)
        R.hT[hrows, :] = mm(R.mT[hrows, :], R.op[...]).astype(BF)

    loop(HEADS, embed_head)

    def pass_on(f):
        for p in [s] + peers:
            block = R.WF.at[f, p, c]
            arrived(block, R.rF.at[f, p, c])
            remote(block, block, R.sFc.at[f, p], R.rF.at[f, p, c], sib).start()

    def wait_whole(f):
        for p in range(4):
            arrived(R.WF.at[f, p, 1 - c], R.rF.at[f, p, 1 - c])

    pass_on(0)

    def turn_tile(i):
        rows = at(i * 256, 256, 256)
        R.hrow[:, rows] = R.hT[rows, :].T

    loop(4, turn_tile)
    for zz in range(3):
        foreign(zz, 1, outer)
    foreign(3, 1, inner)

    @when(top)
    def _():
        spread(3, 1)

    foreign(z ^ 3, 2, inner)
    along(inner & no((s == 3) & first_feed), 3, 0)
    foreign(3, 1, outer)
    wait_whole(0)

    def stream0_part(n):
        cols = at(n * 256, 256, 256)
        R.st0[:, cols] = (mm(R.hrow[...], R.WF[0, n].reshape(1024, 256)) + R.acc[:, cols]).astype(BF)

    loop(4, stream0_part)

    def norm_into(src, dst, which, g):
        def part(i):
            rows = at(g * 256 + i * 64, 64, 64)
            dst[rows, :] = normed_rows(
                src[rows, :].astype(F32), vec[5 + which : 6 + which, :], vec[7 + which : 8 + which, :]
            ).astype(BF)

        loop(4, part)

    norm_into(R.st0, R.nrm, 0, 0)
    norm_into(R.st0, R.nrm, 0, 1)
    foreign(z ^ 3, 3, inner)


    own_cols = at(s * 256, 256, 256)
    own_rows = at(s * OWN, OWN, OWN)

    def wait_half(zz, b):
        arrived(R.W.at[zz, b, 1 - c], R.rW.at[zz, b, 1 - c])

    def project(zz, dst, bias):
        wait_half(zz, 1)
        weight = R.W[zz, 1].reshape(1024, 256)
        for g in range(2):
            rows = slice(g * 256, (g + 1) * 256)
            value = mm(R.nrm[rows, :], weight)
            if bias is not None:
                value = value + vec[bias : bias + 1, own_cols]
            dst[rows, :] = value.astype(BF)

    project(0, R.q, 9)
    project(1, R.k, None)
    project(2, R.v, 10)

    lane_head = iota((1, 256), 1) // HEAD

    def only(hh, x):
        return jnp.where(lane_head == hh, x.astype(F32), 0.0).astype(BF)

    allowed = seg_col == seg_row

    def attend(g):
        rows = slice(g * 256, (g + 1) * 256)
        total = jnp.zeros((256, 256), F32)
        for hh in range(4):
            scores = mm_nt(R.q[rows, :], only(hh, R.k[rows, :])) * (1.0 / math.sqrt(HEAD))
            if g == 0:
                scores = jnp.where(allowed, scores, -1e30)
            e = jnp.exp(scores - jnp.max(scores, axis=1, keepdims=True))
            prob = e / jnp.sum(e, axis=1, keepdims=True)
            R.attp[g * 4 + hh] = prob
            total = total + mm(prob.astype(BF), only(hh, R.v[rows, :]))
        R.mix[rows, own_cols] = total.astype(BF)

    def mixed_of(g, p):
        return R.mix.at[g * 256 : (g + 1) * 256, at(p * 256, 256, 256)]

    for g in range(2):
        attend(g)
        for i, p in enumerate(peers):
            remote(mixed_of(g, s), mixed_of(g, s), R.sMix.at[g, i], R.rMix.at[g, s], dev(p, z, c)).start()

    step(z == 2, 0)
    for b in (2, 3):
        foreign(z ^ 2, b, inner)
        foreign(z ^ 1, b)
    pass_on(1)
    wait_whole(1)
    def stream1_part(g, n):
        rows = slice(g * 256, (g + 1) * 256)
        cols = at(n * 256, 256, 256)
        value = mm(R.mix[rows, :], R.WF[1, n].reshape(1024, 256)) + vec[11:12, cols]
        R.st1[rows, cols] = (value + R.st0[rows, cols].astype(F32)).astype(BF)

    for g in range(2):
        for p in peers:
            arrived(mixed_of(g, p), R.rMix.at[g, p])
        loop(4, functools.partial(stream1_part, g))
        norm_into(R.st1, R.nrm2, 1, g)

    early = jnp.where(z < 2, 0, 1)

    def feed(par):
        def part(i):
            bb = lax.div(i, 2)
            b = par + 2 * bb
            rows = at(lax.rem(i, 2) * 256, 256, 256)
            block = R.W.at[2 + par, 2 + bb]
            grad = jnp.zeros((256, 256), F32)
            for n in range(4):
                tile = block[n // 2, (n % 2) * 256 : (n % 2 + 1) * 256, :]
                grad = grad + mm_nt(gout[rows, n * 256 : (n + 1) * 256], tile)
            bias = vec[pl.ds(12 + b, 1), own_cols]
            x = mm(R.nrm2[rows, :], R.W[par, 2 + bb].reshape(1024, 256)) + bias
            half_cdf = 0.5 + 0.5 * lax.erf(x * math.sqrt(0.5))
            R.act[b, rows, :] = (x * half_cdf).astype(BF)
            slope = half_cdf + x * (jnp.exp(-0.5 * x * x) * (1.0 / math.sqrt(2.0 * math.pi)))
            R.gin[b, rows, :] = (grad * slope).astype(BF)

        loop(4, part)

    def feed_norm(par, rows):
        total = mm_nt(R.gin[par, rows, :], R.W[par, 2].reshape(1024, 256))
        return total + mm_nt(R.gin[par + 2, rows, :], R.W[par, 3].reshape(1024, 256))

    def feed_out(par, n, rows):
        total = jnp.zeros((256, 256), F32)
        for bb in range(2):
            tile = R.W[2 + par, 2 + bb, lax.div(n, 2), at(lax.rem(n, 2) * 256, 256, 256), :]
            total = total + mm(R.act[par + 2 * bb, rows, :], tile)
        return total

    def tiles(body):
        loop(8, lambda i: body(lax.rem(i, 4), at(lax.div(i, 4) * 256, 256, 256)))

    def drain_feed(zz):
        for b in (2, 3):
            sent(R.msgs.at[0], R.sFwd.at[zz, b, 0])

            @when((z != zz) & inner & (z ^ 1 != zz))
            def _():
                sent(R.msgs.at[0], R.sFwd.at[zz, b, 1])

            @when(z == zz)
            def _():
                for i in range(2):
                    sent(R.msgs.at[0], R.sOwn.at[b, i])

    def transposed(src):
        def part(i):
            a = lax.div(i, 2)
            b = lax.rem(i, 2)
            R.tr[at(a * 256, 256, 256), at(b * 256, 256, 256)] = src[
                at(b * 256, 256, 256), at(a * 256, 256, 256)
            ].T

        loop(8, part)

    def slot(zz, b):
        return 12 if isinstance(b, int) and b == 0 else (b - 1) * 4 + zz

    def exchange(zz, b):
        block = R.W.at[zz, b, 1 - c]
        remote(block, R.CR.at[slot(zz, b)], R.sC.at[zz, b], R.rC.at[zz, b], sib).start()

    def column_gradient(zz, b, left, right):
        for h in range(2):
            R.W[zz, b, h] = mm(left[h * 512 : (h + 1) * 512, :], right).astype(BF)
        exchange(zz, b)

    def feed_gradients(par):
        drain_feed(par)
        drain_feed(2 + par)

        def part(bb):
            b = par + 2 * bb
            for n in range(4):
                tile = mm_tn(R.act[b], gout[:, n * 256 : (n + 1) * 256])
                R.W[2 + par, 2 + bb, n // 2, (n % 2) * 256 : (n % 2 + 1) * 256, :] = tile.astype(BF)
            exchange(2 + par, 2 + bb)
            column_gradient(par, 2 + bb, R.tr, R.gin[b])

        loop(2, part)

    def summed(zz, b):
        arrived(R.CR.at[slot(zz, b)], R.rC.at[zz, b])
        sent(R.CR.at[slot(zz, b)], R.sC.at[zz, b])
        R.W[zz, b, c] = (R.W[zz, b, c].astype(F32) + R.CR[slot(zz, b)].astype(F32)).astype(BF)

    def first_send(k, b, cond=True):
        zz = z ^ k
        block = R.W.at[zz, b, c]

        @when(cond)
        def _():
            summed(zz, b)
            if k == 1:
                remote(block, R.RA.at[b], R.sZ.at[zz, b], R.rRA.at[b], dev(s, z ^ 1, c)).start()

        if k > 1:

            @when(cond & outer)
            def _():
                remote(block, R.RC.at[3 - k, b], R.sZ.at[zz, b], R.rRC.at[3 - k, b], dev(s, z ^ 1, c)).start()

    def gradient_sends(cond, ks):
        for k in ks:
            for b in (2, 3):
                first_send(k, b, cond)

    def wait_feed(par):
        for b in (2, 3):
            wait_half(par, b)
            wait_half(2 + par, b)

    for b in (2, 3):
        foreign(z ^ 2, b, outer)
    wait_feed(early)
    feed(early)

    def norm_start(g):
        rows = at(g * 256, 256, 256)
        R.acc[rows, :] = feed_norm(early, rows)

    def out_start(n, rows):
        R.gact[n, rows, :] = feed_out(early, n, rows)

    loop(2, norm_start)
    tiles(out_start)
    transposed(R.nrm2)
    feed_gradients(early)
    for b in (2, 3):
        foreign(z ^ 3, b, outer)
    later = 1 - early
    gradient_sends(outer, (2, 0))
    foreign(2, 0)
    wait_feed(later)
    feed(later)

    def reduce_rows(phase, make):
        for i, p in enumerate(peers):
            make(p)
            block = R.rsS.at[at(p * OWN, OWN, OWN), :]
            remote(block, R.rsR.at[s], R.sR.at[phase, i], R.rR.at[phase, s], dev(p, z, c)).start()
        make(s)

    def reduced(phase):
        total = R.rsS[own_rows, :].astype(F32)
        for p in peers:
            arrived(R.rsR.at[p], R.rR.at[phase, p])
            total = total + R.rsR[p].astype(F32)
        return total

    def norm_end(p):
        rows = at(p * OWN, OWN, OWN)
        R.rsS[rows, :] = (R.acc[rows, :] + feed_norm(later, rows)).astype(BF)

    def out_end(n, rows):
        R.hrow[rows, at(n * 256, 256, 256)] = (R.gact[n, rows, :] + feed_out(later, n, rows)).astype(BF)

    reduce_rows(0, norm_end)

    def drain_own(cond, b):
        @when(cond)
        def _():
            for i in range(2):
                sent(R.msgs.at[0], R.sOwn.at[b, i])

    def drain_spread(zz, b):
        whole, f = full_of(zz, b)

        def side():
            sent(R.msgs.at[0], R.sFwd.at[zz, b, 0])

        def layer():
            for i in range(3):
                sent(R.msgs.at[0], R.sFx.at[f, i])

        (layer if whole else side)()

        @when((z != zz) & inner & (z ^ 1 != zz))
        def _():
            sent(R.msgs.at[0], R.sFwd.at[zz, b, 1])

    def second_send(k, b, cond=True):
        zz = z ^ k
        block = R.W.at[zz, b, c]

        @when(inner & cond)
        def _():
            arrived(R.RC.at[k - 2, b], R.rRC.at[k - 2, b])
            R.W[zz, b, c] = (R.W[zz, b, c].astype(F32) + R.RC[k - 2, b].astype(F32)).astype(BF)
            remote(block, R.RB.at[b], R.sZ.at[zz, b], R.rRB.at[b], dev(s, zz, c)).start()

    def owner_of(b):
        row = (z >= 2) if b >= 2 else (z < 0)
        tc = jnp.where(row, lax.div(s, 2), c)
        m = jnp.where(row, lax.rem(s, 2) * 2 + c, s)
        return tc, m, (s == b) & (tc == c)

    def last_send(cond, b):
        tc, m, own = owner_of(b)
        block = R.W.at[z, b, c]

        @when(cond)
        def _():
            arrived(R.RA.at[b], R.rRA.at[b])
            arrived(R.RB.at[b], R.rRB.at[b])
            R.W[z, b, c] = (R.W[z, b, c].astype(F32) + R.RA[b].astype(F32) + R.RB[b].astype(F32)).astype(BF)

        @when(cond & own)
        def _():
            pltpu.make_async_copy(block, R.FR.at[m], R.rFin.at[m]).start()

        @when(cond & no(own))
        def _():
            remote(block, R.FR.at[m], R.sFin.at[b], R.rFin.at[m], dev(b, z, tc)).start()

    gradient_sends(inner, (1, 3))
    tiles(out_end)
    feed_gradients(later)

    R.small[...] = jnp.zeros((16, 1024), F32)
    for b in range(4):
        R.small[10 + b : 11 + b, own_cols] = column_sum(R.gin[b].astype(F32))
    R.small[14:15, :] = column_sum(gout[own_rows, :].astype(F32))

    gradient_sends(outer, (3, 1))
    gradient_sends(inner, (2, 0))

    g2 = reduced(0)
    gx, gw, gb = norm_back(R.st1[own_rows, :].astype(F32), g2, vec[6:7, :])
    R.small[4:5, :] = gw
    R.small[6:7, :] = gb
    gs1_own = (gout[own_rows, :].astype(F32) + gx).astype(BF)
    R.small[9:10, :] = column_sum(gs1_own.astype(F32))
    R.gs[0] = gs1_own

    def mixed_grad(p):
        total = jnp.zeros((OWN, 256), F32)
        for n in range(4):
            tile = R.WF[1, n, lax.div(p, 2), at(lax.rem(p, 2) * 256, 256, 256), :]
            total = total + mm_nt(R.gs[0, :, n * 256 : (n + 1) * 256], tile)
        return total.astype(BF)

    def swap(phase, src_of, dst):
        for i, p in enumerate(peers):
            remote(src_of(p), dst.at[own_rows, :], R.sG.at[phase, i], R.rG.at[phase, s], dev(p, z, c)).start()

    def swapped(phase, dst):
        for p in peers:
            arrived(dst.at[at(p * OWN, OWN, OWN), :], R.rG.at[phase, p])

    for i, p in enumerate(peers):
        R.gmS[i] = mixed_grad(p)
        remote(R.gmS.at[i], R.gm.at[own_rows, :], R.sG.at[0, i], R.rG.at[0, s], dev(p, z, c)).start()
    R.gm[own_rows, :] = mixed_grad(s)
    swap(1, lambda p: R.gs.at[0, :, at(p * 256, 256, 256)], R.ga)
    R.ga[own_rows, :] = R.gs[0, :, own_cols]

    def send_out(i):
        p = peers[i]
        block = R.hrow.at[:, at(p * 256, 256, 256)]
        remote(block, R.outR.at[s], R.sOut.at[i], R.rOut.at[s], dev(p, z, c)).start()

    send_out(0)
    send_out(1)

    swapped(0, R.gm)

    def attend_back(g):
        rows = at(g * 256, 256, 256)
        qg, kg, vg, gmg = R.q[rows, :], R.k[rows, :], R.v[rows, :], R.gm[rows, :]
        zero = jnp.zeros((256, 256), F32)
        tq, tk, tv = zero, zero, zero
        for hh in range(4):
            prob = R.attp[g * 4 + hh]
            gmh = only(hh, gmg)
            dprob = mm_nt(gmh, vg)
            tv = tv + mm_tn(prob.astype(BF), gmh)
            ds = (prob * (dprob - jnp.sum(prob * dprob, axis=1, keepdims=True))).astype(BF)
            tq = tq + mm(ds, only(hh, kg))
            tk = tk + mm_tn(ds, only(hh, qg))
        scale = 1.0 / math.sqrt(HEAD)
        R.gq[0, rows, :] = (tq * scale).astype(BF)
        R.gq[1, rows, :] = (tk * scale).astype(BF)
        R.gq[2, rows, :] = tv.astype(BF)

    loop(2, attend_back)

    for i in range(3):
        sent(R.rsR.at[0], R.sR.at[0, i])

    def attend_norm(p):
        rows = at(p * OWN, OWN, OWN)
        total = jnp.zeros((OWN, 1024), F32)
        for i in range(3):
            total = total + mm_nt(R.gq[i, rows, :], R.W[i, 1].reshape(1024, 256))
        R.rsS[rows, :] = total.astype(BF)

    reduce_rows(1, attend_norm)
    send_out(2)
    for b in (2, 3):
        second_send(3, b)

    transposed(R.nrm)
    drain_own(always, 1)
    drain_own(top, 0)
    for zz in range(4):
        drain_spread(zz, 1)
    drain_spread(3, 0)

    def attend_gradient(i):
        column_gradient(i, 1, R.tr, R.gq[i])

    loop(3, attend_gradient)
    transposed(R.mix)
    swapped(1, R.ga)
    column_gradient(3, 1, R.tr, R.ga[...])
    R.small[7:8, own_cols] = column_sum(R.gq[0].astype(F32))
    R.small[8:9, own_cols] = column_sum(R.gq[2].astype(F32))
    for k in (2, 3, 1, 0):
        first_send(k, 1)

    for b in (2, 3):
        second_send(2, b)
    g1 = reduced(1)
    gx, gw, gb = norm_back(R.st0[own_rows, :].astype(F32), g1, vec[5:6, :])
    R.small[3:4, :] = gw
    R.small[5:6, :] = gb
    gs0_own = (R.gs[0].astype(F32) + gx).astype(BF)
    gs0_sum = column_sum(gs0_own.astype(F32))
    R.small[1:2, :] = gs0_sum
    R.small[2:3, :] = jnp.where(s < 2, lead_short, lead_long) * gs0_sum
    R.gs[1] = gs0_own
    swap(2, lambda p: R.gs.at[1, :, at(p * 256, 256, 256)], R.gb)
    R.gb[own_rows, :] = R.gs[1, :, own_cols]
    def heads_grad(i):
        rows = at(lax.rem(i, 2) * 256, 256, 256)
        total = jnp.zeros((256, OWN), F32)
        for n in range(4):
            total = total + mm_nt(R.WF[0, n, lax.div(i, 2), rows, :], R.gs[1, :, n * 256 : (n + 1) * 256])
        block = at(i * 256, 256, 256)
        R.ghT[block, :] = total.astype(BF)
        R.gh[:, block] = total.astype(BF).T

    loop(4, heads_grad)
    R.G = R.acc.at[0:256, :]
    R.gpT[...] = jnp.zeros((192, OWN), F32)
    R.G[...] = jnp.zeros((256, 1024), F32)
    for hh in range(4):
        R.op1[hh, 240:256, :] = jnp.where(iota((16, OWN), 0) == 0, 1.0, 0.0).astype(BF)

    def embed_back(h, op1):
        rows = at(h * 48, 48, 16)
        prob = R.att[rows, own_rows]
        low = prob.astype(BF)
        lowf = low.astype(F32)
        weights_of(op1, low, own_rows)
        hrows = at(h * 64, 64, 64)
        gop = mm_tn(R.mT[hrows, :], R.ghT[hrows, :])
        cols = at(lax.div(h, 4) * 256, 256, 256)
        keep = lane_head == lax.rem(h, 4)
        R.G[:, cols] += jnp.where(keep, mm(op1[...], R.gh[:, cols]), 0.0)
        gatt = gop[192:240, :]
        for p in range(4):
            gatt = gatt + gop[p * 48 : (p + 1) * 48, :] * R.patT[p * 48 : (p + 1) * 48, own_rows].astype(F32)
        R.gsc[rows, :] = prob * (gatt - jnp.sum(prob * gatt, axis=0, keepdims=True)) * (1.0 / math.sqrt(HEAD))
        for p in range(4):
            prow = slice(p * 48, (p + 1) * 48)
            R.gpT[prow, :] += gop[prow, :] * lowf

    def embed_back_four(i):
        for hh in range(4):
            embed_back(4 * i + hh, R.op1.at[hh])

    loop(4, embed_back_four)

    gsc = R.gsc[...]
    gsc_high = gsc.astype(BF)
    gsc_low = (gsc - gsc_high.astype(F32)).astype(BF)
    fold = jnp.where(iota((16, 768), 0) == iota((16, 768), 1) // 48, 1.0, 0.0).astype(BF)

    def folded(x, right):
        x_high = x.astype(BF)
        x_low = (x - x_high.astype(F32)).astype(BF)
        return mm(fold, x_high) + mm(fold, x_low)

    ones = jnp.ones((192, OWN), BF)
    pat_own = R.patT[:, own_rows]
    same = iota((768, 192), 0) % 48 == iota((768, 192), 1) % 48
    cross = mm_nt(gsc_high, pat_own) + mm_nt(gsc_low, pat_own)
    plain = mm_nt(gsc_high, ones) + mm_nt(gsc_low, ones)
    R.fc[0, :, 0:192] = folded(jnp.where(same, cross, 0.0), None)
    R.fc[0, :, 192:256] = folded(jnp.where(same, plain, 0.0), None)[:, 0:64] * jnp.where(
        iota((1, 64), 1) < 48, 1.0, 0.0
    )
    remote(R.fc.at[0], R.fc.at[1], R.sFo.at[0], R.rFo.at[0], sib).start()

    R.G[240:256, :] += R.small[...]
    R.gall[...] = R.G[...].astype(BF)
    half = at(c * 128, 128, 128)
    other = at((1 - c) * 128, 128, 128)
    remote(R.gall.at[other, :], R.fromc, R.sAll.at[0], R.rAll.at[0], sib).start()

    gpt = (R.gpT[...] + mm_tn(R.fill[0:768, :], gsc_high)).astype(BF)
    for p in range(4):
        r = iota((48, 192), 0) + p * 48
        select = jnp.where(iota((48, 192), 1) == (r % 4) * 48 + r // 4, 1.0, 0.0).astype(BF)
        R.pixS[p] = mm(select, gpt).astype(BF)
    for i, p in enumerate(peers):
        remote(R.pixS.at[p], R.pixR.at[s], R.sP.at[i], R.rP.at[s], dev(p, z, c)).start()

    arrived(R.fc.at[1], R.rFo.at[0])
    R.fp[s] = R.fc[0] + R.fc[1]
    for i, p in enumerate(peers):
        remote(R.fp.at[s], R.fp.at[s], R.sFo.at[1 + i], R.rFo.at[1 + s], dev(p, z, c)).start()

    arrived(R.fromc, R.rAll.at[0])
    R.gall[half, :] = (R.gall[half, :].astype(F32) + R.fromc[...].astype(F32)).astype(BF)

    def part_of(p):
        return at(c * 128 + p * 32, 32, 32)

    for i, p in enumerate(peers):
        remote(R.gall.at[part_of(p), :], R.fromp.at[s], R.sAll.at[1 + i], R.rAll.at[1 + s], dev(p, z, c)).start()
    last_send(always, 2)
    last_send(always, 3)

    swapped(2, R.gb)
    column_gradient(3, 0, R.hT, R.gb[...])

    for p in peers:
        arrived(R.fp.at[p], R.rFo.at[1 + p])
    R.fz[z] = R.fp[0] + R.fp[1] + R.fp[2] + R.fp[3]
    for i, zz in enumerate(layers):
        remote(R.fz.at[z], R.fz.at[z], R.sFo.at[4 + i], R.rFo.at[5 + z], dev(s, zz, c)).start()

    total = R.gall[part_of(s), :].astype(F32)
    for p in peers:
        arrived(R.fromp.at[p], R.rAll.at[1 + p])
        total = total + R.fromp[p].astype(F32)
    R.fromz[z] = total.astype(BF)
    for i, zz in enumerate(layers):
        remote(R.fromz.at[z], R.fromz.at[z], R.sAll.at[4 + i], R.rAll.at[5 + z], dev(s, zz, c)).start()

    for k in (2, 3, 1, 0):
        first_send(k, 0, z ^ k == 3)
    for k in (2, 3):
        second_send(k, 1)

    for zz in layers:
        arrived(R.fz.at[zz], R.rFo.at[5 + zz])
    fo_grad = (R.fz[0] + R.fz[1]) + (R.fz[2] + R.fz[3])
    fo_high = fo_grad.astype(BF)
    fo_low = (fo_grad - fo_high.astype(F32)).astype(BF)
    gkq = (mm(fo_high, table[...]) + mm(fo_low, table[...])).astype(BF)

    @when(key_owner)
    def _():
        diag = iota((16, 1024), 1) // HEAD == iota((16, 1024), 0)
        own = jnp.where(c == 0, gkq[:, 0:512].astype(F32), gkq[:, 512:1024].astype(F32)).astype(BF)
        row = column_sum(jnp.where(diag, mm(own, bank[...]), 0.0))
        R.qx[0] = jnp.broadcast_to(row, (8, 1024))
        remote(R.qx.at[0], R.qx.at[1], R.sGq.at[15], R.rGq.at[0], sib).start()
        masked = jnp.where(diag, R.qb[...].astype(F32), 0.0).astype(BF)
        gbank[...] = mm_tn(own, masked).astype(BF)
        arrived(R.qx.at[1], R.rGq.at[0])
        row = (R.qx[0] + R.qx[1]).astype(BF)
        R.gqv[...] = jnp.concatenate([row, row], axis=0)
        for i, (p, k) in enumerate(others):
            remote(R.gqv, R.gqv, R.sGq.at[i], R.rGq.at[1], dev(p, k, c)).start()

    for zz in layers:
        arrived(R.fromz.at[zz], R.rAll.at[5 + zz])
    total = R.fromz[0].astype(F32)
    for zz in range(1, 4):
        total = total + R.fromz[zz].astype(F32)
    R.fin[part_of(s), :] = total.astype(BF)
    for i, p in enumerate(peers):
        block = R.fin.at[part_of(s), :]
        remote(block, block, R.sAll.at[7 + i], R.rAll.at[9 + s], dev(p, z, c)).start()

    @when(first_owner)
    def _():
        arrived(R.gqv, R.rGq.at[1])
        R.gaq[c] = mm_nt(R.gqv[...], bank[...])[0:8]
        for i, (p, k) in enumerate(others):
            remote(R.gaq.at[c], R.gaq.at[c], R.sGa.at[i], R.rGa.at[c], dev(p, k, c)).start()
        aq = jnp.where(c == 0, vec[17:18, 0:512], vec[17:18, 512:1024])
        aq = jnp.where(iota((16, 512), 0) == 0, aq, 0.0).astype(BF)
        gbank[...] = mm_tn(aq, R.gqv[...]).astype(BF)


    for p in peers:
        arrived(R.fin.at[part_of(p), :], R.rAll.at[9 + p])
    remote(R.fin.at[half, :], R.fin.at[half, :], R.sAll.at[10], R.rAll.at[13], sib).start()

    for k in (2, 3):
        second_send(k, 0, z ^ k == 3)

    arrived(R.fin.at[other, :], R.rAll.at[13])
    sums[...] = R.fin[240:256, :].astype(F32)
    wait_half(2, 0)
    zero16 = jnp.zeros((112, 256), BF)
    kq_wide = jnp.concatenate([R.kqF[:, own_cols], zero16], axis=0)
    value = mm_tn(jnp.concatenate([fo_high, zero16], axis=0), kq_wide)
    value = value + mm_tn(jnp.concatenate([fo_low, zero16], axis=0), kq_wide)
    for n in range(4):
        tile = R.W[2, 0, n // 2, (n % 2) * 256 : (n % 2 + 1) * 256, :]
        value = value + mm_nt(R.fin[:, n * 256 : (n + 1) * 256], tile)
    R.gt[s] = value.astype(BF)
    for i, p in enumerate(peers):
        remote(R.gt.at[s], R.gt.at[s], R.sGt.at[i], R.rGt.at[s], dev(p, z, c)).start()

    @when(value_owner)
    def _():
        gbank[...] = mm_tn(table[:, half_rows], R.fin[...]).astype(BF)

    last_send(always, 1)
    last_send(top, 0)

    @when(no(first_owner))
    def _():
        arrived(R.gaq.at[c], R.rGa.at[c])

    @when(no(key_owner | first_owner))
    def _():
        arrived(R.gqv, R.rGq.at[1])

    remote(R.gaq.at[c], R.gaq.at[c], R.sGa.at[15], R.rGa.at[c], sib).start()
    arrived(R.gaq.at[1 - c], R.rGa.at[1 - c])
    rows_out[0:8, :] = R.gqv[0:8, :].astype(F32)
    rows_out[8:16, 0:512] = R.gaq[0]
    rows_out[8:16, 512:1024] = R.gaq[1]

    for p in peers:
        arrived(R.gt.at[p], R.rGt.at[p])
    for p in range(4):
        gtab[:, p * 256 : (p + 1) * 256] = R.gt[p]
    total = R.hrow[:, own_cols].astype(F32) + R.st1[:, own_cols].astype(F32) + vec[16:17, own_cols]
    for p in peers:
        arrived(R.outR.at[p], R.rOut.at[p])
        total = total + R.outR[p].astype(F32)
    out[...] = total.astype(BF)

    for i, p in enumerate(peers):
        arrived(R.pixR.at[p], R.rP.at[p])
    R.pixR[s] = R.pixS[s]
    for p in range(4):
        gpix[p // 2, :, (p % 2) * OWN : (p % 2 + 1) * OWN] = R.pixR[p].astype(F32)

    @when(used)
    def _():
        for m in range(4):
            arrived(R.FR.at[m], R.rFin.at[m])

    @when(used & no(is_row))
    def _():
        for m in range(4):
            gbank[:, m * 256 : (m + 1) * 256] = R.FR[m]

    @when(used & is_row)
    def _():
        for m in range(4):
            q, h = m // 2, m % 2
            for n in range(2):
                lo = (2 * h + n) * 256
                gbank[q * 256 : (q + 1) * 256, lo : lo + 256] = R.FR[m, n * 256 : (n + 1) * 256, :]

    stores = [pltpu.make_async_copy(a, b, R.sRes.at[i]) for i, (a, b) in enumerate(zip(results, targets))]
    for store in stores:
        store.start()

    for m in range(4):
        tp, tc, own = message(m)

        @when((used | late) & no(own))
        def _():
            sent(R.msgs.at[m], R.sMsg.at[m])

        @when(value_owner & no((2 * c + m // 2 == s) & (c == m % 2)))
        def _():
            sent(my_piece(m), R.sMa.at[m])

    @when(first_owner)
    def _():
        sent(R.qbuf.at[0], R.sQ.at[0])
        sent(R.qb, R.sQ.at[1])
        for i in range(15):
            sent(R.gaq.at[c], R.sGa.at[i])

    @when(key_owner)
    def _():
        sent(R.qx.at[0], R.sGq.at[15])
        for i in range(15):
            sent(R.kq.at[c], R.sK.at[i])
            sent(R.gqv, R.sGq.at[i])

    @when(z == 2)
    def _():
        for i in range(3):
            sent(R.mS.at[0:128, :], R.sMz.at[i])

    drain_own(z == 2, 0)
    drain_spread(2, 0)
    sent(R.kq.at[c], R.sK.at[15])
    sent(R.gaq.at[c], R.sGa.at[15])
    for f in range(2):
        for p in range(4):
            sent(R.msgs.at[0], R.sFc.at[f, p])
    for p in range(4):
        sent(R.mS.at[0:128, :], R.sMc.at[p])
    sent(R.fc.at[0], R.sFo.at[0])
    sent(R.fromc, R.sAll.at[0])
    sent(R.fromc, R.sAll.at[10])
    for i in range(3):
        sent(R.mS.at[0:128, :], R.sMp.at[i])
        sent(R.mix.at[0:256, 0:256], R.sMix.at[0, i])
        sent(R.mix.at[0:256, 0:256], R.sMix.at[1, i])
        sent(R.msgs.at[0], R.sOut.at[i])
        sent(R.rsR.at[0], R.sR.at[1, i])
        for phase in range(3):
            sent(R.gmS.at[0], R.sG.at[phase, i])
        sent(R.pixS.at[0], R.sP.at[i])
        sent(R.gt.at[0], R.sGt.at[i])
        sent(R.fp.at[0], R.sFo.at[1 + i])
        sent(R.fp.at[0], R.sFo.at[4 + i])
        for phase in range(3):
            sent(R.fromp.at[0], R.sAll.at[1 + 3 * phase + i])
    for b in range(4):
        for zz in range(4):

            @when(at_least(jnp.int32(zz), b) & (z != zz) & (always if b > 0 or zz == 3 else z < 0))
            def _():
                sent(R.msgs.at[0], R.sZ.at[zz, b])

        tc, m, own = owner_of(b)

        @when((top if b == 0 else always) & no(own))
        def _():
            sent(R.msgs.at[0], R.sFin.at[b])
    for store in stores:
        store.wait()


VMEM = pl.BlockSpec(memory_space=pltpu.VMEM)
SMEM = pl.BlockSpec(memory_space=pltpu.SMEM)
ARG_SHAPES = (
    [((2, 192, 256), BF), ((512, 1024), BF), ((512, 1024), BF), ((48, 4, 1024), BF)]
    + [((48, 1024), BF)] * 2
    + [((1024,), BF)]
    + [((n, 1024), BF) for n in (3, 2, 2, 2, 3)]
    + [((4096,), BF), ((1024,), BF), ((1, 2), F32), ((1, 4), jnp.int32)]
)


ANY = pl.BlockSpec(memory_space=pl.ANY)


def block_call(*args):
    shape = jax.ShapeDtypeStruct
    outs = [
        shape((512, 256), BF),
        shape((2, 48, 256), F32),
        shape((512, 1024), BF),
        shape((256, 1024), BF),
        shape((16, 1024), F32),
        shape((16, 1024), F32),
    ]
    return pl.pallas_call(
        block_kernel,
        out_shape=outs,
        in_specs=[ANY] * 14 + [SMEM] * 2,
        out_specs=[ANY] * len(outs),
        scratch_shapes=[pltpu.VMEM(a.shape, a.dtype) for a in (*args[:14], *outs)]
        + [pltpu.VMEM(*v) for v in SCRATCH.values()]
        + [pltpu.SemaphoreType.DMA(v) for v in SEMS.values()],
        compiler_params=pltpu.CompilerParams(
            collective_id=1, has_side_effects=True, vmem_limit_bytes=63 * 2**20
        ),
    )(*args)


def finish_kernel(*refs):
    sources, rest = refs[:6], refs[6:]
    outs, scratch = rest[:14], rest[14:]
    out, gpix, gbank, gtab, sums, rows = scratch[:6]
    sems = scratch[6]
    copies = [pltpu.make_async_copy(a, b, sems.at[i]) for i, (a, b) in enumerate(zip(sources, scratch[:6]))]
    for copy in copies:
        copy.start()
    for copy in copies:
        copy.wait()
    o_out, o_pix, o_bank, o_patch, o_patch_b, o_var, o_query, o_agg, o_lead, o_gain, o_bias, o_attn, o_fc1, o_fc2 = outs
    o_out[...] = out[...]
    o_pix[...] = gpix[...]
    o_bank[...] = gbank[...].astype(F32)
    for p in range(PIX):
        o_patch[:, p, :] = gtab[p * VARS : (p + 1) * VARS, :].astype(F32)
    o_patch_b[...] = gtab[192:240, :].astype(F32)
    o_var[...] = gtab[192:240, :].astype(F32)
    o_query[...] = rows[8, :]
    o_agg[0:1, :] = rows[0:1, :]
    o_agg[1:3, :] = sums[0:2, :]
    o_lead[0:1, :] = sums[2:3, :]
    o_lead[1:2, :] = sums[1:2, :]
    o_gain[...] = sums[3:5, :]
    o_bias[...] = sums[5:7, :]
    o_attn[...] = sums[7:10, :]
    for i in range(4):
        o_fc1[i * 1024 : (i + 1) * 1024] = sums[10 + i, :]
    o_fc2[...] = sums[14, :]


def finish_call(*args):
    shape = jax.ShapeDtypeStruct
    outs = [shape((512, 256), BF), shape((2, 48, 256), F32), shape((512, 1024), F32), shape((48, 4, 1024), F32)]
    outs += [shape((48, 1024), F32)] * 2 + [shape((1024,), F32)]
    outs += [shape((n, 1024), F32) for n in (3, 2, 2, 2, 3)] + [shape((FF,), F32), shape((1024,), F32)]
    return pl.pallas_call(
        finish_kernel,
        out_shape=outs,
        in_specs=[pl.BlockSpec(memory_space=pl.ANY)] * len(args),
        out_specs=[VMEM] * len(outs),
        scratch_shapes=[pltpu.VMEM(a.shape, a.dtype) for a in args] + [pltpu.SemaphoreType.DMA((len(args),))],
        compiler_params=pltpu.CompilerParams(vmem_limit_bytes=63 * 2**20),
    )(*args)


def on_device_fast(
    patches,
    lead_times,
    short_lengths,
    cotangent,
    bank,
    patch_w,
    patch_b,
    var_emb,
    agg_query,
    agg_bias,
    lead_embed,
    norm_gain,
    norm_bias,
    attn_bias,
    fc1_bias,
    fc2_bias,
):
    parts = block_call(
        jnp.transpose(patches, (0, 2, 1)),
        cotangent.reshape(ROWS, D),
        bank[0],
        patch_w,
        patch_b,
        var_emb,
        agg_query,
        agg_bias,
        lead_embed,
        norm_gain,
        norm_bias,
        attn_bias,
        fc1_bias,
        fc2_bias,
        lead_times.T,
        short_lengths,
    )
    o = finish_call(*parts)
    return (
        (o[0].reshape(2, GROUP, 256), jnp.transpose(o[1], (0, 2, 1)), o[2][None])
        + tuple(o[3:])
    )


def specs():
    ins = (
        (P(None, "dp", None), P(None, "dp"), P("dp", None), P(None, "dp", None), P("section", "dp", None))
        + (P(),) * 11
    )
    outs = (P(None, "dp", "section"), P(None, "dp", "section"), P("section", "dp", None)) + (P(),) * 11
    return ins, outs


wide_type = jnp.float32
narrow_type = jnp.bfloat16
highest = lax.Precision.HIGHEST


def shortened(array):

    def short(part):
        return part.astype(jnp.bfloat16) if part.dtype == jnp.float32 else part

    return jax.tree.map(short, array)


def from_behind(array, axis, by):
    length = lax.axis_size(axis)
    pairs = [(i, i + by) for i in range(length) if 0 <= i + by < length]
    return lax.ppermute(array, axis, pairs)


def product(factor_left, factor_right):
    return jnp.dot(factor_left, factor_right, preferred_element_type=wide_type)


def product_left(factor_left, factor_right):
    return lax.dot_general(
        factor_left, factor_right, (((0,), (0,)), ((), ())), preferred_element_type=wide_type
    )


def product_right(factor_left, factor_right):
    return lax.dot_general(
        factor_left, factor_right, (((1,), (1,)), ((), ())), preferred_element_type=wide_type
    )


def norm_layer(stream, gain_row, shift_row):
    centre = stream - jnp.mean(stream, axis=-1, keepdims=True)
    spread = jnp.mean(centre * centre, axis=-1, keepdims=True)
    return centre * lax.rsqrt(spread + 1e-05) * gain_row + shift_row


def gelu_exact(values_in):
    return jax.nn.gelu(values_in, approximate=False)


def position_table(places):
    half_width = D // 2
    frequency = jnp.exp(-math.log(10000.0) * 2.0 * jnp.arange(half_width, dtype=wide_type) / D)
    angles = places.astype(wide_type)[:, None] * frequency[None, :]
    return jnp.concatenate([jnp.sin(angles), jnp.cos(angles)], axis=1)


def layout(lengths_row, row_count):
    segment_ends = jnp.cumsum(lengths_row)
    starts = segment_ends - lengths_row
    places = jnp.arange(row_count, dtype=jnp.int32)
    segment = jnp.sum((places[:, None] >= segment_ends[None, :]).astype(jnp.int32), axis=1)
    member = segment[:, None] == jnp.arange(lengths_row.shape[0], dtype=jnp.int32)[None, :]
    offset = jnp.sum(jnp.where(member, starts[None, :], 0), axis=1)
    offset = jnp.where(segment == lengths_row.shape[0], segment_ends[-1], offset)
    return (segment, places - offset)


def embed_setup(weights, params):
    patch_w, patch_b, var_emb, agg_query, agg_bias = params[:5]
    query_row = product(agg_query[None, :], weights[0])[0] + agg_bias[0].astype(wide_type)
    query_low = query_row.astype(narrow_type)
    key_query = jnp.einsum(
        "dhe,he->dh",
        weights[1].reshape(D, HEADS, HEAD),
        query_low.reshape(HEADS, HEAD),
        preferred_element_type=wide_type,
    )
    key_low = key_query.astype(narrow_type)
    constant = (patch_b.astype(wide_type) + var_emb.astype(wide_type)).astype(narrow_type)
    filters = jnp.einsum("vpd,dh->vph", patch_w, key_low, preferred_element_type=wide_type)
    offsets = product(constant, key_low)
    embed_table = jnp.concatenate([patch_w.reshape(VARS * PIX, D), constant], axis=0)
    return (query_low, key_low, constant, filters, offsets, embed_table)


def embed_rows(pixel_rows, places, lead_time, setup, weights, params):
    query_low, key_low, constant, filters, offsets, embed_table = setup
    agg_bias, lead_embed = (params[4], params[5])
    row_count = pixel_rows.shape[0]
    pixels = pixel_rows.reshape(row_count, VARS, PIX).astype(wide_type)
    scores = (
        jnp.einsum("tvp,vph->tvh", pixels, filters, precision=highest) + offsets[None]
    ) / math.sqrt(HEAD)
    attend = jax.nn.softmax(scores, axis=1)
    attend_low = attend.astype(narrow_type)
    weighted = (attend_low.astype(wide_type)[:, :, :, None] * pixels[:, :, None, :]).astype(
        narrow_type
    )
    operand = jnp.concatenate(
        [
            jnp.transpose(weighted, (0, 2, 1, 3)).reshape(row_count * HEADS, VARS * PIX),
            jnp.transpose(attend_low, (0, 2, 1)).reshape(row_count * HEADS, VARS),
        ],
        axis=1,
    )
    pooled = product(operand, embed_table).astype(narrow_type).reshape(row_count, HEADS, D)
    heads_out = jnp.einsum(
        "thd,dhe->the", pooled, weights[2].reshape(D, HEADS, HEAD), preferred_element_type=wide_type
    ).reshape(row_count, D)
    heads_low = (heads_out + agg_bias[1].astype(wide_type)).astype(narrow_type)
    merged = product(heads_low, weights[3]) + agg_bias[2].astype(wide_type)
    stream = (
        merged
        + position_table(places)
        + lead_time * lead_embed[0].astype(wide_type)
        + lead_embed[1].astype(wide_type)
    )
    return (stream.astype(narrow_type), (pixels, attend, attend_low, operand, pooled, heads_low))


def embed_back(grad_rows, lead_time, setup, saved_state, weights):
    query_low, key_low, constant, filters, offsets, embed_table = setup
    pixels, attend, attend_low, operand, pooled, heads_low = saved_state
    row_count = grad_rows.shape[0]
    grad_wide = grad_rows.astype(wide_type)
    grad_w_out = product_left(heads_low, grad_rows)
    grad_bias_out = jnp.sum(grad_wide, axis=0)
    grad_heads = product_right(grad_rows, weights[3]).astype(narrow_type)
    grad_bias_value = jnp.sum(grad_heads.astype(wide_type), axis=0)
    grad_heads_split = grad_heads.reshape(row_count, HEADS, HEAD)
    grad_w_value = jnp.einsum(
        "thd,the->dhe", pooled, grad_heads_split, preferred_element_type=wide_type
    ).reshape(D, D)
    grad_pooled = jnp.einsum(
        "the,dhe->thd",
        grad_heads_split,
        weights[2].reshape(D, HEADS, HEAD),
        preferred_element_type=wide_type,
    )
    grad_pooled = grad_pooled.astype(narrow_type).reshape(row_count * HEADS, D)
    grad_operand = product_right(grad_pooled, embed_table)
    grad_table = product_left(operand, grad_pooled)
    grad_weighted = grad_operand[:, : VARS * PIX].reshape(row_count, HEADS, VARS, PIX)
    grad_mixing = jnp.transpose(
        grad_operand[:, VARS * PIX :].reshape(row_count, HEADS, VARS), (0, 2, 1)
    )
    grad_attend = (
        jnp.einsum("thvp,tvp->tvh", grad_weighted, pixels, precision=highest) + grad_mixing
    )
    grad_scores = (
        attend
        * (grad_attend - jnp.sum(attend * grad_attend, axis=1, keepdims=True))
        / math.sqrt(HEAD)
    )
    grad_pixels = jnp.einsum(
        "thvp,tvh->tvp", grad_weighted, attend_low.astype(wide_type), precision=highest
    )
    grad_pixels = grad_pixels + jnp.einsum("tvh,vph->tvp", grad_scores, filters, precision=highest)
    grad_filters = jnp.einsum("tvp,tvh->vph", pixels, grad_scores, precision=highest)
    grad_offsets = jnp.sum(grad_scores, axis=0)
    grad_lead = jnp.stack([lead_time * grad_bias_out, grad_bias_out])
    sums = (
        grad_w_out,
        grad_bias_out,
        grad_bias_value,
        grad_w_value,
        grad_table,
        grad_filters,
        grad_offsets,
        grad_lead,
    )
    return (grad_pixels.reshape(row_count, VARS * PIX), sums)


def embed_finish(totals, setup, weights, params):
    (
        grad_w_out,
        grad_bias_out,
        grad_bias_value,
        grad_w_value,
        grad_table,
        grad_filters,
        grad_offsets,
        grad_lead,
    ) = totals
    query_low, key_low, constant, filters, offsets, embed_table = setup
    patch_w, agg_query = (params[0], params[3])
    key_wide = key_low.astype(wide_type)
    grad_patch_w = grad_table[: VARS * PIX].reshape(VARS, PIX, D) + jnp.einsum(
        "vph,dh->vpd", grad_filters, key_wide, precision=highest
    )
    grad_constant = grad_table[VARS * PIX :] + jnp.dot(grad_offsets, key_wide.T, precision=highest)
    grad_key = jnp.einsum("vpd,vph->dh", patch_w.astype(wide_type), grad_filters, precision=highest)
    grad_key = grad_key + jnp.dot(constant.astype(wide_type).T, grad_offsets, precision=highest)
    grad_key_low = grad_key.astype(narrow_type)
    query_heads = query_low.reshape(HEADS, HEAD).astype(wide_type)
    grad_w_key = (grad_key_low.astype(wide_type)[:, :, None] * query_heads[None, :, :]).reshape(
        D, D
    )
    grad_query = jnp.einsum(
        "dhe,dh->he",
        weights[1].reshape(D, HEADS, HEAD),
        grad_key_low,
        preferred_element_type=wide_type,
    )
    grad_query = grad_query.reshape(D).astype(narrow_type)
    grad_query_wide = grad_query.astype(wide_type)
    grad_w_query = agg_query.astype(wide_type)[:, None] * grad_query_wide[None, :]
    grad_agg_query = product(weights[0], grad_query[:, None])[:, 0]
    grad_bank = jnp.concatenate([grad_w_query, grad_w_key, grad_w_value, grad_w_out], axis=0)
    smalls = (
        grad_patch_w,
        grad_constant,
        grad_constant,
        grad_agg_query,
        jnp.stack([grad_query_wide, grad_bias_value, grad_bias_out]),
        grad_lead,
        jnp.zeros((2, D), wide_type),
        jnp.zeros((2, D), wide_type),
        jnp.zeros((3, D), wide_type),
        jnp.zeros((FF,), wide_type),
        jnp.zeros((D,), wide_type),
    )
    return (grad_bank, smalls)


def attention_scores(block_query, block_segment, key_heads, segment):
    raw_scores = jnp.einsum(
        "qhe,khe->hqk", block_query, key_heads, preferred_element_type=wide_type
    ) / math.sqrt(HEAD)
    allowed = (block_segment[:, None] == segment[None, :])[None]
    return jnp.where(allowed, raw_scores, -1e30)


def attention_forward(queries, key_rows, values, segment):
    row_count = queries.shape[0]
    block_rows = min(512, row_count)
    block_total = row_count // block_rows
    key_heads = key_rows.reshape(row_count, HEADS, HEAD)
    value_heads = values.reshape(row_count, HEADS, HEAD)

    def one_block(block_items):
        block_query, block_segment = block_items
        scores = attention_scores(block_query, block_segment, key_heads, segment)
        row_peak = jnp.max(scores, axis=-1, keepdims=True)
        exp_scores = jnp.exp(scores - row_peak)
        exp_total = jnp.sum(exp_scores, axis=-1, keepdims=True)
        probabilities = (exp_scores / exp_total).astype(narrow_type)
        mixed_heads = jnp.einsum(
            "hqk,khe->qhe", probabilities, value_heads, preferred_element_type=wide_type
        )
        return (mixed_heads.astype(narrow_type), (row_peak + jnp.log(exp_total))[:, :, 0])

    mixed_heads, log_totals = lax.map(
        one_block,
        (
            queries.reshape(block_total, block_rows, HEADS, HEAD),
            segment.reshape(block_total, block_rows),
        ),
    )
    return (mixed_heads.reshape(row_count, D), log_totals)


def attention_backward(queries, key_rows, values, segment, log_totals, grad_mixed):
    row_count = queries.shape[0]
    block_rows = min(512, row_count)
    block_total = row_count // block_rows
    key_heads = key_rows.reshape(row_count, HEADS, HEAD)
    value_heads = values.reshape(row_count, HEADS, HEAD)

    def one_block(carry_sums, block_items):
        grad_key_sum, grad_value_sum = carry_sums
        block_query, block_segment, block_log, block_grad = block_items
        scores = attention_scores(block_query, block_segment, key_heads, segment)
        probabilities = jnp.exp(scores - block_log[:, :, None])
        probs_low = probabilities.astype(narrow_type)
        grad_value_sum = grad_value_sum + jnp.einsum(
            "hqk,qhe->khe", probs_low, block_grad, preferred_element_type=wide_type
        )
        grad_probs = jnp.einsum(
            "qhe,khe->hqk", block_grad, value_heads, preferred_element_type=wide_type
        )
        grad_scores = probabilities * (
            grad_probs - jnp.sum(probabilities * grad_probs, axis=-1, keepdims=True)
        )
        grad_low = grad_scores.astype(narrow_type)
        grad_query = jnp.einsum(
            "hqk,khe->qhe", grad_low, key_heads, preferred_element_type=wide_type
        ) / math.sqrt(HEAD)
        grad_key_sum = grad_key_sum + jnp.einsum(
            "hqk,qhe->khe", grad_low, block_query, preferred_element_type=wide_type
        ) / math.sqrt(HEAD)
        return ((grad_key_sum, grad_value_sum), grad_query)

    zero_heads = jnp.zeros((row_count, HEADS, HEAD), wide_type)
    block_items = (
        queries.reshape(block_total, block_rows, HEADS, HEAD),
        segment.reshape(block_total, block_rows),
        log_totals,
        grad_mixed.reshape(block_total, block_rows, HEADS, HEAD),
    )
    (grad_key_sum, grad_value_sum), grad_queries = lax.scan(
        one_block, (zero_heads, zero_heads), block_items
    )
    return (
        grad_queries.reshape(row_count, D),
        grad_key_sum.reshape(row_count, D),
        grad_value_sum.reshape(row_count, D),
    )


def project_heads(normed_low, weights, attn_bias):
    queries = (product(normed_low, weights[0]) + attn_bias[0].astype(wide_type)).astype(narrow_type)
    key_rows = product(normed_low, weights[1]).astype(narrow_type)
    values = (product(normed_low, weights[2]) + attn_bias[1].astype(wide_type)).astype(narrow_type)
    return (queries, key_rows, values)


def feed_half(normed_low, weights, bias_in):
    inner_first = product(normed_low, weights[0]) + bias_in[:D].astype(wide_type)
    inner_second = product(normed_low, weights[1]) + bias_in[D:].astype(wide_type)
    active_first = gelu_exact(inner_first).astype(narrow_type)
    active_second = gelu_exact(inner_second).astype(narrow_type)
    partial_sum = product(active_first, weights[2]) + product(active_second, weights[3])
    return ((inner_first, inner_second), (active_first, active_second), partial_sum)


def feed_half_back(normed_low, weights, inners, actives, grad_rows):
    grad_inners = []
    for number in range(2):
        grad_active = product_right(grad_rows, weights[2 + number])
        value_out, gelu_pull = jax.vjp(gelu_exact, inners[number])
        grad_inners.append(gelu_pull(grad_active)[0].astype(narrow_type))
    grad_normed = product_right(grad_inners[0], weights[0]) + product_right(
        grad_inners[1], weights[1]
    )
    grad_bank = jnp.concatenate(
        [
            product_left(normed_low, grad_inners[0]),
            product_left(normed_low, grad_inners[1]),
            product_left(actives[0], grad_rows),
            product_left(actives[1], grad_rows),
        ],
        axis=0,
    )
    grad_bias_in = jnp.concatenate(
        [
            jnp.sum(grad_inners[0].astype(wide_type), axis=0),
            jnp.sum(grad_inners[1].astype(wide_type), axis=0),
        ]
    )
    return (grad_normed, grad_bank, grad_bias_in)


def on_device(
    patches,
    lead_times,
    short_lengths,
    cotangent,
    bank,
    patch_w,
    patch_b,
    var_emb,
    agg_query,
    agg_bias,
    lead_embed,
    norm_gain,
    norm_bias,
    attn_bias,
    fc1_bias,
    fc2_bias,
):
    params = (
        patch_w,
        patch_b,
        var_emb,
        agg_query,
        agg_bias,
        lead_embed,
        norm_gain,
        norm_bias,
        attn_bias,
        fc1_bias,
        fc2_bias,
    )
    micro_total = patches.shape[0]
    row_count = patches.shape[1]
    section_total = lax.axis_size("section")
    section_index = lax.axis_index("section")
    gathered = lax.all_gather(bank, "dp", axis=1, tiled=True)[0]
    weights = tuple((gathered[number * D : (number + 1) * D] for number in range(4)))
    short_segment, short_places = layout(short_lengths[0], row_count)
    segments = jnp.stack([short_segment, jnp.zeros((row_count,), jnp.int32)])
    places_all = jnp.stack([short_places, jnp.arange(row_count, dtype=jnp.int32)])
    valid_rows = jnp.stack([short_segment < short_lengths.shape[1], jnp.ones((row_count,), bool)])
    grad_out_all = jnp.where(valid_rows[:, :, None], cotangent, jnp.zeros_like(cotangent))
    block_rows = min(512, row_count)
    block_total = row_count // block_rows
    zeros_stream = jnp.zeros((row_count, D), narrow_type)
    zeros_final = jnp.zeros((row_count, D), wide_type)
    zeros_pixels = jnp.zeros((row_count, VARS * PIX), wide_type)
    stash_zero = (
        zeros_stream,
        zeros_stream,
        zeros_stream,
        zeros_stream,
        jnp.zeros((block_total, HEADS, block_rows), wide_type),
    )
    small_zero = tuple((jnp.zeros(array_item.shape, wide_type) for array_item in params))

    def forward_embed(operands):
        first_in, second_in, pixel_rows, places, lead_time, segment = operands
        setup = embed_setup(weights, params)

        def one_block(block_items):
            return embed_rows(block_items[0], block_items[1], lead_time, setup, weights, params)[0]

        streams = lax.map(
            one_block,
            (
                pixel_rows.reshape(block_total, block_rows, VARS * PIX),
                places.reshape(block_total, block_rows),
            ),
        )
        return (streams.reshape(row_count, D), zeros_stream, zeros_final, stash_zero)

    def forward_attend(operands):
        first_in, second_in, pixel_rows, places, lead_time, segment = operands
        stream = first_in.astype(wide_type)
        normed_low = norm_layer(
            stream, norm_gain[0].astype(wide_type), norm_bias[0].astype(wide_type)
        ).astype(narrow_type)
        queries, key_rows, values = project_heads(normed_low, weights, attn_bias)
        mixed_heads, log_totals = attention_forward(queries, key_rows, values, segment)
        new_stream = stream + product(mixed_heads, weights[3]) + attn_bias[2].astype(wide_type)
        return (new_stream.astype(narrow_type), zeros_stream, zeros_final, stash_zero)

    def forward_first(operands):
        first_in, second_in, pixel_rows, places, lead_time, segment = operands
        stream = first_in.astype(wide_type)
        normed_low = norm_layer(
            stream, norm_gain[1].astype(wide_type), norm_bias[1].astype(wide_type)
        ).astype(narrow_type)
        inners, actives, partial_sum = feed_half(normed_low, weights, fc1_bias[: 2 * D])
        return (normed_low, (stream + partial_sum).astype(narrow_type), zeros_final, stash_zero)

    def forward_second(operands):
        first_in, second_in, pixel_rows, places, lead_time, segment = operands
        inners, actives, partial_sum = feed_half(first_in, weights, fc1_bias[2 * D :])
        final_rows = second_in.astype(wide_type) + partial_sum + fc2_bias.astype(wide_type)
        return (zeros_stream, zeros_stream, final_rows, stash_zero)

    def forward_none(operands):
        return (zeros_stream, zeros_stream, zeros_final, stash_zero)

    def backward_embed(operands):
        (
            first_kept,
            second_kept,
            grad_in,
            pixel_rows,
            places,
            lead_time,
            segment,
            grad_rows,
            stash_items,
        ) = operands
        setup = embed_setup(weights, params)

        def one_block(totals, block_items):
            block_pixels, block_places, block_grad = block_items
            block_stream, saved_state = embed_rows(
                block_pixels, block_places, lead_time, setup, weights, params
            )
            block_dx, sums = embed_back(block_grad, lead_time, setup, saved_state, weights)
            return (
                tuple((total_item + sum_item for total_item, sum_item in zip(totals, sums))),
                block_dx,
            )

        zero_totals = (
            jnp.zeros((D, D), wide_type),
            jnp.zeros((D,), wide_type),
            jnp.zeros((D,), wide_type),
            jnp.zeros((D, D), wide_type),
            jnp.zeros((VARS * PIX + VARS, D), wide_type),
            jnp.zeros((VARS, PIX, HEADS), wide_type),
            jnp.zeros((VARS, HEADS), wide_type),
            jnp.zeros((2, D), wide_type),
        )
        block_items = (
            pixel_rows.reshape(block_total, block_rows, VARS * PIX),
            places.reshape(block_total, block_rows),
            grad_in.reshape(block_total, block_rows, D),
        )
        totals, grad_pixels = lax.scan(one_block, zero_totals, block_items)
        grad_bank, smalls = embed_finish(totals, setup, weights, params)
        return (zeros_stream, grad_bank, smalls, grad_pixels.reshape(row_count, VARS * PIX))

    def backward_attend(operands):
        (
            first_kept,
            second_kept,
            grad_in,
            pixel_rows,
            places,
            lead_time,
            segment,
            grad_rows,
            stash_items,
        ) = operands
        stream = first_kept.astype(wide_type)
        normed, norm_pull = jax.vjp(
            norm_layer, stream, norm_gain[0].astype(wide_type), norm_bias[0].astype(wide_type)
        )
        normed_low = normed.astype(narrow_type)
        queries, key_rows, values = project_heads(normed_low, weights, attn_bias)
        mixed_heads, log_totals = attention_forward(queries, key_rows, values, segment)
        grad_in_wide = grad_in.astype(wide_type)
        grad_w_out = product_left(mixed_heads, grad_in)
        grad_mixed = product_right(grad_in, weights[3]).astype(narrow_type)
        grad_queries, grad_keys, grad_values = attention_backward(
            queries, key_rows, values, segment, log_totals, grad_mixed
        )
        grad_queries = grad_queries.astype(narrow_type)
        grad_keys = grad_keys.astype(narrow_type)
        grad_values = grad_values.astype(narrow_type)
        grad_normed = (
            product_right(grad_queries, weights[0])
            + product_right(grad_keys, weights[1])
            + product_right(grad_values, weights[2])
        )
        grad_stream, grad_gain, grad_shift = norm_pull(grad_normed)
        grad_send = (grad_in_wide + grad_stream).astype(narrow_type)
        grad_bank = jnp.concatenate(
            [
                product_left(normed_low, grad_queries),
                product_left(normed_low, grad_keys),
                product_left(normed_low, grad_values),
                grad_w_out,
            ],
            axis=0,
        )
        bias_rows = jnp.stack(
            [
                jnp.sum(grad_queries.astype(wide_type), axis=0),
                jnp.sum(grad_values.astype(wide_type), axis=0),
                jnp.sum(grad_in_wide, axis=0),
            ]
        )
        smalls = (
            small_zero[:6]
            + (
                jnp.zeros((2, D), wide_type).at[0].set(grad_gain),
                jnp.zeros((2, D), wide_type).at[0].set(grad_shift),
                bias_rows,
            )
            + small_zero[9:]
        )
        return (grad_send, grad_bank, smalls, zeros_pixels)

    def backward_first(operands):
        (
            first_kept,
            second_kept,
            grad_in,
            pixel_rows,
            places,
            lead_time,
            segment,
            grad_rows,
            stash_items,
        ) = operands
        stream = first_kept.astype(wide_type)
        normed, norm_pull = jax.vjp(
            norm_layer, stream, norm_gain[1].astype(wide_type), norm_bias[1].astype(wide_type)
        )
        normed_low = normed.astype(narrow_type)
        inners, actives, partial_sum = feed_half(normed_low, weights, fc1_bias[: 2 * D])
        grad_normed, grad_bank, grad_bias_in = feed_half_back(
            normed_low, weights, inners, actives, grad_rows
        )
        grad_stream, grad_gain, grad_shift = norm_pull(grad_normed + grad_in.astype(wide_type))
        grad_send = (grad_rows.astype(wide_type) + grad_stream).astype(narrow_type)
        smalls = small_zero[:6] + (
            jnp.zeros((2, D), wide_type).at[1].set(grad_gain),
            jnp.zeros((2, D), wide_type).at[1].set(grad_shift),
            small_zero[8],
            jnp.zeros((FF,), wide_type).at[: 2 * D].set(grad_bias_in),
            small_zero[10],
        )
        return (grad_send, grad_bank, smalls, zeros_pixels)

    def backward_second(operands):
        (
            first_kept,
            second_kept,
            grad_in,
            pixel_rows,
            places,
            lead_time,
            segment,
            grad_rows,
            stash_items,
        ) = operands
        inners, actives, partial_sum = feed_half(first_kept, weights, fc1_bias[2 * D :])
        grad_normed, grad_bank, grad_bias_in = feed_half_back(
            first_kept, weights, inners, actives, grad_rows
        )
        smalls = small_zero[:9] + (
            jnp.zeros((FF,), wide_type).at[2 * D :].set(grad_bias_in),
            jnp.sum(grad_rows.astype(wide_type), axis=0),
        )
        return (grad_normed.astype(narrow_type), grad_bank, smalls, zeros_pixels)

    def backward_none(operands):
        return (zeros_stream, jnp.zeros((4 * D, D), wide_type), small_zero, zeros_pixels)

    forward_list = [forward_embed, forward_attend, forward_first, forward_second, forward_none]
    backward_list = [
        backward_embed,
        backward_attend,
        backward_first,
        backward_second,
        backward_none,
    ]
    tick_total = micro_total + section_total - 1
    first_message, second_message = (zeros_stream, zeros_stream)
    kept_first = jnp.zeros((micro_total, row_count, D), narrow_type)
    kept_second = jnp.zeros((micro_total, row_count, D), narrow_type)
    stash_all = tuple(
        (
            jnp.zeros((micro_total,) + array_item.shape, array_item.dtype)
            for array_item in stash_zero
        )
    )
    final_all = jnp.zeros((micro_total, row_count, D), wide_type)
    for tick_number in range(tick_total):
        micro_index = tick_number - section_index
        running = jnp.logical_and(micro_index >= 0, micro_index < micro_total)
        slot_index = jnp.clip(micro_index, 0, micro_total - 1)
        kept_first = kept_first.at[slot_index].set(
            jnp.where(running, first_message, kept_first[slot_index])
        )
        kept_second = kept_second.at[slot_index].set(
            jnp.where(running, second_message, kept_second[slot_index])
        )
        branch = jnp.where(running, section_index, section_total)
        operands = (
            first_message,
            second_message,
            patches[slot_index],
            places_all[slot_index],
            lead_times[slot_index, 0],
            segments[slot_index],
        )
        first_out, second_out, final_rows, stash_items = lax.switch(branch, forward_list, operands)
        final_all = final_all.at[slot_index].add(final_rows)
        stash_all = tuple(
            (
                buffer.at[slot_index].set(jnp.where(running, array_item, buffer[slot_index]))
                for buffer, array_item in zip(stash_all, stash_items)
            )
        )
        if tick_number < tick_total - 1:
            first_message, second_message = (
                from_behind(shortened(first_out), "section", 1).astype(first_out.dtype),
                from_behind(shortened(second_out), "section", 1).astype(second_out.dtype),
            )
    grad_message = zeros_stream
    bank_total = jnp.zeros((4 * D, D), wide_type)
    small_total = small_zero
    pixel_total = jnp.zeros((micro_total, row_count, VARS * PIX), wide_type)
    for tick_number in range(tick_total):
        micro_index = tick_number - (section_total - 1 - section_index)
        running = jnp.logical_and(micro_index >= 0, micro_index < micro_total)
        slot_index = jnp.clip(micro_index, 0, micro_total - 1)
        branch = jnp.where(running, section_index, section_total)
        operands = (
            kept_first[slot_index],
            kept_second[slot_index],
            grad_message,
            patches[slot_index],
            places_all[slot_index],
            lead_times[slot_index, 0],
            segments[slot_index],
            grad_out_all[slot_index],
            tuple((buffer[slot_index] for buffer in stash_all)),
        )
        grad_send, grad_bank, smalls, grad_pixels = lax.switch(branch, backward_list, operands)
        bank_total = bank_total + grad_bank
        small_total = tuple(
            (total_item + sum_item for total_item, sum_item in zip(small_total, smalls))
        )
        pixel_total = pixel_total.at[slot_index].add(grad_pixels)
        if tick_number < tick_total - 1:
            grad_message = jax.tree.map(
                lambda part, own: part.astype(own.dtype),
                from_behind(shortened(grad_send), "section", -1),
                grad_send,
            )
    bank_share = lax.psum_scatter(
        bank_total.astype(jnp.bfloat16), "dp", scatter_dimension=0, tiled=True
    ).astype(jnp.float32)[None]
    small_sums = lax.psum(small_total, ("section", "dp"))
    output_share, pixel_share = (
        lax.psum_scatter(
            final_all.astype(jnp.bfloat16), "section", scatter_dimension=2, tiled=True
        ).astype(jnp.float32),
        lax.psum_scatter(
            pixel_total.astype(jnp.bfloat16), "section", scatter_dimension=2, tiled=True
        ).astype(jnp.float32),
    )
    output_low = output_share.astype(narrow_type)
    return (output_low, pixel_share, bank_share) + tuple(small_sums)


def solution(mesh):
    ins, outs = specs()
    small_slice = mesh.shape["section"] == 4 and mesh.shape["dp"] == 8
    body = on_device_fast if small_slice else on_device
    return jax.shard_map(body, mesh=mesh, in_specs=ins, out_specs=outs, check_vma=False)
```

```python
import functools
import math

import jax
import jax.numpy as jnp
from jax import lax
from jax.experimental import pallas as pl
from jax.experimental.pallas import tpu as pltpu
from jax.sharding import PartitionSpec as P

D = 1024
HEADS = 16
HEAD = 64
FF = 4096
VARS = 48
PIX = 4
F32 = jnp.float32
BF = jnp.bfloat16
MESH = pl.DeviceIdType.MESH
ROWS = 512
GROUP = 256
OWN = 128


def mm(a, b):
    return jnp.dot(a, b, preferred_element_type=F32)


def mm_nt(a, b):
    return lax.dot_general(a, b, (((1,), (1,)), ((), ())), preferred_element_type=F32)


def mm_tn(a, b):
    return lax.dot_general(a, b, (((0,), (0,)), ((), ())), preferred_element_type=F32)


def loop(count, body):
    def step(i, carry):
        body(i)
        return carry

    lax.fori_loop(0, count, step, 0)


def at(start, size, unit):
    return pl.ds(pl.multiple_of(start, unit), size)


def iota(shape, axis):
    return lax.broadcasted_iota(jnp.int32, shape, axis)


def normed_rows(x, gain, shift):
    centre = x - jnp.mean(x, axis=1, keepdims=True)
    rs = lax.rsqrt(jnp.mean(centre * centre, axis=1, keepdims=True) + 1e-5)
    return centre * rs * gain + shift


def norm_back(x, g, gain):
    centre = x - jnp.mean(x, axis=1, keepdims=True)
    rs = lax.rsqrt(jnp.mean(centre * centre, axis=1, keepdims=True) + 1e-5)
    xhat = centre * rs
    q = g * gain
    gx = rs * (q - jnp.mean(q, axis=1, keepdims=True) - xhat * jnp.mean(q * xhat, axis=1, keepdims=True))
    return gx, jnp.sum(g * xhat, axis=0, keepdims=True), jnp.sum(g, axis=0, keepdims=True)


def column_sum(x):
    return jnp.sum(x, axis=0, keepdims=True)


class Place:
    def __init__(self):
        self.s = lax.axis_index("section")
        j = lax.axis_index("dp")
        self.z = lax.div(j, 2)
        self.c = lax.rem(j, 2)
        self.outer = (self.z == 0) | (self.z == 3)
        self.far = jnp.where(self.outer, self.z ^ 2, self.z ^ 3)

    def dev(self, s, z, c):
        return (s, z * 2 + c)


def remote(src, dst, ss, rs, dev):
    return pltpu.make_async_remote_copy(
        src_ref=src, dst_ref=dst, send_sem=ss, recv_sem=rs, device_id=dev, device_id_type=MESH
    )


def arrived(dst, sem):
    pltpu.make_async_copy(dst, dst, sem).wait()


def sent(src, sem):
    pltpu.make_async_copy(src, src, sem).wait()


def barrier(devs):
    sem = pltpu.get_barrier_semaphore()
    for dev in devs:
        pl.semaphore_signal(sem, 1, device_id=dev, device_id_type=MESH)
    pl.semaphore_wait(sem, len(devs))


SCRATCH = dict(
    vec=((24, 1024), F32),
    table=((256, 1024), BF),
    tabT=((1024, 256), BF),
    msgs=((4, 512, 256), BF),
    W=((4, 4, 2, 512, 256), BF),
    WF=((2, 4, 2, 512, 256), BF),
    kqF=((16, 1024), BF),
    gt=((4, 256, 256), BF),
    qbuf=((2, 8, 1024), F32),
    qb=((16, 1024), BF),
    kq=((2, 16, 512), BF),
    mT=((1024, 256), BF),
    mS=((512, 256), BF),
    patT=((192, 512), BF),
    fill=((1536, 192), BF),
    fo=((16, 256), F32),
    att=((768, 512), F32),
    op=((256, 512), BF),
    op1=((4, 256, 128), BF),
    hT=((1024, 512), BF),
    hrow=((512, 1024), BF),
    acc=((512, 1024), F32),
    st0=((512, 1024), BF),
    nrm=((512, 1024), BF),
    nrm2=((512, 1024), BF),
    tr=((1024, 512), BF),
    q=((512, 256), BF),
    k=((512, 256), BF),
    v=((512, 256), BF),
    attp=((8, 256, 256), F32),
    mix=((512, 1024), BF),
    st1=((512, 1024), BF),
    act=((4, 512, 256), BF),
    gact=((4, 512, 256), F32),
    gin=((4, 512, 256), BF),
    gout=((512, 1024), BF),
    rsS=((512, 1024), BF),
    rsR=((4, 128, 1024), BF),
    gs=((2, 128, 1024), BF),
    gmS=((4, 128, 256), BF),
    gm=((512, 256), BF),
    ga=((512, 256), BF),
    gb=((512, 256), BF),
    gq=((3, 512, 256), BF),
    CR=((13, 512, 256), BF),
    RC=((2, 4, 512, 256), BF),
    RA=((4, 512, 256), BF),
    RB=((4, 512, 256), BF),
    FR=((4, 512, 256), BF),
    outR=((4, 512, 256), BF),
    gh=((128, 1024), BF),
    ghT=((1024, 128), BF),
    gpT=((192, 128), F32),
    gsc=((768, 128), F32),
    small=((16, 1024), F32),
    pixS=((4, 48, 128), BF),
    pixR=((4, 48, 128), BF),
    gall=((256, 1024), BF),
    fin=((256, 1024), BF),
    fromc=((128, 1024), BF),
    fromp=((4, 32, 1024), BF),
    fromz=((4, 32, 1024), BF),
    fc=((2, 16, 256), F32),
    fp=((4, 16, 256), F32),
    fz=((4, 16, 256), F32),
    gqv=((16, 1024), BF),
    qx=((2, 8, 1024), F32),
    gaq=((2, 8, 512), F32),
)

SEMS = dict(
    sIn=(14,),
    sRes=(6,),
    rW=(4, 4, 2),
    rF=(4, 2),
    rH=(4, 2, 2),
    rA=(2,),
    sA=(4, 2),
    sAo=(2, 2),
    sAf=(2,),
    sAx=(3, 2),
    sAc=(4, 2),
    sMsg=(4,),
    sOwn=(4, 2),
    sFwd=(4, 4, 2),
    sFx=(3,),
    sFc=(4,),
    sGt=(3,),
    rGt=(4,),
    rQ=(2,),
    sQ=(2,),
    rK=(2,),
    sK=(16,),
    rMx=(1,),
    sMx=(1,),
    rM=(4, 2),
    sMa=(4,),
    sMz=(3,),
    sMp=(3,),
    sMc=(4,),
    sMix=(2, 3),
    rMix=(2, 4),
    sOut=(4,),
    rOut=(4,),
    sR=(2, 4),
    rR=(2, 4),
    sG=(3, 4),
    rG=(3, 4),
    sC=(4, 4),
    rC=(4, 4),
    sZ=(4, 4),
    rRC=(2, 4),
    rRA=(4,),
    rRB=(4,),
    sFin=(4,),
    rFin=(4,),
    sP=(4,),
    rP=(4,),
    sAll=(14,),
    rAll=(14,),
    sFo=(8,),
    rFo=(12,),
    sGq=(18,),
    rGq=(2,),
    sGa=(16,),
    rGa=(2,),
)
NAMES = list(SCRATCH) + list(SEMS)


class Refs:
    pass


def block_kernel(*refs):
    sources, lead, lens = refs[0:14], refs[14], refs[15]
    targets, rest = refs[16:22], refs[22:]
    held, results, scratch = rest[0:14], rest[14:20], rest[20:]
    pat, cot, bank, patch, patch_b, var_emb, agg_query, agg_bias, lead_embed = held[0:9]
    norm_gain, norm_bias, attn_bias, fc1, fc2 = held[9:14]
    out, gpix, gbank, gtab, sums, rows_out = results
    R = Refs()
    for name, ref in zip(NAMES, scratch):
        setattr(R, name, ref)
    loads = [pltpu.make_async_copy(a, b, R.sIn.at[i]) for i, (a, b) in enumerate(zip(sources, held))]
    for i in (2, *range(3, 14), 0, 1):
        loads[i].start()
    here = Place()
    s, z, c = here.s, here.z, here.c
    dev = here.dev
    outer = here.outer
    inner = jnp.logical_not(outer)
    sib = dev(s, z, 1 - c)
    is_row = (z >= 2) & ((s >= 2) | ((s == 0) & (z == 2)))
    peers = [s ^ 1, s ^ 2, s ^ 3]
    layers = [z ^ 1, z ^ 2, z ^ 3]
    others = [(s ^ i, z ^ k) for k in range(4) for i in range(4) if (i, k) != (0, 0)]
    vec, table = R.vec, R.table
    when = pl.when
    no = jnp.logical_not

    barrier([dev(p, k, c) for p, k in others] + [dev(p, z, 1 - c) for p in peers] + [sib])

    loads[2].wait()
    first_owner = (s == 0) & (z == 0)
    key_owner = (s == 0) & (z == 1)
    value_owner = (s == 0) & (z == 2)

    late = value_owner
    used = no((s == 0) & (z < 3))

    @when(no(is_row) & used)
    def _():
        for p in range(4):
            R.msgs[p] = bank[:, p * 256 : (p + 1) * 256]

    @when(is_row)
    def _():
        for m in range(4):
            q, h = m // 2, m % 2
            for n in range(2):
                lo = (2 * h + n) * 256
                R.msgs[m, n * 256 : (n + 1) * 256, :] = bank[q * 256 : (q + 1) * 256, lo : lo + 256]

    def message(m):
        tp = jnp.where(is_row, 2 * c + m // 2, m)
        tc = jnp.where(is_row, m % 2, c)
        return tp, tc, (tp == s) & (tc == c)

    def scatter(cond):
        for m in range(4):
            tp, tc, own = message(m)

            @when(cond & own)
            def _():
                pltpu.make_async_copy(R.msgs.at[m], R.W.at[z, s, c], R.rW.at[z, s, c]).start()

            @when(cond & no(own))
            def _():
                remote(R.msgs.at[m], R.W.at[z, s, tc], R.sMsg.at[m], R.rW.at[z, s, tc], dev(tp, z, tc)).start()

    out_owner = (s == 0) & (z == 3)

    def half_of(p, h):
        return R.WF.at[0, p, c, h * 256 : (h + 1) * 256]

    def out_half(h):
        return R.W.at[3, 0, c, h * 256 : (h + 1) * 256]

    @when(out_owner)
    def _():
        for h in range(2):
            for m in range(4):
                block = R.msgs.at[m, h * 256 : (h + 1) * 256]
                if m == 0:
                    pltpu.make_async_copy(block, out_half(h), R.rA.at[h]).start()
                else:
                    remote(block, out_half(h), R.sA.at[m, h], R.rA.at[h], dev(m, z, c)).start()

    scatter(used & no(out_owner))

    for i in range(3, 14):
        loads[i].wait()
    vec[0:3, :] = agg_bias[...].astype(F32)
    vec[3:5, :] = lead_embed[...].astype(F32)
    vec[5:7, :] = norm_gain[...].astype(F32)
    vec[7:9, :] = norm_bias[...].astype(F32)
    vec[9:12, :] = attn_bias[...].astype(F32)
    for i in range(4):
        vec[12 + i : 13 + i, :] = fc1[i * 1024 : (i + 1) * 1024][None].astype(F32)
    vec[16:17, :] = fc2[...][None].astype(F32)
    vec[17:18, :] = agg_query[...][None].astype(F32)

    @when(first_owner)
    def _():
        part = jnp.broadcast_to(vec[17:18, at(c * 512, 512, 512)].astype(BF), (16, 512))
        R.qbuf[0] = mm(part, bank[...])[0:8]
        remote(R.qbuf.at[0], R.qbuf.at[1], R.sQ.at[0], R.rQ.at[0], sib).start()

    perm = jnp.where(
        (iota((192, 192), 0) // 48 == iota((192, 192), 1) % 4) & (iota((192, 192), 0) % 48 == iota((192, 192), 1) // 4),
        1.0,
        0.0,
    ).astype(BF)
    for p in range(PIX):
        table[p * 48 : (p + 1) * 48, :] = patch[:, p, :]
    table[192:240, :] = (patch_b[...].astype(F32) + var_emb[...].astype(F32)).astype(BF)
    table[240:256, :] = jnp.zeros((16, 1024), BF)

    other_rows = at((1 - c) * 512, 512, 512)
    half_rows = at(c * 512, 512, 512)

    @when(value_owner)
    def _():
        for i in range(4):
            R.tabT[i * 256 : (i + 1) * 256, :] = table[:, i * 256 : (i + 1) * 256].T
        for h in range(2):
            R.gact[h] = mm_tn(bank[:, h * 512 : (h + 1) * 512], R.tabT[half_rows, :])
        remote(R.gact.at[1 - c], R.gact.at[2], R.sMx.at[0], R.rMx.at[0], sib).start()

    @when(first_owner)
    def _():
        arrived(R.qbuf.at[1], R.rQ.at[0])
        total = R.qbuf[0] + R.qbuf[1] + vec[0:1, :]
        total = total.astype(BF)
        R.qb[...] = jnp.concatenate([total, total], axis=0)
        remote(R.qb, R.qb, R.sQ.at[1], R.rQ.at[1], dev(0, 1, c)).start()

    def piece_of(p, h):
        return R.mT.at[at(p * 256 + h * 128, 128, 128), :]

    def my_piece(m):
        return R.mS.at[(m // 2) * 256 + (m % 2) * 128 : (m // 2) * 256 + (m % 2) * 128 + 128, :]

    @when(value_owner)
    def _():
        arrived(R.gact.at[2], R.rMx.at[0])
        sent(R.gact.at[2], R.sMx.at[0])
        bias = jnp.broadcast_to(vec[1:2, half_rows], (8, 512)).T[:, 0:1]
        total = R.gact[c] + R.gact[2]
        R.mS[...] = jnp.where(iota((1, 256), 1) == 240, bias, total).astype(BF)
        for m in range(4):
            q, h = m // 2, m % 2
            tp = 2 * c + q
            own = (tp == s) & (c == h)

            @when(own)
            def _():
                pltpu.make_async_copy(my_piece(m), piece_of(tp, h), R.rM.at[tp, h]).start()

            @when(no(own))
            def _():
                remote(my_piece(m), piece_of(tp, h), R.sMa.at[m], R.rM.at[tp, h], dev(tp, z, h)).start()

    @when(key_owner)
    def _():
        arrived(R.qb, R.rQ.at[1])
        masked = jnp.where(iota((16, 1024), 1) // HEAD == iota((16, 1024), 0), R.qb[...].astype(F32), 0.0).astype(BF)
        R.kq[c] = mm_nt(masked, bank[...]).astype(BF)
        for i, (p, k) in enumerate(others):
            remote(R.kq.at[c], R.kq.at[c], R.sK.at[i], R.rK.at[c], dev(p, k, c)).start()

    def at_least(zz, b):
        return zz == 3 if b == 0 else zz >= 0

    def full_of(zz, b):
        return (zz == 3) if b == 1 else None

    def spread(zz, b):
        block = R.W.at[zz, b, c]
        whole = full_of(zz, b)

        def to_sibling():
            remote(block, block, R.sFwd.at[zz, b, 0], R.rW.at[zz, b, c], sib).start()

        def to_layer():
            pltpu.make_async_copy(block, R.WF.at[1, s, c], R.rF.at[s, c]).start()
            for i, p in enumerate(peers):
                remote(block, R.WF.at[1, s, c], R.sFx.at[i], R.rF.at[s, c], dev(p, z, c)).start()

        if whole is None:
            to_sibling()
        elif isinstance(whole, bool):
            (to_layer if whole else to_sibling)()
        else:
            when(no(whole))(to_sibling)
            when(whole)(to_layer)

    def out_layer(h):
        pltpu.make_async_copy(out_half(h), half_of(s, h), R.rH.at[s, c, h]).start()
        for i, p in enumerate(peers):
            remote(out_half(h), half_of(s, h), R.sAx.at[i, h], R.rH.at[s, c, h], dev(p, z, c)).start()

    def out_along(cond):
        @when(cond)
        def _():
            for h in range(2):
                arrived(out_half(h), R.rA.at[h])
                remote(out_half(h), out_half(h), R.sAo.at[1, h], R.rA.at[h], dev(s, z ^ 2, c)).start()
            for h in range(2):
                remote(out_half(h), out_half(h), R.sAo.at[0, h], R.rA.at[h], dev(s, z ^ 1, c)).start()

    def along(cond, b, way):
        block = R.W.at[z, b, c]
        zz = z ^ 1 if way == 0 else here.far

        @when(cond)
        def _():
            remote(block, block, R.sOwn.at[b, way], R.rW.at[z, b, c], dev(s, zz, c)).start()

    def ready(cond, b):
        @when(cond)
        def _():
            arrived(R.W.at[z, b, c], R.rW.at[z, b, c])

    def aside(cond, b):
        @when(cond)
        def _():
            spread(z, b)

    def step(cond, b, side=True):
        ready(cond, b)
        along(cond, b, 1)
        along(cond, b, 0)
        if side:
            aside(cond, b)

    def foreign(zz, b, cond=True):
        block = R.W.at[zz, b, c]

        @when(cond & (z != zz))
        def _():
            arrived(block, R.rW.at[zz, b, c])

        @when(cond & (z != zz) & inner & (z ^ 1 != zz))
        def _():
            remote(block, block, R.sFwd.at[zz, b, 1], R.rW.at[zz, b, c], dev(s, z ^ 1, c)).start()

        @when(cond & (z != zz))
        def _():
            spread(zz, b)

    always = z >= 0
    top = z == 3
    @when(z == 2)
    def _():
        arrived(piece_of(s, c), R.rM.at[s, c])
        for i, zz in enumerate(layers):
            remote(piece_of(s, c), piece_of(s, c), R.sMz.at[i], R.rM.at[s, c], dev(s, zz, c)).start()
        for i, p in enumerate(peers):
            remote(piece_of(s, c), piece_of(s, c), R.sMp.at[i], R.rM.at[s, c], dev(p, z, c)).start()

    out_along(top & (s == 0))
    step(no(top) & (s == 1), 1)
    first_feed = z != 2
    for b in (2, 3):
        mine_first = (s == b) & first_feed
        ready(mine_first, b)
        along(mine_first, b, 1)
        along(mine_first & inner, b, 0)
        aside(mine_first, b)

    tcol = iota((GROUP, 1), 0).astype(F32)
    trow = iota((1, GROUP), 1).astype(F32)
    start_col = jnp.zeros((GROUP, 1), F32)
    seg_col = jnp.zeros((GROUP, 1), F32)
    seg_row = jnp.zeros((1, GROUP), F32)
    end = jnp.float32(0.0)
    for i in range(4):
        end = end + lens[0, i].astype(F32)
        past = tcol >= end
        seg_col = seg_col + jnp.where(past, 1.0, 0.0)
        seg_row = seg_row + jnp.where(trow >= end, 1.0, 0.0)
        start_col = jnp.maximum(start_col, jnp.where(past, end, 0.0))
    place_short = tcol - start_col
    valid = seg_col < 3.5
    lead_short = lead[0, 0]
    lead_long = lead[0, 1]
    freq = jnp.exp(-math.log(10000.0) * 2.0 * iota((1, 512), 1).astype(F32) / D)

    def positions(g):
        place = place_short if g == 0 else tcol
        lead_g = lead_short if g == 0 else lead_long
        base = lead_g * vec[3:4, :] + vec[4:5, :] + vec[2:3, :]
        angle = place * freq
        R.acc[g * GROUP : (g + 1) * GROUP, 0:512] = jnp.sin(angle) + base[:, 0:512]
        R.acc[g * GROUP : (g + 1) * GROUP, 512:1024] = jnp.cos(angle) + base[:, 512:1024]

    positions(0)
    out_along(top & (s != 0))
    step(no(top) & (s != 1), 1)
    step(top, 1, False)

    positions(1)

    gout = R.gout
    loads[1].wait()
    gout[0:GROUP, :] = jnp.where(valid, cot[0:GROUP, :].astype(F32), 0.0).astype(BF)
    gout[GROUP:ROWS, :] = cot[GROUP:ROWS, :]

    @when(no(key_owner))
    def _():
        arrived(R.kq.at[c], R.rK.at[c])

    remote(R.kq.at[c], R.kq.at[c], R.sK.at[15], R.rK.at[c], sib).start()
    loads[0].wait()
    for g in range(2):
        R.patT[:, g * 256 : (g + 1) * 256] = mm(perm, pat[g]).astype(BF)

    @when(z != 2)
    def _():
        arrived(piece_of(s, c), R.rM.at[s, c])
        for i, p in enumerate(peers):
            remote(piece_of(s, c), piece_of(s, c), R.sMp.at[i], R.rM.at[s, c], dev(p, z, c)).start()

    @when(top)
    def _():
        for h in range(2):
            out_layer(h)

    for b in (2, 3):
        mine_first = (s == b) & first_feed
        ready(no(mine_first), b)
        along(no(mine_first), b, 1)
        aside(no(mine_first), b)
    along(outer, 2, 0)
    along(outer, 3, 0)
    scatter(late)

    arrived(R.kq.at[1 - c], R.rK.at[1 - c])
    R.kqF[:, 0:512] = R.kq[0]
    R.kqF[:, 512:1024] = R.kq[1]
    kq_full = R.kqF[...]
    R.fo[...] = mm_nt(kq_full, table[...])

    def fill_head(h):
        row = R.fo[pl.ds(h, 1), 0:192]
        value = jnp.where(iota((48, 192), 1) % 48 == iota((48, 192), 0), row, 0.0)
        high = value.astype(BF)
        R.fill[at(h * 48, 48, 16), :] = high
        R.fill[at(768 + h * 48, 48, 16), :] = (value - high.astype(F32)).astype(BF)

    loop(HEADS, fill_head)

    def score_part(i):
        lo = i * 256
        R.att[at(lo, 256, 256), :] = mm(R.fill[at(lo, 256, 256), :], R.patT[...]) + mm(
            R.fill[at(768 + lo, 256, 256), :], R.patT[...]
        )

    loop(3, score_part)

    @when(no(top))
    def _():
        for h in range(2):
            arrived(out_half(h), R.rA.at[h])

            @when(z == 1)
            def _():
                remote(out_half(h), out_half(h), R.sAf.at[h], R.rA.at[h], dev(s, z ^ 1, c)).start()

            out_layer(h)

    for i, p in enumerate([s] + peers):
        if i > 0:
            arrived(piece_of(p, c), R.rM.at[p, c])
        remote(piece_of(p, c), piece_of(p, c), R.sMc.at[p], R.rM.at[p, c], sib).start()

    for p in range(4):
        arrived(piece_of(p, 1 - c), R.rM.at[p, 1 - c])

    for zz in range(3):
        foreign(zz, 1, inner)
    R.op[240:256, :] = jnp.where(iota((16, 512), 0) == 0, 1.0, 0.0).astype(BF)
    r48 = iota((48, 256), 0)
    c48 = iota((48, 256), 1)

    def weights_of(op, low, cols):
        lowf = low.astype(F32)
        for p in range(4):
            op[p * 48 : (p + 1) * 48, :] = (lowf * R.patT[p * 48 : (p + 1) * 48, cols].astype(F32)).astype(BF)
        op[192:240, :] = low

    def embed_head(h):
        offset = jnp.sum(jnp.where(c48 == r48 + 192, R.fo[pl.ds(h, 1), :], 0.0), axis=1, keepdims=True)
        rows = at(h * 48, 48, 16)
        scores = (R.att[rows, :] + offset) * (1.0 / math.sqrt(HEAD))
        peak = jnp.max(scores, axis=0, keepdims=True)
        e = jnp.exp(scores - peak)
        prob = e / jnp.sum(e, axis=0, keepdims=True)
        R.att[rows, :] = prob
        weights_of(R.op, prob.astype(BF), slice(None))
        hrows = at(h * 64, 64, 64)
        R.hT[hrows, :] = mm(R.mT[hrows, :], R.op[...]).astype(BF)

    loop(HEADS, embed_head)

    def pass_out():
        for h in range(2):
            for p in [s] + peers:
                arrived(half_of(p, h), R.rH.at[p, c, h])
                remote(half_of(p, h), half_of(p, h), R.sAc.at[p, h], R.rH.at[p, c, h], sib).start()

    def wait_out():
        for h in range(2):
            for p in range(4):
                arrived(R.WF.at[0, p, 1 - c, h * 256 : (h + 1) * 256], R.rH.at[p, 1 - c, h])

    def pass_on():
        for p in [s] + peers:
            block = R.WF.at[1, p, c]
            arrived(block, R.rF.at[p, c])
            remote(block, block, R.sFc.at[p], R.rF.at[p, c], sib).start()

    def wait_whole():
        for p in range(4):
            arrived(R.WF.at[1, p, 1 - c], R.rF.at[p, 1 - c])

    pass_out()

    def turn_tile(i):
        rows = at(i * 256, 256, 256)
        R.hrow[:, rows] = R.hT[rows, :].T

    loop(4, turn_tile)
    for zz in range(3):
        foreign(zz, 1, outer)
    foreign(3, 1, inner)

    @when(top)
    def _():
        spread(3, 1)

    foreign(z ^ 3, 2, inner)
    along(inner & no((s == 2) & first_feed), 2, 0)
    along(inner & no((s == 3) & first_feed), 3, 0)
    wait_out()

    def stream0_part(n):
        cols = at(n * 256, 256, 256)
        R.st0[:, cols] = (mm(R.hrow[...], R.WF[0, n].reshape(1024, 256)) + R.acc[:, cols]).astype(BF)

    loop(4, stream0_part)
    foreign(3, 1, outer)

    def norm_into(src, dst, which, g):
        def part(i):
            rows = at(g * 256 + i * 64, 64, 64)
            dst[rows, :] = normed_rows(
                src[rows, :].astype(F32), vec[5 + which : 6 + which, :], vec[7 + which : 8 + which, :]
            ).astype(BF)

        loop(4, part)

    norm_into(R.st0, R.nrm, 0, 0)
    norm_into(R.st0, R.nrm, 0, 1)
    foreign(z ^ 3, 3, inner)


    own_cols = at(s * 256, 256, 256)
    own_rows = at(s * OWN, OWN, OWN)

    def wait_half(zz, b):
        arrived(R.W.at[zz, b, 1 - c], R.rW.at[zz, b, 1 - c])

    def project(zz, dst, bias):
        wait_half(zz, 1)
        weight = R.W[zz, 1].reshape(1024, 256)
        for g in range(2):
            rows = slice(g * 256, (g + 1) * 256)
            value = mm(R.nrm[rows, :], weight)
            if bias is not None:
                value = value + vec[bias : bias + 1, own_cols]
            dst[rows, :] = value.astype(BF)

    project(0, R.q, 9)
    project(1, R.k, None)
    project(2, R.v, 10)

    lane_head = iota((1, 256), 1) // HEAD

    def only(hh, x):
        return jnp.where(lane_head == hh, x.astype(F32), 0.0).astype(BF)

    allowed = seg_col == seg_row

    def attend(g):
        rows = slice(g * 256, (g + 1) * 256)
        total = jnp.zeros((256, 256), F32)
        for hh in range(4):
            scores = mm_nt(R.q[rows, :], only(hh, R.k[rows, :])) * (1.0 / math.sqrt(HEAD))
            if g == 0:
                scores = jnp.where(allowed, scores, -1e30)
            e = jnp.exp(scores - jnp.max(scores, axis=1, keepdims=True))
            prob = e / jnp.sum(e, axis=1, keepdims=True)
            R.attp[g * 4 + hh] = prob
            total = total + mm(prob.astype(BF), only(hh, R.v[rows, :]))
        R.mix[rows, own_cols] = total.astype(BF)

    def mixed_of(g, p):
        return R.mix.at[g * 256 : (g + 1) * 256, at(p * 256, 256, 256)]

    for g in range(2):
        attend(g)
        for i, p in enumerate(peers):
            remote(mixed_of(g, s), mixed_of(g, s), R.sMix.at[g, i], R.rMix.at[g, s], dev(p, z, c)).start()

    step(z == 2, 0)
    for b in (2, 3):
        foreign(z ^ 2, b, inner)
    pass_on()
    wait_whole()
    def stream1_part(g, n):
        rows = slice(g * 256, (g + 1) * 256)
        cols = at(n * 256, 256, 256)
        value = mm(R.mix[rows, :], R.WF[1, n].reshape(1024, 256)) + vec[11:12, cols]
        R.st1[rows, cols] = (value + R.st0[rows, cols].astype(F32)).astype(BF)

    for g in range(2):
        for p in peers:
            arrived(mixed_of(g, p), R.rMix.at[g, p])
        loop(4, functools.partial(stream1_part, g))
        norm_into(R.st1, R.nrm2, 1, g)

    early = jnp.where(z < 2, 0, 1)

    def feed(par):
        def part(i):
            bb = lax.div(i, 2)
            b = par + 2 * bb
            rows = at(lax.rem(i, 2) * 256, 256, 256)
            block = R.W.at[2 + par, 2 + bb]
            grad = jnp.zeros((256, 256), F32)
            for n in range(4):
                tile = block[n // 2, (n % 2) * 256 : (n % 2 + 1) * 256, :]
                grad = grad + mm_nt(gout[rows, n * 256 : (n + 1) * 256], tile)
            bias = vec[pl.ds(12 + b, 1), own_cols]
            x = mm(R.nrm2[rows, :], R.W[par, 2 + bb].reshape(1024, 256)) + bias
            half_cdf = 0.5 + 0.5 * lax.erf(x * math.sqrt(0.5))
            R.act[b, rows, :] = (x * half_cdf).astype(BF)
            slope = half_cdf + x * (jnp.exp(-0.5 * x * x) * (1.0 / math.sqrt(2.0 * math.pi)))
            R.gin[b, rows, :] = (grad * slope).astype(BF)

        loop(4, part)

    def feed_norm(par, rows):
        total = mm_nt(R.gin[par, rows, :], R.W[par, 2].reshape(1024, 256))
        return total + mm_nt(R.gin[par + 2, rows, :], R.W[par, 3].reshape(1024, 256))

    def feed_out(par, n, rows):
        total = jnp.zeros((256, 256), F32)
        for bb in range(2):
            tile = R.W[2 + par, 2 + bb, lax.div(n, 2), at(lax.rem(n, 2) * 256, 256, 256), :]
            total = total + mm(R.act[par + 2 * bb, rows, :], tile)
        return total

    def tiles(body):
        loop(8, lambda i: body(lax.rem(i, 4), at(lax.div(i, 4) * 256, 256, 256)))

    def drain_feed(zz):
        for b in (2, 3):
            sent(R.msgs.at[0], R.sFwd.at[zz, b, 0])

            @when((z != zz) & inner & (z ^ 1 != zz))
            def _():
                sent(R.msgs.at[0], R.sFwd.at[zz, b, 1])

            @when(z == zz)
            def _():
                for i in range(2):
                    sent(R.msgs.at[0], R.sOwn.at[b, i])

    def transposed(src):
        def part(i):
            a = lax.div(i, 2)
            b = lax.rem(i, 2)
            R.tr[at(a * 256, 256, 256), at(b * 256, 256, 256)] = src[
                at(b * 256, 256, 256), at(a * 256, 256, 256)
            ].T

        loop(8, part)

    def slot(zz, b):
        return 12 if isinstance(b, int) and b == 0 else (b - 1) * 4 + zz

    def exchange(zz, b):
        block = R.W.at[zz, b, 1 - c]
        remote(block, R.CR.at[slot(zz, b)], R.sC.at[zz, b], R.rC.at[zz, b], sib).start()

    def column_gradient(zz, b, left, right):
        for h in range(2):
            R.W[zz, b, h] = mm(left[h * 512 : (h + 1) * 512, :], right).astype(BF)
        exchange(zz, b)

    def feed_gradients(par):
        drain_feed(par)
        drain_feed(2 + par)

        def part(bb):
            b = par + 2 * bb
            for n in range(4):
                tile = mm_tn(R.act[b], gout[:, n * 256 : (n + 1) * 256])
                R.W[2 + par, 2 + bb, n // 2, (n % 2) * 256 : (n % 2 + 1) * 256, :] = tile.astype(BF)
            exchange(2 + par, 2 + bb)
            column_gradient(par, 2 + bb, R.tr, R.gin[b])

        loop(2, part)

    def summed(zz, b):
        arrived(R.CR.at[slot(zz, b)], R.rC.at[zz, b])
        sent(R.CR.at[slot(zz, b)], R.sC.at[zz, b])
        R.W[zz, b, c] = (R.W[zz, b, c].astype(F32) + R.CR[slot(zz, b)].astype(F32)).astype(BF)

    def first_send(k, b, cond=True):
        zz = z ^ k
        block = R.W.at[zz, b, c]

        @when(cond)
        def _():
            summed(zz, b)
            if k == 1:
                remote(block, R.RA.at[b], R.sZ.at[zz, b], R.rRA.at[b], dev(s, z ^ 1, c)).start()

        if k > 1:

            @when(cond & outer)
            def _():
                remote(block, R.RC.at[3 - k, b], R.sZ.at[zz, b], R.rRC.at[3 - k, b], dev(s, z ^ 1, c)).start()

    def gradient_sends(cond, ks):
        for k in ks:
            for b in (2, 3):
                first_send(k, b, cond)

    def wait_feed(par):
        for b in (2, 3):
            wait_half(par, b)
            wait_half(2 + par, b)

    for b in (2, 3):
        foreign(z ^ 1, b, inner)
        foreign(z ^ 2, b, outer)
    wait_feed(early)
    feed(early)

    def norm_start(g):
        rows = at(g * 256, 256, 256)
        R.acc[rows, :] = feed_norm(early, rows)

    def out_start(n, rows):
        R.gact[n, rows, :] = feed_out(early, n, rows)

    loop(2, norm_start)
    tiles(out_start)
    transposed(R.nrm2)
    feed_gradients(early)
    for b in (2, 3):
        foreign(z ^ 1, b, outer)
        foreign(z ^ 3, b, outer)
    later = 1 - early
    gradient_sends(outer, (2, 0))
    foreign(2, 0)
    wait_feed(later)
    feed(later)

    def reduce_rows(phase, make):
        for i, p in enumerate(peers):
            make(p)
            block = R.rsS.at[at(p * OWN, OWN, OWN), :]
            remote(block, R.rsR.at[s], R.sR.at[phase, i], R.rR.at[phase, s], dev(p, z, c)).start()
        make(s)

    def reduced(phase):
        total = R.rsS[own_rows, :].astype(F32)
        for p in peers:
            arrived(R.rsR.at[p], R.rR.at[phase, p])
            total = total + R.rsR[p].astype(F32)
        return total

    def norm_end(p):
        rows = at(p * OWN, OWN, OWN)
        R.rsS[rows, :] = (R.acc[rows, :] + feed_norm(later, rows)).astype(BF)

    def out_end(n, rows):
        R.hrow[rows, at(n * 256, 256, 256)] = (R.gact[n, rows, :] + feed_out(later, n, rows)).astype(BF)

    reduce_rows(0, norm_end)

    def drain_own(cond, b):
        @when(cond)
        def _():
            for i in range(2):
                sent(R.msgs.at[0], R.sOwn.at[b, i])

    def drain_spread(zz, b):
        whole = full_of(zz, b)

        def side():
            sent(R.msgs.at[0], R.sFwd.at[zz, b, 0])

        def layer():
            for i in range(3):
                sent(R.msgs.at[0], R.sFx.at[i])

        (layer if whole else side)()

        @when((z != zz) & inner & (z ^ 1 != zz))
        def _():
            sent(R.msgs.at[0], R.sFwd.at[zz, b, 1])

    def second_send(k, b, cond=True):
        zz = z ^ k
        block = R.W.at[zz, b, c]

        @when(inner & cond)
        def _():
            arrived(R.RC.at[k - 2, b], R.rRC.at[k - 2, b])
            R.W[zz, b, c] = (R.W[zz, b, c].astype(F32) + R.RC[k - 2, b].astype(F32)).astype(BF)
            remote(block, R.RB.at[b], R.sZ.at[zz, b], R.rRB.at[b], dev(s, zz, c)).start()

    def owner_of(b):
        row = (z >= 2) if b >= 2 else (z < 0)
        tc = jnp.where(row, lax.div(s, 2), c)
        m = jnp.where(row, lax.rem(s, 2) * 2 + c, s)
        return tc, m, (s == b) & (tc == c)

    def last_send(cond, b):
        tc, m, own = owner_of(b)
        block = R.W.at[z, b, c]

        @when(cond)
        def _():
            arrived(R.RA.at[b], R.rRA.at[b])
            arrived(R.RB.at[b], R.rRB.at[b])
            R.W[z, b, c] = (R.W[z, b, c].astype(F32) + R.RA[b].astype(F32) + R.RB[b].astype(F32)).astype(BF)

        @when(cond & own)
        def _():
            pltpu.make_async_copy(block, R.FR.at[m], R.rFin.at[m]).start()

        @when(cond & no(own))
        def _():
            remote(block, R.FR.at[m], R.sFin.at[b], R.rFin.at[m], dev(b, z, tc)).start()

    gradient_sends(inner, (1, 3))
    tiles(out_end)
    feed_gradients(later)

    R.small[...] = jnp.zeros((16, 1024), F32)
    for b in range(4):
        R.small[10 + b : 11 + b, own_cols] = column_sum(R.gin[b].astype(F32))
    R.small[14:15, :] = column_sum(gout[own_rows, :].astype(F32))

    gradient_sends(outer, (3, 1))
    gradient_sends(inner, (2, 0))

    g2 = reduced(0)
    gx, gw, gb = norm_back(R.st1[own_rows, :].astype(F32), g2, vec[6:7, :])
    R.small[4:5, :] = gw
    R.small[6:7, :] = gb
    gs1_own = (gout[own_rows, :].astype(F32) + gx).astype(BF)
    R.small[9:10, :] = column_sum(gs1_own.astype(F32))
    R.gs[0] = gs1_own

    def mixed_grad(p):
        total = jnp.zeros((OWN, 256), F32)
        for n in range(4):
            tile = R.WF[1, n, lax.div(p, 2), at(lax.rem(p, 2) * 256, 256, 256), :]
            total = total + mm_nt(R.gs[0, :, n * 256 : (n + 1) * 256], tile)
        return total.astype(BF)

    def swap(phase, src_of, dst):
        for i, p in enumerate(peers):
            remote(src_of(p), dst.at[own_rows, :], R.sG.at[phase, i], R.rG.at[phase, s], dev(p, z, c)).start()

    def swapped(phase, dst):
        for p in peers:
            arrived(dst.at[at(p * OWN, OWN, OWN), :], R.rG.at[phase, p])

    for i, p in enumerate(peers):
        R.gmS[i] = mixed_grad(p)
        remote(R.gmS.at[i], R.gm.at[own_rows, :], R.sG.at[0, i], R.rG.at[0, s], dev(p, z, c)).start()
    R.gm[own_rows, :] = mixed_grad(s)
    swap(1, lambda p: R.gs.at[0, :, at(p * 256, 256, 256)], R.ga)
    R.ga[own_rows, :] = R.gs[0, :, own_cols]

    def send_out(i):
        p = peers[i]
        block = R.hrow.at[:, at(p * 256, 256, 256)]
        remote(block, R.outR.at[s], R.sOut.at[i], R.rOut.at[s], dev(p, z, c)).start()


    swapped(0, R.gm)

    def attend_back(g):
        rows = at(g * 256, 256, 256)
        qg, kg, vg, gmg = R.q[rows, :], R.k[rows, :], R.v[rows, :], R.gm[rows, :]
        zero = jnp.zeros((256, 256), F32)
        tq, tk, tv = zero, zero, zero
        for hh in range(4):
            prob = R.attp[g * 4 + hh]
            gmh = only(hh, gmg)
            dprob = mm_nt(gmh, vg)
            tv = tv + mm_tn(prob.astype(BF), gmh)
            ds = (prob * (dprob - jnp.sum(prob * dprob, axis=1, keepdims=True))).astype(BF)
            tq = tq + mm(ds, only(hh, kg))
            tk = tk + mm_tn(ds, only(hh, qg))
        scale = 1.0 / math.sqrt(HEAD)
        R.gq[0, rows, :] = (tq * scale).astype(BF)
        R.gq[1, rows, :] = (tk * scale).astype(BF)
        R.gq[2, rows, :] = tv.astype(BF)

    loop(2, attend_back)

    for i in range(3):
        sent(R.rsR.at[0], R.sR.at[0, i])

    def attend_norm(p):
        rows = at(p * OWN, OWN, OWN)
        total = jnp.zeros((OWN, 1024), F32)
        for i in range(3):
            total = total + mm_nt(R.gq[i, rows, :], R.W[i, 1].reshape(1024, 256))
        R.rsS[rows, :] = total.astype(BF)

    reduce_rows(1, attend_norm)
    for b in (2, 3):
        second_send(3, b)

    transposed(R.nrm)
    drain_own(always, 1)
    for zz in range(4):
        drain_spread(zz, 1)
    piece = R.msgs.at[0, 0:256]
    for h in range(2):
        for i in range(3):
            sent(piece, R.sAx.at[i, h])

        @when(z == 1)
        def _():
            sent(piece, R.sAf.at[h])

        @when(top)
        def _():
            sent(piece, R.sAo.at[0, h])
            sent(piece, R.sAo.at[1, h])


    def attend_gradient(i):
        column_gradient(i, 1, R.tr, R.gq[i])

    loop(3, attend_gradient)
    transposed(R.mix)
    swapped(1, R.ga)
    column_gradient(3, 1, R.tr, R.ga[...])
    R.small[7:8, own_cols] = column_sum(R.gq[0].astype(F32))
    R.small[8:9, own_cols] = column_sum(R.gq[2].astype(F32))
    for k in (2, 3, 1, 0):
        first_send(k, 1)

    for b in (2, 3):
        second_send(2, b)
    g1 = reduced(1)
    gx, gw, gb = norm_back(R.st0[own_rows, :].astype(F32), g1, vec[5:6, :])
    R.small[3:4, :] = gw
    R.small[5:6, :] = gb
    gs0_own = (R.gs[0].astype(F32) + gx).astype(BF)
    gs0_sum = column_sum(gs0_own.astype(F32))
    R.small[1:2, :] = gs0_sum
    R.small[2:3, :] = jnp.where(s < 2, lead_short, lead_long) * gs0_sum
    R.gs[1] = gs0_own
    swap(2, lambda p: R.gs.at[1, :, at(p * 256, 256, 256)], R.gb)
    R.gb[own_rows, :] = R.gs[1, :, own_cols]
    def heads_grad(i):
        rows = at(lax.rem(i, 2) * 256, 256, 256)
        total = jnp.zeros((256, OWN), F32)
        for n in range(4):
            total = total + mm_nt(R.WF[0, n, lax.div(i, 2), rows, :], R.gs[1, :, n * 256 : (n + 1) * 256])
        block = at(i * 256, 256, 256)
        R.ghT[block, :] = total.astype(BF)
        R.gh[:, block] = total.astype(BF).T

    loop(4, heads_grad)
    R.G = R.acc.at[0:256, :]
    R.gpT[...] = jnp.zeros((192, OWN), F32)
    R.G[...] = jnp.zeros((256, 1024), F32)
    for hh in range(4):
        R.op1[hh, 240:256, :] = jnp.where(iota((16, OWN), 0) == 0, 1.0, 0.0).astype(BF)

    def embed_back(h, op1):
        rows = at(h * 48, 48, 16)
        prob = R.att[rows, own_rows]
        low = prob.astype(BF)
        lowf = low.astype(F32)
        weights_of(op1, low, own_rows)
        hrows = at(h * 64, 64, 64)
        gop = mm_tn(R.mT[hrows, :], R.ghT[hrows, :])
        cols = at(lax.div(h, 4) * 256, 256, 256)
        keep = lane_head == lax.rem(h, 4)
        R.G[:, cols] += jnp.where(keep, mm(op1[...], R.gh[:, cols]), 0.0)
        gatt = gop[192:240, :]
        for p in range(4):
            gatt = gatt + gop[p * 48 : (p + 1) * 48, :] * R.patT[p * 48 : (p + 1) * 48, own_rows].astype(F32)
        R.gsc[rows, :] = prob * (gatt - jnp.sum(prob * gatt, axis=0, keepdims=True)) * (1.0 / math.sqrt(HEAD))
        for p in range(4):
            prow = slice(p * 48, (p + 1) * 48)
            R.gpT[prow, :] += gop[prow, :] * lowf

    def embed_back_four(i):
        for hh in range(4):
            embed_back(4 * i + hh, R.op1.at[hh])

    loop(4, embed_back_four)

    gsc = R.gsc[...]
    gsc_high = gsc.astype(BF)
    gsc_low = (gsc - gsc_high.astype(F32)).astype(BF)
    fold = jnp.where(iota((16, 768), 0) == iota((16, 768), 1) // 48, 1.0, 0.0).astype(BF)

    def folded(x, right):
        x_high = x.astype(BF)
        x_low = (x - x_high.astype(F32)).astype(BF)
        return mm(fold, x_high) + mm(fold, x_low)

    ones = jnp.ones((192, OWN), BF)
    pat_own = R.patT[:, own_rows]
    same = iota((768, 192), 0) % 48 == iota((768, 192), 1) % 48
    cross = mm_nt(gsc_high, pat_own) + mm_nt(gsc_low, pat_own)
    plain = mm_nt(gsc_high, ones) + mm_nt(gsc_low, ones)
    R.fc[0, :, 0:192] = folded(jnp.where(same, cross, 0.0), None)
    R.fc[0, :, 192:256] = folded(jnp.where(same, plain, 0.0), None)[:, 0:64] * jnp.where(
        iota((1, 64), 1) < 48, 1.0, 0.0
    )
    remote(R.fc.at[0], R.fc.at[1], R.sFo.at[0], R.rFo.at[0], sib).start()

    R.G[240:256, :] += R.small[...]
    R.gall[...] = R.G[...].astype(BF)
    half = at(c * 128, 128, 128)
    other = at((1 - c) * 128, 128, 128)
    remote(R.gall.at[other, :], R.fromc, R.sAll.at[0], R.rAll.at[0], sib).start()

    gpt = (R.gpT[...] + mm_tn(R.fill[0:768, :], gsc_high)).astype(BF)
    for p in range(4):
        r = iota((48, 192), 0) + p * 48
        select = jnp.where(iota((48, 192), 1) == (r % 4) * 48 + r // 4, 1.0, 0.0).astype(BF)
        R.pixS[p] = mm(select, gpt).astype(BF)
    for i, p in enumerate(peers):
        remote(R.pixS.at[p], R.pixR.at[s], R.sP.at[i], R.rP.at[s], dev(p, z, c)).start()

    arrived(R.fc.at[1], R.rFo.at[0])
    R.fp[s] = R.fc[0] + R.fc[1]
    for i, p in enumerate(peers):
        remote(R.fp.at[s], R.fp.at[s], R.sFo.at[1 + i], R.rFo.at[1 + s], dev(p, z, c)).start()

    arrived(R.fromc, R.rAll.at[0])
    R.gall[half, :] = (R.gall[half, :].astype(F32) + R.fromc[...].astype(F32)).astype(BF)

    def part_of(p):
        return at(c * 128 + p * 32, 32, 32)

    for i, p in enumerate(peers):
        remote(R.gall.at[part_of(p), :], R.fromp.at[s], R.sAll.at[1 + i], R.rAll.at[1 + s], dev(p, z, c)).start()
    last_send(always, 2)
    last_send(always, 3)

    swapped(2, R.gb)
    column_gradient(3, 0, R.hT, R.gb[...])

    for p in peers:
        arrived(R.fp.at[p], R.rFo.at[1 + p])
    R.fz[z] = R.fp[0] + R.fp[1] + R.fp[2] + R.fp[3]
    for i, zz in enumerate(layers):
        remote(R.fz.at[z], R.fz.at[z], R.sFo.at[4 + i], R.rFo.at[5 + z], dev(s, zz, c)).start()

    total = R.gall[part_of(s), :].astype(F32)
    for p in peers:
        arrived(R.fromp.at[p], R.rAll.at[1 + p])
        total = total + R.fromp[p].astype(F32)
    R.fromz[z] = total.astype(BF)
    for i, zz in enumerate(layers):
        remote(R.fromz.at[z], R.fromz.at[z], R.sAll.at[4 + i], R.rAll.at[5 + z], dev(s, zz, c)).start()

    for k in (2, 3, 1, 0):
        first_send(k, 0, z ^ k == 3)
    for k in (2, 3):
        second_send(k, 1)

    for zz in layers:
        arrived(R.fz.at[zz], R.rFo.at[5 + zz])
    fo_grad = (R.fz[0] + R.fz[1]) + (R.fz[2] + R.fz[3])
    fo_high = fo_grad.astype(BF)
    fo_low = (fo_grad - fo_high.astype(F32)).astype(BF)
    gkq = (mm(fo_high, table[...]) + mm(fo_low, table[...])).astype(BF)

    @when(key_owner)
    def _():
        diag = iota((16, 1024), 1) // HEAD == iota((16, 1024), 0)
        own = jnp.where(c == 0, gkq[:, 0:512].astype(F32), gkq[:, 512:1024].astype(F32)).astype(BF)
        row = column_sum(jnp.where(diag, mm(own, bank[...]), 0.0))
        R.qx[0] = jnp.broadcast_to(row, (8, 1024))
        remote(R.qx.at[0], R.qx.at[1], R.sGq.at[15], R.rGq.at[0], sib).start()
        masked = jnp.where(diag, R.qb[...].astype(F32), 0.0).astype(BF)
        gbank[...] = mm_tn(own, masked).astype(BF)
        arrived(R.qx.at[1], R.rGq.at[0])
        row = (R.qx[0] + R.qx[1]).astype(BF)
        R.gqv[...] = jnp.concatenate([row, row], axis=0)
        for i, (p, k) in enumerate(others):
            remote(R.gqv, R.gqv, R.sGq.at[i], R.rGq.at[1], dev(p, k, c)).start()

    for zz in layers:
        arrived(R.fromz.at[zz], R.rAll.at[5 + zz])
    total = R.fromz[0].astype(F32)
    for zz in range(1, 4):
        total = total + R.fromz[zz].astype(F32)
    R.fin[part_of(s), :] = total.astype(BF)
    for i, p in enumerate(peers):
        block = R.fin.at[part_of(s), :]
        remote(block, block, R.sAll.at[7 + i], R.rAll.at[9 + s], dev(p, z, c)).start()
    send_out(0)
    send_out(1)
    send_out(2)

    @when(first_owner)
    def _():
        arrived(R.gqv, R.rGq.at[1])
        R.gaq[c] = mm_nt(R.gqv[...], bank[...])[0:8]
        for i, (p, k) in enumerate(others):
            remote(R.gaq.at[c], R.gaq.at[c], R.sGa.at[i], R.rGa.at[c], dev(p, k, c)).start()
        aq = jnp.where(c == 0, vec[17:18, 0:512], vec[17:18, 512:1024])
        aq = jnp.where(iota((16, 512), 0) == 0, aq, 0.0).astype(BF)
        gbank[...] = mm_tn(aq, R.gqv[...]).astype(BF)


    for p in peers:
        arrived(R.fin.at[part_of(p), :], R.rAll.at[9 + p])
    remote(R.fin.at[half, :], R.fin.at[half, :], R.sAll.at[10], R.rAll.at[13], sib).start()

    for k in (2, 3):
        second_send(k, 0, z ^ k == 3)

    arrived(R.fin.at[other, :], R.rAll.at[13])
    sums[...] = R.fin[240:256, :].astype(F32)
    wait_half(2, 0)
    zero16 = jnp.zeros((112, 256), BF)
    kq_wide = jnp.concatenate([R.kqF[:, own_cols], zero16], axis=0)
    value = mm_tn(jnp.concatenate([fo_high, zero16], axis=0), kq_wide)
    value = value + mm_tn(jnp.concatenate([fo_low, zero16], axis=0), kq_wide)
    for n in range(4):
        tile = R.W[2, 0, n // 2, (n % 2) * 256 : (n % 2 + 1) * 256, :]
        value = value + mm_nt(R.fin[:, n * 256 : (n + 1) * 256], tile)
    R.gt[s] = value.astype(BF)
    for i, p in enumerate(peers):
        remote(R.gt.at[s], R.gt.at[s], R.sGt.at[i], R.rGt.at[s], dev(p, z, c)).start()

    @when(value_owner)
    def _():
        gbank[...] = mm_tn(table[:, half_rows], R.fin[...]).astype(BF)

    last_send(always, 1)
    last_send(top, 0)

    @when(no(first_owner))
    def _():
        arrived(R.gaq.at[c], R.rGa.at[c])

    @when(no(key_owner | first_owner))
    def _():
        arrived(R.gqv, R.rGq.at[1])

    remote(R.gaq.at[c], R.gaq.at[c], R.sGa.at[15], R.rGa.at[c], sib).start()
    arrived(R.gaq.at[1 - c], R.rGa.at[1 - c])
    rows_out[0:8, :] = R.gqv[0:8, :].astype(F32)
    rows_out[8:16, 0:512] = R.gaq[0]
    rows_out[8:16, 512:1024] = R.gaq[1]

    for p in peers:
        arrived(R.gt.at[p], R.rGt.at[p])
    for p in range(4):
        gtab[:, p * 256 : (p + 1) * 256] = R.gt[p]
    total = R.hrow[:, own_cols].astype(F32) + R.st1[:, own_cols].astype(F32) + vec[16:17, own_cols]
    for p in peers:
        arrived(R.outR.at[p], R.rOut.at[p])
        total = total + R.outR[p].astype(F32)
    out[...] = total.astype(BF)

    for i, p in enumerate(peers):
        arrived(R.pixR.at[p], R.rP.at[p])
    R.pixR[s] = R.pixS[s]
    for p in range(4):
        gpix[p // 2, :, (p % 2) * OWN : (p % 2 + 1) * OWN] = R.pixR[p].astype(F32)

    @when(used)
    def _():
        for m in range(4):
            arrived(R.FR.at[m], R.rFin.at[m])

    @when(used & no(is_row))
    def _():
        for m in range(4):
            gbank[:, m * 256 : (m + 1) * 256] = R.FR[m]

    @when(used & is_row)
    def _():
        for m in range(4):
            q, h = m // 2, m % 2
            for n in range(2):
                lo = (2 * h + n) * 256
                gbank[q * 256 : (q + 1) * 256, lo : lo + 256] = R.FR[m, n * 256 : (n + 1) * 256, :]

    stores = [pltpu.make_async_copy(a, b, R.sRes.at[i]) for i, (a, b) in enumerate(zip(results, targets))]
    for store in stores:
        store.start()

    for m in range(4):
        tp, tc, own = message(m)

        @when((used | late) & no(own) & no(out_owner))
        def _():
            sent(R.msgs.at[m], R.sMsg.at[m])

        if m > 0:

            @when(out_owner)
            def _():
                sent(piece, R.sA.at[m, 0])
                sent(piece, R.sA.at[m, 1])

        @when(value_owner & no((2 * c + m // 2 == s) & (c == m % 2)))
        def _():
            sent(my_piece(m), R.sMa.at[m])

    @when(first_owner)
    def _():
        sent(R.qbuf.at[0], R.sQ.at[0])
        sent(R.qb, R.sQ.at[1])
        for i in range(15):
            sent(R.gaq.at[c], R.sGa.at[i])

    @when(key_owner)
    def _():
        sent(R.qx.at[0], R.sGq.at[15])
        for i in range(15):
            sent(R.kq.at[c], R.sK.at[i])
            sent(R.gqv, R.sGq.at[i])

    @when(z == 2)
    def _():
        for i in range(3):
            sent(R.mS.at[0:128, :], R.sMz.at[i])

    drain_own(z == 2, 0)
    drain_spread(2, 0)
    sent(R.kq.at[c], R.sK.at[15])
    sent(R.gaq.at[c], R.sGa.at[15])
    for p in range(4):
        sent(R.msgs.at[0], R.sFc.at[p])
        sent(piece, R.sAc.at[p, 0])
        sent(piece, R.sAc.at[p, 1])
    for p in range(4):
        sent(R.mS.at[0:128, :], R.sMc.at[p])
    sent(R.fc.at[0], R.sFo.at[0])
    sent(R.fromc, R.sAll.at[0])
    sent(R.fromc, R.sAll.at[10])
    for i in range(3):
        sent(R.mS.at[0:128, :], R.sMp.at[i])
        sent(R.mix.at[0:256, 0:256], R.sMix.at[0, i])
        sent(R.mix.at[0:256, 0:256], R.sMix.at[1, i])
        sent(R.msgs.at[0], R.sOut.at[i])
        sent(R.rsR.at[0], R.sR.at[1, i])
        for phase in range(3):
            sent(R.gmS.at[0], R.sG.at[phase, i])
        sent(R.pixS.at[0], R.sP.at[i])
        sent(R.gt.at[0], R.sGt.at[i])
        sent(R.fp.at[0], R.sFo.at[1 + i])
        sent(R.fp.at[0], R.sFo.at[4 + i])
        for phase in range(3):
            sent(R.fromp.at[0], R.sAll.at[1 + 3 * phase + i])
    for b in range(4):
        for zz in range(4):

            @when(at_least(jnp.int32(zz), b) & (z != zz) & (always if b > 0 or zz == 3 else z < 0))
            def _():
                sent(R.msgs.at[0], R.sZ.at[zz, b])

        tc, m, own = owner_of(b)

        @when((top if b == 0 else always) & no(own))
        def _():
            sent(R.msgs.at[0], R.sFin.at[b])
    for store in stores:
        store.wait()


VMEM = pl.BlockSpec(memory_space=pltpu.VMEM)
SMEM = pl.BlockSpec(memory_space=pltpu.SMEM)
ARG_SHAPES = (
    [((2, 192, 256), BF), ((512, 1024), BF), ((512, 1024), BF), ((48, 4, 1024), BF)]
    + [((48, 1024), BF)] * 2
    + [((1024,), BF)]
    + [((n, 1024), BF) for n in (3, 2, 2, 2, 3)]
    + [((4096,), BF), ((1024,), BF), ((1, 2), F32), ((1, 4), jnp.int32)]
)


ANY = pl.BlockSpec(memory_space=pl.ANY)


def block_call(*args):
    shape = jax.ShapeDtypeStruct
    outs = [
        shape((512, 256), BF),
        shape((2, 48, 256), F32),
        shape((512, 1024), BF),
        shape((256, 1024), BF),
        shape((16, 1024), F32),
        shape((16, 1024), F32),
    ]
    return pl.pallas_call(
        block_kernel,
        out_shape=outs,
        in_specs=[ANY] * 14 + [SMEM] * 2,
        out_specs=[ANY] * len(outs),
        scratch_shapes=[pltpu.VMEM(a.shape, a.dtype) for a in (*args[:14], *outs)]
        + [pltpu.VMEM(*v) for v in SCRATCH.values()]
        + [pltpu.SemaphoreType.DMA(v) for v in SEMS.values()],
        compiler_params=pltpu.CompilerParams(
            collective_id=1, has_side_effects=True, vmem_limit_bytes=63 * 2**20
        ),
    )(*args)


def finish_kernel(*refs):
    sources, targets, rest = refs[:6], refs[6:20], refs[20:]
    held, made, ins, outs = rest[:6], rest[6:20], rest[20], rest[21]
    out, gpix, gbank, gtab, sums, rows = held
    o_out, o_pix, o_bank, o_patch, o_patch_b, o_var, o_query, o_agg, o_lead, o_gain, o_bias, o_attn, o_fc1, o_fc2 = made

    def load(i):
        return pltpu.make_async_copy(sources[i], held[i], ins.at[i])

    def part(h):
        rows_h = pl.ds(h * 128, 128)
        return pltpu.make_async_copy(sources[2].at[rows_h], gbank.at[rows_h], ins.at[6 + h])

    def store(i):
        return pltpu.make_async_copy(made[i], targets[i], outs.at[i])

    def store_part(h):
        rows_h = pl.ds(h * 128, 128)
        return pltpu.make_async_copy(o_bank.at[rows_h], targets[2].at[rows_h], outs.at[14 + h])

    for h in range(4):
        part(h).start()
    for i in (3, 4, 5, 0, 1):
        load(i).start()
    direct = [pltpu.make_async_copy(held[i], targets[i], outs.at[i]) for i in range(2)]
    for h in range(4):
        part(h).wait()
        o_bank[h * 128 : (h + 1) * 128, :] = gbank[h * 128 : (h + 1) * 128, :].astype(F32)
        store_part(h).start()
    load(3).wait()
    for p in range(PIX):
        o_patch[:, p, :] = gtab[p * VARS : (p + 1) * VARS, :].astype(F32)
    o_patch_b[...] = gtab[192:240, :].astype(F32)
    o_var[...] = gtab[192:240, :].astype(F32)
    for i in (3, 4, 5):
        store(i).start()
    for i in range(2):
        load(i).wait()
        direct[i].start()
    load(4).wait()
    load(5).wait()
    o_query[...] = rows[8, :]
    o_agg[0:1, :] = rows[0:1, :]
    o_agg[1:3, :] = sums[0:2, :]
    o_lead[0:1, :] = sums[2:3, :]
    o_lead[1:2, :] = sums[1:2, :]
    o_gain[...] = sums[3:5, :]
    o_bias[...] = sums[5:7, :]
    o_attn[...] = sums[7:10, :]
    for i in range(4):
        o_fc1[i * 1024 : (i + 1) * 1024] = sums[10 + i, :]
    o_fc2[...] = sums[14, :]
    for i in range(6, 14):
        store(i).start()
    for copy in direct:
        copy.wait()
    for h in range(4):
        store_part(h).wait()
    for i in range(3, 14):
        store(i).wait()


def finish_call(*args):
    shape = jax.ShapeDtypeStruct
    outs = [shape((512, 256), BF), shape((2, 48, 256), F32), shape((512, 1024), F32), shape((48, 4, 1024), F32)]
    outs += [shape((48, 1024), F32)] * 2 + [shape((1024,), F32)]
    outs += [shape((n, 1024), F32) for n in (3, 2, 2, 2, 3)] + [shape((FF,), F32), shape((1024,), F32)]
    return pl.pallas_call(
        finish_kernel,
        out_shape=outs,
        in_specs=[ANY] * len(args),
        out_specs=[ANY] * len(outs),
        scratch_shapes=[pltpu.VMEM(a.shape, a.dtype) for a in (*args, *outs)]
        + [pltpu.SemaphoreType.DMA((10,)), pltpu.SemaphoreType.DMA((18,))],
        compiler_params=pltpu.CompilerParams(vmem_limit_bytes=63 * 2**20),
    )(*args)


def on_device_fast(
    patches,
    lead_times,
    short_lengths,
    cotangent,
    bank,
    patch_w,
    patch_b,
    var_emb,
    agg_query,
    agg_bias,
    lead_embed,
    norm_gain,
    norm_bias,
    attn_bias,
    fc1_bias,
    fc2_bias,
):
    parts = block_call(
        jnp.transpose(patches, (0, 2, 1)),
        cotangent.reshape(ROWS, D),
        bank[0],
        patch_w,
        patch_b,
        var_emb,
        agg_query,
        agg_bias,
        lead_embed,
        norm_gain,
        norm_bias,
        attn_bias,
        fc1_bias,
        fc2_bias,
        lead_times.T,
        short_lengths,
    )
    o = finish_call(*parts)
    return (
        (o[0].reshape(2, GROUP, 256), jnp.transpose(o[1], (0, 2, 1)), o[2][None])
        + tuple(o[3:])
    )


def specs():
    ins = (
        (P(None, "dp", None), P(None, "dp"), P("dp", None), P(None, "dp", None), P("section", "dp", None))
        + (P(),) * 11
    )
    outs = (P(None, "dp", "section"), P(None, "dp", "section"), P("section", "dp", None)) + (P(),) * 11
    return ins, outs


wide_type = jnp.float32
narrow_type = jnp.bfloat16
highest = lax.Precision.HIGHEST


def shortened(array):

    def short(part):
        return part.astype(jnp.bfloat16) if part.dtype == jnp.float32 else part

    return jax.tree.map(short, array)


def from_behind(array, axis, by):
    length = lax.axis_size(axis)
    pairs = [(i, i + by) for i in range(length) if 0 <= i + by < length]
    return lax.ppermute(array, axis, pairs)


def product(factor_left, factor_right):
    return jnp.dot(factor_left, factor_right, preferred_element_type=wide_type)


def product_left(factor_left, factor_right):
    return lax.dot_general(
        factor_left, factor_right, (((0,), (0,)), ((), ())), preferred_element_type=wide_type
    )


def product_right(factor_left, factor_right):
    return lax.dot_general(
        factor_left, factor_right, (((1,), (1,)), ((), ())), preferred_element_type=wide_type
    )


def norm_layer(stream, gain_row, shift_row):
    centre = stream - jnp.mean(stream, axis=-1, keepdims=True)
    spread = jnp.mean(centre * centre, axis=-1, keepdims=True)
    return centre * lax.rsqrt(spread + 1e-05) * gain_row + shift_row


def gelu_exact(values_in):
    return jax.nn.gelu(values_in, approximate=False)


def position_table(places):
    half_width = D // 2
    frequency = jnp.exp(-math.log(10000.0) * 2.0 * jnp.arange(half_width, dtype=wide_type) / D)
    angles = places.astype(wide_type)[:, None] * frequency[None, :]
    return jnp.concatenate([jnp.sin(angles), jnp.cos(angles)], axis=1)


def layout(lengths_row, row_count):
    segment_ends = jnp.cumsum(lengths_row)
    starts = segment_ends - lengths_row
    places = jnp.arange(row_count, dtype=jnp.int32)
    segment = jnp.sum((places[:, None] >= segment_ends[None, :]).astype(jnp.int32), axis=1)
    member = segment[:, None] == jnp.arange(lengths_row.shape[0], dtype=jnp.int32)[None, :]
    offset = jnp.sum(jnp.where(member, starts[None, :], 0), axis=1)
    offset = jnp.where(segment == lengths_row.shape[0], segment_ends[-1], offset)
    return (segment, places - offset)


def embed_setup(weights, params):
    patch_w, patch_b, var_emb, agg_query, agg_bias = params[:5]
    query_row = product(agg_query[None, :], weights[0])[0] + agg_bias[0].astype(wide_type)
    query_low = query_row.astype(narrow_type)
    key_query = jnp.einsum(
        "dhe,he->dh",
        weights[1].reshape(D, HEADS, HEAD),
        query_low.reshape(HEADS, HEAD),
        preferred_element_type=wide_type,
    )
    key_low = key_query.astype(narrow_type)
    constant = (patch_b.astype(wide_type) + var_emb.astype(wide_type)).astype(narrow_type)
    filters = jnp.einsum("vpd,dh->vph", patch_w, key_low, preferred_element_type=wide_type)
    offsets = product(constant, key_low)
    embed_table = jnp.concatenate([patch_w.reshape(VARS * PIX, D), constant], axis=0)
    return (query_low, key_low, constant, filters, offsets, embed_table)


def embed_rows(pixel_rows, places, lead_time, setup, weights, params):
    query_low, key_low, constant, filters, offsets, embed_table = setup
    agg_bias, lead_embed = (params[4], params[5])
    row_count = pixel_rows.shape[0]
    pixels = pixel_rows.reshape(row_count, VARS, PIX).astype(wide_type)
    scores = (
        jnp.einsum("tvp,vph->tvh", pixels, filters, precision=highest) + offsets[None]
    ) / math.sqrt(HEAD)
    attend = jax.nn.softmax(scores, axis=1)
    attend_low = attend.astype(narrow_type)
    weighted = (attend_low.astype(wide_type)[:, :, :, None] * pixels[:, :, None, :]).astype(
        narrow_type
    )
    operand = jnp.concatenate(
        [
            jnp.transpose(weighted, (0, 2, 1, 3)).reshape(row_count * HEADS, VARS * PIX),
            jnp.transpose(attend_low, (0, 2, 1)).reshape(row_count * HEADS, VARS),
        ],
        axis=1,
    )
    pooled = product(operand, embed_table).astype(narrow_type).reshape(row_count, HEADS, D)
    heads_out = jnp.einsum(
        "thd,dhe->the", pooled, weights[2].reshape(D, HEADS, HEAD), preferred_element_type=wide_type
    ).reshape(row_count, D)
    heads_low = (heads_out + agg_bias[1].astype(wide_type)).astype(narrow_type)
    merged = product(heads_low, weights[3]) + agg_bias[2].astype(wide_type)
    stream = (
        merged
        + position_table(places)
        + lead_time * lead_embed[0].astype(wide_type)
        + lead_embed[1].astype(wide_type)
    )
    return (stream.astype(narrow_type), (pixels, attend, attend_low, operand, pooled, heads_low))


def embed_back(grad_rows, lead_time, setup, saved_state, weights):
    query_low, key_low, constant, filters, offsets, embed_table = setup
    pixels, attend, attend_low, operand, pooled, heads_low = saved_state
    row_count = grad_rows.shape[0]
    grad_wide = grad_rows.astype(wide_type)
    grad_w_out = product_left(heads_low, grad_rows)
    grad_bias_out = jnp.sum(grad_wide, axis=0)
    grad_heads = product_right(grad_rows, weights[3]).astype(narrow_type)
    grad_bias_value = jnp.sum(grad_heads.astype(wide_type), axis=0)
    grad_heads_split = grad_heads.reshape(row_count, HEADS, HEAD)
    grad_w_value = jnp.einsum(
        "thd,the->dhe", pooled, grad_heads_split, preferred_element_type=wide_type
    ).reshape(D, D)
    grad_pooled = jnp.einsum(
        "the,dhe->thd",
        grad_heads_split,
        weights[2].reshape(D, HEADS, HEAD),
        preferred_element_type=wide_type,
    )
    grad_pooled = grad_pooled.astype(narrow_type).reshape(row_count * HEADS, D)
    grad_operand = product_right(grad_pooled, embed_table)
    grad_table = product_left(operand, grad_pooled)
    grad_weighted = grad_operand[:, : VARS * PIX].reshape(row_count, HEADS, VARS, PIX)
    grad_mixing = jnp.transpose(
        grad_operand[:, VARS * PIX :].reshape(row_count, HEADS, VARS), (0, 2, 1)
    )
    grad_attend = (
        jnp.einsum("thvp,tvp->tvh", grad_weighted, pixels, precision=highest) + grad_mixing
    )
    grad_scores = (
        attend
        * (grad_attend - jnp.sum(attend * grad_attend, axis=1, keepdims=True))
        / math.sqrt(HEAD)
    )
    grad_pixels = jnp.einsum(
        "thvp,tvh->tvp", grad_weighted, attend_low.astype(wide_type), precision=highest
    )
    grad_pixels = grad_pixels + jnp.einsum("tvh,vph->tvp", grad_scores, filters, precision=highest)
    grad_filters = jnp.einsum("tvp,tvh->vph", pixels, grad_scores, precision=highest)
    grad_offsets = jnp.sum(grad_scores, axis=0)
    grad_lead = jnp.stack([lead_time * grad_bias_out, grad_bias_out])
    sums = (
        grad_w_out,
        grad_bias_out,
        grad_bias_value,
        grad_w_value,
        grad_table,
        grad_filters,
        grad_offsets,
        grad_lead,
    )
    return (grad_pixels.reshape(row_count, VARS * PIX), sums)


def embed_finish(totals, setup, weights, params):
    (
        grad_w_out,
        grad_bias_out,
        grad_bias_value,
        grad_w_value,
        grad_table,
        grad_filters,
        grad_offsets,
        grad_lead,
    ) = totals
    query_low, key_low, constant, filters, offsets, embed_table = setup
    patch_w, agg_query = (params[0], params[3])
    key_wide = key_low.astype(wide_type)
    grad_patch_w = grad_table[: VARS * PIX].reshape(VARS, PIX, D) + jnp.einsum(
        "vph,dh->vpd", grad_filters, key_wide, precision=highest
    )
    grad_constant = grad_table[VARS * PIX :] + jnp.dot(grad_offsets, key_wide.T, precision=highest)
    grad_key = jnp.einsum("vpd,vph->dh", patch_w.astype(wide_type), grad_filters, precision=highest)
    grad_key = grad_key + jnp.dot(constant.astype(wide_type).T, grad_offsets, precision=highest)
    grad_key_low = grad_key.astype(narrow_type)
    query_heads = query_low.reshape(HEADS, HEAD).astype(wide_type)
    grad_w_key = (grad_key_low.astype(wide_type)[:, :, None] * query_heads[None, :, :]).reshape(
        D, D
    )
    grad_query = jnp.einsum(
        "dhe,dh->he",
        weights[1].reshape(D, HEADS, HEAD),
        grad_key_low,
        preferred_element_type=wide_type,
    )
    grad_query = grad_query.reshape(D).astype(narrow_type)
    grad_query_wide = grad_query.astype(wide_type)
    grad_w_query = agg_query.astype(wide_type)[:, None] * grad_query_wide[None, :]
    grad_agg_query = product(weights[0], grad_query[:, None])[:, 0]
    grad_bank = jnp.concatenate([grad_w_query, grad_w_key, grad_w_value, grad_w_out], axis=0)
    smalls = (
        grad_patch_w,
        grad_constant,
        grad_constant,
        grad_agg_query,
        jnp.stack([grad_query_wide, grad_bias_value, grad_bias_out]),
        grad_lead,
        jnp.zeros((2, D), wide_type),
        jnp.zeros((2, D), wide_type),
        jnp.zeros((3, D), wide_type),
        jnp.zeros((FF,), wide_type),
        jnp.zeros((D,), wide_type),
    )
    return (grad_bank, smalls)


def attention_scores(block_query, block_segment, key_heads, segment):
    raw_scores = jnp.einsum(
        "qhe,khe->hqk", block_query, key_heads, preferred_element_type=wide_type
    ) / math.sqrt(HEAD)
    allowed = (block_segment[:, None] == segment[None, :])[None]
    return jnp.where(allowed, raw_scores, -1e30)


def attention_forward(queries, key_rows, values, segment):
    row_count = queries.shape[0]
    block_rows = min(512, row_count)
    block_total = row_count // block_rows
    key_heads = key_rows.reshape(row_count, HEADS, HEAD)
    value_heads = values.reshape(row_count, HEADS, HEAD)

    def one_block(block_items):
        block_query, block_segment = block_items
        scores = attention_scores(block_query, block_segment, key_heads, segment)
        row_peak = jnp.max(scores, axis=-1, keepdims=True)
        exp_scores = jnp.exp(scores - row_peak)
        exp_total = jnp.sum(exp_scores, axis=-1, keepdims=True)
        probabilities = (exp_scores / exp_total).astype(narrow_type)
        mixed_heads = jnp.einsum(
            "hqk,khe->qhe", probabilities, value_heads, preferred_element_type=wide_type
        )
        return (mixed_heads.astype(narrow_type), (row_peak + jnp.log(exp_total))[:, :, 0])

    mixed_heads, log_totals = lax.map(
        one_block,
        (
            queries.reshape(block_total, block_rows, HEADS, HEAD),
            segment.reshape(block_total, block_rows),
        ),
    )
    return (mixed_heads.reshape(row_count, D), log_totals)


def attention_backward(queries, key_rows, values, segment, log_totals, grad_mixed):
    row_count = queries.shape[0]
    block_rows = min(512, row_count)
    block_total = row_count // block_rows
    key_heads = key_rows.reshape(row_count, HEADS, HEAD)
    value_heads = values.reshape(row_count, HEADS, HEAD)

    def one_block(carry_sums, block_items):
        grad_key_sum, grad_value_sum = carry_sums
        block_query, block_segment, block_log, block_grad = block_items
        scores = attention_scores(block_query, block_segment, key_heads, segment)
        probabilities = jnp.exp(scores - block_log[:, :, None])
        probs_low = probabilities.astype(narrow_type)
        grad_value_sum = grad_value_sum + jnp.einsum(
            "hqk,qhe->khe", probs_low, block_grad, preferred_element_type=wide_type
        )
        grad_probs = jnp.einsum(
            "qhe,khe->hqk", block_grad, value_heads, preferred_element_type=wide_type
        )
        grad_scores = probabilities * (
            grad_probs - jnp.sum(probabilities * grad_probs, axis=-1, keepdims=True)
        )
        grad_low = grad_scores.astype(narrow_type)
        grad_query = jnp.einsum(
            "hqk,khe->qhe", grad_low, key_heads, preferred_element_type=wide_type
        ) / math.sqrt(HEAD)
        grad_key_sum = grad_key_sum + jnp.einsum(
            "hqk,qhe->khe", grad_low, block_query, preferred_element_type=wide_type
        ) / math.sqrt(HEAD)
        return ((grad_key_sum, grad_value_sum), grad_query)

    zero_heads = jnp.zeros((row_count, HEADS, HEAD), wide_type)
    block_items = (
        queries.reshape(block_total, block_rows, HEADS, HEAD),
        segment.reshape(block_total, block_rows),
        log_totals,
        grad_mixed.reshape(block_total, block_rows, HEADS, HEAD),
    )
    (grad_key_sum, grad_value_sum), grad_queries = lax.scan(
        one_block, (zero_heads, zero_heads), block_items
    )
    return (
        grad_queries.reshape(row_count, D),
        grad_key_sum.reshape(row_count, D),
        grad_value_sum.reshape(row_count, D),
    )


def project_heads(normed_low, weights, attn_bias):
    queries = (product(normed_low, weights[0]) + attn_bias[0].astype(wide_type)).astype(narrow_type)
    key_rows = product(normed_low, weights[1]).astype(narrow_type)
    values = (product(normed_low, weights[2]) + attn_bias[1].astype(wide_type)).astype(narrow_type)
    return (queries, key_rows, values)


def feed_half(normed_low, weights, bias_in):
    inner_first = product(normed_low, weights[0]) + bias_in[:D].astype(wide_type)
    inner_second = product(normed_low, weights[1]) + bias_in[D:].astype(wide_type)
    active_first = gelu_exact(inner_first).astype(narrow_type)
    active_second = gelu_exact(inner_second).astype(narrow_type)
    partial_sum = product(active_first, weights[2]) + product(active_second, weights[3])
    return ((inner_first, inner_second), (active_first, active_second), partial_sum)


def feed_half_back(normed_low, weights, inners, actives, grad_rows):
    grad_inners = []
    for number in range(2):
        grad_active = product_right(grad_rows, weights[2 + number])
        value_out, gelu_pull = jax.vjp(gelu_exact, inners[number])
        grad_inners.append(gelu_pull(grad_active)[0].astype(narrow_type))
    grad_normed = product_right(grad_inners[0], weights[0]) + product_right(
        grad_inners[1], weights[1]
    )
    grad_bank = jnp.concatenate(
        [
            product_left(normed_low, grad_inners[0]),
            product_left(normed_low, grad_inners[1]),
            product_left(actives[0], grad_rows),
            product_left(actives[1], grad_rows),
        ],
        axis=0,
    )
    grad_bias_in = jnp.concatenate(
        [
            jnp.sum(grad_inners[0].astype(wide_type), axis=0),
            jnp.sum(grad_inners[1].astype(wide_type), axis=0),
        ]
    )
    return (grad_normed, grad_bank, grad_bias_in)


def on_device(
    patches,
    lead_times,
    short_lengths,
    cotangent,
    bank,
    patch_w,
    patch_b,
    var_emb,
    agg_query,
    agg_bias,
    lead_embed,
    norm_gain,
    norm_bias,
    attn_bias,
    fc1_bias,
    fc2_bias,
):
    params = (
        patch_w,
        patch_b,
        var_emb,
        agg_query,
        agg_bias,
        lead_embed,
        norm_gain,
        norm_bias,
        attn_bias,
        fc1_bias,
        fc2_bias,
    )
    micro_total = patches.shape[0]
    row_count = patches.shape[1]
    section_total = lax.axis_size("section")
    section_index = lax.axis_index("section")
    gathered = lax.all_gather(bank, "dp", axis=1, tiled=True)[0]
    weights = tuple((gathered[number * D : (number + 1) * D] for number in range(4)))
    short_segment, short_places = layout(short_lengths[0], row_count)
    segments = jnp.stack([short_segment, jnp.zeros((row_count,), jnp.int32)])
    places_all = jnp.stack([short_places, jnp.arange(row_count, dtype=jnp.int32)])
    valid_rows = jnp.stack([short_segment < short_lengths.shape[1], jnp.ones((row_count,), bool)])
    grad_out_all = jnp.where(valid_rows[:, :, None], cotangent, jnp.zeros_like(cotangent))
    block_rows = min(512, row_count)
    block_total = row_count // block_rows
    zeros_stream = jnp.zeros((row_count, D), narrow_type)
    zeros_final = jnp.zeros((row_count, D), wide_type)
    zeros_pixels = jnp.zeros((row_count, VARS * PIX), wide_type)
    stash_zero = (
        zeros_stream,
        zeros_stream,
        zeros_stream,
        zeros_stream,
        jnp.zeros((block_total, HEADS, block_rows), wide_type),
    )
    small_zero = tuple((jnp.zeros(array_item.shape, wide_type) for array_item in params))

    def forward_embed(operands):
        first_in, second_in, pixel_rows, places, lead_time, segment = operands
        setup = embed_setup(weights, params)

        def one_block(block_items):
            return embed_rows(block_items[0], block_items[1], lead_time, setup, weights, params)[0]

        streams = lax.map(
            one_block,
            (
                pixel_rows.reshape(block_total, block_rows, VARS * PIX),
                places.reshape(block_total, block_rows),
            ),
        )
        return (streams.reshape(row_count, D), zeros_stream, zeros_final, stash_zero)

    def forward_attend(operands):
        first_in, second_in, pixel_rows, places, lead_time, segment = operands
        stream = first_in.astype(wide_type)
        normed_low = norm_layer(
            stream, norm_gain[0].astype(wide_type), norm_bias[0].astype(wide_type)
        ).astype(narrow_type)
        queries, key_rows, values = project_heads(normed_low, weights, attn_bias)
        mixed_heads, log_totals = attention_forward(queries, key_rows, values, segment)
        new_stream = stream + product(mixed_heads, weights[3]) + attn_bias[2].astype(wide_type)
        return (new_stream.astype(narrow_type), zeros_stream, zeros_final, stash_zero)

    def forward_first(operands):
        first_in, second_in, pixel_rows, places, lead_time, segment = operands
        stream = first_in.astype(wide_type)
        normed_low = norm_layer(
            stream, norm_gain[1].astype(wide_type), norm_bias[1].astype(wide_type)
        ).astype(narrow_type)
        inners, actives, partial_sum = feed_half(normed_low, weights, fc1_bias[: 2 * D])
        return (normed_low, (stream + partial_sum).astype(narrow_type), zeros_final, stash_zero)

    def forward_second(operands):
        first_in, second_in, pixel_rows, places, lead_time, segment = operands
        inners, actives, partial_sum = feed_half(first_in, weights, fc1_bias[2 * D :])
        final_rows = second_in.astype(wide_type) + partial_sum + fc2_bias.astype(wide_type)
        return (zeros_stream, zeros_stream, final_rows, stash_zero)

    def forward_none(operands):
        return (zeros_stream, zeros_stream, zeros_final, stash_zero)

    def backward_embed(operands):
        (
            first_kept,
            second_kept,
            grad_in,
            pixel_rows,
            places,
            lead_time,
            segment,
            grad_rows,
            stash_items,
        ) = operands
        setup = embed_setup(weights, params)

        def one_block(totals, block_items):
            block_pixels, block_places, block_grad = block_items
            block_stream, saved_state = embed_rows(
                block_pixels, block_places, lead_time, setup, weights, params
            )
            block_dx, sums = embed_back(block_grad, lead_time, setup, saved_state, weights)
            return (
                tuple((total_item + sum_item for total_item, sum_item in zip(totals, sums))),
                block_dx,
            )

        zero_totals = (
            jnp.zeros((D, D), wide_type),
            jnp.zeros((D,), wide_type),
            jnp.zeros((D,), wide_type),
            jnp.zeros((D, D), wide_type),
            jnp.zeros((VARS * PIX + VARS, D), wide_type),
            jnp.zeros((VARS, PIX, HEADS), wide_type),
            jnp.zeros((VARS, HEADS), wide_type),
            jnp.zeros((2, D), wide_type),
        )
        block_items = (
            pixel_rows.reshape(block_total, block_rows, VARS * PIX),
            places.reshape(block_total, block_rows),
            grad_in.reshape(block_total, block_rows, D),
        )
        totals, grad_pixels = lax.scan(one_block, zero_totals, block_items)
        grad_bank, smalls = embed_finish(totals, setup, weights, params)
        return (zeros_stream, grad_bank, smalls, grad_pixels.reshape(row_count, VARS * PIX))

    def backward_attend(operands):
        (
            first_kept,
            second_kept,
            grad_in,
            pixel_rows,
            places,
            lead_time,
            segment,
            grad_rows,
            stash_items,
        ) = operands
        stream = first_kept.astype(wide_type)
        normed, norm_pull = jax.vjp(
            norm_layer, stream, norm_gain[0].astype(wide_type), norm_bias[0].astype(wide_type)
        )
        normed_low = normed.astype(narrow_type)
        queries, key_rows, values = project_heads(normed_low, weights, attn_bias)
        mixed_heads, log_totals = attention_forward(queries, key_rows, values, segment)
        grad_in_wide = grad_in.astype(wide_type)
        grad_w_out = product_left(mixed_heads, grad_in)
        grad_mixed = product_right(grad_in, weights[3]).astype(narrow_type)
        grad_queries, grad_keys, grad_values = attention_backward(
            queries, key_rows, values, segment, log_totals, grad_mixed
        )
        grad_queries = grad_queries.astype(narrow_type)
        grad_keys = grad_keys.astype(narrow_type)
        grad_values = grad_values.astype(narrow_type)
        grad_normed = (
            product_right(grad_queries, weights[0])
            + product_right(grad_keys, weights[1])
            + product_right(grad_values, weights[2])
        )
        grad_stream, grad_gain, grad_shift = norm_pull(grad_normed)
        grad_send = (grad_in_wide + grad_stream).astype(narrow_type)
        grad_bank = jnp.concatenate(
            [
                product_left(normed_low, grad_queries),
                product_left(normed_low, grad_keys),
                product_left(normed_low, grad_values),
                grad_w_out,
            ],
            axis=0,
        )
        bias_rows = jnp.stack(
            [
                jnp.sum(grad_queries.astype(wide_type), axis=0),
                jnp.sum(grad_values.astype(wide_type), axis=0),
                jnp.sum(grad_in_wide, axis=0),
            ]
        )
        smalls = (
            small_zero[:6]
            + (
                jnp.zeros((2, D), wide_type).at[0].set(grad_gain),
                jnp.zeros((2, D), wide_type).at[0].set(grad_shift),
                bias_rows,
            )
            + small_zero[9:]
        )
        return (grad_send, grad_bank, smalls, zeros_pixels)

    def backward_first(operands):
        (
            first_kept,
            second_kept,
            grad_in,
            pixel_rows,
            places,
            lead_time,
            segment,
            grad_rows,
            stash_items,
        ) = operands
        stream = first_kept.astype(wide_type)
        normed, norm_pull = jax.vjp(
            norm_layer, stream, norm_gain[1].astype(wide_type), norm_bias[1].astype(wide_type)
        )
        normed_low = normed.astype(narrow_type)
        inners, actives, partial_sum = feed_half(normed_low, weights, fc1_bias[: 2 * D])
        grad_normed, grad_bank, grad_bias_in = feed_half_back(
            normed_low, weights, inners, actives, grad_rows
        )
        grad_stream, grad_gain, grad_shift = norm_pull(grad_normed + grad_in.astype(wide_type))
        grad_send = (grad_rows.astype(wide_type) + grad_stream).astype(narrow_type)
        smalls = small_zero[:6] + (
            jnp.zeros((2, D), wide_type).at[1].set(grad_gain),
            jnp.zeros((2, D), wide_type).at[1].set(grad_shift),
            small_zero[8],
            jnp.zeros((FF,), wide_type).at[: 2 * D].set(grad_bias_in),
            small_zero[10],
        )
        return (grad_send, grad_bank, smalls, zeros_pixels)

    def backward_second(operands):
        (
            first_kept,
            second_kept,
            grad_in,
            pixel_rows,
            places,
            lead_time,
            segment,
            grad_rows,
            stash_items,
        ) = operands
        inners, actives, partial_sum = feed_half(first_kept, weights, fc1_bias[2 * D :])
        grad_normed, grad_bank, grad_bias_in = feed_half_back(
            first_kept, weights, inners, actives, grad_rows
        )
        smalls = small_zero[:9] + (
            jnp.zeros((FF,), wide_type).at[2 * D :].set(grad_bias_in),
            jnp.sum(grad_rows.astype(wide_type), axis=0),
        )
        return (grad_normed.astype(narrow_type), grad_bank, smalls, zeros_pixels)

    def backward_none(operands):
        return (zeros_stream, jnp.zeros((4 * D, D), wide_type), small_zero, zeros_pixels)

    forward_list = [forward_embed, forward_attend, forward_first, forward_second, forward_none]
    backward_list = [
        backward_embed,
        backward_attend,
        backward_first,
        backward_second,
        backward_none,
    ]
    tick_total = micro_total + section_total - 1
    first_message, second_message = (zeros_stream, zeros_stream)
    kept_first = jnp.zeros((micro_total, row_count, D), narrow_type)
    kept_second = jnp.zeros((micro_total, row_count, D), narrow_type)
    stash_all = tuple(
        (
            jnp.zeros((micro_total,) + array_item.shape, array_item.dtype)
            for array_item in stash_zero
        )
    )
    final_all = jnp.zeros((micro_total, row_count, D), wide_type)
    for tick_number in range(tick_total):
        micro_index = tick_number - section_index
        running = jnp.logical_and(micro_index >= 0, micro_index < micro_total)
        slot_index = jnp.clip(micro_index, 0, micro_total - 1)
        kept_first = kept_first.at[slot_index].set(
            jnp.where(running, first_message, kept_first[slot_index])
        )
        kept_second = kept_second.at[slot_index].set(
            jnp.where(running, second_message, kept_second[slot_index])
        )
        branch = jnp.where(running, section_index, section_total)
        operands = (
            first_message,
            second_message,
            patches[slot_index],
            places_all[slot_index],
            lead_times[slot_index, 0],
            segments[slot_index],
        )
        first_out, second_out, final_rows, stash_items = lax.switch(branch, forward_list, operands)
        final_all = final_all.at[slot_index].add(final_rows)
        stash_all = tuple(
            (
                buffer.at[slot_index].set(jnp.where(running, array_item, buffer[slot_index]))
                for buffer, array_item in zip(stash_all, stash_items)
            )
        )
        if tick_number < tick_total - 1:
            first_message, second_message = (
                from_behind(shortened(first_out), "section", 1).astype(first_out.dtype),
                from_behind(shortened(second_out), "section", 1).astype(second_out.dtype),
            )
    grad_message = zeros_stream
    bank_total = jnp.zeros((4 * D, D), wide_type)
    small_total = small_zero
    pixel_total = jnp.zeros((micro_total, row_count, VARS * PIX), wide_type)
    for tick_number in range(tick_total):
        micro_index = tick_number - (section_total - 1 - section_index)
        running = jnp.logical_and(micro_index >= 0, micro_index < micro_total)
        slot_index = jnp.clip(micro_index, 0, micro_total - 1)
        branch = jnp.where(running, section_index, section_total)
        operands = (
            kept_first[slot_index],
            kept_second[slot_index],
            grad_message,
            patches[slot_index],
            places_all[slot_index],
            lead_times[slot_index, 0],
            segments[slot_index],
            grad_out_all[slot_index],
            tuple((buffer[slot_index] for buffer in stash_all)),
        )
        grad_send, grad_bank, smalls, grad_pixels = lax.switch(branch, backward_list, operands)
        bank_total = bank_total + grad_bank
        small_total = tuple(
            (total_item + sum_item for total_item, sum_item in zip(small_total, smalls))
        )
        pixel_total = pixel_total.at[slot_index].add(grad_pixels)
        if tick_number < tick_total - 1:
            grad_message = jax.tree.map(
                lambda part, own: part.astype(own.dtype),
                from_behind(shortened(grad_send), "section", -1),
                grad_send,
            )
    bank_share = lax.psum_scatter(
        bank_total.astype(jnp.bfloat16), "dp", scatter_dimension=0, tiled=True
    ).astype(jnp.float32)[None]
    small_sums = lax.psum(small_total, ("section", "dp"))
    output_share, pixel_share = (
        lax.psum_scatter(
            final_all.astype(jnp.bfloat16), "section", scatter_dimension=2, tiled=True
        ).astype(jnp.float32),
        lax.psum_scatter(
            pixel_total.astype(jnp.bfloat16), "section", scatter_dimension=2, tiled=True
        ).astype(jnp.float32),
    )
    output_low = output_share.astype(narrow_type)
    return (output_low, pixel_share, bank_share) + tuple(small_sums)


def solution(mesh):
    ins, outs = specs()
    small_slice = mesh.shape["section"] == 4 and mesh.shape["dp"] == 8
    body = on_device_fast if small_slice else on_device
    return jax.shard_map(body, mesh=mesh, in_specs=ins, out_specs=outs, check_vma=False)
```

```python
import functools
import math

import jax
import jax.numpy as jnp
from jax import lax
from jax.experimental import pallas as pl
from jax.experimental.pallas import tpu as pltpu
from jax.sharding import PartitionSpec as P

D = 1024
HEADS = 16
HEAD = 64
FF = 4096
VARS = 48
PIX = 4
F32 = jnp.float32
BF = jnp.bfloat16
MESH = pl.DeviceIdType.MESH
ROWS = 512
GROUP = 256
OWN = 128


def mm(a, b):
    return jnp.dot(a, b, preferred_element_type=F32)


def mm_nt(a, b):
    return lax.dot_general(a, b, (((1,), (1,)), ((), ())), preferred_element_type=F32)


def mm_tn(a, b):
    return lax.dot_general(a, b, (((0,), (0,)), ((), ())), preferred_element_type=F32)


def loop(count, body):
    def step(i, carry):
        body(i)
        return carry

    lax.fori_loop(0, count, step, 0)


def at(start, size, unit):
    return pl.ds(pl.multiple_of(start, unit), size)


def iota(shape, axis):
    return lax.broadcasted_iota(jnp.int32, shape, axis)


def normed_rows(x, gain, shift):
    centre = x - jnp.mean(x, axis=1, keepdims=True)
    rs = lax.rsqrt(jnp.mean(centre * centre, axis=1, keepdims=True) + 1e-5)
    return centre * rs * gain + shift


def norm_back(x, g, gain):
    centre = x - jnp.mean(x, axis=1, keepdims=True)
    rs = lax.rsqrt(jnp.mean(centre * centre, axis=1, keepdims=True) + 1e-5)
    xhat = centre * rs
    q = g * gain
    gx = rs * (q - jnp.mean(q, axis=1, keepdims=True) - xhat * jnp.mean(q * xhat, axis=1, keepdims=True))
    return gx, jnp.sum(g * xhat, axis=0, keepdims=True), jnp.sum(g, axis=0, keepdims=True)


def column_sum(x):
    return jnp.sum(x, axis=0, keepdims=True)


class Place:
    def __init__(self):
        self.s = lax.axis_index("section")
        j = lax.axis_index("dp")
        self.z = lax.div(j, 2)
        self.c = lax.rem(j, 2)
        self.outer = (self.z == 0) | (self.z == 3)
        self.far = jnp.where(self.outer, self.z ^ 2, self.z ^ 3)

    def dev(self, s, z, c):
        return (s, z * 2 + c)


def remote(src, dst, ss, rs, dev):
    return pltpu.make_async_remote_copy(
        src_ref=src, dst_ref=dst, send_sem=ss, recv_sem=rs, device_id=dev, device_id_type=MESH
    )


def arrived(dst, sem):
    pltpu.make_async_copy(dst, dst, sem).wait()


def sent(src, sem):
    pltpu.make_async_copy(src, src, sem).wait()


def barrier(devs):
    sem = pltpu.get_barrier_semaphore()
    for dev in devs:
        pl.semaphore_signal(sem, 1, device_id=dev, device_id_type=MESH)
    pl.semaphore_wait(sem, len(devs))


SCRATCH = dict(
    vec=((24, 1024), F32),
    table=((256, 1024), BF),
    tabT=((1024, 256), BF),
    msgs=((4, 512, 256), BF),
    W=((4, 4, 2, 512, 256), BF),
    WF=((2, 4, 2, 512, 256), BF),
    kqF=((16, 1024), BF),
    gt=((4, 256, 256), BF),
    qbuf=((2, 8, 1024), F32),
    qb=((16, 1024), BF),
    kq=((2, 16, 512), BF),
    mT=((1024, 256), BF),
    mS=((512, 256), BF),
    patT=((192, 512), BF),
    fill=((1536, 192), BF),
    fo=((16, 256), F32),
    att=((768, 512), F32),
    op=((256, 512), BF),
    op1=((4, 256, 128), BF),
    hT=((1024, 512), BF),
    hrow=((512, 1024), BF),
    acc=((512, 1024), F32),
    st0=((512, 1024), BF),
    nrm=((512, 1024), BF),
    nrm2=((512, 1024), BF),
    tr=((1024, 512), BF),
    q=((512, 256), BF),
    k=((512, 256), BF),
    v=((512, 256), BF),
    attp=((8, 256, 256), F32),
    mix=((512, 1024), BF),
    st1=((512, 1024), BF),
    act=((4, 512, 256), BF),
    gact=((4, 512, 256), F32),
    gin=((4, 512, 256), BF),
    gout=((512, 1024), BF),
    rsS=((512, 1024), BF),
    rsR=((4, 128, 1024), BF),
    gs=((2, 128, 1024), BF),
    gmS=((4, 128, 256), BF),
    gm=((512, 256), BF),
    ga=((512, 256), BF),
    gb=((512, 256), BF),
    gq=((3, 512, 256), BF),
    CR=((13, 512, 256), BF),
    RC=((2, 4, 512, 256), BF),
    RA=((4, 512, 256), BF),
    RB=((4, 512, 256), BF),
    FR=((4, 512, 256), BF),
    outR=((4, 512, 256), BF),
    gh=((128, 1024), BF),
    ghT=((1024, 128), BF),
    gpT=((192, 128), F32),
    gsc=((768, 128), F32),
    small=((16, 1024), F32),
    pixS=((4, 48, 128), BF),
    pixR=((4, 48, 128), BF),
    gall=((256, 1024), BF),
    fin=((256, 1024), BF),
    fromc=((128, 1024), BF),
    fromp=((4, 32, 1024), BF),
    fromz=((4, 32, 1024), BF),
    fc=((2, 16, 256), F32),
    fp=((4, 16, 256), F32),
    fz=((4, 16, 256), F32),
    gqv=((16, 1024), BF),
    qx=((2, 8, 1024), F32),
    gaq=((2, 8, 512), F32),
)

SEMS = dict(
    sIn=(14,),
    sRes=(6,),
    rW=(4, 4, 2),
    rF=(4, 2),
    rH=(4, 2, 2),
    rA=(2,),
    sA=(4, 2),
    sAo=(2, 2),
    sAf=(2,),
    sAx=(3, 2),
    sAc=(4, 2),
    sMsg=(4,),
    sOwn=(4, 2),
    sFwd=(4, 4, 2),
    sFx=(3,),
    sFc=(4,),
    sGt=(3,),
    rGt=(4,),
    rQ=(2,),
    sQ=(2,),
    rK=(2,),
    sK=(16,),
    rMx=(1,),
    sMx=(1,),
    rM=(4, 2),
    sMa=(4,),
    sMz=(3,),
    sMp=(3,),
    sMc=(4,),
    sMix=(2, 3),
    rMix=(2, 4),
    sOut=(4,),
    rOut=(4,),
    sR=(2, 4),
    rR=(2, 4),
    sG=(3, 4),
    rG=(3, 4),
    sC=(4, 4),
    rC=(4, 4),
    sZ=(4, 4),
    rRC=(2, 4),
    rRA=(4,),
    rRB=(4,),
    sFin=(4,),
    rFin=(4,),
    sP=(4,),
    rP=(4,),
    sAll=(14,),
    rAll=(14,),
    sFo=(8,),
    rFo=(12,),
    sGq=(18,),
    rGq=(2,),
    sGa=(16,),
    rGa=(2,),
)
NAMES = list(SCRATCH) + list(SEMS)


class Refs:
    pass


def block_kernel(*refs):
    sources, lead, lens = refs[0:14], refs[14], refs[15]
    targets, rest = refs[16:22], refs[22:]
    held, results, scratch = rest[0:14], rest[14:20], rest[20:]
    pat, cot, bank, patch, patch_b, var_emb, agg_query, agg_bias, lead_embed = held[0:9]
    norm_gain, norm_bias, attn_bias, fc1, fc2 = held[9:14]
    out, gpix, gbank, gtab, sums, rows_out = results
    R = Refs()
    for name, ref in zip(NAMES, scratch):
        setattr(R, name, ref)
    loads = [pltpu.make_async_copy(a, b, R.sIn.at[i]) for i, (a, b) in enumerate(zip(sources, held))]
    for i in (2, *range(3, 14), 0, 1):
        loads[i].start()
    here = Place()
    s, z, c = here.s, here.z, here.c
    dev = here.dev
    outer = here.outer
    inner = jnp.logical_not(outer)
    sib = dev(s, z, 1 - c)
    is_row = (z >= 2) & ((s >= 2) | ((s == 0) & (z == 2)))
    peers = [s ^ 1, s ^ 2, s ^ 3]
    layers = [z ^ 1, z ^ 2, z ^ 3]
    others = [(s ^ i, z ^ k) for k in range(4) for i in range(4) if (i, k) != (0, 0)]
    vec, table = R.vec, R.table
    when = pl.when
    no = jnp.logical_not

    barrier([dev(p, k, c) for p, k in others] + [dev(p, z, 1 - c) for p in peers] + [sib])

    loads[2].wait()
    first_owner = (s == 0) & (z == 0)
    key_owner = (s == 0) & (z == 1)
    value_owner = (s == 0) & (z == 2)

    late = value_owner
    used = no((s == 0) & (z < 3))

    @when(no(is_row) & used)
    def _():
        for p in range(4):
            R.msgs[p] = bank[:, p * 256 : (p + 1) * 256]

    @when(is_row)
    def _():
        for m in range(4):
            q, h = m // 2, m % 2
            for n in range(2):
                lo = (2 * h + n) * 256
                R.msgs[m, n * 256 : (n + 1) * 256, :] = bank[q * 256 : (q + 1) * 256, lo : lo + 256]

    def message(m):
        tp = jnp.where(is_row, 2 * c + m // 2, m)
        tc = jnp.where(is_row, m % 2, c)
        return tp, tc, (tp == s) & (tc == c)

    def scatter(cond):
        for m in range(4):
            tp, tc, own = message(m)

            @when(cond & own)
            def _():
                pltpu.make_async_copy(R.msgs.at[m], R.W.at[z, s, c], R.rW.at[z, s, c]).start()

            @when(cond & no(own))
            def _():
                remote(R.msgs.at[m], R.W.at[z, s, tc], R.sMsg.at[m], R.rW.at[z, s, tc], dev(tp, z, tc)).start()

    out_owner = (s == 0) & (z == 3)

    def half_of(p, h):
        return R.WF.at[0, p, c, h * 256 : (h + 1) * 256]

    def out_half(h):
        return R.W.at[3, 0, c, h * 256 : (h + 1) * 256]

    @when(out_owner)
    def _():
        for h in range(2):
            for m in range(4):
                block = R.msgs.at[m, h * 256 : (h + 1) * 256]
                if m == 0:
                    pltpu.make_async_copy(block, out_half(h), R.rA.at[h]).start()
                else:
                    remote(block, out_half(h), R.sA.at[m, h], R.rA.at[h], dev(m, z, c)).start()

    scatter(used & no(out_owner))

    for i in range(3, 14):
        loads[i].wait()
    vec[0:3, :] = agg_bias[...].astype(F32)
    vec[3:5, :] = lead_embed[...].astype(F32)
    vec[5:7, :] = norm_gain[...].astype(F32)
    vec[7:9, :] = norm_bias[...].astype(F32)
    vec[9:12, :] = attn_bias[...].astype(F32)
    for i in range(4):
        vec[12 + i : 13 + i, :] = fc1[i * 1024 : (i + 1) * 1024][None].astype(F32)
    vec[16:17, :] = fc2[...][None].astype(F32)
    vec[17:18, :] = agg_query[...][None].astype(F32)

    @when(first_owner)
    def _():
        part = jnp.broadcast_to(vec[17:18, at(c * 512, 512, 512)].astype(BF), (16, 512))
        R.qbuf[0] = mm(part, bank[...])[0:8]
        remote(R.qbuf.at[0], R.qbuf.at[1], R.sQ.at[0], R.rQ.at[0], sib).start()

    perm = jnp.where(
        (iota((192, 192), 0) // 48 == iota((192, 192), 1) % 4) & (iota((192, 192), 0) % 48 == iota((192, 192), 1) // 4),
        1.0,
        0.0,
    ).astype(BF)
    for p in range(PIX):
        table[p * 48 : (p + 1) * 48, :] = patch[:, p, :]
    table[192:240, :] = (patch_b[...].astype(F32) + var_emb[...].astype(F32)).astype(BF)
    table[240:256, :] = jnp.zeros((16, 1024), BF)

    other_rows = at((1 - c) * 512, 512, 512)
    half_rows = at(c * 512, 512, 512)

    @when(value_owner)
    def _():
        for i in range(4):
            R.tabT[i * 256 : (i + 1) * 256, :] = table[:, i * 256 : (i + 1) * 256].T
        for h in range(2):
            R.gact[h] = mm_tn(bank[:, h * 512 : (h + 1) * 512], R.tabT[half_rows, :])
        remote(R.gact.at[1 - c], R.gact.at[2], R.sMx.at[0], R.rMx.at[0], sib).start()

    @when(first_owner)
    def _():
        arrived(R.qbuf.at[1], R.rQ.at[0])
        total = R.qbuf[0] + R.qbuf[1] + vec[0:1, :]
        total = total.astype(BF)
        R.qb[...] = jnp.concatenate([total, total], axis=0)
        remote(R.qb, R.qb, R.sQ.at[1], R.rQ.at[1], dev(0, 1, c)).start()

    def piece_of(p, h):
        return R.mT.at[at(p * 256 + h * 128, 128, 128), :]

    def my_piece(m):
        return R.mS.at[(m // 2) * 256 + (m % 2) * 128 : (m // 2) * 256 + (m % 2) * 128 + 128, :]

    @when(value_owner)
    def _():
        arrived(R.gact.at[2], R.rMx.at[0])
        sent(R.gact.at[2], R.sMx.at[0])
        bias = jnp.broadcast_to(vec[1:2, half_rows], (8, 512)).T[:, 0:1]
        total = R.gact[c] + R.gact[2]
        R.mS[...] = jnp.where(iota((1, 256), 1) == 240, bias, total).astype(BF)
        for m in range(4):
            q, h = m // 2, m % 2
            tp = 2 * c + q
            own = (tp == s) & (c == h)

            @when(own)
            def _():
                pltpu.make_async_copy(my_piece(m), piece_of(tp, h), R.rM.at[tp, h]).start()

            @when(no(own))
            def _():
                remote(my_piece(m), piece_of(tp, h), R.sMa.at[m], R.rM.at[tp, h], dev(tp, z, h)).start()

    @when(key_owner)
    def _():
        arrived(R.qb, R.rQ.at[1])
        masked = jnp.where(iota((16, 1024), 1) // HEAD == iota((16, 1024), 0), R.qb[...].astype(F32), 0.0).astype(BF)
        R.kq[c] = mm_nt(masked, bank[...]).astype(BF)
        for i, (p, k) in enumerate(others):
            remote(R.kq.at[c], R.kq.at[c], R.sK.at[i], R.rK.at[c], dev(p, k, c)).start()

    def at_least(zz, b):
        return zz == 3 if b == 0 else zz >= 0

    def full_of(zz, b):
        return (zz == 3) if b == 1 else None

    def spread(zz, b):
        block = R.W.at[zz, b, c]
        whole = full_of(zz, b)

        def to_sibling():
            remote(block, block, R.sFwd.at[zz, b, 0], R.rW.at[zz, b, c], sib).start()

        def to_layer():
            pltpu.make_async_copy(block, R.WF.at[1, s, c], R.rF.at[s, c]).start()
            for i, p in enumerate(peers):
                remote(block, R.WF.at[1, s, c], R.sFx.at[i], R.rF.at[s, c], dev(p, z, c)).start()

        if whole is None:
            to_sibling()
        elif isinstance(whole, bool):
            (to_layer if whole else to_sibling)()
        else:
            when(no(whole))(to_sibling)
            when(whole)(to_layer)

    def out_layer(h):
        pltpu.make_async_copy(out_half(h), half_of(s, h), R.rH.at[s, c, h]).start()
        for i, p in enumerate(peers):
            remote(out_half(h), half_of(s, h), R.sAx.at[i, h], R.rH.at[s, c, h], dev(p, z, c)).start()

    def out_along(cond):
        @when(cond)
        def _():
            for h in range(2):
                arrived(out_half(h), R.rA.at[h])
                remote(out_half(h), out_half(h), R.sAo.at[1, h], R.rA.at[h], dev(s, z ^ 2, c)).start()
            for h in range(2):
                remote(out_half(h), out_half(h), R.sAo.at[0, h], R.rA.at[h], dev(s, z ^ 1, c)).start()

    def along(cond, b, way):
        block = R.W.at[z, b, c]
        zz = z ^ 1 if way == 0 else here.far

        @when(cond)
        def _():
            remote(block, block, R.sOwn.at[b, way], R.rW.at[z, b, c], dev(s, zz, c)).start()

    def ready(cond, b):
        @when(cond)
        def _():
            arrived(R.W.at[z, b, c], R.rW.at[z, b, c])

    def aside(cond, b):
        @when(cond)
        def _():
            spread(z, b)

    def step(cond, b, side=True):
        ready(cond, b)
        along(cond, b, 1)
        along(cond, b, 0)
        if side:
            aside(cond, b)

    def foreign(zz, b, cond=True):
        block = R.W.at[zz, b, c]

        @when(cond & (z != zz))
        def _():
            arrived(block, R.rW.at[zz, b, c])

        @when(cond & (z != zz) & inner & (z ^ 1 != zz))
        def _():
            remote(block, block, R.sFwd.at[zz, b, 1], R.rW.at[zz, b, c], dev(s, z ^ 1, c)).start()

        @when(cond & (z != zz))
        def _():
            spread(zz, b)

    always = z >= 0
    top = z == 3
    @when(z == 2)
    def _():
        arrived(piece_of(s, c), R.rM.at[s, c])
        for i, zz in enumerate(layers):
            remote(piece_of(s, c), piece_of(s, c), R.sMz.at[i], R.rM.at[s, c], dev(s, zz, c)).start()
        for i, p in enumerate(peers):
            remote(piece_of(s, c), piece_of(s, c), R.sMp.at[i], R.rM.at[s, c], dev(p, z, c)).start()

    out_along(top & (s == 0))
    step(no(top) & (s == 1), 1)
    first_feed = z != 2
    for b in (2, 3):
        mine_first = (s == b) & first_feed
        ready(mine_first, b)
        along(mine_first, b, 1)
        along(mine_first & inner, b, 0)
        aside(mine_first, b)

    tcol = iota((GROUP, 1), 0).astype(F32)
    trow = iota((1, GROUP), 1).astype(F32)
    start_col = jnp.zeros((GROUP, 1), F32)
    seg_col = jnp.zeros((GROUP, 1), F32)
    seg_row = jnp.zeros((1, GROUP), F32)
    end = jnp.float32(0.0)
    for i in range(4):
        end = end + lens[0, i].astype(F32)
        past = tcol >= end
        seg_col = seg_col + jnp.where(past, 1.0, 0.0)
        seg_row = seg_row + jnp.where(trow >= end, 1.0, 0.0)
        start_col = jnp.maximum(start_col, jnp.where(past, end, 0.0))
    place_short = tcol - start_col
    valid = seg_col < 3.5
    lead_short = lead[0, 0]
    lead_long = lead[0, 1]
    freq = jnp.exp(-math.log(10000.0) * 2.0 * iota((1, 512), 1).astype(F32) / D)

    def positions(g):
        place = place_short if g == 0 else tcol
        lead_g = lead_short if g == 0 else lead_long
        base = lead_g * vec[3:4, :] + vec[4:5, :] + vec[2:3, :]
        angle = place * freq
        R.acc[g * GROUP : (g + 1) * GROUP, 0:512] = jnp.sin(angle) + base[:, 0:512]
        R.acc[g * GROUP : (g + 1) * GROUP, 512:1024] = jnp.cos(angle) + base[:, 512:1024]

    positions(0)
    out_along(top & (s != 0))
    step(no(top) & (s != 1), 1)
    step(top, 1, False)

    positions(1)

    gout = R.gout
    loads[1].wait()
    gout[0:GROUP, :] = jnp.where(valid, cot[0:GROUP, :].astype(F32), 0.0).astype(BF)
    gout[GROUP:ROWS, :] = cot[GROUP:ROWS, :]

    @when(no(key_owner))
    def _():
        arrived(R.kq.at[c], R.rK.at[c])

    remote(R.kq.at[c], R.kq.at[c], R.sK.at[15], R.rK.at[c], sib).start()
    loads[0].wait()
    for g in range(2):
        R.patT[:, g * 256 : (g + 1) * 256] = mm(perm, pat[g]).astype(BF)

    @when(z != 2)
    def _():
        arrived(piece_of(s, c), R.rM.at[s, c])
        for i, p in enumerate(peers):
            remote(piece_of(s, c), piece_of(s, c), R.sMp.at[i], R.rM.at[s, c], dev(p, z, c)).start()

    @when(top)
    def _():
        for h in range(2):
            out_layer(h)

    for b in (2, 3):
        mine_first = (s == b) & first_feed
        ready(no(mine_first), b)
        along(no(mine_first), b, 1)
        aside(no(mine_first), b)
    along(outer, 2, 0)
    along(outer, 3, 0)
    scatter(late)

    arrived(R.kq.at[1 - c], R.rK.at[1 - c])
    R.kqF[:, 0:512] = R.kq[0]
    R.kqF[:, 512:1024] = R.kq[1]
    kq_full = R.kqF[...]
    R.fo[...] = mm_nt(kq_full, table[...])

    def fill_head(h):
        row = R.fo[pl.ds(h, 1), 0:192]
        value = jnp.where(iota((48, 192), 1) % 48 == iota((48, 192), 0), row, 0.0)
        high = value.astype(BF)
        R.fill[at(h * 48, 48, 16), :] = high
        R.fill[at(768 + h * 48, 48, 16), :] = (value - high.astype(F32)).astype(BF)

    loop(HEADS, fill_head)

    def score_part(i):
        lo = i * 256
        R.att[at(lo, 256, 256), :] = mm(R.fill[at(lo, 256, 256), :], R.patT[...]) + mm(
            R.fill[at(768 + lo, 256, 256), :], R.patT[...]
        )

    loop(3, score_part)

    @when(no(top))
    def _():
        for h in range(2):
            arrived(out_half(h), R.rA.at[h])

            @when(z == 1)
            def _():
                remote(out_half(h), out_half(h), R.sAf.at[h], R.rA.at[h], dev(s, z ^ 1, c)).start()

            out_layer(h)

    for i, p in enumerate([s] + peers):
        if i > 0:
            arrived(piece_of(p, c), R.rM.at[p, c])
        remote(piece_of(p, c), piece_of(p, c), R.sMc.at[p], R.rM.at[p, c], sib).start()

    for p in range(4):
        arrived(piece_of(p, 1 - c), R.rM.at[p, 1 - c])

    for zz in range(3):
        foreign(zz, 1, inner)
    R.op[240:256, :] = jnp.where(iota((16, 512), 0) == 0, 1.0, 0.0).astype(BF)
    r48 = iota((48, 256), 0)
    c48 = iota((48, 256), 1)

    def weights_of(op, low, cols):
        lowf = low.astype(F32)
        for p in range(4):
            op[p * 48 : (p + 1) * 48, :] = (lowf * R.patT[p * 48 : (p + 1) * 48, cols].astype(F32)).astype(BF)
        op[192:240, :] = low

    def embed_head(h):
        offset = jnp.sum(jnp.where(c48 == r48 + 192, R.fo[pl.ds(h, 1), :], 0.0), axis=1, keepdims=True)
        rows = at(h * 48, 48, 16)
        scores = (R.att[rows, :] + offset) * (1.0 / math.sqrt(HEAD))
        peak = jnp.max(scores, axis=0, keepdims=True)
        e = jnp.exp(scores - peak)
        prob = e / jnp.sum(e, axis=0, keepdims=True)
        R.att[rows, :] = prob
        weights_of(R.op, prob.astype(BF), slice(None))
        hrows = at(h * 64, 64, 64)
        R.hT[hrows, :] = mm(R.mT[hrows, :], R.op[...]).astype(BF)

    loop(HEADS, embed_head)

    def pass_out():
        for h in range(2):
            for p in [s] + peers:
                arrived(half_of(p, h), R.rH.at[p, c, h])
                remote(half_of(p, h), half_of(p, h), R.sAc.at[p, h], R.rH.at[p, c, h], sib).start()

    def wait_out():
        for h in range(2):
            for p in range(4):
                arrived(R.WF.at[0, p, 1 - c, h * 256 : (h + 1) * 256], R.rH.at[p, 1 - c, h])

    def pass_on():
        for p in [s] + peers:
            block = R.WF.at[1, p, c]
            arrived(block, R.rF.at[p, c])
            remote(block, block, R.sFc.at[p], R.rF.at[p, c], sib).start()

    def wait_whole():
        for p in range(4):
            arrived(R.WF.at[1, p, 1 - c], R.rF.at[p, 1 - c])

    pass_out()

    def turn_tile(i):
        rows = at(i * 256, 256, 256)
        R.hrow[:, rows] = R.hT[rows, :].T

    loop(4, turn_tile)
    for zz in range(3):
        foreign(zz, 1, outer)
    foreign(3, 1, inner)

    @when(top)
    def _():
        spread(3, 1)

    foreign(z ^ 3, 2, inner)
    along(inner & no((s == 2) & first_feed), 2, 0)
    along(inner & no((s == 3) & first_feed), 3, 0)
    wait_out()

    def stream0_part(n):
        cols = at(n * 256, 256, 256)
        R.st0[:, cols] = (mm(R.hrow[...], R.WF[0, n].reshape(1024, 256)) + R.acc[:, cols]).astype(BF)

    loop(4, stream0_part)
    foreign(3, 1, outer)

    def norm_into(src, dst, which, g):
        def part(i):
            rows = at(g * 256 + i * 64, 64, 64)
            dst[rows, :] = normed_rows(
                src[rows, :].astype(F32), vec[5 + which : 6 + which, :], vec[7 + which : 8 + which, :]
            ).astype(BF)

        loop(4, part)

    norm_into(R.st0, R.nrm, 0, 0)
    norm_into(R.st0, R.nrm, 0, 1)
    foreign(z ^ 3, 3, inner)


    own_cols = at(s * 256, 256, 256)
    own_rows = at(s * OWN, OWN, OWN)

    def wait_half(zz, b):
        arrived(R.W.at[zz, b, 1 - c], R.rW.at[zz, b, 1 - c])

    def project(zz, dst, bias):
        wait_half(zz, 1)
        weight = R.W[zz, 1].reshape(1024, 256)
        for g in range(2):
            rows = slice(g * 256, (g + 1) * 256)
            value = mm(R.nrm[rows, :], weight)
            if bias is not None:
                value = value + vec[bias : bias + 1, own_cols]
            dst[rows, :] = value.astype(BF)

    project(0, R.q, 9)
    project(1, R.k, None)
    project(2, R.v, 10)

    lane_head = iota((1, 256), 1) // HEAD

    def only(hh, x):
        return jnp.where(lane_head == hh, x.astype(F32), 0.0).astype(BF)

    allowed = seg_col == seg_row

    def attend(g):
        rows = slice(g * 256, (g + 1) * 256)
        total = jnp.zeros((256, 256), F32)
        for hh in range(4):
            scores = mm_nt(R.q[rows, :], only(hh, R.k[rows, :])) * (1.0 / math.sqrt(HEAD))
            if g == 0:
                scores = jnp.where(allowed, scores, -1e30)
            e = jnp.exp(scores - jnp.max(scores, axis=1, keepdims=True))
            prob = e / jnp.sum(e, axis=1, keepdims=True)
            R.attp[g * 4 + hh] = prob
            total = total + mm(prob.astype(BF), only(hh, R.v[rows, :]))
        R.mix[rows, own_cols] = total.astype(BF)

    def mixed_of(g, p):
        return R.mix.at[g * 256 : (g + 1) * 256, at(p * 256, 256, 256)]

    for g in range(2):
        attend(g)
        for i, p in enumerate(peers):
            remote(mixed_of(g, s), mixed_of(g, s), R.sMix.at[g, i], R.rMix.at[g, s], dev(p, z, c)).start()

    step(z == 2, 0)
    for b in (2, 3):
        foreign(z ^ 2, b, inner)
    pass_on()
    wait_whole()
    def stream1_part(g, n):
        rows = slice(g * 256, (g + 1) * 256)
        cols = at(n * 256, 256, 256)
        value = mm(R.mix[rows, :], R.WF[1, n].reshape(1024, 256)) + vec[11:12, cols]
        R.st1[rows, cols] = (value + R.st0[rows, cols].astype(F32)).astype(BF)

    for g in range(2):
        for p in peers:
            arrived(mixed_of(g, p), R.rMix.at[g, p])
        loop(4, functools.partial(stream1_part, g))
        norm_into(R.st1, R.nrm2, 1, g)

    early = jnp.where(z < 2, 0, 1)

    def feed(par):
        def part(i):
            bb = lax.div(i, 2)
            b = par + 2 * bb
            rows = at(lax.rem(i, 2) * 256, 256, 256)
            block = R.W.at[2 + par, 2 + bb]
            grad = jnp.zeros((256, 256), F32)
            for n in range(4):
                tile = block[n // 2, (n % 2) * 256 : (n % 2 + 1) * 256, :]
                grad = grad + mm_nt(gout[rows, n * 256 : (n + 1) * 256], tile)
            bias = vec[pl.ds(12 + b, 1), own_cols]
            x = mm(R.nrm2[rows, :], R.W[par, 2 + bb].reshape(1024, 256)) + bias
            half_cdf = 0.5 + 0.5 * lax.erf(x * math.sqrt(0.5))
            R.act[b, rows, :] = (x * half_cdf).astype(BF)
            slope = half_cdf + x * (jnp.exp(-0.5 * x * x) * (1.0 / math.sqrt(2.0 * math.pi)))
            R.gin[b, rows, :] = (grad * slope).astype(BF)

        loop(4, part)

    def feed_norm(par, rows):
        total = mm_nt(R.gin[par, rows, :], R.W[par, 2].reshape(1024, 256))
        return total + mm_nt(R.gin[par + 2, rows, :], R.W[par, 3].reshape(1024, 256))

    def feed_out(par, n, rows):
        total = jnp.zeros((256, 256), F32)
        for bb in range(2):
            tile = R.W[2 + par, 2 + bb, lax.div(n, 2), at(lax.rem(n, 2) * 256, 256, 256), :]
            total = total + mm(R.act[par + 2 * bb, rows, :], tile)
        return total

    def tiles(body):
        loop(8, lambda i: body(lax.rem(i, 4), at(lax.div(i, 4) * 256, 256, 256)))

    def drain_feed(zz):
        for b in (2, 3):
            sent(R.msgs.at[0], R.sFwd.at[zz, b, 0])

            @when((z != zz) & inner & (z ^ 1 != zz))
            def _():
                sent(R.msgs.at[0], R.sFwd.at[zz, b, 1])

            @when(z == zz)
            def _():
                for i in range(2):
                    sent(R.msgs.at[0], R.sOwn.at[b, i])

    def transposed(src):
        def part(i):
            a = lax.div(i, 2)
            b = lax.rem(i, 2)
            R.tr[at(a * 256, 256, 256), at(b * 256, 256, 256)] = src[
                at(b * 256, 256, 256), at(a * 256, 256, 256)
            ].T

        loop(8, part)

    def slot(zz, b):
        return 12 if isinstance(b, int) and b == 0 else (b - 1) * 4 + zz

    def exchange(zz, b):
        block = R.W.at[zz, b, 1 - c]
        remote(block, R.CR.at[slot(zz, b)], R.sC.at[zz, b], R.rC.at[zz, b], sib).start()

    def column_gradient(zz, b, left, right):
        for h in range(2):
            R.W[zz, b, h] = mm(left[h * 512 : (h + 1) * 512, :], right).astype(BF)
        exchange(zz, b)

    def feed_gradients(par):
        drain_feed(par)
        drain_feed(2 + par)

        def part(bb):
            b = par + 2 * bb
            for n in range(4):
                tile = mm_tn(R.act[b], gout[:, n * 256 : (n + 1) * 256])
                R.W[2 + par, 2 + bb, n // 2, (n % 2) * 256 : (n % 2 + 1) * 256, :] = tile.astype(BF)
            exchange(2 + par, 2 + bb)
            column_gradient(par, 2 + bb, R.tr, R.gin[b])

        loop(2, part)

    def summed(zz, b):
        arrived(R.CR.at[slot(zz, b)], R.rC.at[zz, b])
        sent(R.CR.at[slot(zz, b)], R.sC.at[zz, b])
        R.W[zz, b, c] = (R.W[zz, b, c].astype(F32) + R.CR[slot(zz, b)].astype(F32)).astype(BF)

    def first_send(k, b, cond=True):
        zz = z ^ k
        block = R.W.at[zz, b, c]

        @when(cond)
        def _():
            summed(zz, b)
            if k == 1:
                remote(block, R.RA.at[b], R.sZ.at[zz, b], R.rRA.at[b], dev(s, z ^ 1, c)).start()

        if k > 1:

            @when(cond & outer)
            def _():
                remote(block, R.RC.at[3 - k, b], R.sZ.at[zz, b], R.rRC.at[3 - k, b], dev(s, z ^ 1, c)).start()

    def gradient_sends(cond, ks):
        for k in ks:
            for b in (2, 3):
                first_send(k, b, cond)

    def wait_feed(par):
        for b in (2, 3):
            wait_half(par, b)
            wait_half(2 + par, b)

    for b in (2, 3):
        foreign(z ^ 1, b, inner)
        foreign(z ^ 2, b, outer)
    wait_feed(early)
    feed(early)

    def norm_start(g):
        rows = at(g * 256, 256, 256)
        R.acc[rows, :] = feed_norm(early, rows)

    def out_start(n, rows):
        R.gact[n, rows, :] = feed_out(early, n, rows)

    loop(2, norm_start)
    tiles(out_start)
    transposed(R.nrm2)
    feed_gradients(early)
    for b in (2, 3):
        foreign(z ^ 1, b, outer)
        foreign(z ^ 3, b, outer)
    later = 1 - early
    gradient_sends(outer, (2, 0))
    foreign(2, 0)
    wait_feed(later)
    feed(later)

    def reduce_rows(phase, make):
        for i, p in enumerate(peers):
            make(p)
            block = R.rsS.at[at(p * OWN, OWN, OWN), :]
            remote(block, R.rsR.at[s], R.sR.at[phase, i], R.rR.at[phase, s], dev(p, z, c)).start()
        make(s)

    def reduced(phase):
        total = R.rsS[own_rows, :].astype(F32)
        for p in peers:
            arrived(R.rsR.at[p], R.rR.at[phase, p])
            total = total + R.rsR[p].astype(F32)
        return total

    def norm_end(p):
        rows = at(p * OWN, OWN, OWN)
        R.rsS[rows, :] = (R.acc[rows, :] + feed_norm(later, rows)).astype(BF)

    def out_end(n, rows):
        R.hrow[rows, at(n * 256, 256, 256)] = (R.gact[n, rows, :] + feed_out(later, n, rows)).astype(BF)

    reduce_rows(0, norm_end)

    def drain_own(cond, b):
        @when(cond)
        def _():
            for i in range(2):
                sent(R.msgs.at[0], R.sOwn.at[b, i])

    def drain_spread(zz, b):
        whole = full_of(zz, b)

        def side():
            sent(R.msgs.at[0], R.sFwd.at[zz, b, 0])

        def layer():
            for i in range(3):
                sent(R.msgs.at[0], R.sFx.at[i])

        (layer if whole else side)()

        @when((z != zz) & inner & (z ^ 1 != zz))
        def _():
            sent(R.msgs.at[0], R.sFwd.at[zz, b, 1])

    def second_send(k, b, cond=True):
        zz = z ^ k
        block = R.W.at[zz, b, c]

        @when(inner & cond)
        def _():
            arrived(R.RC.at[k - 2, b], R.rRC.at[k - 2, b])
            R.W[zz, b, c] = (R.W[zz, b, c].astype(F32) + R.RC[k - 2, b].astype(F32)).astype(BF)
            remote(block, R.RB.at[b], R.sZ.at[zz, b], R.rRB.at[b], dev(s, zz, c)).start()

    def owner_of(b):
        row = (z >= 2) if b >= 2 else (z < 0)
        tc = jnp.where(row, lax.div(s, 2), c)
        m = jnp.where(row, lax.rem(s, 2) * 2 + c, s)
        return tc, m, (s == b) & (tc == c)

    def last_send(cond, b):
        tc, m, own = owner_of(b)
        block = R.W.at[z, b, c]

        @when(cond)
        def _():
            arrived(R.RA.at[b], R.rRA.at[b])
            arrived(R.RB.at[b], R.rRB.at[b])
            R.W[z, b, c] = (R.W[z, b, c].astype(F32) + R.RA[b].astype(F32) + R.RB[b].astype(F32)).astype(BF)

        @when(cond & own)
        def _():
            pltpu.make_async_copy(block, R.FR.at[m], R.rFin.at[m]).start()

        @when(cond & no(own))
        def _():
            remote(block, R.FR.at[m], R.sFin.at[b], R.rFin.at[m], dev(b, z, tc)).start()

    gradient_sends(inner, (1, 3))
    tiles(out_end)
    feed_gradients(later)

    R.small[...] = jnp.zeros((16, 1024), F32)
    for b in range(4):
        R.small[10 + b : 11 + b, own_cols] = column_sum(R.gin[b].astype(F32))
    R.small[14:15, :] = column_sum(gout[own_rows, :].astype(F32))

    gradient_sends(outer, (3, 1))
    gradient_sends(inner, (2, 0))

    g2 = reduced(0)
    gx, gw, gb = norm_back(R.st1[own_rows, :].astype(F32), g2, vec[6:7, :])
    R.small[4:5, :] = gw
    R.small[6:7, :] = gb
    gs1_own = (gout[own_rows, :].astype(F32) + gx).astype(BF)
    R.small[9:10, :] = column_sum(gs1_own.astype(F32))
    R.gs[0] = gs1_own

    def mixed_grad(p):
        total = jnp.zeros((OWN, 256), F32)
        for n in range(4):
            tile = R.WF[1, n, lax.div(p, 2), at(lax.rem(p, 2) * 256, 256, 256), :]
            total = total + mm_nt(R.gs[0, :, n * 256 : (n + 1) * 256], tile)
        return total.astype(BF)

    def swap(phase, src_of, dst):
        for i, p in enumerate(peers):
            remote(src_of(p), dst.at[own_rows, :], R.sG.at[phase, i], R.rG.at[phase, s], dev(p, z, c)).start()

    def swapped(phase, dst):
        for p in peers:
            arrived(dst.at[at(p * OWN, OWN, OWN), :], R.rG.at[phase, p])

    for i, p in enumerate(peers):
        R.gmS[i] = mixed_grad(p)
        remote(R.gmS.at[i], R.gm.at[own_rows, :], R.sG.at[0, i], R.rG.at[0, s], dev(p, z, c)).start()
    R.gm[own_rows, :] = mixed_grad(s)
    swap(1, lambda p: R.gs.at[0, :, at(p * 256, 256, 256)], R.ga)
    R.ga[own_rows, :] = R.gs[0, :, own_cols]

    def send_out(i):
        p = peers[i]
        block = R.hrow.at[:, at(p * 256, 256, 256)]
        remote(block, R.outR.at[s], R.sOut.at[i], R.rOut.at[s], dev(p, z, c)).start()


    swapped(0, R.gm)

    def attend_back(g):
        rows = at(g * 256, 256, 256)
        qg, kg, vg, gmg = R.q[rows, :], R.k[rows, :], R.v[rows, :], R.gm[rows, :]
        zero = jnp.zeros((256, 256), F32)
        tq, tk, tv = zero, zero, zero
        for hh in range(4):
            prob = R.attp[g * 4 + hh]
            gmh = only(hh, gmg)
            dprob = mm_nt(gmh, vg)
            tv = tv + mm_tn(prob.astype(BF), gmh)
            ds = (prob * (dprob - jnp.sum(prob * dprob, axis=1, keepdims=True))).astype(BF)
            tq = tq + mm(ds, only(hh, kg))
            tk = tk + mm_tn(ds, only(hh, qg))
        scale = 1.0 / math.sqrt(HEAD)
        R.gq[0, rows, :] = (tq * scale).astype(BF)
        R.gq[1, rows, :] = (tk * scale).astype(BF)
        R.gq[2, rows, :] = tv.astype(BF)

    loop(2, attend_back)

    for i in range(3):
        sent(R.rsR.at[0], R.sR.at[0, i])

    def attend_norm(p):
        rows = at(p * OWN, OWN, OWN)
        total = jnp.zeros((OWN, 1024), F32)
        for i in range(3):
            total = total + mm_nt(R.gq[i, rows, :], R.W[i, 1].reshape(1024, 256))
        R.rsS[rows, :] = total.astype(BF)

    reduce_rows(1, attend_norm)
    for b in (2, 3):
        second_send(3, b)

    transposed(R.nrm)
    drain_own(always, 1)
    for zz in range(4):
        drain_spread(zz, 1)
    piece = R.msgs.at[0, 0:256]
    for h in range(2):
        for i in range(3):
            sent(piece, R.sAx.at[i, h])

        @when(z == 1)
        def _():
            sent(piece, R.sAf.at[h])

        @when(top)
        def _():
            sent(piece, R.sAo.at[0, h])
            sent(piece, R.sAo.at[1, h])


    def attend_gradient(i):
        column_gradient(i, 1, R.tr, R.gq[i])

    loop(3, attend_gradient)
    transposed(R.mix)
    swapped(1, R.ga)
    column_gradient(3, 1, R.tr, R.ga[...])
    R.small[7:8, own_cols] = column_sum(R.gq[0].astype(F32))
    R.small[8:9, own_cols] = column_sum(R.gq[2].astype(F32))
    for k in (2, 3, 1, 0):
        first_send(k, 1)

    for b in (2, 3):
        second_send(2, b)
    g1 = reduced(1)
    gx, gw, gb = norm_back(R.st0[own_rows, :].astype(F32), g1, vec[5:6, :])
    R.small[3:4, :] = gw
    R.small[5:6, :] = gb
    gs0_own = (R.gs[0].astype(F32) + gx).astype(BF)
    gs0_sum = column_sum(gs0_own.astype(F32))
    R.small[1:2, :] = gs0_sum
    R.small[2:3, :] = jnp.where(s < 2, lead_short, lead_long) * gs0_sum
    R.gs[1] = gs0_own
    swap(2, lambda p: R.gs.at[1, :, at(p * 256, 256, 256)], R.gb)
    R.gb[own_rows, :] = R.gs[1, :, own_cols]
    def heads_grad(i):
        rows = at(lax.rem(i, 2) * 256, 256, 256)
        total = jnp.zeros((256, OWN), F32)
        for n in range(4):
            total = total + mm_nt(R.WF[0, n, lax.div(i, 2), rows, :], R.gs[1, :, n * 256 : (n + 1) * 256])
        block = at(i * 256, 256, 256)
        R.ghT[block, :] = total.astype(BF)
        R.gh[:, block] = total.astype(BF).T

    loop(4, heads_grad)
    R.G = R.acc.at[0:256, :]
    R.gpT[...] = jnp.zeros((192, OWN), F32)
    R.G[...] = jnp.zeros((256, 1024), F32)
    for hh in range(4):
        R.op1[hh, 240:256, :] = jnp.where(iota((16, OWN), 0) == 0, 1.0, 0.0).astype(BF)

    def embed_back(h, op1):
        rows = at(h * 48, 48, 16)
        prob = R.att[rows, own_rows]
        low = prob.astype(BF)
        lowf = low.astype(F32)
        weights_of(op1, low, own_rows)
        hrows = at(h * 64, 64, 64)
        gop = mm_tn(R.mT[hrows, :], R.ghT[hrows, :])
        cols = at(lax.div(h, 4) * 256, 256, 256)
        keep = lane_head == lax.rem(h, 4)
        R.G[:, cols] += jnp.where(keep, mm(op1[...], R.gh[:, cols]), 0.0)
        gatt = gop[192:240, :]
        for p in range(4):
            gatt = gatt + gop[p * 48 : (p + 1) * 48, :] * R.patT[p * 48 : (p + 1) * 48, own_rows].astype(F32)
        R.gsc[rows, :] = prob * (gatt - jnp.sum(prob * gatt, axis=0, keepdims=True)) * (1.0 / math.sqrt(HEAD))
        for p in range(4):
            prow = slice(p * 48, (p + 1) * 48)
            R.gpT[prow, :] += gop[prow, :] * lowf

    def embed_back_four(i):
        for hh in range(4):
            embed_back(4 * i + hh, R.op1.at[hh])

    loop(4, embed_back_four)

    gsc = R.gsc[...]
    gsc_high = gsc.astype(BF)
    gsc_low = (gsc - gsc_high.astype(F32)).astype(BF)
    fold = jnp.where(iota((16, 768), 0) == iota((16, 768), 1) // 48, 1.0, 0.0).astype(BF)

    def folded(x, right):
        x_high = x.astype(BF)
        x_low = (x - x_high.astype(F32)).astype(BF)
        return mm(fold, x_high) + mm(fold, x_low)

    ones = jnp.ones((192, OWN), BF)
    pat_own = R.patT[:, own_rows]
    same = iota((768, 192), 0) % 48 == iota((768, 192), 1) % 48
    cross = mm_nt(gsc_high, pat_own) + mm_nt(gsc_low, pat_own)
    plain = mm_nt(gsc_high, ones) + mm_nt(gsc_low, ones)
    R.fc[0, :, 0:192] = folded(jnp.where(same, cross, 0.0), None)
    R.fc[0, :, 192:256] = folded(jnp.where(same, plain, 0.0), None)[:, 0:64] * jnp.where(
        iota((1, 64), 1) < 48, 1.0, 0.0
    )
    remote(R.fc.at[0], R.fc.at[1], R.sFo.at[0], R.rFo.at[0], sib).start()

    R.G[240:256, :] += R.small[...]
    R.gall[...] = R.G[...].astype(BF)
    half = at(c * 128, 128, 128)
    other = at((1 - c) * 128, 128, 128)
    remote(R.gall.at[other, :], R.fromc, R.sAll.at[0], R.rAll.at[0], sib).start()

    gpt = (R.gpT[...] + mm_tn(R.fill[0:768, :], gsc_high)).astype(BF)
    for p in range(4):
        r = iota((48, 192), 0) + p * 48
        select = jnp.where(iota((48, 192), 1) == (r % 4) * 48 + r // 4, 1.0, 0.0).astype(BF)
        R.pixS[p] = mm(select, gpt).astype(BF)
    for i, p in enumerate(peers):
        remote(R.pixS.at[p], R.pixR.at[s], R.sP.at[i], R.rP.at[s], dev(p, z, c)).start()

    arrived(R.fc.at[1], R.rFo.at[0])
    R.fp[s] = R.fc[0] + R.fc[1]
    for i, p in enumerate(peers):
        remote(R.fp.at[s], R.fp.at[s], R.sFo.at[1 + i], R.rFo.at[1 + s], dev(p, z, c)).start()

    arrived(R.fromc, R.rAll.at[0])
    R.gall[half, :] = (R.gall[half, :].astype(F32) + R.fromc[...].astype(F32)).astype(BF)

    def part_of(p):
        return at(c * 128 + p * 32, 32, 32)

    for i, p in enumerate(peers):
        remote(R.gall.at[part_of(p), :], R.fromp.at[s], R.sAll.at[1 + i], R.rAll.at[1 + s], dev(p, z, c)).start()
    last_send(always, 2)
    last_send(always, 3)

    swapped(2, R.gb)
    column_gradient(3, 0, R.hT, R.gb[...])

    for p in peers:
        arrived(R.fp.at[p], R.rFo.at[1 + p])
    R.fz[z] = R.fp[0] + R.fp[1] + R.fp[2] + R.fp[3]
    for i, zz in enumerate(layers):
        remote(R.fz.at[z], R.fz.at[z], R.sFo.at[4 + i], R.rFo.at[5 + z], dev(s, zz, c)).start()

    total = R.gall[part_of(s), :].astype(F32)
    for p in peers:
        arrived(R.fromp.at[p], R.rAll.at[1 + p])
        total = total + R.fromp[p].astype(F32)
    R.fromz[z] = total.astype(BF)
    for i, zz in enumerate(layers):
        remote(R.fromz.at[z], R.fromz.at[z], R.sAll.at[4 + i], R.rAll.at[5 + z], dev(s, zz, c)).start()

    for k in (2, 3, 1, 0):
        first_send(k, 0, z ^ k == 3)
    for k in (2, 3):
        second_send(k, 1)

    for zz in layers:
        arrived(R.fz.at[zz], R.rFo.at[5 + zz])
    fo_grad = (R.fz[0] + R.fz[1]) + (R.fz[2] + R.fz[3])
    fo_high = fo_grad.astype(BF)
    fo_low = (fo_grad - fo_high.astype(F32)).astype(BF)
    gkq = (mm(fo_high, table[...]) + mm(fo_low, table[...])).astype(BF)

    @when(key_owner)
    def _():
        diag = iota((16, 1024), 1) // HEAD == iota((16, 1024), 0)
        own = jnp.where(c == 0, gkq[:, 0:512].astype(F32), gkq[:, 512:1024].astype(F32)).astype(BF)
        row = column_sum(jnp.where(diag, mm(own, bank[...]), 0.0))
        R.qx[0] = jnp.broadcast_to(row, (8, 1024))
        remote(R.qx.at[0], R.qx.at[1], R.sGq.at[15], R.rGq.at[0], sib).start()
        masked = jnp.where(diag, R.qb[...].astype(F32), 0.0).astype(BF)
        gbank[...] = mm_tn(own, masked).astype(BF)

    def query_grad():
        arrived(R.qx.at[1], R.rGq.at[0])
        row = (R.qx[0] + R.qx[1]).astype(BF)
        R.gqv[...] = jnp.concatenate([row, row], axis=0)
        for i, (p, k) in enumerate(others):
            remote(R.gqv, R.gqv, R.sGq.at[i], R.rGq.at[1], dev(p, k, c)).start()

    for zz in layers:
        arrived(R.fromz.at[zz], R.rAll.at[5 + zz])
    total = R.fromz[0].astype(F32)
    for zz in range(1, 4):
        total = total + R.fromz[zz].astype(F32)
    R.fin[part_of(s), :] = total.astype(BF)
    for i, p in enumerate(peers):
        block = R.fin.at[part_of(s), :]
        remote(block, block, R.sAll.at[7 + i], R.rAll.at[9 + s], dev(p, z, c)).start()
    send_out(0)
    send_out(1)
    send_out(2)

    when(key_owner)(query_grad)

    for p in peers:
        arrived(R.fin.at[part_of(p), :], R.rAll.at[9 + p])
    remote(R.fin.at[half, :], R.fin.at[half, :], R.sAll.at[10], R.rAll.at[13], sib).start()

    for k in (2, 3):
        second_send(k, 0, z ^ k == 3)

    arrived(R.fin.at[other, :], R.rAll.at[13])
    sums[...] = R.fin[240:256, :].astype(F32)
    wait_half(2, 0)
    zero16 = jnp.zeros((112, 256), BF)
    kq_wide = jnp.concatenate([R.kqF[:, own_cols], zero16], axis=0)
    value = mm_tn(jnp.concatenate([fo_high, zero16], axis=0), kq_wide)
    value = value + mm_tn(jnp.concatenate([fo_low, zero16], axis=0), kq_wide)
    for n in range(4):
        tile = R.W[2, 0, n // 2, (n % 2) * 256 : (n % 2 + 1) * 256, :]
        value = value + mm_nt(R.fin[:, n * 256 : (n + 1) * 256], tile)
    R.gt[s] = value.astype(BF)
    for i, p in enumerate(peers):
        remote(R.gt.at[s], R.gt.at[s], R.sGt.at[i], R.rGt.at[s], dev(p, z, c)).start()

    @when(value_owner)
    def _():
        gbank[...] = mm_tn(table[:, half_rows], R.fin[...]).astype(BF)

    @when(first_owner)
    def _():
        arrived(R.gqv, R.rGq.at[1])
        R.gaq[c] = mm_nt(R.gqv[...], bank[...])[0:8]
        for i, (p, k) in enumerate(others):
            remote(R.gaq.at[c], R.gaq.at[c], R.sGa.at[i], R.rGa.at[c], dev(p, k, c)).start()
        aq = jnp.where(c == 0, vec[17:18, 0:512], vec[17:18, 512:1024])
        aq = jnp.where(iota((16, 512), 0) == 0, aq, 0.0).astype(BF)
        gbank[...] = mm_tn(aq, R.gqv[...]).astype(BF)


    last_send(always, 1)
    last_send(top, 0)

    @when(no(first_owner))
    def _():
        arrived(R.gaq.at[c], R.rGa.at[c])

    @when(no(key_owner | first_owner))
    def _():
        arrived(R.gqv, R.rGq.at[1])

    remote(R.gaq.at[c], R.gaq.at[c], R.sGa.at[15], R.rGa.at[c], sib).start()
    arrived(R.gaq.at[1 - c], R.rGa.at[1 - c])
    rows_out[0:8, :] = R.gqv[0:8, :].astype(F32)
    rows_out[8:16, 0:512] = R.gaq[0]
    rows_out[8:16, 512:1024] = R.gaq[1]

    for p in peers:
        arrived(R.gt.at[p], R.rGt.at[p])
    for p in range(4):
        gtab[:, p * 256 : (p + 1) * 256] = R.gt[p]
    total = R.hrow[:, own_cols].astype(F32) + R.st1[:, own_cols].astype(F32) + vec[16:17, own_cols]
    for p in peers:
        arrived(R.outR.at[p], R.rOut.at[p])
        total = total + R.outR[p].astype(F32)
    out[...] = total.astype(BF)

    for i, p in enumerate(peers):
        arrived(R.pixR.at[p], R.rP.at[p])
    R.pixR[s] = R.pixS[s]
    for p in range(4):
        gpix[p // 2, :, (p % 2) * OWN : (p % 2 + 1) * OWN] = R.pixR[p].astype(F32)

    @when(used)
    def _():
        for m in range(4):
            arrived(R.FR.at[m], R.rFin.at[m])

    @when(used & no(is_row))
    def _():
        for m in range(4):
            gbank[:, m * 256 : (m + 1) * 256] = R.FR[m]

    @when(used & is_row)
    def _():
        for m in range(4):
            q, h = m // 2, m % 2
            for n in range(2):
                lo = (2 * h + n) * 256
                gbank[q * 256 : (q + 1) * 256, lo : lo + 256] = R.FR[m, n * 256 : (n + 1) * 256, :]

    stores = [pltpu.make_async_copy(a, b, R.sRes.at[i]) for i, (a, b) in enumerate(zip(results, targets))]
    for store in stores:
        store.start()

    for m in range(4):
        tp, tc, own = message(m)

        @when((used | late) & no(own) & no(out_owner))
        def _():
            sent(R.msgs.at[m], R.sMsg.at[m])

        if m > 0:

            @when(out_owner)
            def _():
                sent(piece, R.sA.at[m, 0])
                sent(piece, R.sA.at[m, 1])

        @when(value_owner & no((2 * c + m // 2 == s) & (c == m % 2)))
        def _():
            sent(my_piece(m), R.sMa.at[m])

    @when(first_owner)
    def _():
        sent(R.qbuf.at[0], R.sQ.at[0])
        sent(R.qb, R.sQ.at[1])
        for i in range(15):
            sent(R.gaq.at[c], R.sGa.at[i])

    @when(key_owner)
    def _():
        sent(R.qx.at[0], R.sGq.at[15])
        for i in range(15):
            sent(R.kq.at[c], R.sK.at[i])
            sent(R.gqv, R.sGq.at[i])

    @when(z == 2)
    def _():
        for i in range(3):
            sent(R.mS.at[0:128, :], R.sMz.at[i])

    drain_own(z == 2, 0)
    drain_spread(2, 0)
    sent(R.kq.at[c], R.sK.at[15])
    sent(R.gaq.at[c], R.sGa.at[15])
    for p in range(4):
        sent(R.msgs.at[0], R.sFc.at[p])
        sent(piece, R.sAc.at[p, 0])
        sent(piece, R.sAc.at[p, 1])
    for p in range(4):
        sent(R.mS.at[0:128, :], R.sMc.at[p])
    sent(R.fc.at[0], R.sFo.at[0])
    sent(R.fromc, R.sAll.at[0])
    sent(R.fromc, R.sAll.at[10])
    for i in range(3):
        sent(R.mS.at[0:128, :], R.sMp.at[i])
        sent(R.mix.at[0:256, 0:256], R.sMix.at[0, i])
        sent(R.mix.at[0:256, 0:256], R.sMix.at[1, i])
        sent(R.msgs.at[0], R.sOut.at[i])
        sent(R.rsR.at[0], R.sR.at[1, i])
        for phase in range(3):
            sent(R.gmS.at[0], R.sG.at[phase, i])
        sent(R.pixS.at[0], R.sP.at[i])
        sent(R.gt.at[0], R.sGt.at[i])
        sent(R.fp.at[0], R.sFo.at[1 + i])
        sent(R.fp.at[0], R.sFo.at[4 + i])
        for phase in range(3):
            sent(R.fromp.at[0], R.sAll.at[1 + 3 * phase + i])
    for b in range(4):
        for zz in range(4):

            @when(at_least(jnp.int32(zz), b) & (z != zz) & (always if b > 0 or zz == 3 else z < 0))
            def _():
                sent(R.msgs.at[0], R.sZ.at[zz, b])

        tc, m, own = owner_of(b)

        @when((top if b == 0 else always) & no(own))
        def _():
            sent(R.msgs.at[0], R.sFin.at[b])
    for store in stores:
        store.wait()


VMEM = pl.BlockSpec(memory_space=pltpu.VMEM)
SMEM = pl.BlockSpec(memory_space=pltpu.SMEM)
ARG_SHAPES = (
    [((2, 192, 256), BF), ((512, 1024), BF), ((512, 1024), BF), ((48, 4, 1024), BF)]
    + [((48, 1024), BF)] * 2
    + [((1024,), BF)]
    + [((n, 1024), BF) for n in (3, 2, 2, 2, 3)]
    + [((4096,), BF), ((1024,), BF), ((1, 2), F32), ((1, 4), jnp.int32)]
)


ANY = pl.BlockSpec(memory_space=pl.ANY)


def block_call(*args):
    shape = jax.ShapeDtypeStruct
    outs = [
        shape((512, 256), BF),
        shape((2, 48, 256), F32),
        shape((512, 1024), BF),
        shape((256, 1024), BF),
        shape((16, 1024), F32),
        shape((16, 1024), F32),
    ]
    return pl.pallas_call(
        block_kernel,
        out_shape=outs,
        in_specs=[ANY] * 14 + [SMEM] * 2,
        out_specs=[ANY] * len(outs),
        scratch_shapes=[pltpu.VMEM(a.shape, a.dtype) for a in (*args[:14], *outs)]
        + [pltpu.VMEM(*v) for v in SCRATCH.values()]
        + [pltpu.SemaphoreType.DMA(v) for v in SEMS.values()],
        compiler_params=pltpu.CompilerParams(
            collective_id=1, has_side_effects=True, vmem_limit_bytes=63 * 2**20
        ),
    )(*args)


def finish_kernel(*refs):
    sources, targets, rest = refs[:6], refs[6:20], refs[20:]
    held, made, ins, outs = rest[:6], rest[6:20], rest[20], rest[21]
    out, gpix, gbank, gtab, sums, rows = held
    o_out, o_pix, o_bank, o_patch, o_patch_b, o_var, o_query, o_agg, o_lead, o_gain, o_bias, o_attn, o_fc1, o_fc2 = made

    def load(i):
        return pltpu.make_async_copy(sources[i], held[i], ins.at[i])

    def part(h):
        rows_h = pl.ds(h * 128, 128)
        return pltpu.make_async_copy(sources[2].at[rows_h], gbank.at[rows_h], ins.at[6 + h])

    def store(i):
        return pltpu.make_async_copy(made[i], targets[i], outs.at[i])

    def store_part(h):
        rows_h = pl.ds(h * 128, 128)
        return pltpu.make_async_copy(o_bank.at[rows_h], targets[2].at[rows_h], outs.at[14 + h])

    for h in range(4):
        part(h).start()
    for i in (3, 4, 5, 0, 1):
        load(i).start()
    direct = [pltpu.make_async_copy(held[i], targets[i], outs.at[i]) for i in range(2)]
    for h in range(4):
        part(h).wait()
        o_bank[h * 128 : (h + 1) * 128, :] = gbank[h * 128 : (h + 1) * 128, :].astype(F32)
        store_part(h).start()
    load(3).wait()
    for p in range(PIX):
        o_patch[:, p, :] = gtab[p * VARS : (p + 1) * VARS, :].astype(F32)
    o_patch_b[...] = gtab[192:240, :].astype(F32)
    o_var[...] = gtab[192:240, :].astype(F32)
    for i in (3, 4, 5):
        store(i).start()
    for i in range(2):
        load(i).wait()
        direct[i].start()
    load(4).wait()
    load(5).wait()
    o_query[...] = rows[8, :]
    o_agg[0:1, :] = rows[0:1, :]
    o_agg[1:3, :] = sums[0:2, :]
    o_lead[0:1, :] = sums[2:3, :]
    o_lead[1:2, :] = sums[1:2, :]
    o_gain[...] = sums[3:5, :]
    o_bias[...] = sums[5:7, :]
    o_attn[...] = sums[7:10, :]
    for i in range(4):
        o_fc1[i * 1024 : (i + 1) * 1024] = sums[10 + i, :]
    o_fc2[...] = sums[14, :]
    for i in range(6, 14):
        store(i).start()
    for copy in direct:
        copy.wait()
    for h in range(4):
        store_part(h).wait()
    for i in range(3, 14):
        store(i).wait()


def finish_call(*args):
    shape = jax.ShapeDtypeStruct
    outs = [shape((512, 256), BF), shape((2, 48, 256), F32), shape((512, 1024), F32), shape((48, 4, 1024), F32)]
    outs += [shape((48, 1024), F32)] * 2 + [shape((1024,), F32)]
    outs += [shape((n, 1024), F32) for n in (3, 2, 2, 2, 3)] + [shape((FF,), F32), shape((1024,), F32)]
    return pl.pallas_call(
        finish_kernel,
        out_shape=outs,
        in_specs=[ANY] * len(args),
        out_specs=[ANY] * len(outs),
        scratch_shapes=[pltpu.VMEM(a.shape, a.dtype) for a in (*args, *outs)]
        + [pltpu.SemaphoreType.DMA((10,)), pltpu.SemaphoreType.DMA((18,))],
        compiler_params=pltpu.CompilerParams(vmem_limit_bytes=63 * 2**20),
    )(*args)


def on_device_fast(
    patches,
    lead_times,
    short_lengths,
    cotangent,
    bank,
    patch_w,
    patch_b,
    var_emb,
    agg_query,
    agg_bias,
    lead_embed,
    norm_gain,
    norm_bias,
    attn_bias,
    fc1_bias,
    fc2_bias,
):
    parts = block_call(
        jnp.transpose(patches, (0, 2, 1)),
        cotangent.reshape(ROWS, D),
        bank[0],
        patch_w,
        patch_b,
        var_emb,
        agg_query,
        agg_bias,
        lead_embed,
        norm_gain,
        norm_bias,
        attn_bias,
        fc1_bias,
        fc2_bias,
        lead_times.T,
        short_lengths,
    )
    o = finish_call(*parts)
    return (
        (o[0].reshape(2, GROUP, 256), jnp.transpose(o[1], (0, 2, 1)), o[2][None])
        + tuple(o[3:])
    )


def specs():
    ins = (
        (P(None, "dp", None), P(None, "dp"), P("dp", None), P(None, "dp", None), P("section", "dp", None))
        + (P(),) * 11
    )
    outs = (P(None, "dp", "section"), P(None, "dp", "section"), P("section", "dp", None)) + (P(),) * 11
    return ins, outs


wide_type = jnp.float32
narrow_type = jnp.bfloat16
highest = lax.Precision.HIGHEST


def shortened(array):

    def short(part):
        return part.astype(jnp.bfloat16) if part.dtype == jnp.float32 else part

    return jax.tree.map(short, array)


def from_behind(array, axis, by):
    length = lax.axis_size(axis)
    pairs = [(i, i + by) for i in range(length) if 0 <= i + by < length]
    return lax.ppermute(array, axis, pairs)


def product(factor_left, factor_right):
    return jnp.dot(factor_left, factor_right, preferred_element_type=wide_type)


def product_left(factor_left, factor_right):
    return lax.dot_general(
        factor_left, factor_right, (((0,), (0,)), ((), ())), preferred_element_type=wide_type
    )


def product_right(factor_left, factor_right):
    return lax.dot_general(
        factor_left, factor_right, (((1,), (1,)), ((), ())), preferred_element_type=wide_type
    )


def norm_layer(stream, gain_row, shift_row):
    centre = stream - jnp.mean(stream, axis=-1, keepdims=True)
    spread = jnp.mean(centre * centre, axis=-1, keepdims=True)
    return centre * lax.rsqrt(spread + 1e-05) * gain_row + shift_row


def gelu_exact(values_in):
    return jax.nn.gelu(values_in, approximate=False)


def position_table(places):
    half_width = D // 2
    frequency = jnp.exp(-math.log(10000.0) * 2.0 * jnp.arange(half_width, dtype=wide_type) / D)
    angles = places.astype(wide_type)[:, None] * frequency[None, :]
    return jnp.concatenate([jnp.sin(angles), jnp.cos(angles)], axis=1)


def layout(lengths_row, row_count):
    segment_ends = jnp.cumsum(lengths_row)
    starts = segment_ends - lengths_row
    places = jnp.arange(row_count, dtype=jnp.int32)
    segment = jnp.sum((places[:, None] >= segment_ends[None, :]).astype(jnp.int32), axis=1)
    member = segment[:, None] == jnp.arange(lengths_row.shape[0], dtype=jnp.int32)[None, :]
    offset = jnp.sum(jnp.where(member, starts[None, :], 0), axis=1)
    offset = jnp.where(segment == lengths_row.shape[0], segment_ends[-1], offset)
    return (segment, places - offset)


def embed_setup(weights, params):
    patch_w, patch_b, var_emb, agg_query, agg_bias = params[:5]
    query_row = product(agg_query[None, :], weights[0])[0] + agg_bias[0].astype(wide_type)
    query_low = query_row.astype(narrow_type)
    key_query = jnp.einsum(
        "dhe,he->dh",
        weights[1].reshape(D, HEADS, HEAD),
        query_low.reshape(HEADS, HEAD),
        preferred_element_type=wide_type,
    )
    key_low = key_query.astype(narrow_type)
    constant = (patch_b.astype(wide_type) + var_emb.astype(wide_type)).astype(narrow_type)
    filters = jnp.einsum("vpd,dh->vph", patch_w, key_low, preferred_element_type=wide_type)
    offsets = product(constant, key_low)
    embed_table = jnp.concatenate([patch_w.reshape(VARS * PIX, D), constant], axis=0)
    return (query_low, key_low, constant, filters, offsets, embed_table)


def embed_rows(pixel_rows, places, lead_time, setup, weights, params):
    query_low, key_low, constant, filters, offsets, embed_table = setup
    agg_bias, lead_embed = (params[4], params[5])
    row_count = pixel_rows.shape[0]
    pixels = pixel_rows.reshape(row_count, VARS, PIX).astype(wide_type)
    scores = (
        jnp.einsum("tvp,vph->tvh", pixels, filters, precision=highest) + offsets[None]
    ) / math.sqrt(HEAD)
    attend = jax.nn.softmax(scores, axis=1)
    attend_low = attend.astype(narrow_type)
    weighted = (attend_low.astype(wide_type)[:, :, :, None] * pixels[:, :, None, :]).astype(
        narrow_type
    )
    operand = jnp.concatenate(
        [
            jnp.transpose(weighted, (0, 2, 1, 3)).reshape(row_count * HEADS, VARS * PIX),
            jnp.transpose(attend_low, (0, 2, 1)).reshape(row_count * HEADS, VARS),
        ],
        axis=1,
    )
    pooled = product(operand, embed_table).astype(narrow_type).reshape(row_count, HEADS, D)
    heads_out = jnp.einsum(
        "thd,dhe->the", pooled, weights[2].reshape(D, HEADS, HEAD), preferred_element_type=wide_type
    ).reshape(row_count, D)
    heads_low = (heads_out + agg_bias[1].astype(wide_type)).astype(narrow_type)
    merged = product(heads_low, weights[3]) + agg_bias[2].astype(wide_type)
    stream = (
        merged
        + position_table(places)
        + lead_time * lead_embed[0].astype(wide_type)
        + lead_embed[1].astype(wide_type)
    )
    return (stream.astype(narrow_type), (pixels, attend, attend_low, operand, pooled, heads_low))


def embed_back(grad_rows, lead_time, setup, saved_state, weights):
    query_low, key_low, constant, filters, offsets, embed_table = setup
    pixels, attend, attend_low, operand, pooled, heads_low = saved_state
    row_count = grad_rows.shape[0]
    grad_wide = grad_rows.astype(wide_type)
    grad_w_out = product_left(heads_low, grad_rows)
    grad_bias_out = jnp.sum(grad_wide, axis=0)
    grad_heads = product_right(grad_rows, weights[3]).astype(narrow_type)
    grad_bias_value = jnp.sum(grad_heads.astype(wide_type), axis=0)
    grad_heads_split = grad_heads.reshape(row_count, HEADS, HEAD)
    grad_w_value = jnp.einsum(
        "thd,the->dhe", pooled, grad_heads_split, preferred_element_type=wide_type
    ).reshape(D, D)
    grad_pooled = jnp.einsum(
        "the,dhe->thd",
        grad_heads_split,
        weights[2].reshape(D, HEADS, HEAD),
        preferred_element_type=wide_type,
    )
    grad_pooled = grad_pooled.astype(narrow_type).reshape(row_count * HEADS, D)
    grad_operand = product_right(grad_pooled, embed_table)
    grad_table = product_left(operand, grad_pooled)
    grad_weighted = grad_operand[:, : VARS * PIX].reshape(row_count, HEADS, VARS, PIX)
    grad_mixing = jnp.transpose(
        grad_operand[:, VARS * PIX :].reshape(row_count, HEADS, VARS), (0, 2, 1)
    )
    grad_attend = (
        jnp.einsum("thvp,tvp->tvh", grad_weighted, pixels, precision=highest) + grad_mixing
    )
    grad_scores = (
        attend
        * (grad_attend - jnp.sum(attend * grad_attend, axis=1, keepdims=True))
        / math.sqrt(HEAD)
    )
    grad_pixels = jnp.einsum(
        "thvp,tvh->tvp", grad_weighted, attend_low.astype(wide_type), precision=highest
    )
    grad_pixels = grad_pixels + jnp.einsum("tvh,vph->tvp", grad_scores, filters, precision=highest)
    grad_filters = jnp.einsum("tvp,tvh->vph", pixels, grad_scores, precision=highest)
    grad_offsets = jnp.sum(grad_scores, axis=0)
    grad_lead = jnp.stack([lead_time * grad_bias_out, grad_bias_out])
    sums = (
        grad_w_out,
        grad_bias_out,
        grad_bias_value,
        grad_w_value,
        grad_table,
        grad_filters,
        grad_offsets,
        grad_lead,
    )
    return (grad_pixels.reshape(row_count, VARS * PIX), sums)


def embed_finish(totals, setup, weights, params):
    (
        grad_w_out,
        grad_bias_out,
        grad_bias_value,
        grad_w_value,
        grad_table,
        grad_filters,
        grad_offsets,
        grad_lead,
    ) = totals
    query_low, key_low, constant, filters, offsets, embed_table = setup
    patch_w, agg_query = (params[0], params[3])
    key_wide = key_low.astype(wide_type)
    grad_patch_w = grad_table[: VARS * PIX].reshape(VARS, PIX, D) + jnp.einsum(
        "vph,dh->vpd", grad_filters, key_wide, precision=highest
    )
    grad_constant = grad_table[VARS * PIX :] + jnp.dot(grad_offsets, key_wide.T, precision=highest)
    grad_key = jnp.einsum("vpd,vph->dh", patch_w.astype(wide_type), grad_filters, precision=highest)
    grad_key = grad_key + jnp.dot(constant.astype(wide_type).T, grad_offsets, precision=highest)
    grad_key_low = grad_key.astype(narrow_type)
    query_heads = query_low.reshape(HEADS, HEAD).astype(wide_type)
    grad_w_key = (grad_key_low.astype(wide_type)[:, :, None] * query_heads[None, :, :]).reshape(
        D, D
    )
    grad_query = jnp.einsum(
        "dhe,dh->he",
        weights[1].reshape(D, HEADS, HEAD),
        grad_key_low,
        preferred_element_type=wide_type,
    )
    grad_query = grad_query.reshape(D).astype(narrow_type)
    grad_query_wide = grad_query.astype(wide_type)
    grad_w_query = agg_query.astype(wide_type)[:, None] * grad_query_wide[None, :]
    grad_agg_query = product(weights[0], grad_query[:, None])[:, 0]
    grad_bank = jnp.concatenate([grad_w_query, grad_w_key, grad_w_value, grad_w_out], axis=0)
    smalls = (
        grad_patch_w,
        grad_constant,
        grad_constant,
        grad_agg_query,
        jnp.stack([grad_query_wide, grad_bias_value, grad_bias_out]),
        grad_lead,
        jnp.zeros((2, D), wide_type),
        jnp.zeros((2, D), wide_type),
        jnp.zeros((3, D), wide_type),
        jnp.zeros((FF,), wide_type),
        jnp.zeros((D,), wide_type),
    )
    return (grad_bank, smalls)


def attention_scores(block_query, block_segment, key_heads, segment):
    raw_scores = jnp.einsum(
        "qhe,khe->hqk", block_query, key_heads, preferred_element_type=wide_type
    ) / math.sqrt(HEAD)
    allowed = (block_segment[:, None] == segment[None, :])[None]
    return jnp.where(allowed, raw_scores, -1e30)


def attention_forward(queries, key_rows, values, segment):
    row_count = queries.shape[0]
    block_rows = min(512, row_count)
    block_total = row_count // block_rows
    key_heads = key_rows.reshape(row_count, HEADS, HEAD)
    value_heads = values.reshape(row_count, HEADS, HEAD)

    def one_block(block_items):
        block_query, block_segment = block_items
        scores = attention_scores(block_query, block_segment, key_heads, segment)
        row_peak = jnp.max(scores, axis=-1, keepdims=True)
        exp_scores = jnp.exp(scores - row_peak)
        exp_total = jnp.sum(exp_scores, axis=-1, keepdims=True)
        probabilities = (exp_scores / exp_total).astype(narrow_type)
        mixed_heads = jnp.einsum(
            "hqk,khe->qhe", probabilities, value_heads, preferred_element_type=wide_type
        )
        return (mixed_heads.astype(narrow_type), (row_peak + jnp.log(exp_total))[:, :, 0])

    mixed_heads, log_totals = lax.map(
        one_block,
        (
            queries.reshape(block_total, block_rows, HEADS, HEAD),
            segment.reshape(block_total, block_rows),
        ),
    )
    return (mixed_heads.reshape(row_count, D), log_totals)


def attention_backward(queries, key_rows, values, segment, log_totals, grad_mixed):
    row_count = queries.shape[0]
    block_rows = min(512, row_count)
    block_total = row_count // block_rows
    key_heads = key_rows.reshape(row_count, HEADS, HEAD)
    value_heads = values.reshape(row_count, HEADS, HEAD)

    def one_block(carry_sums, block_items):
        grad_key_sum, grad_value_sum = carry_sums
        block_query, block_segment, block_log, block_grad = block_items
        scores = attention_scores(block_query, block_segment, key_heads, segment)
        probabilities = jnp.exp(scores - block_log[:, :, None])
        probs_low = probabilities.astype(narrow_type)
        grad_value_sum = grad_value_sum + jnp.einsum(
            "hqk,qhe->khe", probs_low, block_grad, preferred_element_type=wide_type
        )
        grad_probs = jnp.einsum(
            "qhe,khe->hqk", block_grad, value_heads, preferred_element_type=wide_type
        )
        grad_scores = probabilities * (
            grad_probs - jnp.sum(probabilities * grad_probs, axis=-1, keepdims=True)
        )
        grad_low = grad_scores.astype(narrow_type)
        grad_query = jnp.einsum(
            "hqk,khe->qhe", grad_low, key_heads, preferred_element_type=wide_type
        ) / math.sqrt(HEAD)
        grad_key_sum = grad_key_sum + jnp.einsum(
            "hqk,qhe->khe", grad_low, block_query, preferred_element_type=wide_type
        ) / math.sqrt(HEAD)
        return ((grad_key_sum, grad_value_sum), grad_query)

    zero_heads = jnp.zeros((row_count, HEADS, HEAD), wide_type)
    block_items = (
        queries.reshape(block_total, block_rows, HEADS, HEAD),
        segment.reshape(block_total, block_rows),
        log_totals,
        grad_mixed.reshape(block_total, block_rows, HEADS, HEAD),
    )
    (grad_key_sum, grad_value_sum), grad_queries = lax.scan(
        one_block, (zero_heads, zero_heads), block_items
    )
    return (
        grad_queries.reshape(row_count, D),
        grad_key_sum.reshape(row_count, D),
        grad_value_sum.reshape(row_count, D),
    )


def project_heads(normed_low, weights, attn_bias):
    queries = (product(normed_low, weights[0]) + attn_bias[0].astype(wide_type)).astype(narrow_type)
    key_rows = product(normed_low, weights[1]).astype(narrow_type)
    values = (product(normed_low, weights[2]) + attn_bias[1].astype(wide_type)).astype(narrow_type)
    return (queries, key_rows, values)


def feed_half(normed_low, weights, bias_in):
    inner_first = product(normed_low, weights[0]) + bias_in[:D].astype(wide_type)
    inner_second = product(normed_low, weights[1]) + bias_in[D:].astype(wide_type)
    active_first = gelu_exact(inner_first).astype(narrow_type)
    active_second = gelu_exact(inner_second).astype(narrow_type)
    partial_sum = product(active_first, weights[2]) + product(active_second, weights[3])
    return ((inner_first, inner_second), (active_first, active_second), partial_sum)


def feed_half_back(normed_low, weights, inners, actives, grad_rows):
    grad_inners = []
    for number in range(2):
        grad_active = product_right(grad_rows, weights[2 + number])
        value_out, gelu_pull = jax.vjp(gelu_exact, inners[number])
        grad_inners.append(gelu_pull(grad_active)[0].astype(narrow_type))
    grad_normed = product_right(grad_inners[0], weights[0]) + product_right(
        grad_inners[1], weights[1]
    )
    grad_bank = jnp.concatenate(
        [
            product_left(normed_low, grad_inners[0]),
            product_left(normed_low, grad_inners[1]),
            product_left(actives[0], grad_rows),
            product_left(actives[1], grad_rows),
        ],
        axis=0,
    )
    grad_bias_in = jnp.concatenate(
        [
            jnp.sum(grad_inners[0].astype(wide_type), axis=0),
            jnp.sum(grad_inners[1].astype(wide_type), axis=0),
        ]
    )
    return (grad_normed, grad_bank, grad_bias_in)


def on_device(
    patches,
    lead_times,
    short_lengths,
    cotangent,
    bank,
    patch_w,
    patch_b,
    var_emb,
    agg_query,
    agg_bias,
    lead_embed,
    norm_gain,
    norm_bias,
    attn_bias,
    fc1_bias,
    fc2_bias,
):
    params = (
        patch_w,
        patch_b,
        var_emb,
        agg_query,
        agg_bias,
        lead_embed,
        norm_gain,
        norm_bias,
        attn_bias,
        fc1_bias,
        fc2_bias,
    )
    micro_total = patches.shape[0]
    row_count = patches.shape[1]
    section_total = lax.axis_size("section")
    section_index = lax.axis_index("section")
    gathered = lax.all_gather(bank, "dp", axis=1, tiled=True)[0]
    weights = tuple((gathered[number * D : (number + 1) * D] for number in range(4)))
    short_segment, short_places = layout(short_lengths[0], row_count)
    segments = jnp.stack([short_segment, jnp.zeros((row_count,), jnp.int32)])
    places_all = jnp.stack([short_places, jnp.arange(row_count, dtype=jnp.int32)])
    valid_rows = jnp.stack([short_segment < short_lengths.shape[1], jnp.ones((row_count,), bool)])
    grad_out_all = jnp.where(valid_rows[:, :, None], cotangent, jnp.zeros_like(cotangent))
    block_rows = min(512, row_count)
    block_total = row_count // block_rows
    zeros_stream = jnp.zeros((row_count, D), narrow_type)
    zeros_final = jnp.zeros((row_count, D), wide_type)
    zeros_pixels = jnp.zeros((row_count, VARS * PIX), wide_type)
    stash_zero = (
        zeros_stream,
        zeros_stream,
        zeros_stream,
        zeros_stream,
        jnp.zeros((block_total, HEADS, block_rows), wide_type),
    )
    small_zero = tuple((jnp.zeros(array_item.shape, wide_type) for array_item in params))

    def forward_embed(operands):
        first_in, second_in, pixel_rows, places, lead_time, segment = operands
        setup = embed_setup(weights, params)

        def one_block(block_items):
            return embed_rows(block_items[0], block_items[1], lead_time, setup, weights, params)[0]

        streams = lax.map(
            one_block,
            (
                pixel_rows.reshape(block_total, block_rows, VARS * PIX),
                places.reshape(block_total, block_rows),
            ),
        )
        return (streams.reshape(row_count, D), zeros_stream, zeros_final, stash_zero)

    def forward_attend(operands):
        first_in, second_in, pixel_rows, places, lead_time, segment = operands
        stream = first_in.astype(wide_type)
        normed_low = norm_layer(
            stream, norm_gain[0].astype(wide_type), norm_bias[0].astype(wide_type)
        ).astype(narrow_type)
        queries, key_rows, values = project_heads(normed_low, weights, attn_bias)
        mixed_heads, log_totals = attention_forward(queries, key_rows, values, segment)
        new_stream = stream + product(mixed_heads, weights[3]) + attn_bias[2].astype(wide_type)
        return (new_stream.astype(narrow_type), zeros_stream, zeros_final, stash_zero)

    def forward_first(operands):
        first_in, second_in, pixel_rows, places, lead_time, segment = operands
        stream = first_in.astype(wide_type)
        normed_low = norm_layer(
            stream, norm_gain[1].astype(wide_type), norm_bias[1].astype(wide_type)
        ).astype(narrow_type)
        inners, actives, partial_sum = feed_half(normed_low, weights, fc1_bias[: 2 * D])
        return (normed_low, (stream + partial_sum).astype(narrow_type), zeros_final, stash_zero)

    def forward_second(operands):
        first_in, second_in, pixel_rows, places, lead_time, segment = operands
        inners, actives, partial_sum = feed_half(first_in, weights, fc1_bias[2 * D :])
        final_rows = second_in.astype(wide_type) + partial_sum + fc2_bias.astype(wide_type)
        return (zeros_stream, zeros_stream, final_rows, stash_zero)

    def forward_none(operands):
        return (zeros_stream, zeros_stream, zeros_final, stash_zero)

    def backward_embed(operands):
        (
            first_kept,
            second_kept,
            grad_in,
            pixel_rows,
            places,
            lead_time,
            segment,
            grad_rows,
            stash_items,
        ) = operands
        setup = embed_setup(weights, params)

        def one_block(totals, block_items):
            block_pixels, block_places, block_grad = block_items
            block_stream, saved_state = embed_rows(
                block_pixels, block_places, lead_time, setup, weights, params
            )
            block_dx, sums = embed_back(block_grad, lead_time, setup, saved_state, weights)
            return (
                tuple((total_item + sum_item for total_item, sum_item in zip(totals, sums))),
                block_dx,
            )

        zero_totals = (
            jnp.zeros((D, D), wide_type),
            jnp.zeros((D,), wide_type),
            jnp.zeros((D,), wide_type),
            jnp.zeros((D, D), wide_type),
            jnp.zeros((VARS * PIX + VARS, D), wide_type),
            jnp.zeros((VARS, PIX, HEADS), wide_type),
            jnp.zeros((VARS, HEADS), wide_type),
            jnp.zeros((2, D), wide_type),
        )
        block_items = (
            pixel_rows.reshape(block_total, block_rows, VARS * PIX),
            places.reshape(block_total, block_rows),
            grad_in.reshape(block_total, block_rows, D),
        )
        totals, grad_pixels = lax.scan(one_block, zero_totals, block_items)
        grad_bank, smalls = embed_finish(totals, setup, weights, params)
        return (zeros_stream, grad_bank, smalls, grad_pixels.reshape(row_count, VARS * PIX))

    def backward_attend(operands):
        (
            first_kept,
            second_kept,
            grad_in,
            pixel_rows,
            places,
            lead_time,
            segment,
            grad_rows,
            stash_items,
        ) = operands
        stream = first_kept.astype(wide_type)
        normed, norm_pull = jax.vjp(
            norm_layer, stream, norm_gain[0].astype(wide_type), norm_bias[0].astype(wide_type)
        )
        normed_low = normed.astype(narrow_type)
        queries, key_rows, values = project_heads(normed_low, weights, attn_bias)
        mixed_heads, log_totals = attention_forward(queries, key_rows, values, segment)
        grad_in_wide = grad_in.astype(wide_type)
        grad_w_out = product_left(mixed_heads, grad_in)
        grad_mixed = product_right(grad_in, weights[3]).astype(narrow_type)
        grad_queries, grad_keys, grad_values = attention_backward(
            queries, key_rows, values, segment, log_totals, grad_mixed
        )
        grad_queries = grad_queries.astype(narrow_type)
        grad_keys = grad_keys.astype(narrow_type)
        grad_values = grad_values.astype(narrow_type)
        grad_normed = (
            product_right(grad_queries, weights[0])
            + product_right(grad_keys, weights[1])
            + product_right(grad_values, weights[2])
        )
        grad_stream, grad_gain, grad_shift = norm_pull(grad_normed)
        grad_send = (grad_in_wide + grad_stream).astype(narrow_type)
        grad_bank = jnp.concatenate(
            [
                product_left(normed_low, grad_queries),
                product_left(normed_low, grad_keys),
                product_left(normed_low, grad_values),
                grad_w_out,
            ],
            axis=0,
        )
        bias_rows = jnp.stack(
            [
                jnp.sum(grad_queries.astype(wide_type), axis=0),
                jnp.sum(grad_values.astype(wide_type), axis=0),
                jnp.sum(grad_in_wide, axis=0),
            ]
        )
        smalls = (
            small_zero[:6]
            + (
                jnp.zeros((2, D), wide_type).at[0].set(grad_gain),
                jnp.zeros((2, D), wide_type).at[0].set(grad_shift),
                bias_rows,
            )
            + small_zero[9:]
        )
        return (grad_send, grad_bank, smalls, zeros_pixels)

    def backward_first(operands):
        (
            first_kept,
            second_kept,
            grad_in,
            pixel_rows,
            places,
            lead_time,
            segment,
            grad_rows,
            stash_items,
        ) = operands
        stream = first_kept.astype(wide_type)
        normed, norm_pull = jax.vjp(
            norm_layer, stream, norm_gain[1].astype(wide_type), norm_bias[1].astype(wide_type)
        )
        normed_low = normed.astype(narrow_type)
        inners, actives, partial_sum = feed_half(normed_low, weights, fc1_bias[: 2 * D])
        grad_normed, grad_bank, grad_bias_in = feed_half_back(
            normed_low, weights, inners, actives, grad_rows
        )
        grad_stream, grad_gain, grad_shift = norm_pull(grad_normed + grad_in.astype(wide_type))
        grad_send = (grad_rows.astype(wide_type) + grad_stream).astype(narrow_type)
        smalls = small_zero[:6] + (
            jnp.zeros((2, D), wide_type).at[1].set(grad_gain),
            jnp.zeros((2, D), wide_type).at[1].set(grad_shift),
            small_zero[8],
            jnp.zeros((FF,), wide_type).at[: 2 * D].set(grad_bias_in),
            small_zero[10],
        )
        return (grad_send, grad_bank, smalls, zeros_pixels)

    def backward_second(operands):
        (
            first_kept,
            second_kept,
            grad_in,
            pixel_rows,
            places,
            lead_time,
            segment,
            grad_rows,
            stash_items,
        ) = operands
        inners, actives, partial_sum = feed_half(first_kept, weights, fc1_bias[2 * D :])
        grad_normed, grad_bank, grad_bias_in = feed_half_back(
            first_kept, weights, inners, actives, grad_rows
        )
        smalls = small_zero[:9] + (
            jnp.zeros((FF,), wide_type).at[2 * D :].set(grad_bias_in),
            jnp.sum(grad_rows.astype(wide_type), axis=0),
        )
        return (grad_normed.astype(narrow_type), grad_bank, smalls, zeros_pixels)

    def backward_none(operands):
        return (zeros_stream, jnp.zeros((4 * D, D), wide_type), small_zero, zeros_pixels)

    forward_list = [forward_embed, forward_attend, forward_first, forward_second, forward_none]
    backward_list = [
        backward_embed,
        backward_attend,
        backward_first,
        backward_second,
        backward_none,
    ]
    tick_total = micro_total + section_total - 1
    first_message, second_message = (zeros_stream, zeros_stream)
    kept_first = jnp.zeros((micro_total, row_count, D), narrow_type)
    kept_second = jnp.zeros((micro_total, row_count, D), narrow_type)
    stash_all = tuple(
        (
            jnp.zeros((micro_total,) + array_item.shape, array_item.dtype)
            for array_item in stash_zero
        )
    )
    final_all = jnp.zeros((micro_total, row_count, D), wide_type)
    for tick_number in range(tick_total):
        micro_index = tick_number - section_index
        running = jnp.logical_and(micro_index >= 0, micro_index < micro_total)
        slot_index = jnp.clip(micro_index, 0, micro_total - 1)
        kept_first = kept_first.at[slot_index].set(
            jnp.where(running, first_message, kept_first[slot_index])
        )
        kept_second = kept_second.at[slot_index].set(
            jnp.where(running, second_message, kept_second[slot_index])
        )
        branch = jnp.where(running, section_index, section_total)
        operands = (
            first_message,
            second_message,
            patches[slot_index],
            places_all[slot_index],
            lead_times[slot_index, 0],
            segments[slot_index],
        )
        first_out, second_out, final_rows, stash_items = lax.switch(branch, forward_list, operands)
        final_all = final_all.at[slot_index].add(final_rows)
        stash_all = tuple(
            (
                buffer.at[slot_index].set(jnp.where(running, array_item, buffer[slot_index]))
                for buffer, array_item in zip(stash_all, stash_items)
            )
        )
        if tick_number < tick_total - 1:
            first_message, second_message = (
                from_behind(shortened(first_out), "section", 1).astype(first_out.dtype),
                from_behind(shortened(second_out), "section", 1).astype(second_out.dtype),
            )
    grad_message = zeros_stream
    bank_total = jnp.zeros((4 * D, D), wide_type)
    small_total = small_zero
    pixel_total = jnp.zeros((micro_total, row_count, VARS * PIX), wide_type)
    for tick_number in range(tick_total):
        micro_index = tick_number - (section_total - 1 - section_index)
        running = jnp.logical_and(micro_index >= 0, micro_index < micro_total)
        slot_index = jnp.clip(micro_index, 0, micro_total - 1)
        branch = jnp.where(running, section_index, section_total)
        operands = (
            kept_first[slot_index],
            kept_second[slot_index],
            grad_message,
            patches[slot_index],
            places_all[slot_index],
            lead_times[slot_index, 0],
            segments[slot_index],
            grad_out_all[slot_index],
            tuple((buffer[slot_index] for buffer in stash_all)),
        )
        grad_send, grad_bank, smalls, grad_pixels = lax.switch(branch, backward_list, operands)
        bank_total = bank_total + grad_bank
        small_total = tuple(
            (total_item + sum_item for total_item, sum_item in zip(small_total, smalls))
        )
        pixel_total = pixel_total.at[slot_index].add(grad_pixels)
        if tick_number < tick_total - 1:
            grad_message = jax.tree.map(
                lambda part, own: part.astype(own.dtype),
                from_behind(shortened(grad_send), "section", -1),
                grad_send,
            )
    bank_share = lax.psum_scatter(
        bank_total.astype(jnp.bfloat16), "dp", scatter_dimension=0, tiled=True
    ).astype(jnp.float32)[None]
    small_sums = lax.psum(small_total, ("section", "dp"))
    output_share, pixel_share = (
        lax.psum_scatter(
            final_all.astype(jnp.bfloat16), "section", scatter_dimension=2, tiled=True
        ).astype(jnp.float32),
        lax.psum_scatter(
            pixel_total.astype(jnp.bfloat16), "section", scatter_dimension=2, tiled=True
        ).astype(jnp.float32),
    )
    output_low = output_share.astype(narrow_type)
    return (output_low, pixel_share, bank_share) + tuple(small_sums)


def solution(mesh):
    ins, outs = specs()
    small_slice = mesh.shape["section"] == 4 and mesh.shape["dp"] == 8
    body = on_device_fast if small_slice else on_device
    return jax.shard_map(body, mesh=mesh, in_specs=ins, out_specs=outs, check_vma=False)
```
